32 devices in a mesh: dp: 16 (over z, y, core), tensor: 2 (over x).
Axes of the slice: x: 2, y: 2, z: 4, core: 2. Of those that a mesh axis runs over, the one named last changes fastest.
Arguments:
- tokens: bfloat16 [8192, 1024], P(('dp', 'tensor')), may hold values from -6 to 6
- lengths: int32 [32], P(('dp', 'tensor')), may hold values from 64 to 256, as said below
- cotangent: bfloat16 [8192, 1024], P(('dp', 'tensor')), may hold values from -6 to 6
- norm_gain: float32 [1024], replicated, may hold values from 0.5 to 1.5
- w_query: bfloat16 [1024, 512], P(None, 'tensor'), may hold values from -0.1875 to 0.1875
- w_key: bfloat16 [1024, 128], replicated, may hold values from -0.1875 to 0.1875
- w_value: bfloat16 [1024, 128], replicated, may hold values from -0.1875 to 0.1875
- w_gate_z: bfloat16 [1024, 1536], P(None, 'tensor'), may hold values from -0.1875 to 0.1875
- w_ssm_x: bfloat16 [1024, 1536], P(None, 'tensor'), may hold values from -0.1875 to 0.1875
- w_ssm_b: bfloat16 [1024, 128], replicated, may hold values from -0.1875 to 0.1875
- w_ssm_c: bfloat16 [1024, 128], replicated, may hold values from -0.1875 to 0.1875
- w_step: bfloat16 [1024, 24], P(None, 'tensor'), may hold values from -0.1875 to 0.1875
- conv_x_weight: float32 [4, 1536], P(None, 'tensor'), may hold values from -3 to 3
- conv_x_bias: float32 [1536], P('tensor'), may hold values from -0.5 to 0.5
- conv_bc_weight: float32 [4, 256], replicated, may hold values from -3 to 3
- conv_bc_bias: float32 [256], replicated, may hold values from -0.5 to 0.5
- step_bias: float32 [24], P('tensor'), may hold values from -6.9 to -2.3
- decay_log: float32 [24], P('tensor'), may hold values from 0 to 2.77
- skip_gain: float32 [24], P('tensor'), may hold values from 0.5 to 1.5
- ssm_norm_gain: float32 [1536], P('tensor'), may hold values from 0.5 to 1.5
- w_out_att: bfloat16 [512, 1024], P('tensor'), may hold values from -0.75 to 0.75
- w_out_ssm: bfloat16 [1536, 1024], P('tensor'), may hold values from -0.15625 to 0.15625
- ffn_norm_gain: float32 [1024], replicated, may hold values from 0.5 to 1.5
- w_gate: bfloat16 [1024, 2048], P(None, 'tensor'), may hold values from -0.1875 to 0.1875
- w_up: bfloat16 [1024, 2048], P(None, 'tensor'), may hold values from -0.1875 to 0.1875
- w_down: bfloat16 [2048, 1024], P('tensor'), may hold values from -0.125 to 0.125
Outputs:
- layer_output: bfloat16 [8192, 1024], P(('dp', 'tensor'))
- grad_input: float32 [8192, 1024], P(('dp', 'tensor'))
- grad_norm_gain: float32 [1024], replicated
- grad_w_query: float32 [1024, 512], P(None, 'tensor')
- grad_w_key: float32 [1024, 128], replicated
- grad_w_value: float32 [1024, 128], replicated
- grad_w_gate_z: float32 [1024, 1536], P(None, 'tensor')
- grad_w_ssm_x: float32 [1024, 1536], P(None, 'tensor')
- grad_w_ssm_b: float32 [1024, 128], replicated
- grad_w_ssm_c: float32 [1024, 128], replicated
- grad_w_step: float32 [1024, 24], P(None, 'tensor')
- grad_conv_x_weight: float32 [4, 1536], P(None, 'tensor')
- grad_conv_x_bias: float32 [1536], P('tensor')
- grad_conv_bc_weight: float32 [4, 256], replicated
- grad_conv_bc_bias: float32 [256], replicated
- grad_step_bias: float32 [24], P('tensor')
- grad_decay_log: float32 [24], P('tensor')
- grad_skip_gain: float32 [24], P('tensor')
- grad_ssm_norm_gain: float32 [1536], P('tensor')
- grad_w_out_att: float32 [512, 1024], P('tensor')
- grad_w_out_ssm: float32 [1536, 1024], P('tensor')
- grad_ffn_norm_gain: float32 [1024], replicated
- grad_w_gate: float32 [1024, 2048], P(None, 'tensor')
- grad_w_up: float32 [1024, 2048], P(None, 'tensor')
- grad_w_down: float32 [2048, 1024], P('tensor')
The draws below stay inside these ranges and needn't reach their ends.
Inputs may be any that keep to these rules, and one draw needn't show every extreme that they name: Tokens of a sequence fill its first lengths slots; the rest are padding. Some sequence has exactly 256 tokens and some exactly 64.
All inputs are finite; a program needn't handle non-finite values.
Results may differ from the reference program's by a relative error of at most 0.029.
Values may be sent and summed in bfloat16 or wider, within the bound.
A program may use at most 192 MiB of HBM per device.

```python
import math
import jax
import jax.numpy as jnp
from jax import lax

D = 1024
HEADS = 8
KV_HEADS = 2
HEAD_DIM = 64
SSM_HEADS = 24
SSM_DIM = 64
STATE = 128
CONV = 4
FF = 2048
LEN = 256
SPAN = 128
SEQS = 32
TOKENS = 8192
ATT_WIDTH = 512
KV_WIDTH = 128
SSM_WIDTH = 1536


def draw_lengths(key, part):
    key = jax.random.fold_in(key, 7)
    first_key, second_key = jax.random.split(key)
    drawn = jax.random.randint(first_key, (SEQS,), LEN // 4, LEN + 1)
    order = jax.random.permutation(second_key, SEQS)
    drawn = drawn.at[order[0]].set(LEN)
    drawn = drawn.at[order[1]].set(LEN // 4)
    return drawn.astype(jnp.int32)


def block_scale(key, extent, shards, smallest, largest):
    level, own = 1.0, jax.random.fold_in(key, 6)
    for dim, parts in shards:
        heights = jnp.exp(jax.random.uniform(jax.random.fold_in(own, dim), (parts,), jnp.float32, smallest / len(shards), largest / len(shards)))
        level = level * jnp.repeat(heights, extent[dim] // parts).reshape([-1 if axis == dim else 1 for axis in range(len(extent))])
    return level


def scatter_about(rng, shape, scale, bound, pieces=(), dtype=jnp.bfloat16):
    level = block_scale(rng, shape, pieces, -0.22, 0.18) if pieces else 1.0
    entries = jax.random.normal(rng, shape, jnp.float32) * scale * level
    return jnp.minimum(jnp.maximum(entries, -bound), bound).astype(dtype)


def setup_inputs(seed: int = 0) -> dict:
    arg_keys = jax.random.split(jax.random.key(seed), 27)
    tokens = scatter_about(arg_keys[0], (TOKENS, D), 1.0, 6.0, ((0, 32),))
    lengths = draw_lengths(jax.random.fold_in(arg_keys[26], 71), 0)
    cotangent = scatter_about(arg_keys[2], (TOKENS, D), 1.0, 6.0, ((0, 32),))
    norm_gain = jnp.clip(1.0 + 0.1 * jax.random.normal(arg_keys[3], (D,), jnp.float32), 0.5, 1.5)
    w_query = scatter_about(arg_keys[4], (D, ATT_WIDTH), D ** -0.5, 0.1875, ((1, 2),))
    w_key = scatter_about(arg_keys[5], (D, KV_WIDTH), D ** -0.5, 0.1875)
    w_value = scatter_about(arg_keys[6], (D, KV_WIDTH), D ** -0.5, 0.1875)
    w_gate_z = scatter_about(arg_keys[7], (D, SSM_WIDTH), D ** -0.5, 0.1875, ((1, 2),))
    w_ssm_x = scatter_about(arg_keys[8], (D, SSM_WIDTH), D ** -0.5, 0.1875, ((1, 2),))
    w_ssm_b = scatter_about(arg_keys[9], (D, STATE), D ** -0.5, 0.1875)
    w_ssm_c = scatter_about(arg_keys[10], (D, STATE), D ** -0.5, 0.1875)
    w_step = scatter_about(arg_keys[11], (D, SSM_HEADS), D ** -0.5, 0.1875, ((1, 2),))
    conv_x_weight = scatter_about(arg_keys[12], (CONV, SSM_WIDTH), CONV ** -0.5, 3.0, ((1, 2),), jnp.float32)
    conv_x_bias = jnp.clip(jax.random.uniform(arg_keys[13], (SSM_WIDTH,), jnp.float32, -0.5, 0.5) * block_scale(arg_keys[13], (SSM_WIDTH,), ((0, 2),), -0.4, 0.0), -0.5, 0.5)
    conv_bc_weight = scatter_about(arg_keys[14], (CONV, 2 * STATE), CONV ** -0.5, 3.0, (), jnp.float32)
    conv_bc_bias = jnp.clip(jax.random.uniform(arg_keys[15], (2 * STATE,), jnp.float32, -0.5, 0.5), -0.5, 0.5)
    step_bias = jnp.clip(-6.9 + 4.6000001430511475 * jax.random.uniform(arg_keys[16], (SSM_HEADS,), jnp.float32) ** block_scale(arg_keys[16], (SSM_HEADS,), ((0, 2),), -0.2, 0.2), -6.9, -2.3)
    decay_log = jnp.clip(2.77 * jax.random.uniform(arg_keys[17], (SSM_HEADS,), jnp.float32) ** block_scale(arg_keys[17], (SSM_HEADS,), ((0, 2),), -0.2, 0.2), 0.0, 2.77)
    skip_gain = jnp.clip(0.5 + 1.0 * jax.random.uniform(arg_keys[18], (SSM_HEADS,), jnp.float32) ** block_scale(arg_keys[18], (SSM_HEADS,), ((0, 2),), -0.2, 0.2), 0.5, 1.5)
    ssm_norm_gain = jnp.clip(1.0 + 0.1 * jax.random.normal(arg_keys[19], (SSM_WIDTH,), jnp.float32), 0.5, 1.5)
    w_out_att = scatter_about(arg_keys[20], (ATT_WIDTH, D), HEAD_DIM ** -0.5, 0.75, ((0, 2),))
    w_out_ssm = scatter_about(arg_keys[21], (SSM_WIDTH, D), SSM_WIDTH ** -0.5, 0.15625, ((0, 2),))
    ffn_norm_gain = jnp.clip(1.0 + 0.1 * jax.random.normal(arg_keys[22], (D,), jnp.float32), 0.5, 1.5)
    w_gate = scatter_about(arg_keys[23], (D, FF), D ** -0.5, 0.1875, ((1, 2),))
    w_up = scatter_about(arg_keys[24], (D, FF), D ** -0.5, 0.1875, ((1, 2),))
    w_down = scatter_about(arg_keys[25], (FF, D), FF ** -0.5, 0.125, ((0, 2),))
    return {"tokens": tokens, "lengths": lengths, "cotangent": cotangent, "norm_gain": norm_gain, "w_query": w_query, "w_key": w_key, "w_value": w_value, "w_gate_z": w_gate_z, "w_ssm_x": w_ssm_x, "w_ssm_b": w_ssm_b, "w_ssm_c": w_ssm_c, "w_step": w_step, "conv_x_weight": conv_x_weight, "conv_x_bias": conv_x_bias, "conv_bc_weight": conv_bc_weight, "conv_bc_bias": conv_bc_bias, "step_bias": step_bias, "decay_log": decay_log, "skip_gain": skip_gain, "ssm_norm_gain": ssm_norm_gain, "w_out_att": w_out_att, "w_out_ssm": w_out_ssm, "ffn_norm_gain": ffn_norm_gain, "w_gate": w_gate, "w_up": w_up, "w_down": w_down}


EPSILON = 1e-05
ROPE_BASE = 100000000000.0
HIGHEST = lax.Precision.HIGHEST

@jax.custom_vjp
def low(v):
    return lax.optimization_barrier(v.astype(jnp.bfloat16)).astype(jnp.float32)

@jax.custom_vjp
def low_back(v):
    return v

def low_keep(v):
    return (low(v), None)

def low_pass(kept, grad):
    return (grad,)

def back_keep(v):
    return (v, None)

def back_low(kept, grad):
    return (low(grad),)
low.defvjp(low_keep, low_pass)
low_back.defvjp(back_keep, back_low)

def matmul(left, right):
    return jnp.dot(left, right, precision=HIGHEST)

def rms_norm(values, gain):
    return values * lax.rsqrt(lax.optimization_barrier(jnp.mean(values * values, axis=-1, keepdims=True)) + EPSILON) * gain

def rope_turn(values, positions):
    head_width = values.shape[-1]
    half_width = head_width // 2
    freqs = ROPE_BASE ** (-(jnp.arange(half_width).astype(jnp.float32) * 2.0 / head_width))
    angles = positions[:, None] * freqs[None, :]
    cosine = jnp.cos(angles)[:, None, :]
    sine = jnp.sin(angles)[:, None, :]
    first_half = values[..., :half_width]
    second_half = values[..., half_width:]
    return jnp.concatenate([first_half * cosine - second_half * sine, second_half * cosine + first_half * sine], axis=-1)

def causal_conv(values, weight, bias):
    taps = weight.shape[0]
    seq_steps = values.shape[0]
    padded = jnp.pad(values, ((taps - 1, 0), (0, 0)))
    total = bias[None, :] + jnp.zeros_like(values)
    for offset in range(taps):
        total = total + weight[offset][None, :] * padded[offset:offset + seq_steps]
    return total

def ssd_scan(inputs, step_sizes, rate_vec, in_map, out_map):
    seq_steps, num_heads, head_width = inputs.shape
    state_size = in_map.shape[1]
    blocks = seq_steps // SPAN
    log_decay = (-(step_sizes * rate_vec[None, :])).reshape(blocks, SPAN, num_heads)
    cumulative = jnp.cumsum(log_decay, axis=1)
    weighted = (inputs * step_sizes[:, :, None]).reshape(blocks, SPAN, num_heads, head_width)
    in_blocks = in_map.reshape(blocks, SPAN, state_size)
    out_blocks = out_map.reshape(blocks, SPAN, state_size)
    lower_mask = (jnp.arange(SPAN)[:, None] >= jnp.arange(SPAN)[None, :])[None, :, :, None]
    differ = cumulative[:, :, None, :] - cumulative[:, None, :, :]
    decay_mat = jnp.where(lower_mask, jnp.exp(jnp.where(lower_mask, differ, 0.0)), 0.0)
    affinity = jnp.einsum('cin,cjn->cij', out_blocks, in_blocks, precision=HIGHEST)
    inner_part = jnp.einsum('cijh,cjhp->cihp', affinity[:, :, :, None] * decay_mat, weighted, precision=HIGHEST)
    last_log = cumulative[:, -1, :]
    to_end = jnp.exp(last_log[:, None, :] - cumulative)
    block_states = jnp.einsum('cjhp,cjn->chpn', weighted * to_end[:, :, :, None], in_blocks, precision=HIGHEST)

    def carry_step(carried, scan_item):
        block_log, block_state = scan_item
        return (jnp.exp(block_log)[:, None, None] * carried + block_state, carried)
    start_state = jnp.zeros((num_heads, head_width, state_size), jnp.float32)
    _, entering = lax.scan(carry_step, start_state, (last_log, block_states))
    outer_part = jnp.einsum('cin,chpn->cihp', out_blocks, entering, precision=HIGHEST) * jnp.exp(cumulative)[:, :, :, None]
    return (inner_part + outer_part).reshape(seq_steps, num_heads, head_width)

def attend(queries, keys, values, key_mask):
    repeat_count = HEADS // KV_HEADS
    key_heads = jnp.repeat(keys, repeat_count, axis=1)
    value_heads = jnp.repeat(values, repeat_count, axis=1)
    seq_steps = queries.shape[0]
    scores = low_back(jnp.einsum('qhd,khd->hqk', queries, key_heads, precision=HIGHEST) * HEAD_DIM ** (-0.5))
    allowed = (jnp.arange(seq_steps)[:, None] >= jnp.arange(seq_steps)[None, :]) & (key_mask[None, :] > 0.5)
    scores = jnp.where(allowed[None], scores, -1e+30)
    softmaxed = jax.nn.softmax(scores, axis=-1)
    return jnp.einsum('hqk,khd->qhd', low(softmaxed), value_heads, precision=HIGHEST)

def layer(rows_in, seq_mask, weights):
    gain_one, wq, wk, wv, wz, wx, wb, wc, wdt, conv_xw, conv_xb, conv_bcw, conv_bcb, bias_step, log_rate, skip_vec, ssm_gain, wo_att, wo_ssm, gain_two, wg, wu, wd = weights
    num_seqs, seq_steps = seq_mask.shape
    positions = jnp.arange(seq_steps).astype(jnp.float32)
    first_normed = low(rms_norm(rows_in, gain_one))
    query_proj = low_back(matmul(first_normed, wq)).reshape(num_seqs, seq_steps, HEADS, HEAD_DIM)
    key_proj = low_back(matmul(first_normed, wk)).reshape(num_seqs, seq_steps, KV_HEADS, HEAD_DIM)
    value_proj = low(low_back(matmul(first_normed, wv))).reshape(num_seqs, seq_steps, KV_HEADS, HEAD_DIM)
    query_turned = low(jax.vmap(rope_turn, in_axes=(0, None))(query_proj, positions))
    key_turned = low(jax.vmap(rope_turn, in_axes=(0, None))(key_proj, positions))
    att_out = jax.vmap(jax.checkpoint(attend))(query_turned, key_turned, value_proj, seq_mask)
    gate_proj = low_back(matmul(first_normed, wz))
    x_proj = low_back(matmul(first_normed, wx)).reshape(num_seqs, seq_steps, SSM_HEADS * SSM_DIM)
    map_proj = low_back(jnp.concatenate([matmul(first_normed, wb), matmul(first_normed, wc)], axis=1))
    step_proj = low_back(matmul(first_normed, wdt)).reshape(num_seqs, seq_steps, SSM_HEADS)
    conv_x = jax.nn.silu(jax.vmap(causal_conv, in_axes=(0, None, None))(x_proj, conv_xw, conv_xb))
    maps = low(jax.nn.silu(jax.vmap(causal_conv, in_axes=(0, None, None))(map_proj.reshape(num_seqs, seq_steps, 2 * STATE), conv_bcw, conv_bcb)))
    step_sizes = jax.nn.softplus(step_proj + bias_step) * seq_mask[:, :, None]
    heads_view = conv_x.reshape(num_seqs, seq_steps, SSM_HEADS, SSM_DIM)
    scanned = jax.vmap(jax.checkpoint(ssd_scan), in_axes=(0, 0, None, 0, 0))(heads_view, step_sizes, jnp.exp(log_rate), maps[:, :, :STATE], maps[:, :, STATE:])
    ssm_out = scanned + skip_vec[None, None, :, None] * heads_view
    gated = ssm_out.reshape(num_seqs * seq_steps, SSM_HEADS * SSM_DIM) * jax.nn.silu(gate_proj)
    ssm_normed = gated * lax.rsqrt(lax.optimization_barrier(jnp.mean(gated * gated, axis=-1, keepdims=True)) + EPSILON) * ssm_gain
    mix_att = low(low_back(att_out.reshape(num_seqs * seq_steps, HEADS * HEAD_DIM)))
    mix_ssm = low(low_back(ssm_normed))
    branch = low_back(matmul(mix_att, wo_att) + matmul(mix_ssm, wo_ssm))
    resid = rows_in + branch
    second_normed = low(rms_norm(resid, gain_two))
    gate_vals = low_back(matmul(second_normed, wg))
    up_vals = low_back(matmul(second_normed, wu))
    hidden = low(low_back(jax.nn.silu(gate_vals) * up_vals))
    return resid + matmul(hidden, wd)

def reference(tokens, lengths, cotangent, norm_gain, w_query, w_key, w_value, w_gate_z, w_ssm_x, w_ssm_b, w_ssm_c, w_step, conv_x_weight, conv_x_bias, conv_bc_weight, conv_bc_bias, step_bias, decay_log, skip_gain, ssm_norm_gain, w_out_att, w_out_ssm, ffn_norm_gain, w_gate, w_up, w_down):
    params = tuple((array_in.astype(jnp.float32) for array_in in (norm_gain, w_query, w_key, w_value, w_gate_z, w_ssm_x, w_ssm_b, w_ssm_c, w_step, conv_x_weight, conv_x_bias, conv_bc_weight, conv_bc_bias, step_bias, decay_log, skip_gain, ssm_norm_gain, w_out_att, w_out_ssm, ffn_norm_gain, w_gate, w_up, w_down)))
    num_seqs = lengths.shape[0]
    per_block = math.gcd(num_seqs, max(1, 4096 // LEN))
    num_blocks = num_seqs // per_block
    seq_mask = (jnp.arange(LEN)[None, :] < lengths[:, None]).astype(jnp.float32)
    rows_all = tokens.astype(jnp.float32).reshape(num_blocks, per_block * LEN, D)
    cot_all = (cotangent.astype(jnp.float32) * seq_mask.reshape(-1)[:, None]).reshape(num_blocks, per_block * LEN, D)
    mask_all = seq_mask.reshape(num_blocks, per_block, LEN)

    def block_step(totals, block):
        block_rows, block_mask, block_cot = block

        def forward(row_vals, *weights):
            return layer(row_vals, block_mask, weights)
        result, pull_back = jax.vjp(forward, block_rows, *params)
        pulled = pull_back(block_cot)
        new_totals = tuple((acc + fresh for acc, fresh in zip(totals, pulled[1:])))
        return (new_totals, (result.astype(jnp.bfloat16), pulled[0]))
    zero_grads = tuple((jnp.zeros_like(param) for param in params))
    totals, (outputs, input_grads) = lax.scan(block_step, zero_grads, (rows_all, mask_all, cot_all))
    g_norm, g_query, g_key, g_value, g_gate_z, g_ssm_x, g_ssm_b, g_ssm_c, g_step, g_cxw, g_cxb, g_cbw, g_cbb, g_sbias, g_dlog, g_skip, g_sgain, g_oatt, g_ossm, g_ffn_gain, g_gate, g_up, g_down = totals
    return (outputs.reshape(num_seqs * LEN, D), input_grads.reshape(num_seqs * LEN, D), g_norm, g_query, g_key, g_value, g_gate_z, g_ssm_x, g_ssm_b, g_ssm_c, g_step, g_cxw, g_cxb, g_cbw, g_cbb, g_sbias, g_dlog, g_skip, g_sgain, g_oatt, g_ossm, g_ffn_gain, g_gate, g_up, g_down)
```

```python
import functools

import jax
import jax.numpy as jnp
from jax import lax
from jax.experimental import pallas as pl
from jax.experimental.pallas import tpu as pltpu
from jax.sharding import PartitionSpec as P

HEADS = 8
KV_HEADS = 2
HEAD_DIM = 64
SSM_HEADS = 24
SSM_DIM = 64
STATE = 128
SPAN = 128
LANES = 128

EPSILON = 1e-05
ROPE_BASE = 100000000000.0
F32 = jnp.float32
BF16 = jnp.bfloat16
VMEM_LIMIT = 50 * 1024 * 1024


def mm(left, right):
    return jnp.dot(left, right, preferred_element_type=F32)


def mm_nt(left, right):
    return lax.dot_general(left, right, (((1,), (1,)), ((), ())), preferred_element_type=F32)


def mm_tn(left, right):
    return lax.dot_general(left, right, (((0,), (0,)), ((), ())), preferred_element_type=F32)


def pieces(values, count):
    terms = []
    for _ in range(count):
        term = values.astype(BF16)
        terms.append(term)
        values = values - term.astype(F32)
    return terms


def sigmoid(values):
    return 1.0 / (1.0 + jnp.exp(-values))


def softplus(values):
    return jnp.maximum(values, 0.0) + jnp.log1p(jnp.exp(-jnp.abs(values)))


def lane_ids(shape):
    return lax.broadcasted_iota(jnp.int32, shape, 1)


def row_ids(shape):
    return lax.broadcasted_iota(jnp.int32, shape, 0)


def repeat_lanes(column, count):
    return jnp.concatenate([column] * count, axis=1) if count > 1 else column


def column_of(row):
    ones = jnp.where(row_ids((16, LANES)) == 0, 1.0, 0.0).astype(BF16)
    total = None
    for term in pieces(row, 3):
        part = mm_tn(term, ones)
        total = part if total is None else total + part
    return total


def row_sums(values):
    ones = jnp.ones((16, values.shape[1]), BF16)
    high, low = pieces(values, 2)
    return mm_nt(ones, high) + mm_nt(ones, low)


def causal_shift(values, steps):
    if steps == 0:
        return values
    rolled = pltpu.roll(values, steps, 0)
    return jnp.where(row_ids(values.shape) >= steps, rolled, 0.0)


def anti_shift(values, steps):
    if steps == 0:
        return values
    length = values.shape[0]
    rolled = pltpu.roll(values, length - steps, 0)
    return jnp.where(row_ids(values.shape) < length - steps, rolled, 0.0)


def conv(values, weight, bias):
    taps = weight.shape[0]
    total = bias + weight[taps - 1 : taps] * values
    for offset in range(taps - 1):
        total = total + weight[offset : offset + 1] * causal_shift(values, taps - 1 - offset)
    return total


def conv_back(grad, values, weight):
    taps = weight.shape[0]
    total, rows = None, []
    for offset in range(taps):
        steps = taps - 1 - offset
        moved = anti_shift(grad, steps)
        part = weight[offset : offset + 1] * moved
        total = part if total is None else total + part
        rows.append(jnp.sum(moved * values, axis=0, keepdims=True))
    rows.append(jnp.sum(grad, axis=0, keepdims=True))
    return total, rows


def rope(values, cosine, sine_first, sine_second):
    ahead = pltpu.roll(values, LANES - HEAD_DIM // 2, 1)
    behind = pltpu.roll(values, HEAD_DIM // 2, 1)
    return values * cosine + ahead * sine_first + behind * sine_second


def lower_mask():
    return row_ids((SPAN, SPAN)) >= lane_ids((SPAN, SPAN))


def span_sums(values):
    lower = jnp.where(lower_mask(), 1.0, 0.0).astype(BF16)
    out = []
    for start in range(0, values.shape[0], SPAN):
        total = None
        for term in pieces(values[start : start + SPAN], 3):
            part = mm(lower, term)
            total = part if total is None else total + part
        out.append(total)
    return jnp.concatenate(out, axis=0)


def span_sums_rows(values):
    upper = jnp.where(row_ids((SPAN, SPAN)) <= lane_ids((SPAN, SPAN)), 1.0, 0.0).astype(BF16)
    out = []
    for start in range(0, values.shape[1], SPAN):
        total = None
        for term in pieces(values[:, start : start + SPAN], 3):
            part = mm(term, upper)
            total = part if total is None else total + part
        out.append(total)
    return jnp.concatenate(out, axis=1)


def span_sums_back(values):
    upper = jnp.where(row_ids((SPAN, SPAN)) <= lane_ids((SPAN, SPAN)), 1.0, 0.0).astype(BF16)
    out = []
    for start in range(0, values.shape[0], SPAN):
        total = None
        for term in pieces(values[start : start + SPAN], 3):
            part = mm(upper, term)
            total = part if total is None else total + part
        out.append(total)
    return jnp.concatenate(out, axis=0)


def steps_of(tp, tp_row, bias, bias_col, rate, rate_col, length):
    seq_len = tp.shape[0]
    valid = jnp.where(row_ids((seq_len, 1)) < length, 1.0, 0.0)
    valid_row = jnp.where(lane_ids((1, seq_len)) < length, 1.0, 0.0)
    dt = softplus(tp + bias) * valid
    dt_row = softplus(tp_row + bias_col) * valid_row
    cum = span_sums(-(dt * rate))
    cum_row = span_sums_rows(-(dt_row * rate_col))
    return valid, dt, cum, cum_row


def spread(values, head):
    return jnp.broadcast_to(values[:, head : head + 1], (values.shape[0], LANES))


def decays(cum_first, cum_second, cum_row, pair, span):
    rows = slice(span * SPAN, (span + 1) * SPAN)
    lower = lower_mask()
    out = []
    for head, column in ((2 * pair, cum_first), (2 * pair + 1, cum_second)):
        differ = column[rows] - cum_row[head : head + 1, rows]
        out.append(jnp.exp(jnp.where(lower, differ, -1e30)))
    return out


def split_heads(values):
    first = lane_ids(values.shape) < HEAD_DIM
    zero = jnp.zeros_like(values)
    return jnp.concatenate([jnp.where(first, values, zero), jnp.where(first, zero, values)], axis=0)


def state_of(in_map, weighted_first, cum_pair_first):
    to_end = jnp.exp(cum_pair_first[SPAN - 1 : SPAN] - cum_pair_first)
    ending = (weighted_first * to_end).astype(BF16)
    return to_end, ending, mm_tn(in_map[:SPAN], ending)


def mixer_forward_kernel(
    len_ref, h_ref, wq_ref, wkv_ref, wz_ref, wx_ref, wb_ref, wc_ref, wt_ref, cxw_ref, cxb_ref,
    cbw_ref, cbb_ref, bias_ref, rate_ref, bias_col_ref, rate_col_ref, skip_ref, cos_ref, sa_ref,
    sb_ref, q_ref, kd_ref, vd_ref, z_ref, x_ref, bcp_ref, bc_ref, tp_ref, tpr_ref, y_ref, ss_ref,
):
    h = h_ref[...]
    pairs = wx_ref.shape[1] // LANES
    z_ref[...] = mm(h, wz_ref[...])
    x_ref[...] = mm(h, wx_ref[...])
    bcp_ref[:, :STATE] = mm(h, wb_ref[...])
    bcp_ref[:, STATE:] = mm(h, wc_ref[...])
    tp = mm_nt(h, wt_ref[...])
    tp_row = mm_nt(wt_ref[...], h)
    tp_ref[...] = tp
    tpr_ref[...] = tp_row
    cosine, sine_first, sine_second = cos_ref[...], sa_ref[...], sb_ref[...]
    for pair in range(wq_ref.shape[1] // LANES):
        lanes = slice(pair * LANES, (pair + 1) * LANES)
        q_ref[:, lanes] = rope(mm(h, wq_ref[:, lanes]), cosine, sine_first, sine_second).astype(BF16)
    kv = mm(h, wkv_ref[...])
    turned = pltpu.roll(kv, HEAD_DIM, 1)
    first = lane_ids(kv.shape) < HEAD_DIM
    kd_ref[...] = rope(jnp.where(first, kv, turned), cosine, sine_first, sine_second).astype(BF16)
    vd_ref[...] = jnp.where(first, turned, kv).astype(BF16)

    mapped = conv(bcp_ref[...], cbw_ref[...], cbb_ref[...])
    bc = (mapped * sigmoid(mapped)).astype(BF16)
    bc_ref[...] = bc
    in_map, out_map = bc[:, :STATE], bc[:, STATE:]
    affinity = [
        mm_nt(out_map[s * SPAN : (s + 1) * SPAN], in_map[s * SPAN : (s + 1) * SPAN]) for s in range(2)
    ]
    _, dt, cum, cum_row = steps_of(
        tp, tp_row, bias_ref[...], bias_col_ref[...], rate_ref[...], rate_col_ref[...], len_ref[0]
    )
    squares = None
    for pair in range(pairs):
        lanes = slice(pair * LANES, (pair + 1) * LANES)
        cx = conv(x_ref[:, lanes], cxw_ref[:, lanes], cxb_ref[:, lanes])
        xc = cx * sigmoid(cx)
        dt_pair = jnp.where(first, spread(dt, 2 * pair), spread(dt, 2 * pair + 1))
        cum_first, cum_second = spread(cum, 2 * pair), spread(cum, 2 * pair + 1)
        cum_pair = jnp.where(first, cum_first, cum_second)
        weighted = xc * dt_pair
        low = weighted.astype(BF16)
        _, _, state = state_of(in_map, weighted[:SPAN], cum_pair[:SPAN])
        parts = []
        for s in range(2):
            rows = slice(s * SPAN, (s + 1) * SPAN)
            mats = [
                (affinity[s] * decay).astype(BF16)
                for decay in decays(cum_first, cum_second, cum_row, pair, s)
            ]
            part = mm(jnp.concatenate(mats, axis=1), split_heads(low[rows]))
            if s:
                part = part + mm(out_map[rows], state.astype(BF16)) * jnp.exp(cum_pair[rows])
            parts.append(part)
        y = jnp.concatenate(parts, axis=0)
        y_ref[:, lanes] = y
        z = z_ref[:, lanes]
        gated = (y + skip_ref[:, lanes] * xc) * (z * sigmoid(z))
        square = gated * gated
        squares = square if squares is None else squares + square
    ss_ref[...] = row_sums(squares)


def masked_probs(queries, kd, length, scale):
    seq_len = kd.shape[0]
    scores = mm_nt(split_heads(queries), kd) * scale
    rows = row_ids(scores.shape)
    rows = jnp.where(rows >= seq_len, rows - seq_len, rows)
    columns = lane_ids(scores.shape)
    scores = jnp.where((rows >= columns) & (columns < length), scores, -1e30)
    weights = jnp.exp(scores - jnp.max(scores, axis=1, keepdims=True))
    return weights / jnp.sum(weights, axis=1, keepdims=True)


def attend_kernel(len_ref, q_ref, kd_ref, vd_ref, out_ref):
    seq_len = q_ref.shape[0]
    values = split_heads(vd_ref[...])
    for pair in range(q_ref.shape[1] // LANES):
        lanes = slice(pair * LANES, (pair + 1) * LANES)
        probs = masked_probs(q_ref[:, lanes], kd_ref[...], len_ref[0], HEAD_DIM ** (-0.5)).astype(BF16)
        both = jnp.concatenate([probs[:seq_len], probs[seq_len:]], axis=1)
        out_ref[:, lanes] = mm(both, values).astype(BF16)


def join_halves(values):
    return values + pltpu.roll(values, HEAD_DIM, 1)


def attend_back_kernel(len_ref, q_ref, kd_ref, vd_ref, da_ref, cos_ref, sa_ref, sb_ref, dq_ref, dkv_ref):
    seq_len = q_ref.shape[0]
    scale = HEAD_DIM ** (-0.5)
    cosine, sine_first, sine_second = cos_ref[...], -sa_ref[...], -sb_ref[...]
    kd, vd = kd_ref[...], vd_ref[...]
    keys = split_heads(kd)
    grad_k, grad_v = None, None
    for pair in range(q_ref.shape[1] // LANES):
        lanes = slice(pair * LANES, (pair + 1) * LANES)
        probs = masked_probs(q_ref[:, lanes], kd, len_ref[0], scale)
        da = split_heads(da_ref[:, lanes])
        dprob = mm_nt(da, vd)
        dscore = (probs * (dprob - jnp.sum(probs * dprob, axis=1, keepdims=True))).astype(BF16)
        both = jnp.concatenate([dscore[:seq_len], dscore[seq_len:]], axis=1)
        dq = mm(both, keys) * scale
        dq_ref[:, lanes] = rope(dq, cosine, sine_first, sine_second).astype(BF16)
        part_k = mm_tn(dscore, split_heads(q_ref[:, lanes]))
        part_v = mm_tn(probs.astype(BF16), da)
        grad_k = part_k if grad_k is None else grad_k + part_k
        grad_v = part_v if grad_v is None else grad_v + part_v
    dk = rope(join_halves(grad_k) * scale, cosine, sine_first, sine_second)
    first = lane_ids(dk.shape) < HEAD_DIM
    dkv_ref[...] = jnp.where(first, dk, join_halves(grad_v)).astype(BF16)


def out_kernel(att_ref, y_ref, x_ref, z_ref, ss_ref, cxw_ref, cxb_ref, skip_ref, gain_ref, wa_ref, ws_ref,
               part_ref, mix_ref, *, width):
    total = mm(att_ref[...], wa_ref[...])
    inv = column_of(lax.rsqrt(ss_ref[...] / width + EPSILON))
    for pair in range(y_ref.shape[1] // LANES):
        lanes = slice(pair * LANES, (pair + 1) * LANES)
        cx = conv(x_ref[:, lanes], cxw_ref[:, lanes], cxb_ref[:, lanes])
        z = z_ref[:, lanes]
        gated = (y_ref[:, lanes] + skip_ref[:, lanes] * (cx * sigmoid(cx))) * (z * sigmoid(z))
        mix_ref[:, lanes] = (gated * inv * gain_ref[:, lanes]).astype(BF16)
    part_ref[...] = (total + mm(mix_ref[...], ws_ref[...])).astype(part_ref.dtype)


def mix_grad_kernel(db_ref, y_ref, x_ref, z_ref, cxw_ref, cxb_ref, skip_ref, gain_ref, wa_ref, ws_ref,
                    da_ref, dm_ref, bs_ref):
    db = db_ref[...]
    da_ref[...] = mm_nt(db, wa_ref[...]).astype(BF16)
    dm_ref[...] = mm_nt(db, ws_ref[...]).astype(BF16)
    total = None
    for pair in range(y_ref.shape[1] // LANES):
        lanes = slice(pair * LANES, (pair + 1) * LANES)
        cx = conv(x_ref[:, lanes], cxw_ref[:, lanes], cxb_ref[:, lanes])
        z = z_ref[:, lanes]
        gated = (y_ref[:, lanes] + skip_ref[:, lanes] * (cx * sigmoid(cx))) * (z * sigmoid(z))
        part = gated * (gain_ref[:, lanes] * dm_ref[:, lanes].astype(F32))
        total = part if total is None else total + part
    bs_ref[...] = row_sums(total)


def head_sums(values, pair):
    rows, columns = row_ids((LANES, 16)), lane_ids((LANES, 16))
    chosen = jnp.where(columns == 2 * pair + jnp.where(rows < HEAD_DIM, 0, 1), 1.0, 0.0).astype(BF16)
    high, low = pieces(values, 2)
    return mm(jnp.concatenate([high, low], axis=1), jnp.concatenate([chosen, chosen], axis=0))


def mixer_back_kernel(
    len_ref, dm_ref, y_ref, x_ref, z_ref, bcp_ref, bc_ref, tp_ref, tpr_ref, ss_ref, bs_ref, dq_ref,
    dkv_ref, wq_ref, wkv_ref, wz_ref, wx_ref, wb_ref, wc_ref, wt_ref, cxw_ref, cxb_ref, cbw_ref,
    cbb_ref, bias_ref, rate_ref, bias_col_ref, rate_col_ref, skip_ref, gain_ref,
    dh_ref, dx_ref, dz_ref, dbc_ref, dt_ref, wide_ref, bcg_ref, small_ref, *, width,
):
    pairs = x_ref.shape[1] // LANES
    bc = bc_ref[...]
    in_map, out_map = bc[:, :STATE], bc[:, STATE:]
    affinity = [
        mm_nt(out_map[s * SPAN : (s + 1) * SPAN], in_map[s * SPAN : (s + 1) * SPAN]) for s in range(2)
    ]
    valid, dt, cum, cum_row = steps_of(
        tp_ref[...], tpr_ref[...], bias_ref[...], bias_col_ref[...], rate_ref[...], rate_col_ref[...], len_ref[0]
    )
    inv_row = lax.rsqrt(ss_ref[...] / width + EPSILON)
    inv = column_of(inv_row)
    back = column_of(inv_row * inv_row * inv_row * bs_ref[...] / width)
    first = lane_ids((x_ref.shape[0], LANES)) < HEAD_DIM
    last_row = row_ids((SPAN, LANES)) == SPAN - 1
    d_cum, d_step = None, None
    d_aff, d_out, d_in = [None, None], None, None

    def plus(total, part):
        return part if total is None else total + part

    for pair in range(pairs):
        lanes = slice(pair * LANES, (pair + 1) * LANES)
        x = x_ref[:, lanes]
        cxw = cxw_ref[:, lanes]
        cx = conv(x, cxw, cxb_ref[:, lanes])
        sx = sigmoid(cx)
        xc = cx * sx
        z = z_ref[:, lanes]
        sz = sigmoid(z)
        silu_z = z * sz
        scanned = y_ref[:, lanes]
        y = scanned + skip_ref[:, lanes] * xc
        gated = y * silu_z
        d_mix = dm_ref[:, lanes].astype(F32)
        d_gated = inv * (gain_ref[:, lanes] * d_mix) - gated * back
        wide_ref[6:7, lanes] = jnp.sum(d_mix * gated * inv, axis=0, keepdims=True)
        dy = d_gated * silu_z
        dz_ref[:, lanes] = (d_gated * y * (sz * (1.0 + z * (1.0 - sz)))).astype(BF16)
        wide_ref[5:6, lanes] = jnp.sum(dy * xc, axis=0, keepdims=True)
        dt_pair = jnp.where(first, spread(dt, 2 * pair), spread(dt, 2 * pair + 1))
        cum_first, cum_second = spread(cum, 2 * pair), spread(cum, 2 * pair + 1)
        cum_pair = jnp.where(first, cum_first, cum_second)
        weighted = xc * dt_pair
        low = weighted.astype(BF16)
        dy_low = dy.astype(BF16)
        to_end, ending, state = state_of(in_map, weighted[:SPAN], cum_pair[:SPAN])
        d_weighted = []
        for s in range(2):
            rows = slice(s * SPAN, (s + 1) * SPAN)
            decay = decays(cum_first, cum_second, cum_row, pair, s)
            mats = jnp.concatenate([(affinity[s] * one).astype(BF16) for one in decay], axis=0)
            both = split_heads(dy_low[rows])
            d_mats = mm_nt(both, low[rows])
            d_aff[s] = plus(d_aff[s], d_mats[:SPAN] * decay[0] + d_mats[SPAN:] * decay[1])
            d_weighted.append(mm_tn(mats, both))
        reached = (dy[SPAN:] * jnp.exp(cum_pair[SPAN:])).astype(BF16)
        d_out = plus(d_out, mm_nt(reached, state.astype(BF16)))
        d_state = mm_tn(out_map[SPAN:], reached).astype(BF16)
        d_in = plus(d_in, mm_nt(ending, d_state))
        d_ending = mm(in_map[:SPAN], d_state)
        through = ending.astype(F32) * d_ending
        low_f, dy_f = low.astype(F32), dy_low.astype(F32)
        change = dy_f * scanned - low_f * jnp.concatenate(d_weighted, axis=0)
        ended = jnp.where(last_row, jnp.sum(through, axis=0, keepdims=True), 0.0) - through
        change = jnp.concatenate([change[:SPAN] + ended, change[SPAN:]], axis=0)
        d_weight = jnp.concatenate([d_weighted[0] + d_ending * to_end, d_weighted[1]], axis=0)
        d_cum = plus(d_cum, head_sums(change, pair))
        d_step = plus(d_step, head_sums(d_weight * xc, pair))
        d_xc = dy * skip_ref[:, lanes] + d_weight * dt_pair
        d_cx = d_xc * (sx * (1.0 + cx * (1.0 - sx)))
        d_x, rows_x = conv_back(d_cx, x, cxw)
        dx_ref[:, lanes] = d_x.astype(BF16)
        for index, row in enumerate(rows_x):
            wide_ref[index : index + 1, lanes] = row

    rate = rate_ref[...]
    d_log = span_sums_back(d_cum)
    d_dt = d_step - rate * d_log
    d_tp = d_dt * valid * sigmoid(tp_ref[...] + bias_ref[...])
    small_ref[...] = jnp.zeros(small_ref.shape, F32)
    small_ref[0:1, :] = jnp.sum(d_tp, axis=0, keepdims=True)
    small_ref[1:2, :] = -rate * jnp.sum(dt * d_log, axis=0, keepdims=True)
    dt_ref[...] = d_tp.astype(BF16)

    d_maps = []
    low_aff = [part.astype(BF16) for part in d_aff]
    d_ins, d_outs = [], []
    for s in range(2):
        rows = slice(s * SPAN, (s + 1) * SPAN)
        d_outs.append(mm(low_aff[s], in_map[rows]))
        d_ins.append(mm_tn(low_aff[s], out_map[rows]))
    d_outs[1] = d_outs[1] + d_out
    d_ins[0] = d_ins[0] + d_in
    d_maps = jnp.concatenate(
        [jnp.concatenate(d_ins, axis=0), jnp.concatenate(d_outs, axis=0)], axis=1
    )
    mapped = conv(bcp_ref[...], cbw_ref[...], cbb_ref[...])
    sm = sigmoid(mapped)
    d_bc, rows_bc = conv_back(d_maps * (sm * (1.0 + mapped * (1.0 - sm))), bcp_ref[...], cbw_ref[...])
    bcg_ref[...] = jnp.zeros(bcg_ref.shape, F32)
    for index, row in enumerate(rows_bc):
        bcg_ref[index : index + 1, :] = row
    d_bc = d_bc.astype(BF16)
    dbc_ref[...] = d_bc
    total = mm_nt(dx_ref[...], wx_ref[...]) + mm_nt(dz_ref[...], wz_ref[...])
    total = total + mm_nt(dq_ref[...], wq_ref[...]) + mm_nt(dkv_ref[...], wkv_ref[...])
    total = total + mm_nt(d_bc[:, :STATE], wb_ref[...]) + mm_nt(d_bc[:, STATE:], wc_ref[...])
    total = total + mm(dt_ref[...], wt_ref[...])
    dh_ref[...] = total.astype(dh_ref.dtype)


def ffn_kernel(h_ref, ct_ref, wg_ref, wu_ref, wd_ref, hid_ref, dg_ref, du_ref, ff_ref, dh_ref, ff_acc, dh_acc):
    step = pl.program_id(0)
    h = h_ref[...]
    gate = mm(h, wg_ref[...])
    up = mm(h, wu_ref[...])
    d_hidden = mm_nt(ct_ref[...], wd_ref[...]).astype(BF16).astype(F32)
    sg = sigmoid(gate)
    silu = gate * sg
    hidden = (silu * up).astype(BF16)
    d_gate = (d_hidden * up * (sg * (1.0 + gate * (1.0 - sg)))).astype(BF16)
    d_up = (d_hidden * silu).astype(BF16)
    hid_ref[...] = hidden
    dg_ref[...] = d_gate
    du_ref[...] = d_up
    ff_part = mm(hidden, wd_ref[...])
    dh_part = mm_nt(d_gate, wg_ref[...]) + mm_nt(d_up, wu_ref[...])

    @pl.when(step == 0)
    def _():
        ff_acc[...] = ff_part
        dh_acc[...] = dh_part

    @pl.when(step > 0)
    def _():
        ff_acc[...] += ff_part
        dh_acc[...] += dh_part

    @pl.when(step == pl.num_programs(0) - 1)
    def _():
        ff_ref[...] = ff_acc[...].astype(ff_ref.dtype)
        dh_ref[...] = dh_acc[...].astype(dh_ref.dtype)


def shaped(shape, dtype=F32):
    return jax.ShapeDtypeStruct(shape, dtype)


def whole_call(kernel, outs, scalars, args, flops, name):
    specs = [pl.BlockSpec(memory_space=pltpu.SMEM)] * scalars
    specs += [pl.BlockSpec(memory_space=pltpu.VMEM)] * (len(args) - scalars)
    moved = sum(arg.size * arg.dtype.itemsize for arg in args)
    return pl.pallas_call(
        kernel,
        out_shape=outs,
        in_specs=specs,
        out_specs=[pl.BlockSpec(memory_space=pltpu.VMEM)] * len(outs),
        compiler_params=pltpu.CompilerParams(vmem_limit_bytes=VMEM_LIMIT),
        cost_estimate=pl.CostEstimate(flops=flops, bytes_accessed=moved, transcendentals=0),
        name=name,
    )(*args)


def pad_columns(values, width):
    return jnp.pad(values, ((0, 0), (0, width - values.shape[1]))) if width != values.shape[1] else values


def pad_rows(values, height):
    return jnp.pad(values, ((0, height - values.shape[0]), (0, 0))) if height != values.shape[0] else values


def contract_rows(left, right):
    return mm_tn(jnp.concatenate(left, axis=0), jnp.concatenate(right, axis=0))


def on_device(
    tokens, lengths, cotangent, norm_gain, w_query, w_key, w_value, w_gate_z, w_ssm_x, w_ssm_b, w_ssm_c,
    w_step, conv_x_weight, conv_x_bias, conv_bc_weight, conv_bc_bias, step_bias, decay_log, skip_gain,
    ssm_norm_gain, w_out_att, w_out_ssm, ffn_norm_gain, w_gate, w_up, w_down,
):
    seq_len, model = tokens.shape
    groups = lax.axis_size("tensor")
    position = lax.axis_index("tensor")
    att_width, ssm_width = w_query.shape[1], w_gate_z.shape[1]
    att_pad = -(-att_width // LANES) * LANES
    ssm_pad = -(-ssm_width // LANES) * LANES
    ssm_heads = ssm_width // SSM_DIM
    ssm_width_all = SSM_HEADS * SSM_DIM
    ff_width = w_gate.shape[1]

    def fetch(values, shift):
        return lax.ppermute(values, "tensor", [((i + shift) % groups, i) for i in range(groups)])

    def deliver(values, shift):
        return lax.ppermute(values, "tensor", [(i, (i + shift) % groups) for i in range(groups)])

    def gather(values):
        return [values] + [fetch(values, k) for k in range(1, groups)]

    def scatter_sum(own, others):
        total = own
        for k in range(1, groups):
            total = total + deliver(others[k - 1], k).astype(F32)
        return total

    kv_head = position * (att_width // HEAD_DIM) // (HEADS // KV_HEADS)
    w_kv = jnp.concatenate(
        [lax.dynamic_slice_in_dim(w, kv_head * HEAD_DIM, HEAD_DIM, 1) for w in (w_key, w_value)], axis=1
    )
    wq = pad_columns(w_query, att_pad)
    wz, wx = pad_columns(w_gate_z, ssm_pad), pad_columns(w_ssm_x, ssm_pad)
    wt = pad_rows(w_step.T, 16)
    wa, ws = pad_rows(w_out_att, att_pad), pad_rows(w_out_ssm, ssm_pad)
    cxw, cxb = pad_columns(conv_x_weight, ssm_pad), pad_columns(conv_x_bias[None], ssm_pad)
    cbb = conv_bc_bias[None]
    gain = pad_columns(ssm_norm_gain[None], ssm_pad)
    skip = pad_columns(jnp.repeat(skip_gain, SSM_DIM)[None], ssm_pad)
    bias = pad_columns(step_bias[None], 16)
    rate = pad_columns(jnp.exp(decay_log)[None], 16)
    bias_col, rate_col = bias.T, rate.T
    half = HEAD_DIM // 2
    freqs = ROPE_BASE ** (-(jnp.arange(half).astype(F32) * 2.0 / HEAD_DIM))
    angles = jnp.arange(seq_len).astype(F32)[:, None] * freqs[None, :]
    cosine, sine, none = jnp.cos(angles), jnp.sin(angles), jnp.zeros_like(angles)
    cos_table = jnp.concatenate([cosine] * 4, axis=1)
    sine_first = jnp.concatenate([-sine, none] * 2, axis=1)
    sine_second = jnp.concatenate([none, sine] * 2, axis=1)

    inputs = tokens.astype(F32)
    inv1 = lax.rsqrt(jnp.mean(inputs * inputs, axis=1, keepdims=True) + EPSILON)
    h_own = (inputs * inv1 * norm_gain).astype(BF16)
    own_mask = jnp.arange(seq_len) < lengths[0]
    ct_own = jnp.where(own_mask[:, None], cotangent, jnp.zeros_like(cotangent))
    h_all = gather(h_own)
    len_all = gather(lengths)
    ct_all = gather(ct_own)

    def forward(k):
        outs = [
            shaped((seq_len, att_pad), BF16), shaped((seq_len, LANES), BF16), shaped((seq_len, LANES), BF16),
            shaped((seq_len, ssm_pad)), shaped((seq_len, ssm_pad)), shaped((seq_len, 2 * STATE)),
            shaped((seq_len, 2 * STATE), BF16), shaped((seq_len, 16)), shaped((16, seq_len)),
            shaped((seq_len, ssm_pad)), shaped((16, seq_len)),
        ]
        args = [
            len_all[k], h_all[k], wq, w_kv, wz, wx, w_ssm_b, w_ssm_c, wt, cxw, cxb, conv_bc_weight, cbb,
            bias, rate, bias_col, rate_col, skip, cos_table, sine_first, sine_second,
        ]
        return whole_call(mixer_forward_kernel, outs, 1, args, 8 * 10**9, "mixer_forward")

    def attend(k):
        q, kd, vd = kept[k][:3]
        return whole_call(
            attend_kernel, [shaped((seq_len, att_pad), BF16)], 1, [len_all[k], q, kd, vd], 2 * 10**9, "attend"
        )[0]

    kept = [forward(k) for k in range(groups)]
    squares_part = [one[10] for one in kept]
    squares = [squares_part[k] for k in range(groups)]
    for shift in range(1, groups):
        for k in range(groups):
            squares[k] = squares[k] + fetch(squares_part[(k - shift) % groups], shift)
    mix_att = [attend(k) for k in range(groups)]

    def project(k, dtype):
        q, kd, vd, z, x, bcp, bc, tp, tpr, y, _ = kept[k]
        return whole_call(
            functools.partial(out_kernel, width=ssm_width_all),
            [shaped((seq_len, model), dtype), shaped((seq_len, ssm_pad), BF16)],
            0,
            [mix_att[k], y, x, z, squares[k], cxw, cxb, skip, gain, wa, ws],
            4 * 10**9,
            "out_project",
        )

    projected = [project(k, F32 if k == 0 else BF16) for k in range(groups)]
    mix_ssm = [one[1] for one in projected]
    branch = scatter_sum(projected[0][0], [one[0] for one in projected[1:]])
    resid = inputs + branch
    inv2 = lax.rsqrt(jnp.mean(resid * resid, axis=1, keepdims=True) + EPSILON)
    h2_own = (resid * inv2 * ffn_norm_gain).astype(BF16)
    h2_all = gather(h2_own)

    def feed(k):
        dtype = F32 if k == 0 else BF16
        block = min(256, ff_width)
        full = pl.BlockSpec((seq_len, model), lambda i: (0, 0))
        columns = pl.BlockSpec((model, block), lambda i: (0, i))
        rows = pl.BlockSpec((block, model), lambda i: (i, 0))
        tall = pl.BlockSpec((seq_len, block), lambda i: (0, i))
        return pl.pallas_call(
            ffn_kernel,
            grid=(ff_width // block,),
            out_shape=[shaped((seq_len, ff_width), BF16)] * 3 + [shaped((seq_len, model), dtype)] * 2,
            in_specs=[full, full, columns, columns, rows],
            out_specs=[tall] * 3 + [full] * 2,
            scratch_shapes=[pltpu.VMEM((seq_len, model), F32)] * 2,
            compiler_params=pltpu.CompilerParams(vmem_limit_bytes=VMEM_LIMIT),
            cost_estimate=pl.CostEstimate(flops=8 * 10**9, bytes_accessed=10**7, transcendentals=0),
            name="feed_forward",
        )(h2_all[k], ct_all[k], w_gate, w_up, w_down)

    fed = [feed(k) for k in range(groups)]
    d_second = scatter_sum(fed[0][4], [one[4] for one in fed[1:]])
    ffn_result = scatter_sum(fed[0][3], [one[3] for one in fed[1:]])
    layer_output = (resid + ffn_result).astype(BF16)
    grad_gate = contract_rows(h2_all, [one[1] for one in fed])
    grad_up = contract_rows(h2_all, [one[2] for one in fed])
    grad_down = contract_rows([one[0] for one in fed], ct_all)

    scaled = d_second * ffn_norm_gain
    d_resid = (
        ct_own.astype(F32)
        + inv2 * scaled
        - resid * (inv2**3) * jnp.mean(scaled * resid, axis=1, keepdims=True)
    )
    grad_ffn_gain = jnp.sum(d_second * resid * inv2, axis=0)
    db_all = gather(d_resid.astype(BF16))

    def mix_grad(k):
        q, kd, vd, z, x, bcp, bc, tp, tpr, y, _ = kept[k]
        return whole_call(
            mix_grad_kernel,
            [shaped((seq_len, att_pad), BF16), shaped((seq_len, ssm_pad), BF16), shaped((16, seq_len))],
            0,
            [db_all[k], y, x, z, cxw, cxb, skip, gain, wa, ws],
            4 * 10**9,
            "mix_grad",
        )

    mixed = [mix_grad(k) for k in range(groups)]
    backs_part = [one[2] for one in mixed]
    backs = [backs_part[k] for k in range(groups)]
    for shift in range(1, groups):
        for k in range(groups):
            backs[k] = backs[k] + fetch(backs_part[(k - shift) % groups], shift)

    def attend_back(k):
        q, kd, vd = kept[k][:3]
        return whole_call(
            attend_back_kernel,
            [shaped((seq_len, att_pad), BF16), shaped((seq_len, LANES), BF16)],
            1,
            [len_all[k], q, kd, vd, mixed[k][0], cos_table, sine_first, sine_second],
            4 * 10**9,
            "attend_back",
        )

    turned = [attend_back(k) for k in range(groups)]

    def backward(k):
        q, kd, vd, z, x, bcp, bc, tp, tpr, y, _ = kept[k]
        outs = [
            shaped((seq_len, model), F32 if k == 0 else BF16), shaped((seq_len, ssm_pad), BF16),
            shaped((seq_len, ssm_pad), BF16), shaped((seq_len, 2 * STATE), BF16), shaped((seq_len, 16), BF16),
            shaped((8, ssm_pad)), shaped((8, 2 * STATE)), shaped((8, 16)),
        ]
        args = [
            len_all[k], mixed[k][1], y, x, z, bcp, bc, tp, tpr, squares[k], backs[k], turned[k][0], turned[k][1],
            wq, w_kv, wz, wx, w_ssm_b, w_ssm_c, wt, cxw, cxb, conv_bc_weight, cbb, bias, rate, bias_col, rate_col,
            skip, gain,
        ]
        return whole_call(
            functools.partial(mixer_back_kernel, width=ssm_width_all), outs, 1, args, 16 * 10**9, "mixer_back"
        )

    gone = [None] * groups
    for k in list(range(1, groups)) + [0]:
        gone[k] = backward(k)
    d_first = scatter_sum(gone[0][0], [one[0] for one in gone[1:]])
    scaled = d_first * norm_gain
    grad_input = (
        d_resid
        + inv1 * scaled
        - inputs * (inv1**3) * jnp.mean(scaled * inputs, axis=1, keepdims=True)
    )
    grad_norm_gain = jnp.sum(d_first * inputs * inv1, axis=0)

    grad_out_att = contract_rows(mix_att, db_all)[:att_width]
    grad_out_ssm = contract_rows(mix_ssm, db_all)[:ssm_width]
    grad_query = contract_rows(h_all, [one[0] for one in turned])[:, :att_width]
    grad_kv = contract_rows(h_all, [one[1] for one in turned])
    grad_x = contract_rows(h_all, [one[1] for one in gone])[:, :ssm_width]
    grad_z = contract_rows(h_all, [one[2] for one in gone])[:, :ssm_width]
    grad_bc = contract_rows(h_all, [one[3] for one in gone])
    grad_step = contract_rows(h_all, [one[4] for one in gone])[:, :ssm_heads]
    wide, bcg, small = (sum(one[i] for one in gone) for i in (5, 6, 7))
    grad_skip = jnp.sum(wide[5, :ssm_width].reshape(ssm_heads, SSM_DIM), axis=1)

    def total_dp(values):
        return lax.psum(values.astype(BF16), "dp").astype(F32)

    zeros = jnp.zeros((model, KV_HEADS * HEAD_DIM), F32)
    grad_key = lax.dynamic_update_slice(zeros, grad_kv[:, :HEAD_DIM], (0, kv_head * HEAD_DIM))
    grad_value = lax.dynamic_update_slice(zeros, grad_kv[:, HEAD_DIM:], (0, kv_head * HEAD_DIM))
    grad_key, grad_value, grad_bc, bcg, grad_norm_gain, grad_ffn_gain = lax.psum(
        (grad_key, grad_value, grad_bc, bcg, grad_norm_gain, grad_ffn_gain), ("dp", "tensor")
    )
    return (
        layer_output,
        grad_input,
        grad_norm_gain,
        total_dp(grad_query),
        grad_key,
        grad_value,
        total_dp(grad_z),
        total_dp(grad_x),
        grad_bc[:, :STATE],
        grad_bc[:, STATE:],
        total_dp(grad_step),
        total_dp(wide[:4, :ssm_width]),
        total_dp(wide[4, :ssm_width]),
        bcg[:4],
        bcg[4],
        total_dp(small[0, :ssm_heads]),
        total_dp(small[1, :ssm_heads]),
        total_dp(grad_skip),
        total_dp(wide[6, :ssm_width]),
        total_dp(grad_out_att),
        total_dp(grad_out_ssm),
        grad_ffn_gain,
        total_dp(grad_gate),
        total_dp(grad_up),
        total_dp(grad_down),
    )


def solution(mesh):
    rows, split, tall = P(("dp", "tensor"), None), P(None, "tensor"), P("tensor", None)
    vector, copied = P("tensor"), P()
    return jax.shard_map(
        on_device,
        mesh=mesh,
        in_specs=(
            rows, P(("dp", "tensor")), rows, copied, split, copied, copied, split, split, copied, copied, split,
            split, vector, copied, copied, vector, vector, vector, vector, tall, tall, copied, split, split, tall,
        ),
        out_specs=(
            rows, rows, copied, split, copied, copied, split, split, copied, copied, split, split, vector, copied,
            copied, vector, vector, vector, vector, tall, tall, copied, split, split, tall,
        ),
        check_vma=False,
    )
```

```python
import functools

import jax
import jax.numpy as jnp
from jax import lax
from jax.experimental import pallas as pl
from jax.experimental.pallas import tpu as pltpu
from jax.sharding import PartitionSpec as P

HEADS = 8
KV_HEADS = 2
HEAD_DIM = 64
SSM_HEADS = 24
SSM_DIM = 64
STATE = 128
SPAN = 128
LANES = 128

EPSILON = 1e-05
ROPE_BASE = 100000000000.0
F32 = jnp.float32
BF16 = jnp.bfloat16
VMEM_LIMIT = 50 * 1024 * 1024
REDUCE_LIMIT = 56 * 1024 * 1024
MESH = pl.DeviceIdType.MESH


def mm(left, right):
    return jnp.dot(left, right, preferred_element_type=F32)


def mm_nt(left, right):
    return lax.dot_general(left, right, (((1,), (1,)), ((), ())), preferred_element_type=F32)


def mm_tn(left, right):
    return lax.dot_general(left, right, (((0,), (0,)), ((), ())), preferred_element_type=F32)


def pieces(values, count):
    terms = []
    for _ in range(count):
        term = values.astype(BF16)
        terms.append(term)
        values = values - term.astype(F32)
    return terms


def sigmoid(values):
    return 1.0 / (1.0 + jnp.exp(-values))


def softplus(values):
    return jnp.maximum(values, 0.0) + jnp.log1p(jnp.exp(-jnp.abs(values)))


def lane_ids(shape):
    return lax.broadcasted_iota(jnp.int32, shape, 1)


def row_ids(shape):
    return lax.broadcasted_iota(jnp.int32, shape, 0)


def repeat_lanes(column, count):
    return jnp.concatenate([column] * count, axis=1) if count > 1 else column


def column_of(row):
    ones = jnp.where(row_ids((16, LANES)) == 0, 1.0, 0.0).astype(BF16)
    total = None
    for term in pieces(row, 3):
        part = mm_tn(term, ones)
        total = part if total is None else total + part
    return total


def row_sums(values):
    ones = jnp.ones((16, values.shape[1]), BF16)
    high, low = pieces(values, 2)
    return mm_nt(ones, high) + mm_nt(ones, low)


def causal_shift(values, steps):
    if steps == 0:
        return values
    rolled = pltpu.roll(values, steps, 0)
    return jnp.where(row_ids(values.shape) >= steps, rolled, 0.0)


def anti_shift(values, steps):
    if steps == 0:
        return values
    length = values.shape[0]
    rolled = pltpu.roll(values, length - steps, 0)
    return jnp.where(row_ids(values.shape) < length - steps, rolled, 0.0)


def conv(values, weight, bias):
    taps = weight.shape[0]
    total = bias + weight[taps - 1 : taps] * values
    for offset in range(taps - 1):
        total = total + weight[offset : offset + 1] * causal_shift(values, taps - 1 - offset)
    return total


def conv_back(grad, values, weight):
    taps = weight.shape[0]
    total, rows = None, []
    for offset in range(taps):
        steps = taps - 1 - offset
        moved = anti_shift(grad, steps)
        part = weight[offset : offset + 1] * moved
        total = part if total is None else total + part
        rows.append(jnp.sum(moved * values, axis=0, keepdims=True))
    rows.append(jnp.sum(grad, axis=0, keepdims=True))
    return total, rows


def rope(values, cosine, sine_first, sine_second):
    ahead = pltpu.roll(values, LANES - HEAD_DIM // 2, 1)
    behind = pltpu.roll(values, HEAD_DIM // 2, 1)
    return values * cosine + ahead * sine_first + behind * sine_second


def lower_mask():
    return row_ids((SPAN, SPAN)) >= lane_ids((SPAN, SPAN))


def span_sums(values):
    lower = jnp.where(lower_mask(), 1.0, 0.0).astype(BF16)
    out = []
    for start in range(0, values.shape[0], SPAN):
        total = None
        for term in pieces(values[start : start + SPAN], 3):
            part = mm(lower, term)
            total = part if total is None else total + part
        out.append(total)
    return jnp.concatenate(out, axis=0)


def span_sums_rows(values):
    upper = jnp.where(row_ids((SPAN, SPAN)) <= lane_ids((SPAN, SPAN)), 1.0, 0.0).astype(BF16)
    out = []
    for start in range(0, values.shape[1], SPAN):
        total = None
        for term in pieces(values[:, start : start + SPAN], 3):
            part = mm(term, upper)
            total = part if total is None else total + part
        out.append(total)
    return jnp.concatenate(out, axis=1)


def span_sums_back(values):
    upper = jnp.where(row_ids((SPAN, SPAN)) <= lane_ids((SPAN, SPAN)), 1.0, 0.0).astype(BF16)
    out = []
    for start in range(0, values.shape[0], SPAN):
        total = None
        for term in pieces(values[start : start + SPAN], 3):
            part = mm(upper, term)
            total = part if total is None else total + part
        out.append(total)
    return jnp.concatenate(out, axis=0)


def steps_of(tp, tp_row, bias, bias_col, rate, rate_col, length):
    seq_len = tp.shape[0]
    valid = jnp.where(row_ids((seq_len, 1)) < length, 1.0, 0.0)
    valid_row = jnp.where(lane_ids((1, seq_len)) < length, 1.0, 0.0)
    dt = softplus(tp + bias) * valid
    dt_row = softplus(tp_row + bias_col) * valid_row
    cum = span_sums(-(dt * rate))
    cum_row = span_sums_rows(-(dt_row * rate_col))
    return valid, dt, cum, cum_row


def spread(values, head):
    return jnp.broadcast_to(values[:, head : head + 1], (values.shape[0], LANES))


def decays(cum_first, cum_second, cum_row, pair, span):
    rows = slice(span * SPAN, (span + 1) * SPAN)
    lower = lower_mask()
    out = []
    for head, column in ((2 * pair, cum_first), (2 * pair + 1, cum_second)):
        differ = column[rows] - cum_row[head : head + 1, rows]
        out.append(jnp.exp(jnp.where(lower, differ, -1e30)))
    return out


def split_heads(values):
    first = lane_ids(values.shape) < HEAD_DIM
    zero = jnp.zeros_like(values)
    return jnp.concatenate([jnp.where(first, values, zero), jnp.where(first, zero, values)], axis=0)


def state_of(in_map, weighted_first, cum_pair_first):
    to_end = jnp.exp(cum_pair_first[SPAN - 1 : SPAN] - cum_pair_first)
    ending = (weighted_first * to_end).astype(BF16)
    return to_end, ending, mm_tn(in_map[:SPAN], ending)


def mixer_forward_kernel(
    len_ref, h_ref, wq_ref, wkv_ref, wz_ref, wx_ref, wb_ref, wc_ref, wt_ref, cxw_ref, cxb_ref,
    cbw_ref, cbb_ref, bias_ref, rate_ref, bias_col_ref, rate_col_ref, skip_ref, cos_ref, sa_ref,
    sb_ref, q_ref, kd_ref, vd_ref, z_ref, x_ref, bcp_ref, bc_ref, tp_ref, tpr_ref, y_ref, ss_ref,
):
    h = h_ref[...]
    pairs = wx_ref.shape[1] // LANES
    z_ref[...] = mm(h, wz_ref[...])
    x_ref[...] = mm(h, wx_ref[...])
    bcp_ref[:, :STATE] = mm(h, wb_ref[...])
    bcp_ref[:, STATE:] = mm(h, wc_ref[...])
    tp = mm_nt(h, wt_ref[...])
    tp_row = mm_nt(wt_ref[...], h)
    tp_ref[...] = tp
    tpr_ref[...] = tp_row
    cosine, sine_first, sine_second = cos_ref[...], sa_ref[...], sb_ref[...]
    for pair in range(wq_ref.shape[1] // LANES):
        lanes = slice(pair * LANES, (pair + 1) * LANES)
        q_ref[:, lanes] = rope(mm(h, wq_ref[:, lanes]), cosine, sine_first, sine_second).astype(BF16)
    kv = mm(h, wkv_ref[...])
    turned = pltpu.roll(kv, HEAD_DIM, 1)
    first = lane_ids(kv.shape) < HEAD_DIM
    kd_ref[...] = rope(jnp.where(first, kv, turned), cosine, sine_first, sine_second).astype(BF16)
    vd_ref[...] = jnp.where(first, turned, kv).astype(BF16)

    mapped = conv(bcp_ref[...], cbw_ref[...], cbb_ref[...])
    bc = (mapped * sigmoid(mapped)).astype(BF16)
    bc_ref[...] = bc
    in_map, out_map = bc[:, :STATE], bc[:, STATE:]
    affinity = [
        mm_nt(out_map[s * SPAN : (s + 1) * SPAN], in_map[s * SPAN : (s + 1) * SPAN]) for s in range(2)
    ]
    _, dt, cum, cum_row = steps_of(
        tp, tp_row, bias_ref[...], bias_col_ref[...], rate_ref[...], rate_col_ref[...], len_ref[0]
    )
    squares = None
    for pair in range(pairs):
        lanes = slice(pair * LANES, (pair + 1) * LANES)
        cx = conv(x_ref[:, lanes], cxw_ref[:, lanes], cxb_ref[:, lanes])
        xc = cx * sigmoid(cx)
        dt_pair = jnp.where(first, spread(dt, 2 * pair), spread(dt, 2 * pair + 1))
        cum_first, cum_second = spread(cum, 2 * pair), spread(cum, 2 * pair + 1)
        cum_pair = jnp.where(first, cum_first, cum_second)
        weighted = xc * dt_pair
        low = weighted.astype(BF16)
        _, _, state = state_of(in_map, weighted[:SPAN], cum_pair[:SPAN])
        parts = []
        for s in range(2):
            rows = slice(s * SPAN, (s + 1) * SPAN)
            mats = [
                (affinity[s] * decay).astype(BF16)
                for decay in decays(cum_first, cum_second, cum_row, pair, s)
            ]
            part = mm(jnp.concatenate(mats, axis=1), split_heads(low[rows]))
            if s:
                part = part + mm(out_map[rows], state.astype(BF16)) * jnp.exp(cum_pair[rows])
            parts.append(part)
        y = jnp.concatenate(parts, axis=0)
        y_ref[:, lanes] = y
        z = z_ref[:, lanes]
        gated = (y + skip_ref[:, lanes] * xc) * (z * sigmoid(z))
        square = gated * gated
        squares = square if squares is None else squares + square
    ss_ref[...] = row_sums(squares)


def masked_probs(queries, kd, length, scale):
    seq_len = kd.shape[0]
    scores = mm_nt(split_heads(queries), kd) * scale
    rows = row_ids(scores.shape)
    rows = jnp.where(rows >= seq_len, rows - seq_len, rows)
    columns = lane_ids(scores.shape)
    scores = jnp.where((rows >= columns) & (columns < length), scores, -1e30)
    weights = jnp.exp(scores - jnp.max(scores, axis=1, keepdims=True))
    return weights / jnp.sum(weights, axis=1, keepdims=True)


def attend_kernel(len_ref, q_ref, kd_ref, vd_ref, out_ref):
    seq_len = q_ref.shape[0]
    values = split_heads(vd_ref[...])
    for pair in range(q_ref.shape[1] // LANES):
        lanes = slice(pair * LANES, (pair + 1) * LANES)
        probs = masked_probs(q_ref[:, lanes], kd_ref[...], len_ref[0], HEAD_DIM ** (-0.5)).astype(BF16)
        both = jnp.concatenate([probs[:seq_len], probs[seq_len:]], axis=1)
        out_ref[:, lanes] = mm(both, values).astype(BF16)


def join_halves(values):
    return values + pltpu.roll(values, HEAD_DIM, 1)


def attend_back_kernel(len_ref, q_ref, kd_ref, vd_ref, da_ref, cos_ref, sa_ref, sb_ref, dq_ref, dkv_ref):
    seq_len = q_ref.shape[0]
    scale = HEAD_DIM ** (-0.5)
    cosine, sine_first, sine_second = cos_ref[...], -sa_ref[...], -sb_ref[...]
    kd, vd = kd_ref[...], vd_ref[...]
    keys = split_heads(kd)
    grad_k, grad_v = None, None
    for pair in range(q_ref.shape[1] // LANES):
        lanes = slice(pair * LANES, (pair + 1) * LANES)
        probs = masked_probs(q_ref[:, lanes], kd, len_ref[0], scale)
        da = split_heads(da_ref[:, lanes])
        dprob = mm_nt(da, vd)
        dscore = (probs * (dprob - jnp.sum(probs * dprob, axis=1, keepdims=True))).astype(BF16)
        both = jnp.concatenate([dscore[:seq_len], dscore[seq_len:]], axis=1)
        dq = mm(both, keys) * scale
        dq_ref[:, lanes] = rope(dq, cosine, sine_first, sine_second).astype(BF16)
        part_k = mm_tn(dscore, split_heads(q_ref[:, lanes]))
        part_v = mm_tn(probs.astype(BF16), da)
        grad_k = part_k if grad_k is None else grad_k + part_k
        grad_v = part_v if grad_v is None else grad_v + part_v
    dk = rope(join_halves(grad_k) * scale, cosine, sine_first, sine_second)
    first = lane_ids(dk.shape) < HEAD_DIM
    dkv_ref[...] = jnp.where(first, dk, join_halves(grad_v)).astype(BF16)


def out_kernel(att_ref, y_ref, x_ref, z_ref, ss_ref, cxw_ref, cxb_ref, skip_ref, gain_ref, wa_ref, ws_ref,
               part_ref, mix_ref, *, width):
    total = mm(att_ref[...], wa_ref[...])
    inv = column_of(lax.rsqrt(ss_ref[...] / width + EPSILON))
    for pair in range(y_ref.shape[1] // LANES):
        lanes = slice(pair * LANES, (pair + 1) * LANES)
        cx = conv(x_ref[:, lanes], cxw_ref[:, lanes], cxb_ref[:, lanes])
        z = z_ref[:, lanes]
        gated = (y_ref[:, lanes] + skip_ref[:, lanes] * (cx * sigmoid(cx))) * (z * sigmoid(z))
        mix_ref[:, lanes] = (gated * inv * gain_ref[:, lanes]).astype(BF16)
    part_ref[...] = (total + mm(mix_ref[...], ws_ref[...])).astype(part_ref.dtype)


def mix_grad_kernel(db_ref, y_ref, x_ref, z_ref, cxw_ref, cxb_ref, skip_ref, gain_ref, wa_ref, ws_ref,
                    da_ref, dm_ref, bs_ref):
    db = db_ref[...]
    da_ref[...] = mm_nt(db, wa_ref[...]).astype(BF16)
    dm_ref[...] = mm_nt(db, ws_ref[...]).astype(BF16)
    total = None
    for pair in range(y_ref.shape[1] // LANES):
        lanes = slice(pair * LANES, (pair + 1) * LANES)
        cx = conv(x_ref[:, lanes], cxw_ref[:, lanes], cxb_ref[:, lanes])
        z = z_ref[:, lanes]
        gated = (y_ref[:, lanes] + skip_ref[:, lanes] * (cx * sigmoid(cx))) * (z * sigmoid(z))
        part = gated * (gain_ref[:, lanes] * dm_ref[:, lanes].astype(F32))
        total = part if total is None else total + part
    bs_ref[...] = row_sums(total)


def head_sums(values, pair):
    rows, columns = row_ids((LANES, 16)), lane_ids((LANES, 16))
    chosen = jnp.where(columns == 2 * pair + jnp.where(rows < HEAD_DIM, 0, 1), 1.0, 0.0).astype(BF16)
    high, low = pieces(values, 2)
    return mm(jnp.concatenate([high, low], axis=1), jnp.concatenate([chosen, chosen], axis=0))


def mixer_back_kernel(
    len_ref, dm_ref, y_ref, x_ref, z_ref, bcp_ref, bc_ref, tp_ref, tpr_ref, ss_ref, bs_ref, dq_ref,
    dkv_ref, wq_ref, wkv_ref, wz_ref, wx_ref, wb_ref, wc_ref, wt_ref, cxw_ref, cxb_ref, cbw_ref,
    cbb_ref, bias_ref, rate_ref, bias_col_ref, rate_col_ref, skip_ref, gain_ref,
    dh_ref, dx_ref, dz_ref, dbc_ref, dt_ref, wide_ref, bcg_ref, small_ref, *, width,
):
    pairs = x_ref.shape[1] // LANES
    bc = bc_ref[...]
    in_map, out_map = bc[:, :STATE], bc[:, STATE:]
    affinity = [
        mm_nt(out_map[s * SPAN : (s + 1) * SPAN], in_map[s * SPAN : (s + 1) * SPAN]) for s in range(2)
    ]
    valid, dt, cum, cum_row = steps_of(
        tp_ref[...], tpr_ref[...], bias_ref[...], bias_col_ref[...], rate_ref[...], rate_col_ref[...], len_ref[0]
    )
    inv_row = lax.rsqrt(ss_ref[...] / width + EPSILON)
    inv = column_of(inv_row)
    back = column_of(inv_row * inv_row * inv_row * bs_ref[...] / width)
    first = lane_ids((x_ref.shape[0], LANES)) < HEAD_DIM
    last_row = row_ids((SPAN, LANES)) == SPAN - 1
    d_cum, d_step = None, None
    d_aff, d_out, d_in = [None, None], None, None

    def plus(total, part):
        return part if total is None else total + part

    for pair in range(pairs):
        lanes = slice(pair * LANES, (pair + 1) * LANES)
        x = x_ref[:, lanes]
        cxw = cxw_ref[:, lanes]
        cx = conv(x, cxw, cxb_ref[:, lanes])
        sx = sigmoid(cx)
        xc = cx * sx
        z = z_ref[:, lanes]
        sz = sigmoid(z)
        silu_z = z * sz
        scanned = y_ref[:, lanes]
        y = scanned + skip_ref[:, lanes] * xc
        gated = y * silu_z
        d_mix = dm_ref[:, lanes].astype(F32)
        d_gated = inv * (gain_ref[:, lanes] * d_mix) - gated * back
        wide_ref[6:7, lanes] = jnp.sum(d_mix * gated * inv, axis=0, keepdims=True)
        dy = d_gated * silu_z
        dz_ref[:, lanes] = (d_gated * y * (sz * (1.0 + z * (1.0 - sz)))).astype(BF16)
        wide_ref[5:6, lanes] = jnp.sum(dy * xc, axis=0, keepdims=True)
        dt_pair = jnp.where(first, spread(dt, 2 * pair), spread(dt, 2 * pair + 1))
        cum_first, cum_second = spread(cum, 2 * pair), spread(cum, 2 * pair + 1)
        cum_pair = jnp.where(first, cum_first, cum_second)
        weighted = xc * dt_pair
        low = weighted.astype(BF16)
        dy_low = dy.astype(BF16)
        to_end, ending, state = state_of(in_map, weighted[:SPAN], cum_pair[:SPAN])
        d_weighted = []
        for s in range(2):
            rows = slice(s * SPAN, (s + 1) * SPAN)
            decay = decays(cum_first, cum_second, cum_row, pair, s)
            mats = jnp.concatenate([(affinity[s] * one).astype(BF16) for one in decay], axis=0)
            both = split_heads(dy_low[rows])
            d_mats = mm_nt(both, low[rows])
            d_aff[s] = plus(d_aff[s], d_mats[:SPAN] * decay[0] + d_mats[SPAN:] * decay[1])
            d_weighted.append(mm_tn(mats, both))
        reached = (dy[SPAN:] * jnp.exp(cum_pair[SPAN:])).astype(BF16)
        d_out = plus(d_out, mm_nt(reached, state.astype(BF16)))
        d_state = mm_tn(out_map[SPAN:], reached).astype(BF16)
        d_in = plus(d_in, mm_nt(ending, d_state))
        d_ending = mm(in_map[:SPAN], d_state)
        through = ending.astype(F32) * d_ending
        low_f, dy_f = low.astype(F32), dy_low.astype(F32)
        change = dy_f * scanned - low_f * jnp.concatenate(d_weighted, axis=0)
        ended = jnp.where(last_row, jnp.sum(through, axis=0, keepdims=True), 0.0) - through
        change = jnp.concatenate([change[:SPAN] + ended, change[SPAN:]], axis=0)
        d_weight = jnp.concatenate([d_weighted[0] + d_ending * to_end, d_weighted[1]], axis=0)
        d_cum = plus(d_cum, head_sums(change, pair))
        d_step = plus(d_step, head_sums(d_weight * xc, pair))
        d_xc = dy * skip_ref[:, lanes] + d_weight * dt_pair
        d_cx = d_xc * (sx * (1.0 + cx * (1.0 - sx)))
        d_x, rows_x = conv_back(d_cx, x, cxw)
        dx_ref[:, lanes] = d_x.astype(BF16)
        for index, row in enumerate(rows_x):
            wide_ref[index : index + 1, lanes] = row

    rate = rate_ref[...]
    d_log = span_sums_back(d_cum)
    d_dt = d_step - rate * d_log
    d_tp = d_dt * valid * sigmoid(tp_ref[...] + bias_ref[...])
    small_ref[...] = jnp.zeros(small_ref.shape, F32)
    small_ref[0:1, :] = jnp.sum(d_tp, axis=0, keepdims=True)
    small_ref[1:2, :] = -rate * jnp.sum(dt * d_log, axis=0, keepdims=True)
    dt_ref[...] = d_tp.astype(BF16)

    d_maps = []
    low_aff = [part.astype(BF16) for part in d_aff]
    d_ins, d_outs = [], []
    for s in range(2):
        rows = slice(s * SPAN, (s + 1) * SPAN)
        d_outs.append(mm(low_aff[s], in_map[rows]))
        d_ins.append(mm_tn(low_aff[s], out_map[rows]))
    d_outs[1] = d_outs[1] + d_out
    d_ins[0] = d_ins[0] + d_in
    d_maps = jnp.concatenate(
        [jnp.concatenate(d_ins, axis=0), jnp.concatenate(d_outs, axis=0)], axis=1
    )
    mapped = conv(bcp_ref[...], cbw_ref[...], cbb_ref[...])
    sm = sigmoid(mapped)
    d_bc, rows_bc = conv_back(d_maps * (sm * (1.0 + mapped * (1.0 - sm))), bcp_ref[...], cbw_ref[...])
    bcg_ref[...] = jnp.zeros(bcg_ref.shape, F32)
    for index, row in enumerate(rows_bc):
        bcg_ref[index : index + 1, :] = row
    d_bc = d_bc.astype(BF16)
    dbc_ref[...] = d_bc
    total = mm_nt(dx_ref[...], wx_ref[...]) + mm_nt(dz_ref[...], wz_ref[...])
    total = total + mm_nt(dq_ref[...], wq_ref[...]) + mm_nt(dkv_ref[...], wkv_ref[...])
    total = total + mm_nt(d_bc[:, :STATE], wb_ref[...]) + mm_nt(d_bc[:, STATE:], wc_ref[...])
    total = total + mm(dt_ref[...], wt_ref[...])
    dh_ref[...] = total.astype(dh_ref.dtype)


def ffn_kernel(h_ref, ct_ref, wg_ref, wu_ref, wd_ref, hid_ref, dg_ref, du_ref, ff_ref, dh_ref, ff_acc, dh_acc):
    step = pl.program_id(0)
    h = h_ref[...]
    gate = mm(h, wg_ref[...])
    up = mm(h, wu_ref[...])
    d_hidden = mm_nt(ct_ref[...], wd_ref[...]).astype(BF16).astype(F32)
    sg = sigmoid(gate)
    silu = gate * sg
    hidden = (silu * up).astype(BF16)
    d_gate = (d_hidden * up * (sg * (1.0 + gate * (1.0 - sg)))).astype(BF16)
    d_up = (d_hidden * silu).astype(BF16)
    hid_ref[...] = hidden
    dg_ref[...] = d_gate
    du_ref[...] = d_up
    ff_part = mm(hidden, wd_ref[...])
    dh_part = mm_nt(d_gate, wg_ref[...]) + mm_nt(d_up, wu_ref[...])

    @pl.when(step == 0)
    def _():
        ff_acc[...] = ff_part
        dh_acc[...] = dh_part

    @pl.when(step > 0)
    def _():
        ff_acc[...] += ff_part
        dh_acc[...] += dh_part

    @pl.when(step == pl.num_programs(0) - 1)
    def _():
        ff_ref[...] = ff_acc[...].astype(ff_ref.dtype)
        dh_ref[...] = dh_acc[...].astype(dh_ref.dtype)


def reduce_kernel(*refs, widths, special, block, lag, pattern):
    count = len(widths)
    ins, out_ref, rest = refs[:count], refs[count], refs[count + 1 :]
    has_x = special > 0
    if has_x:
        xout_ref, rest = rest[0], rest[1:]
    acc, res, rc, ry, zin, zmid = rest[:6]
    rest = rest[6:]
    if has_x:
        xres, rest = rest[0], rest[1:]
    in_sem, out_sem, send_sem, recv_sem = rest
    rows = acc.shape[0]
    half, quarter = rows // 2, rows // 4
    me = lax.axis_index("dp")
    core, y, z = me % 2, (me // 2) % 2, me // 4
    side = lax.axis_index("tensor")
    sibling = me + 1 - 2 * core
    across = me + 2 - 4 * y
    z_out = z + 1 - 2 * (z % 2)
    outer = z_out * 4 + y * 2 + core
    z_mid = 3 - z
    inner = z_mid * 4 + y * 2 + core
    is_mid = (z == 1) | (z == 2)
    is_end = (z == 0) | (z == 3)

    def at(offset, size):
        return pl.ds(pl.multiple_of(offset, quarter), size)

    mine, other = at(core * half, half), at((1 - core) * half, half)
    my_y, other_y = at(core * half + y * quarter, quarter), at(core * half + (1 - y) * quarter, quarter)
    zq = jnp.where(z <= 1, 0, 1)
    my_z = at(core * half + zq * quarter, quarter)
    other_z = at(core * half + (1 - zq) * quarter, quarter)

    total = sum(widths)
    chunks = [(start, min(block, total - start)) for start in range(0, total, block)]
    starts = [sum(widths[:i]) for i in range(count)]
    loads = [
        pltpu.make_async_copy(ins[i], acc.at[:, starts[i] : starts[i] + widths[i]], in_sem.at[i])
        for i in range(count)
    ]
    for load in loads:
        load.start()
    barrier = pltpu.get_barrier_semaphore()
    pl.semaphore_signal(barrier, inc=1, device_id={"dp": sibling}, device_id_type=MESH)
    pl.semaphore_signal(barrier, inc=1, device_id={"dp": across}, device_id_type=MESH)
    pl.semaphore_signal(barrier, inc=1, device_id={"dp": outer}, device_id_type=MESH)
    if has_x:
        pl.semaphore_signal(barrier, inc=1, device_id={"tensor": 1 - side}, device_id_type=MESH)

    @pl.when(is_mid)
    def _():
        pl.semaphore_signal(barrier, inc=1, device_id={"dp": inner}, device_id_type=MESH)
        pl.semaphore_wait(barrier, 4 + has_x)

    @pl.when(is_end)
    def _():
        pl.semaphore_wait(barrier, 3 + has_x)

    loaded = [False] * count

    def need(start, size):
        for i in range(count):
            if not loaded[i] and starts[i] < start + size and starts[i] + widths[i] > start:
                loads[i].wait()
                loaded[i] = True

    def copy(src, dst, slot, chunk, device):
        return pltpu.make_async_remote_copy(
            src_ref=src, dst_ref=dst, send_sem=send_sem.at[slot, chunk], recv_sem=recv_sem.at[slot, chunk],
            device_id=device, device_id_type=MESH,
        )

    def add(dst, first, second):
        dst[...] = (first[...].astype(F32) + second[...].astype(F32)).astype(BF16)

    ends = []

    def store(chunk, start, size):
        out = pltpu.make_async_copy(res.at[:, start : start + size], out_ref.at[:, start : start + size], out_sem.at[chunk])
        out.start()
        ends.append((None, out.wait))

    def chunk_steps(chunk, kind):
        start, size = chunks[chunk]
        cols = slice(start, start + size)
        own = functools.partial(copy, chunk=chunk)
        to_core = own(acc.at[other, cols], rc.at[:, cols], 0, device={"dp": sibling})
        back_core = own(res.at[mine, cols], res.at[mine, cols], 6, device={"dp": sibling})
        wait_core = own(res.at[mine, cols], res.at[other, cols], 6, device={"dp": sibling})

        def step0():
            need(start, size)
            to_core.start()
            ends.append((None, to_core.wait_send))

        def merge_core():
            to_core.wait_recv()
            add(acc.at[mine, cols], acc.at[mine, cols], rc.at[:, cols])

        def send_core():
            back_core.start()
            ends.append((None, back_core.wait_send))

        def last():
            wait_core.wait_recv()
            store(chunk, start, size)

        if kind == "P":
            to_y = own(acc.at[other_y, cols], ry.at[:, cols], 1, device={"dp": across})
            to_mid = own(acc.at[my_y, cols], zin.at[:quarter, cols], 2, device={"dp": outer})
            swap = own(acc.at[my_y, cols], zmid.at[:, cols], 3, device={"dp": inner})
            to_end = own(res.at[my_y, cols], res.at[my_y, cols], 4, device={"dp": outer})
            back_y = own(res.at[my_y, cols], res.at[my_y, cols], 5, device={"dp": across})
            wait_y = own(res.at[my_y, cols], res.at[other_y, cols], 5, device={"dp": across})

            def step1():
                merge_core()
                to_y.start()
                ends.append((None, to_y.wait_send))

            def step2():
                to_y.wait_recv()
                add(acc.at[my_y, cols], acc.at[my_y, cols], ry.at[:, cols])

                @pl.when(is_end)
                def _():
                    to_mid.start()

                ends.append((is_end, to_mid.wait_send))

            def step3():
                @pl.when(is_mid)
                def _():
                    to_mid.wait_recv()
                    add(acc.at[my_y, cols], acc.at[my_y, cols], zin.at[:quarter, cols])
                    swap.start()

                ends.append((is_mid, swap.wait_send))

            def step4():
                @pl.when(is_mid)
                def _():
                    swap.wait_recv()
                    add(res.at[my_y, cols], acc.at[my_y, cols], zmid.at[:, cols])
                    to_end.start()
                    back_y.start()

                ends.append((is_mid, to_end.wait_send))

            def step5():
                @pl.when(is_end)
                def _():
                    to_end.wait_recv()
                    back_y.start()

                ends.append((None, back_y.wait_send))

            def step6():
                wait_y.wait_recv()
                send_core()

            steps = [step0, step1, step2, step3, step4, step5, step6, last]
            if start < special:
                to_x = own(res.at[mine, cols], xres.at[mine, cols], 7, device={"tensor": 1 - side})
                x_core = own(xres.at[mine, cols], xres.at[mine, cols], 8, device={"dp": sibling})
                wait_x = own(xres.at[mine, cols], xres.at[other, cols], 8, device={"dp": sibling})

                def step6x():
                    step6()
                    to_x.start()
                    ends.append((None, to_x.wait_send))

                def step7x():
                    last()
                    to_x.wait_recv()
                    x_core.start()
                    ends.append((None, x_core.wait_send))

                def step8x():
                    wait_x.wait_recv()
                    out = pltpu.make_async_copy(xres.at[:, cols], xout_ref.at[:, cols], out_sem.at[len(chunks) + chunk])
                    out.start()
                    ends.append((None, out.wait))

                steps[6:] = [step6x, step7x, step8x]
            return steps

        to_mid = own(acc.at[mine, cols], zin.at[:, cols], 1, device={"dp": outer})
        swap = own(acc.at[other_z, cols], zmid.at[:, cols], 2, device={"dp": inner})
        to_y = own(acc.at[my_z, cols], ry.at[:, cols], 3, device={"dp": across})
        to_inner = own(res.at[my_z, cols], res.at[my_z, cols], 4, device={"dp": inner})
        wait_inner = own(res.at[my_z, cols], res.at[other_z, cols], 4, device={"dp": inner})
        to_end = own(res.at[my_z, cols], res.at[my_z, cols], 5, device={"dp": outer})
        pass_end = own(res.at[other_z, cols], res.at[other_z, cols], 7, device={"dp": outer})

        def step1():
            merge_core()

            @pl.when(is_end)
            def _():
                to_mid.start()

            ends.append((is_end, to_mid.wait_send))

        def step2():
            @pl.when(is_mid)
            def _():
                to_mid.wait_recv()
                add(acc.at[mine, cols], acc.at[mine, cols], zin.at[:, cols])
                swap.start()

            ends.append((is_mid, swap.wait_send))

        def step3():
            @pl.when(is_mid)
            def _():
                swap.wait_recv()
                add(acc.at[my_z, cols], acc.at[my_z, cols], zmid.at[:, cols])
                to_y.start()

            ends.append((is_mid, to_y.wait_send))

        def step4():
            @pl.when(is_mid)
            def _():
                to_y.wait_recv()
                add(res.at[my_z, cols], acc.at[my_z, cols], ry.at[:, cols])
                to_inner.start()
                to_end.start()

            ends.append((is_mid, to_inner.wait_send))
            ends.append((is_mid, to_end.wait_send))

        def step5():
            @pl.when(is_mid)
            def _():
                wait_inner.wait_recv()
                pass_end.start()
                back_core.start()

            ends.append((is_mid, pass_end.wait_send))

        def step6():
            @pl.when(is_end)
            def _():
                to_end.wait_recv()
                pass_end.wait_recv()
                back_core.start()

            ends.append((None, back_core.wait_send))

        return [step0, step1, step2, step3, step4, step5, step6, last]

    plan = []
    for chunk in range(len(chunks)):
        kind = "P" if chunks[chunk][0] < special else pattern[chunk % len(pattern)]
        for index, step in enumerate(chunk_steps(chunk, kind)):
            plan.append((chunk + 2 * lag * index, -index, chunk, step))
    plan.sort(key=lambda item: item[:3])
    for item in plan:
        item[3]()
    for role, wait in ends:
        if role is None:
            wait()
        else:
            pl.when(role)(wait)


def reduce_dp(arrays, special, block=128, lag=1, pattern="PQ", collective_id=0):
    rows = arrays[0].shape[0]
    widths = tuple(a.shape[1] for a in arrays)
    total = sum(widths)
    nchunks = -(-total // block)
    anyspec = pl.BlockSpec(memory_space=pl.ANY)
    outs = [jax.ShapeDtypeStruct((rows, total), BF16)]
    scratch = [
        pltpu.VMEM((rows, total), BF16), pltpu.VMEM((rows, total), BF16), pltpu.VMEM((rows // 2, total), BF16),
        pltpu.VMEM((rows // 4, total), BF16), pltpu.VMEM((rows // 2, total), BF16), pltpu.VMEM((rows // 4, total), BF16),
    ]
    nouts = nchunks
    if special:
        outs.append(jax.ShapeDtypeStruct((rows, special), BF16))
        scratch.append(pltpu.VMEM((rows, special), BF16))
        nouts += -(-special // block)
    scratch += [
        pltpu.SemaphoreType.DMA((len(arrays),)), pltpu.SemaphoreType.DMA((nouts,)),
        pltpu.SemaphoreType.DMA((9, nchunks)), pltpu.SemaphoreType.DMA((9, nchunks)),
    ]
    return pl.pallas_call(
        functools.partial(reduce_kernel, widths=widths, special=special, block=block, lag=lag, pattern=pattern),
        out_shape=outs,
        in_specs=[anyspec] * len(arrays),
        out_specs=[anyspec] * len(outs),
        scratch_shapes=scratch,
        compiler_params=pltpu.CompilerParams(
            collective_id=collective_id, has_side_effects=True, vmem_limit_bytes=REDUCE_LIMIT
        ),
        name="reduce_dp",
    )(*arrays)

def shaped(shape, dtype=F32):
    return jax.ShapeDtypeStruct(shape, dtype)


def whole_call(kernel, outs, scalars, args, flops, name):
    specs = [pl.BlockSpec(memory_space=pltpu.SMEM)] * scalars
    specs += [pl.BlockSpec(memory_space=pltpu.VMEM)] * (len(args) - scalars)
    moved = sum(arg.size * arg.dtype.itemsize for arg in args)
    return pl.pallas_call(
        kernel,
        out_shape=outs,
        in_specs=specs,
        out_specs=[pl.BlockSpec(memory_space=pltpu.VMEM)] * len(outs),
        compiler_params=pltpu.CompilerParams(vmem_limit_bytes=VMEM_LIMIT),
        cost_estimate=pl.CostEstimate(flops=flops, bytes_accessed=moved, transcendentals=0),
        name=name,
    )(*args)


def pad_columns(values, width):
    return jnp.pad(values, ((0, 0), (0, width - values.shape[1]))) if width != values.shape[1] else values


def pad_rows(values, height):
    return jnp.pad(values, ((0, height - values.shape[0]), (0, 0))) if height != values.shape[0] else values


def contract_rows(left, right):
    return mm_tn(jnp.concatenate(left, axis=0), jnp.concatenate(right, axis=0))


def on_device(
    tokens, lengths, cotangent, norm_gain, w_query, w_key, w_value, w_gate_z, w_ssm_x, w_ssm_b, w_ssm_c,
    w_step, conv_x_weight, conv_x_bias, conv_bc_weight, conv_bc_bias, step_bias, decay_log, skip_gain,
    ssm_norm_gain, w_out_att, w_out_ssm, ffn_norm_gain, w_gate, w_up, w_down,
):
    seq_len, model = tokens.shape
    groups = lax.axis_size("tensor")
    position = lax.axis_index("tensor")
    att_width, ssm_width = w_query.shape[1], w_gate_z.shape[1]
    att_pad = -(-att_width // LANES) * LANES
    ssm_pad = -(-ssm_width // LANES) * LANES
    ssm_heads = ssm_width // SSM_DIM
    ssm_width_all = SSM_HEADS * SSM_DIM
    ff_width = w_gate.shape[1]

    def fetch(values, shift):
        return lax.ppermute(values, "tensor", [((i + shift) % groups, i) for i in range(groups)])

    def deliver(values, shift):
        return lax.ppermute(values, "tensor", [(i, (i + shift) % groups) for i in range(groups)])

    def gather(values):
        return [values] + [fetch(values, k) for k in range(1, groups)]

    def scatter_sum(own, others):
        total = own
        for k in range(1, groups):
            total = total + deliver(others[k - 1], k).astype(F32)
        return total

    kv_head = position * (att_width // HEAD_DIM) // (HEADS // KV_HEADS)
    w_kv = jnp.concatenate(
        [lax.dynamic_slice_in_dim(w, kv_head * HEAD_DIM, HEAD_DIM, 1) for w in (w_key, w_value)], axis=1
    )
    wq = pad_columns(w_query, att_pad)
    wz, wx = pad_columns(w_gate_z, ssm_pad), pad_columns(w_ssm_x, ssm_pad)
    wt = pad_rows(w_step.T, 16)
    wa, ws = pad_rows(w_out_att, att_pad), pad_rows(w_out_ssm, ssm_pad)
    cxw, cxb = pad_columns(conv_x_weight, ssm_pad), pad_columns(conv_x_bias[None], ssm_pad)
    cbb = conv_bc_bias[None]
    gain = pad_columns(ssm_norm_gain[None], ssm_pad)
    skip = pad_columns(jnp.repeat(skip_gain, SSM_DIM)[None], ssm_pad)
    bias = pad_columns(step_bias[None], 16)
    rate = pad_columns(jnp.exp(decay_log)[None], 16)
    bias_col, rate_col = bias.T, rate.T
    half = HEAD_DIM // 2
    freqs = ROPE_BASE ** (-(jnp.arange(half).astype(F32) * 2.0 / HEAD_DIM))
    angles = jnp.arange(seq_len).astype(F32)[:, None] * freqs[None, :]
    cosine, sine, none = jnp.cos(angles), jnp.sin(angles), jnp.zeros_like(angles)
    cos_table = jnp.concatenate([cosine] * 4, axis=1)
    sine_first = jnp.concatenate([-sine, none] * 2, axis=1)
    sine_second = jnp.concatenate([none, sine] * 2, axis=1)

    inputs = tokens.astype(F32)
    inv1 = lax.rsqrt(jnp.mean(inputs * inputs, axis=1, keepdims=True) + EPSILON)
    h_own = (inputs * inv1 * norm_gain).astype(BF16)
    own_mask = jnp.arange(seq_len) < lengths[0]
    ct_own = jnp.where(own_mask[:, None], cotangent, jnp.zeros_like(cotangent))
    h_all = gather(h_own)
    len_all = gather(lengths)
    ct_all = gather(ct_own)

    def forward(k):
        outs = [
            shaped((seq_len, att_pad), BF16), shaped((seq_len, LANES), BF16), shaped((seq_len, LANES), BF16),
            shaped((seq_len, ssm_pad)), shaped((seq_len, ssm_pad)), shaped((seq_len, 2 * STATE)),
            shaped((seq_len, 2 * STATE), BF16), shaped((seq_len, 16)), shaped((16, seq_len)),
            shaped((seq_len, ssm_pad)), shaped((16, seq_len)),
        ]
        args = [
            len_all[k], h_all[k], wq, w_kv, wz, wx, w_ssm_b, w_ssm_c, wt, cxw, cxb, conv_bc_weight, cbb,
            bias, rate, bias_col, rate_col, skip, cos_table, sine_first, sine_second,
        ]
        return whole_call(mixer_forward_kernel, outs, 1, args, 8 * 10**9, "mixer_forward")

    def attend(k):
        q, kd, vd = kept[k][:3]
        return whole_call(
            attend_kernel, [shaped((seq_len, att_pad), BF16)], 1, [len_all[k], q, kd, vd], 2 * 10**9, "attend"
        )[0]

    kept = [forward(k) for k in range(groups)]
    squares_part = [one[10] for one in kept]
    squares = [squares_part[k] for k in range(groups)]
    for shift in range(1, groups):
        for k in range(groups):
            squares[k] = squares[k] + fetch(squares_part[(k - shift) % groups], shift)
    mix_att = [attend(k) for k in range(groups)]

    def project(k, dtype):
        q, kd, vd, z, x, bcp, bc, tp, tpr, y, _ = kept[k]
        return whole_call(
            functools.partial(out_kernel, width=ssm_width_all),
            [shaped((seq_len, model), dtype), shaped((seq_len, ssm_pad), BF16)],
            0,
            [mix_att[k], y, x, z, squares[k], cxw, cxb, skip, gain, wa, ws],
            4 * 10**9,
            "out_project",
        )

    projected = [project(k, F32 if k == 0 else BF16) for k in range(groups)]
    mix_ssm = [one[1] for one in projected]
    branch = scatter_sum(projected[0][0], [one[0] for one in projected[1:]])
    resid = inputs + branch
    inv2 = lax.rsqrt(jnp.mean(resid * resid, axis=1, keepdims=True) + EPSILON)
    h2_own = (resid * inv2 * ffn_norm_gain).astype(BF16)
    h2_all = gather(h2_own)

    def feed(k):
        dtype = F32 if k == 0 else BF16
        block = min(256, ff_width)
        full = pl.BlockSpec((seq_len, model), lambda i: (0, 0))
        columns = pl.BlockSpec((model, block), lambda i: (0, i))
        rows = pl.BlockSpec((block, model), lambda i: (i, 0))
        tall = pl.BlockSpec((seq_len, block), lambda i: (0, i))
        return pl.pallas_call(
            ffn_kernel,
            grid=(ff_width // block,),
            out_shape=[shaped((seq_len, ff_width), BF16)] * 3 + [shaped((seq_len, model), dtype)] * 2,
            in_specs=[full, full, columns, columns, rows],
            out_specs=[tall] * 3 + [full] * 2,
            scratch_shapes=[pltpu.VMEM((seq_len, model), F32)] * 2,
            compiler_params=pltpu.CompilerParams(vmem_limit_bytes=VMEM_LIMIT),
            cost_estimate=pl.CostEstimate(flops=8 * 10**9, bytes_accessed=10**7, transcendentals=0),
            name="feed_forward",
        )(h2_all[k], ct_all[k], w_gate, w_up, w_down)

    fed = [feed(k) for k in range(groups)]
    d_second = scatter_sum(fed[0][4], [one[4] for one in fed[1:]])
    ffn_result = scatter_sum(fed[0][3], [one[3] for one in fed[1:]])
    layer_output = (resid + ffn_result).astype(BF16)
    grad_gate = contract_rows(h2_all, [one[1] for one in fed])
    grad_up = contract_rows(h2_all, [one[2] for one in fed])
    grad_down = contract_rows([one[0] for one in fed], ct_all)

    scaled = d_second * ffn_norm_gain
    d_resid = (
        ct_own.astype(F32)
        + inv2 * scaled
        - resid * (inv2**3) * jnp.mean(scaled * resid, axis=1, keepdims=True)
    )
    grad_ffn_gain = jnp.sum(d_second * resid * inv2, axis=0)
    db_all = gather(d_resid.astype(BF16))

    def mix_grad(k):
        q, kd, vd, z, x, bcp, bc, tp, tpr, y, _ = kept[k]
        return whole_call(
            mix_grad_kernel,
            [shaped((seq_len, att_pad), BF16), shaped((seq_len, ssm_pad), BF16), shaped((16, seq_len))],
            0,
            [db_all[k], y, x, z, cxw, cxb, skip, gain, wa, ws],
            4 * 10**9,
            "mix_grad",
        )

    mixed = [mix_grad(k) for k in range(groups)]
    backs_part = [one[2] for one in mixed]
    backs = [backs_part[k] for k in range(groups)]
    for shift in range(1, groups):
        for k in range(groups):
            backs[k] = backs[k] + fetch(backs_part[(k - shift) % groups], shift)

    def attend_back(k):
        q, kd, vd = kept[k][:3]
        return whole_call(
            attend_back_kernel,
            [shaped((seq_len, att_pad), BF16), shaped((seq_len, LANES), BF16)],
            1,
            [len_all[k], q, kd, vd, mixed[k][0], cos_table, sine_first, sine_second],
            4 * 10**9,
            "attend_back",
        )

    turned = [attend_back(k) for k in range(groups)]

    def backward(k):
        q, kd, vd, z, x, bcp, bc, tp, tpr, y, _ = kept[k]
        outs = [
            shaped((seq_len, model), F32 if k == 0 else BF16), shaped((seq_len, ssm_pad), BF16),
            shaped((seq_len, ssm_pad), BF16), shaped((seq_len, 2 * STATE), BF16), shaped((seq_len, 16), BF16),
            shaped((8, ssm_pad)), shaped((8, 2 * STATE)), shaped((8, 16)),
        ]
        args = [
            len_all[k], mixed[k][1], y, x, z, bcp, bc, tp, tpr, squares[k], backs[k], turned[k][0], turned[k][1],
            wq, w_kv, wz, wx, w_ssm_b, w_ssm_c, wt, cxw, cxb, conv_bc_weight, cbb, bias, rate, bias_col, rate_col,
            skip, gain,
        ]
        return whole_call(
            functools.partial(mixer_back_kernel, width=ssm_width_all), outs, 1, args, 16 * 10**9, "mixer_back"
        )

    gone = [None] * groups
    for k in list(range(1, groups)) + [0]:
        gone[k] = backward(k)
    d_first = scatter_sum(gone[0][0], [one[0] for one in gone[1:]])
    scaled = d_first * norm_gain
    grad_input = (
        d_resid
        + inv1 * scaled
        - inputs * (inv1**3) * jnp.mean(scaled * inputs, axis=1, keepdims=True)
    )
    grad_norm_gain = jnp.sum(d_first * inputs * inv1, axis=0)

    wide, bcg, small = (sum(one[i] for one in gone) for i in (5, 6, 7))
    grad_skip = jnp.sum(wide[5, :ssm_width].reshape(ssm_heads, SSM_DIM), axis=1)
    grad_q = contract_rows(h_all, [one[0] for one in turned])
    grad_kv = contract_rows(h_all, [one[1] for one in turned])
    grad_bc = contract_rows(h_all, [one[3] for one in gone])
    grad_x = contract_rows(h_all, [one[1] for one in gone])
    grad_z = contract_rows(h_all, [one[2] for one in gone])
    grad_step = contract_rows(h_all, [one[4] for one in gone])
    grad_att = contract_rows(mix_att, db_all)
    grad_ssm = contract_rows(mix_ssm, db_all)
    norms = jnp.concatenate([bcg[:5].reshape(-1), grad_norm_gain, grad_ffn_gain])

    if lax.axis_size("dp") == 16 and groups == 2:
        norms = norms + fetch(norms, 1)
        own_bc = lax.dynamic_slice_in_dim(grad_bc, position * STATE, STATE, 1)
        peer_bc = lax.dynamic_slice_in_dim(grad_bc, (1 - position) * STATE, STATE, 1).astype(BF16)
        own_bc = own_bc + deliver(peer_bc, 1).astype(F32)
        flat = jnp.concatenate([wide[:7].reshape(-1), small[:2].reshape(-1), norms])
        flat = jnp.pad(flat, (0, -flat.shape[0] % HEAD_DIM)).reshape(-1, HEAD_DIM)
        flat = jnp.pad(flat, ((0, model - flat.shape[0]), (0, 0)))
        misc = jnp.concatenate([pad_columns(grad_step, HEAD_DIM), flat], axis=1)
        out = jnp.concatenate([grad_att, grad_ssm], axis=0)
        arrays = [part.astype(BF16) for part in (grad_kv, own_bc, misc, grad_q, grad_z, grad_x, out)]
        total, peer = reduce_dp(arrays, 2 * LANES)
        ends = [0]
        for part in arrays:
            ends.append(ends[-1] + part.shape[1])
        kv, own_bc, misc, grad_q, grad_z, grad_x, out = (
            total[:, first:last].astype(F32) for first, last in zip(ends, ends[1:])
        )
        peer = peer.astype(F32)
        even = position == 0

        def by_place(own, other):
            return jnp.where(even, jnp.concatenate([own, other], axis=1), jnp.concatenate([other, own], axis=1))

        grad_key = by_place(kv[:, :HEAD_DIM], peer[:, :HEAD_DIM])
        grad_value = by_place(kv[:, HEAD_DIM:], peer[:, HEAD_DIM:LANES])
        grad_b = jnp.where(even, own_bc, peer[:, LANES:])
        grad_c = jnp.where(even, peer[:, LANES:], own_bc)
        grad_step = misc[:, :16]
        flat = misc[:, HEAD_DIM:].reshape(-1)
        wide = flat[: 7 * ssm_pad].reshape(7, ssm_pad)
        small = flat[7 * ssm_pad : 7 * ssm_pad + 32].reshape(2, 16)
        norms = flat[7 * ssm_pad + 32 :]
        grad_att, grad_ssm = out[:att_width], out[att_width:]
        grad_skip = jnp.sum(wide[5].reshape(ssm_heads, SSM_DIM), axis=1)
    else:
        zeros = jnp.zeros((model, KV_HEADS * HEAD_DIM), F32)
        grad_key = lax.dynamic_update_slice(zeros, grad_kv[:, :HEAD_DIM], (0, kv_head * HEAD_DIM))
        grad_value = lax.dynamic_update_slice(zeros, grad_kv[:, HEAD_DIM:], (0, kv_head * HEAD_DIM))
        grad_key, grad_value, grad_bc, norms = lax.psum((grad_key, grad_value, grad_bc, norms), ("dp", "tensor"))
        grad_b, grad_c = grad_bc[:, :STATE], grad_bc[:, STATE:]
        grad_q, grad_z, grad_x, grad_step, grad_att, grad_ssm, wide, small, grad_skip = (
            lax.psum(part.astype(BF16), "dp").astype(F32)
            for part in (grad_q, grad_z, grad_x, grad_step, grad_att, grad_ssm, wide, small, grad_skip)
        )
    grad_gate, grad_up, grad_down = (
        lax.psum(part.astype(BF16), "dp").astype(F32) for part in (grad_gate, grad_up, grad_down)
    )
    bcg = norms[: 10 * STATE].reshape(5, 2 * STATE)
    return (
        layer_output,
        grad_input,
        norms[10 * STATE : 10 * STATE + model],
        grad_q[:, :att_width],
        grad_key,
        grad_value,
        grad_z[:, :ssm_width],
        grad_x[:, :ssm_width],
        grad_b,
        grad_c,
        grad_step[:, :ssm_heads],
        wide[:4, :ssm_width],
        wide[4, :ssm_width],
        bcg[:4],
        bcg[4],
        small[0, :ssm_heads],
        small[1, :ssm_heads],
        grad_skip,
        wide[6, :ssm_width],
        grad_att[:att_width],
        grad_ssm[:ssm_width],
        norms[10 * STATE + model : 10 * STATE + 2 * model],
        grad_gate,
        grad_up,
        grad_down,
    )


def solution(mesh):
    rows, split, tall = P(("dp", "tensor"), None), P(None, "tensor"), P("tensor", None)
    vector, copied = P("tensor"), P()
    return jax.shard_map(
        on_device,
        mesh=mesh,
        in_specs=(
            rows, P(("dp", "tensor")), rows, copied, split, copied, copied, split, split, copied, copied, split,
            split, vector, copied, copied, vector, vector, vector, vector, tall, tall, copied, split, split, tall,
        ),
        out_specs=(
            rows, rows, copied, split, copied, copied, split, split, copied, copied, split, split, vector, copied,
            copied, vector, vector, vector, vector, tall, tall, copied, split, split, tall,
        ),
        check_vma=False,
    )
```

```python
import functools

import jax
import jax.numpy as jnp
from jax import lax
from jax.experimental import pallas as pl
from jax.experimental.pallas import tpu as pltpu
from jax.sharding import PartitionSpec as P

HEADS = 8
KV_HEADS = 2
HEAD_DIM = 64
SSM_HEADS = 24
SSM_DIM = 64
STATE = 128
SPAN = 128
LANES = 128

EPSILON = 1e-05
ROPE_BASE = 100000000000.0
F32 = jnp.float32
BF16 = jnp.bfloat16
VMEM_LIMIT = 50 * 1024 * 1024
REDUCE_LIMIT = 62 * 1024 * 1024
MESH = pl.DeviceIdType.MESH


def mm(left, right):
    return jnp.dot(left, right, preferred_element_type=F32)


def mm_nt(left, right):
    return lax.dot_general(left, right, (((1,), (1,)), ((), ())), preferred_element_type=F32)


def mm_tn(left, right):
    return lax.dot_general(left, right, (((0,), (0,)), ((), ())), preferred_element_type=F32)


def pieces(values, count):
    terms = []
    for _ in range(count):
        term = values.astype(BF16)
        terms.append(term)
        values = values - term.astype(F32)
    return terms


def sigmoid(values):
    return 1.0 / (1.0 + jnp.exp(-values))


def softplus(values):
    return jnp.maximum(values, 0.0) + jnp.log1p(jnp.exp(-jnp.abs(values)))


def lane_ids(shape):
    return lax.broadcasted_iota(jnp.int32, shape, 1)


def row_ids(shape):
    return lax.broadcasted_iota(jnp.int32, shape, 0)


def repeat_lanes(column, count):
    return jnp.concatenate([column] * count, axis=1) if count > 1 else column


def column_of(row):
    ones = jnp.where(row_ids((16, LANES)) == 0, 1.0, 0.0).astype(BF16)
    total = None
    for term in pieces(row, 3):
        part = mm_tn(term, ones)
        total = part if total is None else total + part
    return total


def row_sums(values):
    ones = jnp.ones((16, values.shape[1]), BF16)
    high, low = pieces(values, 2)
    return mm_nt(ones, high) + mm_nt(ones, low)


def causal_shift(values, steps):
    if steps == 0:
        return values
    rolled = pltpu.roll(values, steps, 0)
    return jnp.where(row_ids(values.shape) >= steps, rolled, 0.0)


def anti_shift(values, steps):
    if steps == 0:
        return values
    length = values.shape[0]
    rolled = pltpu.roll(values, length - steps, 0)
    return jnp.where(row_ids(values.shape) < length - steps, rolled, 0.0)


def conv(values, weight, bias):
    taps = weight.shape[0]
    total = bias + weight[taps - 1 : taps] * values
    for offset in range(taps - 1):
        total = total + weight[offset : offset + 1] * causal_shift(values, taps - 1 - offset)
    return total


def conv_back(grad, values, weight):
    taps = weight.shape[0]
    total, rows = None, []
    for offset in range(taps):
        steps = taps - 1 - offset
        moved = anti_shift(grad, steps)
        part = weight[offset : offset + 1] * moved
        total = part if total is None else total + part
        rows.append(jnp.sum(moved * values, axis=0, keepdims=True))
    rows.append(jnp.sum(grad, axis=0, keepdims=True))
    return total, rows


def rope(values, cosine, sine_first, sine_second):
    ahead = pltpu.roll(values, LANES - HEAD_DIM // 2, 1)
    behind = pltpu.roll(values, HEAD_DIM // 2, 1)
    return values * cosine + ahead * sine_first + behind * sine_second


def lower_mask():
    return row_ids((SPAN, SPAN)) >= lane_ids((SPAN, SPAN))


def span_sums(values):
    lower = jnp.where(lower_mask(), 1.0, 0.0).astype(BF16)
    out = []
    for start in range(0, values.shape[0], SPAN):
        total = None
        for term in pieces(values[start : start + SPAN], 3):
            part = mm(lower, term)
            total = part if total is None else total + part
        out.append(total)
    return jnp.concatenate(out, axis=0)


def span_sums_rows(values):
    upper = jnp.where(row_ids((SPAN, SPAN)) <= lane_ids((SPAN, SPAN)), 1.0, 0.0).astype(BF16)
    out = []
    for start in range(0, values.shape[1], SPAN):
        total = None
        for term in pieces(values[:, start : start + SPAN], 3):
            part = mm(term, upper)
            total = part if total is None else total + part
        out.append(total)
    return jnp.concatenate(out, axis=1)


def span_sums_back(values):
    upper = jnp.where(row_ids((SPAN, SPAN)) <= lane_ids((SPAN, SPAN)), 1.0, 0.0).astype(BF16)
    out = []
    for start in range(0, values.shape[0], SPAN):
        total = None
        for term in pieces(values[start : start + SPAN], 3):
            part = mm(upper, term)
            total = part if total is None else total + part
        out.append(total)
    return jnp.concatenate(out, axis=0)


def steps_of(tp, tp_row, bias, bias_col, rate, rate_col, length):
    seq_len = tp.shape[0]
    valid = jnp.where(row_ids((seq_len, 1)) < length, 1.0, 0.0)
    valid_row = jnp.where(lane_ids((1, seq_len)) < length, 1.0, 0.0)
    dt = softplus(tp + bias) * valid
    dt_row = softplus(tp_row + bias_col) * valid_row
    cum = span_sums(-(dt * rate))
    cum_row = span_sums_rows(-(dt_row * rate_col))
    return valid, dt, cum, cum_row


def spread(values, head):
    return jnp.broadcast_to(values[:, head : head + 1], (values.shape[0], LANES))


def decays(cum_first, cum_second, cum_row, pair, span):
    rows = slice(span * SPAN, (span + 1) * SPAN)
    lower = lower_mask()
    out = []
    for head, column in ((2 * pair, cum_first), (2 * pair + 1, cum_second)):
        differ = column[rows] - cum_row[head : head + 1, rows]
        out.append(jnp.exp(jnp.where(lower, differ, -1e30)))
    return out


def split_heads(values):
    first = lane_ids(values.shape) < HEAD_DIM
    zero = jnp.zeros_like(values)
    return jnp.concatenate([jnp.where(first, values, zero), jnp.where(first, zero, values)], axis=0)


def state_of(in_map, weighted_first, cum_pair_first):
    to_end = jnp.exp(cum_pair_first[SPAN - 1 : SPAN] - cum_pair_first)
    ending = (weighted_first * to_end).astype(BF16)
    return to_end, ending, mm_tn(in_map[:SPAN], ending)


def mixer_forward_kernel(
    len_ref, h_ref, wq_ref, wkv_ref, wz_ref, wx_ref, wb_ref, wc_ref, wt_ref, cxw_ref, cxb_ref,
    cbw_ref, cbb_ref, bias_ref, rate_ref, bias_col_ref, rate_col_ref, skip_ref, cos_ref, sa_ref,
    sb_ref, q_ref, kd_ref, vd_ref, z_ref, x_ref, bcp_ref, bc_ref, tp_ref, tpr_ref, y_ref, ss_ref,
):
    h = h_ref[...]
    pairs = wx_ref.shape[1] // LANES
    z_ref[...] = mm(h, wz_ref[...])
    x_ref[...] = mm(h, wx_ref[...])
    bcp_ref[:, :STATE] = mm(h, wb_ref[...])
    bcp_ref[:, STATE:] = mm(h, wc_ref[...])
    tp = mm_nt(h, wt_ref[...])
    tp_row = mm_nt(wt_ref[...], h)
    tp_ref[...] = tp
    tpr_ref[...] = tp_row
    cosine, sine_first, sine_second = cos_ref[...], sa_ref[...], sb_ref[...]
    for pair in range(wq_ref.shape[1] // LANES):
        lanes = slice(pair * LANES, (pair + 1) * LANES)
        q_ref[:, lanes] = rope(mm(h, wq_ref[:, lanes]), cosine, sine_first, sine_second).astype(BF16)
    kv = mm(h, wkv_ref[...])
    turned = pltpu.roll(kv, HEAD_DIM, 1)
    first = lane_ids(kv.shape) < HEAD_DIM
    kd_ref[...] = rope(jnp.where(first, kv, turned), cosine, sine_first, sine_second).astype(BF16)
    vd_ref[...] = jnp.where(first, turned, kv).astype(BF16)

    mapped = conv(bcp_ref[...], cbw_ref[...], cbb_ref[...])
    bc = (mapped * sigmoid(mapped)).astype(BF16)
    bc_ref[...] = bc
    in_map, out_map = bc[:, :STATE], bc[:, STATE:]
    affinity = [
        mm_nt(out_map[s * SPAN : (s + 1) * SPAN], in_map[s * SPAN : (s + 1) * SPAN]) for s in range(2)
    ]
    _, dt, cum, cum_row = steps_of(
        tp, tp_row, bias_ref[...], bias_col_ref[...], rate_ref[...], rate_col_ref[...], len_ref[0]
    )
    squares = None
    for pair in range(pairs):
        lanes = slice(pair * LANES, (pair + 1) * LANES)
        cx = conv(x_ref[:, lanes], cxw_ref[:, lanes], cxb_ref[:, lanes])
        xc = cx * sigmoid(cx)
        dt_pair = jnp.where(first, spread(dt, 2 * pair), spread(dt, 2 * pair + 1))
        cum_first, cum_second = spread(cum, 2 * pair), spread(cum, 2 * pair + 1)
        cum_pair = jnp.where(first, cum_first, cum_second)
        weighted = xc * dt_pair
        low = weighted.astype(BF16)
        _, _, state = state_of(in_map, weighted[:SPAN], cum_pair[:SPAN])
        parts = []
        for s in range(2):
            rows = slice(s * SPAN, (s + 1) * SPAN)
            mats = [
                (affinity[s] * decay).astype(BF16)
                for decay in decays(cum_first, cum_second, cum_row, pair, s)
            ]
            part = mm(jnp.concatenate(mats, axis=1), split_heads(low[rows]))
            if s:
                part = part + mm(out_map[rows], state.astype(BF16)) * jnp.exp(cum_pair[rows])
            parts.append(part)
        y = jnp.concatenate(parts, axis=0)
        y_ref[:, lanes] = y
        z = z_ref[:, lanes]
        gated = (y + skip_ref[:, lanes] * xc) * (z * sigmoid(z))
        square = gated * gated
        squares = square if squares is None else squares + square
    ss_ref[...] = row_sums(squares)


def masked_probs(queries, kd, length, scale):
    seq_len = kd.shape[0]
    scores = mm_nt(split_heads(queries), kd) * scale
    rows = row_ids(scores.shape)
    rows = jnp.where(rows >= seq_len, rows - seq_len, rows)
    columns = lane_ids(scores.shape)
    scores = jnp.where((rows >= columns) & (columns < length), scores, -1e30)
    weights = jnp.exp(scores - jnp.max(scores, axis=1, keepdims=True))
    return weights / jnp.sum(weights, axis=1, keepdims=True)


def attend_kernel(len_ref, q_ref, kd_ref, vd_ref, out_ref):
    seq_len = q_ref.shape[0]
    values = split_heads(vd_ref[...])
    for pair in range(q_ref.shape[1] // LANES):
        lanes = slice(pair * LANES, (pair + 1) * LANES)
        probs = masked_probs(q_ref[:, lanes], kd_ref[...], len_ref[0], HEAD_DIM ** (-0.5)).astype(BF16)
        both = jnp.concatenate([probs[:seq_len], probs[seq_len:]], axis=1)
        out_ref[:, lanes] = mm(both, values).astype(BF16)


def join_halves(values):
    return values + pltpu.roll(values, HEAD_DIM, 1)


def attend_back_kernel(len_ref, q_ref, kd_ref, vd_ref, da_ref, cos_ref, sa_ref, sb_ref, dq_ref, dkv_ref):
    seq_len = q_ref.shape[0]
    scale = HEAD_DIM ** (-0.5)
    cosine, sine_first, sine_second = cos_ref[...], -sa_ref[...], -sb_ref[...]
    kd, vd = kd_ref[...], vd_ref[...]
    keys = split_heads(kd)
    grad_k, grad_v = None, None
    for pair in range(q_ref.shape[1] // LANES):
        lanes = slice(pair * LANES, (pair + 1) * LANES)
        probs = masked_probs(q_ref[:, lanes], kd, len_ref[0], scale)
        da = split_heads(da_ref[:, lanes])
        dprob = mm_nt(da, vd)
        dscore = (probs * (dprob - jnp.sum(probs * dprob, axis=1, keepdims=True))).astype(BF16)
        both = jnp.concatenate([dscore[:seq_len], dscore[seq_len:]], axis=1)
        dq = mm(both, keys) * scale
        dq_ref[:, lanes] = rope(dq, cosine, sine_first, sine_second).astype(BF16)
        part_k = mm_tn(dscore, split_heads(q_ref[:, lanes]))
        part_v = mm_tn(probs.astype(BF16), da)
        grad_k = part_k if grad_k is None else grad_k + part_k
        grad_v = part_v if grad_v is None else grad_v + part_v
    dk = rope(join_halves(grad_k) * scale, cosine, sine_first, sine_second)
    first = lane_ids(dk.shape) < HEAD_DIM
    dkv_ref[...] = jnp.where(first, dk, join_halves(grad_v)).astype(BF16)


def out_kernel(att_ref, y_ref, x_ref, z_ref, ss_ref, cxw_ref, cxb_ref, skip_ref, gain_ref, wa_ref, ws_ref,
               part_ref, mix_ref, *, width):
    total = mm(att_ref[...], wa_ref[...])
    inv = column_of(lax.rsqrt(ss_ref[...] / width + EPSILON))
    for pair in range(y_ref.shape[1] // LANES):
        lanes = slice(pair * LANES, (pair + 1) * LANES)
        cx = conv(x_ref[:, lanes], cxw_ref[:, lanes], cxb_ref[:, lanes])
        z = z_ref[:, lanes]
        gated = (y_ref[:, lanes] + skip_ref[:, lanes] * (cx * sigmoid(cx))) * (z * sigmoid(z))
        mix_ref[:, lanes] = (gated * inv * gain_ref[:, lanes]).astype(BF16)
    part_ref[...] = (total + mm(mix_ref[...], ws_ref[...])).astype(part_ref.dtype)


def mix_grad_kernel(db_ref, y_ref, x_ref, z_ref, cxw_ref, cxb_ref, skip_ref, gain_ref, wa_ref, ws_ref,
                    da_ref, dm_ref, bs_ref):
    db = db_ref[...]
    da_ref[...] = mm_nt(db, wa_ref[...]).astype(BF16)
    dm_ref[...] = mm_nt(db, ws_ref[...]).astype(BF16)
    total = None
    for pair in range(y_ref.shape[1] // LANES):
        lanes = slice(pair * LANES, (pair + 1) * LANES)
        cx = conv(x_ref[:, lanes], cxw_ref[:, lanes], cxb_ref[:, lanes])
        z = z_ref[:, lanes]
        gated = (y_ref[:, lanes] + skip_ref[:, lanes] * (cx * sigmoid(cx))) * (z * sigmoid(z))
        part = gated * (gain_ref[:, lanes] * dm_ref[:, lanes].astype(F32))
        total = part if total is None else total + part
    bs_ref[...] = row_sums(total)


def head_sums(values, pair):
    rows, columns = row_ids((LANES, 16)), lane_ids((LANES, 16))
    chosen = jnp.where(columns == 2 * pair + jnp.where(rows < HEAD_DIM, 0, 1), 1.0, 0.0).astype(BF16)
    high, low = pieces(values, 2)
    return mm(jnp.concatenate([high, low], axis=1), jnp.concatenate([chosen, chosen], axis=0))


def mixer_back_kernel(
    len_ref, dm_ref, y_ref, x_ref, z_ref, bcp_ref, bc_ref, tp_ref, tpr_ref, ss_ref, bs_ref, dq_ref,
    dkv_ref, wq_ref, wkv_ref, wz_ref, wx_ref, wb_ref, wc_ref, wt_ref, cxw_ref, cxb_ref, cbw_ref,
    cbb_ref, bias_ref, rate_ref, bias_col_ref, rate_col_ref, skip_ref, gain_ref,
    dh_ref, dx_ref, dz_ref, dbc_ref, dt_ref, wide_ref, bcg_ref, small_ref, *, width, tick=lambda: None,
):
    pairs = x_ref.shape[1] // LANES
    bc = bc_ref[...]
    in_map, out_map = bc[:, :STATE], bc[:, STATE:]
    affinity = [
        mm_nt(out_map[s * SPAN : (s + 1) * SPAN], in_map[s * SPAN : (s + 1) * SPAN]) for s in range(2)
    ]
    valid, dt, cum, cum_row = steps_of(
        tp_ref[...], tpr_ref[...], bias_ref[...], bias_col_ref[...], rate_ref[...], rate_col_ref[...], len_ref[0]
    )
    inv_row = lax.rsqrt(ss_ref[...] / width + EPSILON)
    inv = column_of(inv_row)
    back = column_of(inv_row * inv_row * inv_row * bs_ref[...] / width)
    first = lane_ids((x_ref.shape[0], LANES)) < HEAD_DIM
    last_row = row_ids((SPAN, LANES)) == SPAN - 1
    d_cum, d_step, d_skip = None, None, None
    wide_ref[7:8, :] = jnp.zeros((1, wide_ref.shape[1]), F32)
    d_aff, d_out, d_in = [None, None], None, None

    def plus(total, part):
        return part if total is None else total + part

    for pair in range(pairs):
        lanes = slice(pair * LANES, (pair + 1) * LANES)
        x = x_ref[:, lanes]
        cxw = cxw_ref[:, lanes]
        cx = conv(x, cxw, cxb_ref[:, lanes])
        sx = sigmoid(cx)
        xc = cx * sx
        z = z_ref[:, lanes]
        sz = sigmoid(z)
        silu_z = z * sz
        scanned = y_ref[:, lanes]
        y = scanned + skip_ref[:, lanes] * xc
        gated = y * silu_z
        d_mix = dm_ref[:, lanes].astype(F32)
        d_gated = inv * (gain_ref[:, lanes] * d_mix) - gated * back
        wide_ref[6:7, lanes] = jnp.sum(d_mix * gated * inv, axis=0, keepdims=True)
        dy = d_gated * silu_z
        dz_ref[:, lanes] = (d_gated * y * (sz * (1.0 + z * (1.0 - sz)))).astype(BF16)
        wide_ref[5:6, lanes] = jnp.sum(dy * xc, axis=0, keepdims=True)
        dt_pair = jnp.where(first, spread(dt, 2 * pair), spread(dt, 2 * pair + 1))
        cum_first, cum_second = spread(cum, 2 * pair), spread(cum, 2 * pair + 1)
        cum_pair = jnp.where(first, cum_first, cum_second)
        weighted = xc * dt_pair
        low = weighted.astype(BF16)
        dy_low = dy.astype(BF16)
        to_end, ending, state = state_of(in_map, weighted[:SPAN], cum_pair[:SPAN])
        d_weighted = []
        for s in range(2):
            rows = slice(s * SPAN, (s + 1) * SPAN)
            decay = decays(cum_first, cum_second, cum_row, pair, s)
            mats = jnp.concatenate([(affinity[s] * one).astype(BF16) for one in decay], axis=0)
            both = split_heads(dy_low[rows])
            d_mats = mm_nt(both, low[rows])
            d_aff[s] = plus(d_aff[s], d_mats[:SPAN] * decay[0] + d_mats[SPAN:] * decay[1])
            d_weighted.append(mm_tn(mats, both))
        reached = (dy[SPAN:] * jnp.exp(cum_pair[SPAN:])).astype(BF16)
        d_out = plus(d_out, mm_nt(reached, state.astype(BF16)))
        d_state = mm_tn(out_map[SPAN:], reached).astype(BF16)
        d_in = plus(d_in, mm_nt(ending, d_state))
        d_ending = mm(in_map[:SPAN], d_state)
        through = ending.astype(F32) * d_ending
        low_f, dy_f = low.astype(F32), dy_low.astype(F32)
        change = dy_f * scanned - low_f * jnp.concatenate(d_weighted, axis=0)
        ended = jnp.where(last_row, jnp.sum(through, axis=0, keepdims=True), 0.0) - through
        change = jnp.concatenate([change[:SPAN] + ended, change[SPAN:]], axis=0)
        d_weight = jnp.concatenate([d_weighted[0] + d_ending * to_end, d_weighted[1]], axis=0)
        d_cum = plus(d_cum, head_sums(change, pair))
        d_step = plus(d_step, head_sums(d_weight * xc, pair))
        d_xc = dy * skip_ref[:, lanes] + d_weight * dt_pair
        d_cx = d_xc * (sx * (1.0 + cx * (1.0 - sx)))
        d_x, rows_x = conv_back(d_cx, x, cxw)
        dx_ref[:, lanes] = d_x.astype(BF16)
        for index, row in enumerate(rows_x):
            wide_ref[index : index + 1, lanes] = row
        d_skip = plus(d_skip, head_sums(wide_ref[:, lanes], pair))
        tick()

    rate = rate_ref[...]
    d_log = span_sums_back(d_cum)
    d_dt = d_step - rate * d_log
    d_tp = d_dt * valid * sigmoid(tp_ref[...] + bias_ref[...])
    small_ref[...] = jnp.zeros(small_ref.shape, F32)
    small_ref[0:1, :] = jnp.sum(d_tp, axis=0, keepdims=True)
    small_ref[1:2, :] = -rate * jnp.sum(dt * d_log, axis=0, keepdims=True)
    small_ref[2:3, :] = d_skip[5:6]
    dt_ref[...] = d_tp.astype(BF16)

    d_maps = []
    low_aff = [part.astype(BF16) for part in d_aff]
    d_ins, d_outs = [], []
    for s in range(2):
        rows = slice(s * SPAN, (s + 1) * SPAN)
        d_outs.append(mm(low_aff[s], in_map[rows]))
        d_ins.append(mm_tn(low_aff[s], out_map[rows]))
    d_outs[1] = d_outs[1] + d_out
    d_ins[0] = d_ins[0] + d_in
    d_maps = jnp.concatenate(
        [jnp.concatenate(d_ins, axis=0), jnp.concatenate(d_outs, axis=0)], axis=1
    )
    mapped = conv(bcp_ref[...], cbw_ref[...], cbb_ref[...])
    sm = sigmoid(mapped)
    d_bc, rows_bc = conv_back(d_maps * (sm * (1.0 + mapped * (1.0 - sm))), bcp_ref[...], cbw_ref[...])
    bcg_ref[...] = jnp.zeros(bcg_ref.shape, F32)
    for index, row in enumerate(rows_bc):
        bcg_ref[index : index + 1, :] = row
    d_bc = d_bc.astype(BF16)
    dbc_ref[...] = d_bc
    total = mm_nt(dx_ref[...], wx_ref[...]) + mm_nt(dz_ref[...], wz_ref[...])
    total = total + mm_nt(dq_ref[...], wq_ref[...]) + mm_nt(dkv_ref[...], wkv_ref[...])
    total = total + mm_nt(d_bc[:, :STATE], wb_ref[...]) + mm_nt(d_bc[:, STATE:], wc_ref[...])
    total = total + mm(dt_ref[...], wt_ref[...])
    dh_ref[...] = total.astype(dh_ref.dtype)


def ffn_kernel(h_ref, ct_ref, wg_ref, wu_ref, wd_ref, hid_ref, dg_ref, du_ref, ff_ref, dh_ref, ff_acc, dh_acc):
    step = pl.program_id(0)
    h = h_ref[...]
    gate = mm(h, wg_ref[...])
    up = mm(h, wu_ref[...])
    d_hidden = mm_nt(ct_ref[...], wd_ref[...]).astype(BF16).astype(F32)
    sg = sigmoid(gate)
    silu = gate * sg
    hidden = (silu * up).astype(BF16)
    d_gate = (d_hidden * up * (sg * (1.0 + gate * (1.0 - sg)))).astype(BF16)
    d_up = (d_hidden * silu).astype(BF16)
    hid_ref[...] = hidden
    dg_ref[...] = d_gate
    du_ref[...] = d_up
    ff_part = mm(hidden, wd_ref[...])
    dh_part = mm_nt(d_gate, wg_ref[...]) + mm_nt(d_up, wu_ref[...])

    @pl.when(step == 0)
    def _():
        ff_acc[...] = ff_part
        dh_acc[...] = dh_part

    @pl.when(step > 0)
    def _():
        ff_acc[...] += ff_part
        dh_acc[...] += dh_part

    @pl.when(step == pl.num_programs(0) - 1)
    def _():
        ff_ref[...] = ff_acc[...].astype(ff_ref.dtype)
        dh_ref[...] = dh_acc[...].astype(dh_ref.dtype)


class Entry:
    def __init__(self, ref):
        self.ref = ref

    def __getitem__(self, index):
        return self.ref[0]


PARTS = 9
GATE, UP, DOWN, SHARED, STEP, QUERY, ZED, EX, OUT = range(PARTS)
KV_AT, B_AT, C_AT, MISC_AT = 0, LANES, 2 * LANES, 3 * LANES
SHARED_WIDTH = 4 * LANES


def chunk_order(widths):
    order = [(part, column) for part in (GATE, UP, DOWN) for column in range(0, widths[part], LANES)]
    order += [(OUT, column) for column in range(0, widths[OUT], LANES)]
    order += [(QUERY, column) for column in range(0, widths[QUERY], LANES)]
    order += [(SHARED, KV_AT), (SHARED, B_AT), (SHARED, C_AT)]
    order += [(EX, column) for column in range(0, widths[EX], LANES)]
    order += [(STEP, 0), (SHARED, MISC_AT)]
    order += [(ZED, column) for column in range(0, widths[ZED], LANES)]
    return [
        (part, column, "P" if part == SHARED or index % 2 else "Q") for index, (part, column) in enumerate(order)
    ]


def back_kernel(*refs, small_names, big_names, widths, width, lag, pace):
    it = iter(refs)
    lens = [Entry(next(it)), Entry(next(it))]
    s = {name: next(it) for name in small_names}
    big_in = {name: next(it) for name in big_names}
    ffn = [next(it) for _ in range(3)]
    outs = [next(it) for _ in range(PARTS)]
    xout, d_first = next(it), next(it)
    b = {name: next(it) for name in big_names}
    (db, bs, bsr, da, dm, dq, dkv, dx, dz, dbc, dt, dt_cat, dh_peer, dh_got, wide, bcg, small, misc,
     mine_f, acc_o, rc, res, ry, zin_p, zin_q, zmid, in_sem, ffn_sem, out_sem, xs, xr, send_sem, recv_sem) = it
    rows = outs[GATE].shape[0]
    half, quarter = rows // 2, rows // 4
    seq_len = db.shape[0] // 2
    me = lax.axis_index("dp")
    core, y, z = me % 2, (me // 2) % 2, me // 4
    side = lax.axis_index("tensor")
    sibling = {"dp": me + 1 - 2 * core}
    across = {"dp": me + 2 - 4 * y}
    outer = {"dp": (z + 1 - 2 * (z % 2)) * 4 + y * 2 + core}
    inner = {"dp": (3 - z) * 4 + y * 2 + core}
    pair = {"tensor": 1 - side}
    is_mid = (z == 1) | (z == 2)
    is_end = (z == 0) | (z == 3)

    def at(offset, size):
        return pl.ds(pl.multiple_of(offset, quarter), size)

    mine, other = at(core * half, half), at((1 - core) * half, half)
    my_y, other_y = at(y * quarter, quarter), at((1 - y) * quarter, quarter)
    zq = jnp.where(z <= 1, 0, 1)
    my_z, other_z = at(zq * quarter, quarter), at((1 - zq) * quarter, quarter)

    loads = {}
    for index, name in enumerate(big_names):
        dst = db.at[:seq_len] if name == "db" else b[name]
        loads[name] = pltpu.make_async_copy(big_in[name], dst, in_sem.at[index])
    ffn_loads = [
        pltpu.make_async_copy(ffn[i].at[mine], mine_f.at[:, i * widths[i] : (i + 1) * widths[i]], ffn_sem.at[i])
        for i in range(3)
    ]
    loads["db"].start()
    ffn_loads[0].start()
    for name in big_names:
        if name != "db":
            loads[name].start()
    ffn_loads[1].start()
    ffn_loads[2].start()
    ready = set()

    def need(*names):
        for name in names:
            if name not in ready:
                (loads[name] if isinstance(name, str) else ffn_loads[name]).wait()
                ready.add(name)

    barrier = pltpu.get_barrier_semaphore()
    for device in (sibling, across, outer, pair):
        pl.semaphore_signal(barrier, inc=1, device_id=device, device_id_type=MESH)

    @pl.when(is_mid)
    def _():
        pl.semaphore_signal(barrier, inc=1, device_id=inner, device_id_type=MESH)
        pl.semaphore_wait(barrier, 5)

    @pl.when(is_end)
    def _():
        pl.semaphore_wait(barrier, 4)

    ends = []

    def remote(src, dst, send, recv, device):
        return pltpu.make_async_remote_copy(
            src_ref=src, dst_ref=dst, send_sem=send, recv_sem=recv, device_id=device, device_id_type=MESH
        )

    def exchange(src, dst, slot):
        copy = remote(src, dst, xs.at[slot], xr.at[slot], pair)
        copy.start()
        return copy

    def make(part, column, span):
        lanes = slice(column, column + LANES)
        if part == SHARED and column == MISC_AT:
            return misc[span, :].astype(F32)
        if part == OUT:
            need("mix_t")
            return mm(b["mix_t"][span, :], db[:, lanes])
        need("h_t")
        if part == SHARED:
            values = dkv[...] if column == KV_AT else dbc[:, column - LANES : column]
        else:
            values = {STEP: dt_cat, QUERY: dq, ZED: dz, EX: dx}[part][:, lanes]
        return mm(b["h_t"][span, :], values)

    def add(dst, first, second):
        dst[...] = (first[...].astype(F32) + second[...].astype(F32)).astype(BF16)

    order = chunk_order(widths)
    made = set()

    def chunk_steps(index):
        part, column, kind = order[index]
        place = sum(1 for other_chunk in order[:index] if other_chunk[2] == kind)
        cols = slice(index * LANES, (index + 1) * LANES)
        local = slice(column, column + LANES)
        tight = slice(place * LANES, (place + 1) * LANES)
        out = outs[part]

        def own(src, dst, slot, device):
            return remote(src, dst, send_sem.at[slot, index], recv_sem.at[slot, index], device)

        if part < SHARED:
            source = ffn[part].at[other, local]
        else:
            start = sum(1 for other_chunk in order[:index] if other_chunk[0] >= SHARED) * LANES
            source = acc_o.at[:, start : start + LANES]
        to_core = own(source, rc.at[:, cols], 0, sibling)
        back_core = own(res.at[:, cols], out.at[mine, local], 6, sibling)
        wait_core = own(res.at[:, cols], out.at[other, local], 6, sibling)
        store = pltpu.make_async_copy(res.at[:, cols], out.at[mine, local], out_sem.at[index])

        def step0():
            if part >= SHARED:
                assert (part, column) in made
                source[...] = make(part, column, other).astype(BF16)
            to_core.start()
            ends.append((None, to_core.wait_send))

        def merge_core():
            if part < SHARED:
                need(part)
                term = mine_f[:, part * widths[part] + column : part * widths[part] + column + LANES].astype(F32)
            else:
                term = make(part, column, mine)
            to_core.wait_recv()
            rc[:, cols] = (rc[:, cols].astype(F32) + term).astype(BF16)

        def send_core():
            back_core.start()
            store.start()

        def last():
            wait_core.wait_recv()

        ends.append((None, back_core.wait_send))
        ends.append((None, store.wait))

        if kind == "P":
            zin = zin_p.at[:, tight]
            to_y = own(rc.at[other_y, cols], ry.at[:, cols], 1, across)
            to_mid = own(rc.at[my_y, cols], zin, 2, outer)
            swap = own(rc.at[my_y, cols], zmid.at[:, cols], 3, inner)
            to_end = own(res.at[my_y, cols], res.at[my_y, cols], 4, outer)
            back_y = own(res.at[my_y, cols], res.at[my_y, cols], 5, across)
            wait_y = own(res.at[my_y, cols], res.at[other_y, cols], 5, across)

            def step1():
                merge_core()
                to_y.start()
                ends.append((None, to_y.wait_send))

            def step2():
                to_y.wait_recv()
                add(rc.at[my_y, cols], rc.at[my_y, cols], ry.at[:, cols])
                pl.when(is_end)(to_mid.start)
                ends.append((is_end, to_mid.wait_send))

            def step3():
                @pl.when(is_mid)
                def _():
                    to_mid.wait_recv()
                    add(rc.at[my_y, cols], rc.at[my_y, cols], zin)
                    swap.start()

                ends.append((is_mid, swap.wait_send))

            def step4():
                @pl.when(is_mid)
                def _():
                    swap.wait_recv()
                    add(res.at[my_y, cols], rc.at[my_y, cols], zmid.at[:, cols])
                    to_end.start()
                    back_y.start()

                ends.append((is_mid, to_end.wait_send))

            def step5():
                @pl.when(is_end)
                def _():
                    to_end.wait_recv()
                    back_y.start()

                ends.append((None, back_y.wait_send))

            def step6():
                wait_y.wait_recv()
                send_core()

            steps = [step0, step1, step2, step3, step4, step5, step6, last]
            if part == SHARED:
                to_x = own(res.at[:, cols], xout.at[mine, local], 7, pair)
                x_core = own(xout.at[mine, local], xout.at[mine, local], 8, sibling)
                wait_x = own(xout.at[mine, local], xout.at[other, local], 8, sibling)

                def step6x():
                    step6()
                    to_x.start()
                    ends.append((None, to_x.wait_send))

                def step7x():
                    last()
                    to_x.wait_recv()
                    x_core.start()
                    ends.append((None, x_core.wait_send))

                steps[6:] = [step6x, step7x, wait_x.wait_recv]
            return steps

        zin = zin_q.at[:, tight]
        to_mid = own(rc.at[:, cols], zin, 1, outer)
        swap = own(rc.at[other_z, cols], zmid.at[:, cols], 2, inner)
        to_y = own(rc.at[my_z, cols], ry.at[:, cols], 3, across)
        to_inner = own(res.at[my_z, cols], res.at[my_z, cols], 4, inner)
        wait_inner = own(res.at[my_z, cols], res.at[other_z, cols], 4, inner)
        to_end = own(res.at[my_z, cols], res.at[my_z, cols], 5, outer)
        pass_end = own(res.at[other_z, cols], res.at[other_z, cols], 7, outer)

        def step1():
            merge_core()
            pl.when(is_end)(to_mid.start)
            ends.append((is_end, to_mid.wait_send))

        def step2():
            @pl.when(is_mid)
            def _():
                to_mid.wait_recv()
                add(rc.at[:, cols], rc.at[:, cols], zin)
                swap.start()

            ends.append((is_mid, swap.wait_send))

        def step3():
            @pl.when(is_mid)
            def _():
                swap.wait_recv()
                add(rc.at[my_z, cols], rc.at[my_z, cols], zmid.at[:, cols])
                to_y.start()

            ends.append((is_mid, to_y.wait_send))

        def step4():
            @pl.when(is_mid)
            def _():
                to_y.wait_recv()
                add(res.at[my_z, cols], rc.at[my_z, cols], ry.at[:, cols])
                to_inner.start()
                to_end.start()

            ends.append((is_mid, to_inner.wait_send))
            ends.append((is_mid, to_end.wait_send))

        def step5():
            @pl.when(is_mid)
            def _():
                wait_inner.wait_recv()
                pass_end.start()
                send_core()

            ends.append((is_mid, pass_end.wait_send))

        def step6():
            @pl.when(is_end)
            def _():
                to_end.wait_recv()
                pass_end.wait_recv()
                send_core()

        return [step0, step1, step2, step3, step4, step5, step6, last]

    plan = [
        (index + 2 * lag * number, -number, index, step)
        for index in range(len(order))
        for number, step in enumerate(chunk_steps(index))
    ]
    plan.sort(key=lambda item: item[:3])
    clock, done = [0.0], [0]

    def tick(time=pace):
        clock[0] += time
        while done[0] < len(plan) and plan[done[0]][0] <= clock[0]:
            plan[done[0]][3]()
            done[0] += 1

    need("db")
    got_db = exchange(db.at[:seq_len], db.at[seq_len:], 0)
    tick(0.0)

    def seq(k):
        return pl.ds(k * seq_len, seq_len)

    def mix(k):
        need("wa", "ws", f"y{k}", f"x{k}", f"z{k}")
        mix_grad_kernel(
            db.at[seq(k)], b[f"y{k}"], b[f"x{k}"], b[f"z{k}"], s["cxw"], s["cxb"], s["skip"], s["gain"], b["wa"],
            b["ws"], da.at[k], dm.at[k], bs.at[k],
        )
        return exchange(bs.at[k], bsr.at[1 - k], 1 + k)

    def attend(k):
        need(f"q{k}", f"kd{k}", f"vd{k}")
        attend_back_kernel(
            lens[k], b[f"q{k}"], b[f"kd{k}"], b[f"vd{k}"], da.at[k], s["cos"], s["sa"], s["sb"], dq.at[seq(k)],
            dkv.at[seq(k)],
        )

    def mixer(k, dh):
        need("wq", "wkv", "wz", "wx", "wb", "wc", f"bcp{k}", f"bc{k}")
        bs[k] = bs[k] + bsr[k]
        mixer_back_kernel(
            lens[k], dm.at[k], b[f"y{k}"], b[f"x{k}"], b[f"z{k}"], b[f"bcp{k}"], b[f"bc{k}"], s[f"tp{k}"],
            s[f"tpr{k}"], s[f"ss{k}"], bs.at[k], dq.at[seq(k)], dkv.at[seq(k)], b["wq"], b["wkv"], b["wz"],
            b["wx"], b["wb"], b["wc"], s["wt"], s["cxw"], s["cxb"], s["cbw"], s["cbb"], s["bias"], s["rate"],
            s["bias_col"], s["rate_col"], s["skip"], s["gain"], dh, dx.at[seq(k)], dz.at[seq(k)],
            dbc.at[seq(k)], dt.at[k], wide.at[k], bcg.at[k], small.at[k], width=width, tick=tick,
        )
        tick()

    got_first = mix(0)
    tick()
    attend(0)
    tick()
    got_db.wait_recv()
    got_second = mix(1)
    tick()
    attend(1)
    tick()
    made.update([(OUT, column) for column in range(0, widths[OUT], LANES)])
    made.update([(QUERY, column) for column in range(0, widths[QUERY], LANES)])
    made.add((SHARED, KV_AT))
    got_first.wait_recv()
    got_second.wait_recv()
    got_first.wait_send()
    got_second.wait_send()
    mixer(1, dh_peer)
    got_dh = exchange(dh_peer, dh_got, 3)
    mixer(0, d_first)
    dt_cat[...] = jnp.zeros(dt_cat.shape, BF16)
    dt_cat[:seq_len, :16] = dt[0]
    dt_cat[seq_len:, :16] = dt[1]
    for part in (ZED, EX, STEP):
        made.update([(part, column) for column in range(0, widths[part], LANES)])
    made.update([(SHARED, B_AT), (SHARED, C_AT)])
    misc_key = order.index((SHARED, MISC_AT, "P"))
    tick(max(0.0, misc_key - 6 - clock[0]))
    got_dh.wait()
    total = d_first[...] + dh_got[...].astype(F32)
    d_first[...] = total
    need("xhat")
    norm = jnp.sum(total * b["xhat"][...], axis=0, keepdims=True)
    wide_sum, bcg_sum, small_sum = wide[0] + wide[1], bcg[0] + bcg[1], small[0] + small[1]
    model = norm.shape[1]
    first_row = row_ids((8, model)) == 0
    second_row = row_ids((8, model)) == 1
    norms = jnp.where(first_row, norm, jnp.where(second_row, s["ffn_gain"][...], 0.0))
    blocks = [array[:, i : i + LANES] for array in (wide_sum, bcg_sum) for i in range(0, array.shape[1], LANES)]
    blocks.append(jnp.concatenate([small_sum, jnp.zeros((8, LANES - 16), F32)], axis=1))
    blocks += [norms[:, i : i + LANES] for i in range(0, model, LANES)]
    if len(blocks) % 2:
        blocks.append(jnp.zeros((8, LANES), F32))
    misc[...] = jnp.zeros(misc.shape, BF16)
    misc[: 8 * len(blocks), :] = jnp.concatenate(blocks, axis=0).astype(BF16)
    made.add((SHARED, MISC_AT))
    tick(1e6)
    got_db.wait_send()
    for devices, wait in ends:
        if devices is None:
            wait()
        else:
            pl.when(devices)(wait)


def back_call(lens, smalls, bigs, grads, tail_widths, width, lag=1, pace=1.5):
    rows, (seq_len, model) = grads[0].shape[0], bigs["db"].shape
    widths = [grad.shape[1] for grad in grads] + list(tail_widths)
    order = chunk_order(widths)
    tails = sum(1 for item in order if item[0] >= SHARED)
    ones = sum(1 for item in order if item[2] == "P")
    count = len(order)
    half, quarter = rows // 2, rows // 4
    ssm_pad, att_pad = bigs["x0"].shape[1], bigs["q0"].shape[1]
    anywhere, vmem = pl.BlockSpec(memory_space=pl.ANY), pl.BlockSpec(memory_space=pltpu.VMEM)
    outs = [shaped((rows, w), BF16) for w in widths] + [shaped((rows, SHARED_WIDTH), BF16), shaped((seq_len, model))]
    scratch = []
    for name, array in bigs.items():
        shape = (8, LANES) if name == "db" else array.shape
        scratch.append(pltpu.VMEM(shape, array.dtype))
    both = 2 * seq_len
    scratch += [
        pltpu.VMEM((both, model), BF16),
        pltpu.VMEM((2, 16, seq_len), F32), pltpu.VMEM((2, 16, seq_len), F32),
        pltpu.VMEM((2, seq_len, att_pad), BF16), pltpu.VMEM((2, seq_len, ssm_pad), BF16),
        pltpu.VMEM((both, att_pad), BF16), pltpu.VMEM((both, LANES), BF16), pltpu.VMEM((both, ssm_pad), BF16),
        pltpu.VMEM((both, ssm_pad), BF16), pltpu.VMEM((both, 2 * STATE), BF16), pltpu.VMEM((2, seq_len, 16), BF16),
        pltpu.VMEM((both, LANES), BF16),
        pltpu.VMEM((seq_len, model), BF16), pltpu.VMEM((seq_len, model), BF16),
        pltpu.VMEM((2, 8, ssm_pad), F32), pltpu.VMEM((2, 8, 2 * STATE), F32), pltpu.VMEM((2, 8, 16), F32),
        pltpu.VMEM((rows, LANES), BF16),
        pltpu.VMEM((half, sum(widths[:3])), BF16), pltpu.VMEM((half, tails * LANES), BF16),
        pltpu.VMEM((half, count * LANES), BF16), pltpu.VMEM((half, count * LANES), BF16),
        pltpu.VMEM((quarter, count * LANES), BF16), pltpu.VMEM((quarter, ones * LANES), BF16),
        pltpu.VMEM((half, (count - ones) * LANES), BF16), pltpu.VMEM((quarter, count * LANES), BF16),
        pltpu.SemaphoreType.DMA((len(bigs),)), pltpu.SemaphoreType.DMA((3,)), pltpu.SemaphoreType.DMA((count,)),
        pltpu.SemaphoreType.DMA((4,)), pltpu.SemaphoreType.DMA((4,)),
        pltpu.SemaphoreType.DMA((9, count)), pltpu.SemaphoreType.DMA((9, count)),
    ]
    return pl.pallas_call(
        functools.partial(
            back_kernel, small_names=tuple(smalls), big_names=tuple(bigs), widths=tuple(widths), width=width,
            lag=lag, pace=pace,
        ),
        out_shape=outs,
        in_specs=[pl.BlockSpec(memory_space=pltpu.SMEM)] * 2 + [vmem] * len(smalls) + [anywhere] * (len(bigs) + 3),
        out_specs=[anywhere] * (PARTS + 1) + [vmem],
        scratch_shapes=scratch,
        compiler_params=pltpu.CompilerParams(
            collective_id=0, has_side_effects=True, vmem_limit_bytes=REDUCE_LIMIT
        ),
        name="back_and_reduce",
    )(*lens, *smalls.values(), *bigs.values(), *grads)


def unpack_kernel(own_ref, peer_ref, step_ref, out_ref, key_ref, value_ref, b_ref, c_ref, stp_ref, cxw_ref, cxb_ref, cbw_ref,
                  cbb_ref, bias_ref, decay_ref, skip_ref, sgain_ref, norm_ref, ffn_ref, att_ref, ssm_ref):
    att_ref[...] = out_ref[: att_ref.shape[0], :].astype(F32)
    ssm_ref[...] = out_ref[att_ref.shape[0] :, :].astype(F32)
    even = lax.axis_index("tensor") == 0
    kv, kv_peer = own_ref[:, :LANES].astype(F32), peer_ref[:, :LANES].astype(F32)
    low, high = jnp.where(even, kv, kv_peer), jnp.where(even, kv_peer, kv)
    first = lane_ids(kv.shape) < HEAD_DIM
    key_ref[...] = jnp.where(first, low, pltpu.roll(high, HEAD_DIM, 1))
    value_ref[...] = jnp.where(first, pltpu.roll(low, HEAD_DIM, 1), high)
    for ref, column in ((b_ref, B_AT), (c_ref, C_AT)):
        lanes = slice(column, column + LANES)
        ref[...] = own_ref[:, lanes].astype(F32) + peer_ref[:, lanes].astype(F32)
    stp_ref[...] = step_ref[...].astype(F32)[:, : stp_ref.shape[1]]
    wide_blocks, model_blocks = cxw_ref.shape[1] // LANES, norm_ref.shape[1] // LANES
    count = 8 * (wide_blocks + 2 + 1 + model_blocks)
    count += -count % 16
    mine = own_ref[:count, MISC_AT:].astype(F32)
    both = mine + peer_ref[:count, MISC_AT:].astype(F32)

    def rows(values, block, row, length=1):
        return values[8 * block + row : 8 * block + row + length]

    for block in range(wide_blocks):
        lanes = slice(block * LANES, (block + 1) * LANES)
        cxw_ref[:, lanes] = rows(mine, block, 0, 4)
        cxb_ref[:, lanes] = rows(mine, block, 4)
        sgain_ref[:, lanes] = rows(mine, block, 6)
    for block in range(2):
        lanes = slice(block * LANES, (block + 1) * LANES)
        cbw_ref[:, lanes] = rows(both, wide_blocks + block, 0, 4)
        cbb_ref[:, lanes] = rows(both, wide_blocks + block, 4)
    heads = bias_ref.shape[1]
    for row, ref in enumerate((bias_ref, decay_ref, skip_ref)):
        ref[...] = rows(mine, wide_blocks + 2, row)[:, :heads]
    for block in range(model_blocks):
        lanes = slice(block * LANES, (block + 1) * LANES)
        norm_ref[:, lanes] = rows(both, wide_blocks + 3 + block, 0)
        ffn_ref[:, lanes] = rows(both, wide_blocks + 3 + block, 1)


def shaped(shape, dtype=F32):
    return jax.ShapeDtypeStruct(shape, dtype)


def whole_call(kernel, outs, scalars, args, flops, name):
    specs = [pl.BlockSpec(memory_space=pltpu.SMEM)] * scalars
    specs += [pl.BlockSpec(memory_space=pltpu.VMEM)] * (len(args) - scalars)
    moved = sum(arg.size * arg.dtype.itemsize for arg in args)
    return pl.pallas_call(
        kernel,
        out_shape=outs,
        in_specs=specs,
        out_specs=[pl.BlockSpec(memory_space=pltpu.VMEM)] * len(outs),
        compiler_params=pltpu.CompilerParams(vmem_limit_bytes=VMEM_LIMIT),
        cost_estimate=pl.CostEstimate(flops=flops, bytes_accessed=moved, transcendentals=0),
        name=name,
    )(*args)


def pad_columns(values, width):
    return jnp.pad(values, ((0, 0), (0, width - values.shape[1]))) if width != values.shape[1] else values


def pad_rows(values, height):
    return jnp.pad(values, ((0, height - values.shape[0]), (0, 0))) if height != values.shape[0] else values


def contract_rows(left, right):
    return mm_tn(jnp.concatenate(left, axis=0), jnp.concatenate(right, axis=0))


def on_device(
    tokens, lengths, cotangent, norm_gain, w_query, w_key, w_value, w_gate_z, w_ssm_x, w_ssm_b, w_ssm_c,
    w_step, conv_x_weight, conv_x_bias, conv_bc_weight, conv_bc_bias, step_bias, decay_log, skip_gain,
    ssm_norm_gain, w_out_att, w_out_ssm, ffn_norm_gain, w_gate, w_up, w_down,
):
    seq_len, model = tokens.shape
    groups = lax.axis_size("tensor")
    position = lax.axis_index("tensor")
    att_width, ssm_width = w_query.shape[1], w_gate_z.shape[1]
    att_pad = -(-att_width // LANES) * LANES
    ssm_pad = -(-ssm_width // LANES) * LANES
    ssm_heads = ssm_width // SSM_DIM
    ssm_width_all = SSM_HEADS * SSM_DIM
    ff_width = w_gate.shape[1]

    def fetch(values, shift):
        return lax.ppermute(values, "tensor", [((i + shift) % groups, i) for i in range(groups)])

    def deliver(values, shift):
        return lax.ppermute(values, "tensor", [(i, (i + shift) % groups) for i in range(groups)])

    def gather(values):
        return [values] + [fetch(values, k) for k in range(1, groups)]

    def scatter_sum(own, others):
        total = own
        for k in range(1, groups):
            total = total + deliver(others[k - 1], k).astype(F32)
        return total

    kv_head = position * (att_width // HEAD_DIM) // (HEADS // KV_HEADS)
    w_kv = jnp.concatenate(
        [lax.dynamic_slice_in_dim(w, kv_head * HEAD_DIM, HEAD_DIM, 1) for w in (w_key, w_value)], axis=1
    )
    wq = pad_columns(w_query, att_pad)
    wz, wx = pad_columns(w_gate_z, ssm_pad), pad_columns(w_ssm_x, ssm_pad)
    wt = pad_rows(w_step.T, 16)
    wa, ws = pad_rows(w_out_att, att_pad), pad_rows(w_out_ssm, ssm_pad)
    cxw, cxb = pad_columns(conv_x_weight, ssm_pad), pad_columns(conv_x_bias[None], ssm_pad)
    cbb = conv_bc_bias[None]
    gain = pad_columns(ssm_norm_gain[None], ssm_pad)
    skip = pad_columns(jnp.repeat(skip_gain, SSM_DIM)[None], ssm_pad)
    bias = pad_columns(step_bias[None], 16)
    rate = pad_columns(jnp.exp(decay_log)[None], 16)
    bias_col, rate_col = bias.T, rate.T
    half = HEAD_DIM // 2
    freqs = ROPE_BASE ** (-(jnp.arange(half).astype(F32) * 2.0 / HEAD_DIM))
    angles = jnp.arange(seq_len).astype(F32)[:, None] * freqs[None, :]
    cosine, sine, none = jnp.cos(angles), jnp.sin(angles), jnp.zeros_like(angles)
    cos_table = jnp.concatenate([cosine] * 4, axis=1)
    sine_first = jnp.concatenate([-sine, none] * 2, axis=1)
    sine_second = jnp.concatenate([none, sine] * 2, axis=1)

    inputs = tokens.astype(F32)
    inv1 = lax.rsqrt(jnp.mean(inputs * inputs, axis=1, keepdims=True) + EPSILON)
    h_own = (inputs * inv1 * norm_gain).astype(BF16)
    own_mask = jnp.arange(seq_len) < lengths[0]
    ct_own = jnp.where(own_mask[:, None], cotangent, jnp.zeros_like(cotangent))
    h_all = gather(h_own)
    len_all = gather(lengths)
    ct_all = gather(ct_own)

    def forward(k):
        outs = [
            shaped((seq_len, att_pad), BF16), shaped((seq_len, LANES), BF16), shaped((seq_len, LANES), BF16),
            shaped((seq_len, ssm_pad)), shaped((seq_len, ssm_pad)), shaped((seq_len, 2 * STATE)),
            shaped((seq_len, 2 * STATE), BF16), shaped((seq_len, 16)), shaped((16, seq_len)),
            shaped((seq_len, ssm_pad)), shaped((16, seq_len)),
        ]
        args = [
            len_all[k], h_all[k], wq, w_kv, wz, wx, w_ssm_b, w_ssm_c, wt, cxw, cxb, conv_bc_weight, cbb,
            bias, rate, bias_col, rate_col, skip, cos_table, sine_first, sine_second,
        ]
        return whole_call(mixer_forward_kernel, outs, 1, args, 8 * 10**9, "mixer_forward")

    def attend(k):
        q, kd, vd = kept[k][:3]
        return whole_call(
            attend_kernel, [shaped((seq_len, att_pad), BF16)], 1, [len_all[k], q, kd, vd], 2 * 10**9, "attend"
        )[0]

    kept = [forward(k) for k in range(groups)]
    squares_part = [one[10] for one in kept]
    squares = [squares_part[k] for k in range(groups)]
    for shift in range(1, groups):
        for k in range(groups):
            squares[k] = squares[k] + fetch(squares_part[(k - shift) % groups], shift)
    mix_att = [attend(k) for k in range(groups)]

    def project(k, dtype):
        q, kd, vd, z, x, bcp, bc, tp, tpr, y, _ = kept[k]
        return whole_call(
            functools.partial(out_kernel, width=ssm_width_all),
            [shaped((seq_len, model), dtype), shaped((seq_len, ssm_pad), BF16)],
            0,
            [mix_att[k], y, x, z, squares[k], cxw, cxb, skip, gain, wa, ws],
            4 * 10**9,
            "out_project",
        )

    projected = [project(k, F32 if k == 0 else BF16) for k in range(groups)]
    mix_ssm = [one[1] for one in projected]
    branch = scatter_sum(projected[0][0], [one[0] for one in projected[1:]])
    resid = inputs + branch
    inv2 = lax.rsqrt(jnp.mean(resid * resid, axis=1, keepdims=True) + EPSILON)
    h2_own = (resid * inv2 * ffn_norm_gain).astype(BF16)
    h2_all = gather(h2_own)

    def feed(k):
        dtype = F32 if k == 0 else BF16
        block = min(256, ff_width)
        full = pl.BlockSpec((seq_len, model), lambda i: (0, 0))
        columns = pl.BlockSpec((model, block), lambda i: (0, i))
        rows = pl.BlockSpec((block, model), lambda i: (i, 0))
        tall = pl.BlockSpec((seq_len, block), lambda i: (0, i))
        return pl.pallas_call(
            ffn_kernel,
            grid=(ff_width // block,),
            out_shape=[shaped((seq_len, ff_width), BF16)] * 3 + [shaped((seq_len, model), dtype)] * 2,
            in_specs=[full, full, columns, columns, rows],
            out_specs=[tall] * 3 + [full] * 2,
            scratch_shapes=[pltpu.VMEM((seq_len, model), F32)] * 2,
            compiler_params=pltpu.CompilerParams(vmem_limit_bytes=VMEM_LIMIT),
            cost_estimate=pl.CostEstimate(flops=8 * 10**9, bytes_accessed=10**7, transcendentals=0),
            name="feed_forward",
        )(h2_all[k], ct_all[k], w_gate, w_up, w_down)

    fed = [feed(k) for k in range(groups)]
    d_second = scatter_sum(fed[0][4], [one[4] for one in fed[1:]])
    fed_parts = lax.optimization_barrier(tuple(one[3] for one in fed) + (d_second,))
    d_second = fed_parts[-1]
    ffn_result = scatter_sum(fed_parts[0], fed_parts[1:-1])
    layer_output = (resid + ffn_result).astype(BF16)
    grad_gate = contract_rows(h2_all, [one[1] for one in fed])
    grad_up = contract_rows(h2_all, [one[2] for one in fed])
    grad_down = contract_rows([one[0] for one in fed], ct_all)

    scaled = d_second * ffn_norm_gain
    d_resid = (
        ct_own.astype(F32)
        + inv2 * scaled
        - resid * (inv2**3) * jnp.mean(scaled * resid, axis=1, keepdims=True)
    )
    grad_ffn_gain = jnp.sum(d_second * resid * inv2, axis=0)
    if lax.axis_size("dp") == 16 and groups == 2:
        smalls = {
            "wt": wt, "cxw": cxw, "cxb": cxb, "cbw": conv_bc_weight, "cbb": cbb, "bias": bias, "rate": rate,
            "bias_col": bias_col, "rate_col": rate_col, "skip": skip, "gain": gain, "cos": cos_table,
            "sa": sine_first, "sb": sine_second, "ffn_gain": grad_ffn_gain[None],
        }
        bigs = {"db": d_resid.astype(BF16), "wa": wa, "ws": ws}
        for k in range(groups):
            q, kd, vd, z, x, bcp, bc, tp, tpr, y, _ = kept[k]
            smalls.update({f"tp{k}": tp, f"tpr{k}": tpr, f"ss{k}": squares[k]})
            bigs.update({f"y{k}": y, f"x{k}": x, f"z{k}": z, f"q{k}": q, f"kd{k}": kd, f"vd{k}": vd})
        bigs.update({"wq": wq, "wkv": w_kv, "wz": wz, "wx": wx, "wb": w_ssm_b, "wc": w_ssm_c})
        for k in range(groups):
            bigs.update({f"bcp{k}": kept[k][5], f"bc{k}": kept[k][6]})
        bigs["mix_t"] = jnp.concatenate(
            [jnp.concatenate([one.T for one in part], axis=1) for part in (mix_att, mix_ssm)], axis=0
        )
        bigs["h_t"] = jnp.concatenate([one.T for one in h_all], axis=1)
        bigs["xhat"] = inputs * inv1
        tail_widths = (SHARED_WIDTH, LANES, att_pad, ssm_pad, ssm_pad, model)
        results = back_call(
            len_all, smalls, bigs, [part.astype(BF16) for part in (grad_gate, grad_up, grad_down)], tail_widths,
            ssm_width_all,
        )
        shared, step = results[SHARED], results[STEP]
        grad_gate, grad_up, grad_down, grad_q, grad_z, grad_x = (
            results[part].astype(F32) for part in (GATE, UP, DOWN, QUERY, ZED, EX)
        )
        peer, d_first = results[PARTS], results[PARTS + 1]
        outs = [shaped((model, LANES))] * 4 + [
            shaped((model, ssm_heads)), shaped((4, ssm_pad)), shaped((1, ssm_pad)), shaped((4, 2 * STATE)),
            shaped((1, 2 * STATE)), shaped((1, ssm_heads)), shaped((1, ssm_heads)), shaped((1, ssm_heads)),
            shaped((1, ssm_pad)), shaped((1, model)), shaped((1, model)), shaped((att_pad, model)),
            shaped((ssm_pad, model)),
        ]
        (grad_key, grad_value, grad_b, grad_c, grad_step, grad_cxw, grad_cxb, grad_cbw, grad_cbb, grad_bias,
         grad_decay, grad_skip, grad_sgain, grad_norm_gain, grad_ffn_gain, grad_att, grad_ssm) = whole_call(
            unpack_kernel, outs, 0, [shared, peer, step, results[OUT]], 10**7, "unpack"
        )
    else:
        db_all = gather(d_resid.astype(BF16))

        def mix_grad(k):
            q, kd, vd, z, x, bcp, bc, tp, tpr, y, _ = kept[k]
            return whole_call(
                mix_grad_kernel,
                [shaped((seq_len, att_pad), BF16), shaped((seq_len, ssm_pad), BF16), shaped((16, seq_len))],
                0,
                [db_all[k], y, x, z, cxw, cxb, skip, gain, wa, ws],
                4 * 10**9,
                "mix_grad",
            )

        mixed = [mix_grad(k) for k in range(groups)]
        backs_part = [one[2] for one in mixed]
        backs = [backs_part[k] for k in range(groups)]
        for shift in range(1, groups):
            for k in range(groups):
                backs[k] = backs[k] + fetch(backs_part[(k - shift) % groups], shift)

        def attend_back(k):
            q, kd, vd = kept[k][:3]
            return whole_call(
                attend_back_kernel,
                [shaped((seq_len, att_pad), BF16), shaped((seq_len, LANES), BF16)],
                1,
                [len_all[k], q, kd, vd, mixed[k][0], cos_table, sine_first, sine_second],
                4 * 10**9,
                "attend_back",
            )

        turned = [attend_back(k) for k in range(groups)]

        def backward(k):
            q, kd, vd, z, x, bcp, bc, tp, tpr, y, _ = kept[k]
            outs = [
                shaped((seq_len, model), F32 if k == 0 else BF16), shaped((seq_len, ssm_pad), BF16),
                shaped((seq_len, ssm_pad), BF16), shaped((seq_len, 2 * STATE), BF16), shaped((seq_len, 16), BF16),
                shaped((8, ssm_pad)), shaped((8, 2 * STATE)), shaped((8, 16)),
            ]
            args = [
                len_all[k], mixed[k][1], y, x, z, bcp, bc, tp, tpr, squares[k], backs[k], turned[k][0], turned[k][1],
                wq, w_kv, wz, wx, w_ssm_b, w_ssm_c, wt, cxw, cxb, conv_bc_weight, cbb, bias, rate, bias_col, rate_col,
                skip, gain,
            ]
            return whole_call(
                functools.partial(mixer_back_kernel, width=ssm_width_all), outs, 1, args, 16 * 10**9, "mixer_back"
            )

        gone = [None] * groups
        for k in list(range(1, groups)) + [0]:
            gone[k] = backward(k)
        d_first = scatter_sum(gone[0][0], [one[0] for one in gone[1:]])
        grad_norm_gain = jnp.sum(d_first * inputs * inv1, axis=0)

        wide, bcg, small = (sum(one[i] for one in gone) for i in (5, 6, 7))
        grad_q = contract_rows(h_all, [one[0] for one in turned])
        grad_kv = contract_rows(h_all, [one[1] for one in turned])
        grad_bc = contract_rows(h_all, [one[3] for one in gone])
        grad_x = contract_rows(h_all, [one[1] for one in gone])
        grad_z = contract_rows(h_all, [one[2] for one in gone])
        grad_step = contract_rows(h_all, [one[4] for one in gone])
        grad_att = contract_rows(mix_att, db_all)
        grad_ssm = contract_rows(mix_ssm, db_all)
        norms = jnp.concatenate([bcg[:5].reshape(-1), grad_norm_gain, grad_ffn_gain])
        zeros = jnp.zeros((model, KV_HEADS * HEAD_DIM), F32)
        grad_key = lax.dynamic_update_slice(zeros, grad_kv[:, :HEAD_DIM], (0, kv_head * HEAD_DIM))
        grad_value = lax.dynamic_update_slice(zeros, grad_kv[:, HEAD_DIM:], (0, kv_head * HEAD_DIM))
        grad_key, grad_value, grad_bc, norms = lax.psum((grad_key, grad_value, grad_bc, norms), ("dp", "tensor"))
        grad_b, grad_c = grad_bc[:, :STATE], grad_bc[:, STATE:]
        grad_q, grad_z, grad_x, grad_step, grad_att, grad_ssm, wide, small = (
            lax.psum(part.astype(BF16), "dp").astype(F32)
            for part in (grad_q, grad_z, grad_x, grad_step, grad_att, grad_ssm, wide, small)
        )
        grad_gate, grad_up, grad_down = (
            lax.psum(part.astype(BF16), "dp").astype(F32) for part in (grad_gate, grad_up, grad_down)
        )
        grad_step = grad_step[:, :ssm_heads]
        grad_cxw, grad_cxb, grad_sgain = wide[:4], wide[4:5], wide[6:7]
        bcg = norms[: 10 * STATE].reshape(5, 2 * STATE)
        grad_cbw, grad_cbb = bcg[:4], bcg[4:]
        grad_bias, grad_decay, grad_skip = small[0:1, :ssm_heads], small[1:2, :ssm_heads], small[2:3, :ssm_heads]
        grad_norm_gain = norms[10 * STATE : 10 * STATE + model]
        grad_ffn_gain = norms[10 * STATE + model :]

    scaled = d_first * norm_gain
    grad_input = d_resid + inv1 * scaled - inputs * (inv1**3) * jnp.mean(scaled * inputs, axis=1, keepdims=True)
    return (
        layer_output,
        grad_input,
        grad_norm_gain.reshape(-1),
        grad_q[:, :att_width],
        grad_key,
        grad_value,
        grad_z[:, :ssm_width],
        grad_x[:, :ssm_width],
        grad_b,
        grad_c,
        grad_step,
        grad_cxw[:, :ssm_width],
        grad_cxb.reshape(-1)[:ssm_width],
        grad_cbw,
        grad_cbb.reshape(-1),
        grad_bias.reshape(-1),
        grad_decay.reshape(-1),
        grad_skip.reshape(-1),
        grad_sgain.reshape(-1)[:ssm_width],
        grad_att[:att_width],
        grad_ssm[:ssm_width],
        grad_ffn_gain.reshape(-1),
        grad_gate,
        grad_up,
        grad_down,
    )


def solution(mesh):
    rows, split, tall = P(("dp", "tensor"), None), P(None, "tensor"), P("tensor", None)
    vector, copied = P("tensor"), P()
    return jax.shard_map(
        on_device,
        mesh=mesh,
        in_specs=(
            rows, P(("dp", "tensor")), rows, copied, split, copied, copied, split, split, copied, copied, split,
            split, vector, copied, copied, vector, vector, vector, vector, tall, tall, copied, split, split, tall,
        ),
        out_specs=(
            rows, rows, copied, split, copied, copied, split, split, copied, copied, split, split, vector, copied,
            copied, vector, vector, vector, vector, tall, tall, copied, split, split, tall,
        ),
        check_vma=False,
    )
```

```python
import functools

import jax
import jax.numpy as jnp
from jax import lax
from jax.experimental import pallas as pl
from jax.experimental.pallas import tpu as pltpu
from jax.sharding import PartitionSpec as P

HEADS = 8
KV_HEADS = 2
HEAD_DIM = 64
SSM_HEADS = 24
SSM_DIM = 64
STATE = 128
SPAN = 128
LANES = 128

EPSILON = 1e-05
ROPE_BASE = 100000000000.0
F32 = jnp.float32
BF16 = jnp.bfloat16
VMEM_LIMIT = 62 * 1024 * 1024
REDUCE_LIMIT = 62 * 1024 * 1024
MESH = pl.DeviceIdType.MESH


def mm(left, right):
    return jnp.dot(left, right, preferred_element_type=F32)


def mm_nt(left, right):
    return lax.dot_general(left, right, (((1,), (1,)), ((), ())), preferred_element_type=F32)


def mm_tn(left, right):
    return lax.dot_general(left, right, (((0,), (0,)), ((), ())), preferred_element_type=F32)


def pieces(values, count):
    terms = []
    for _ in range(count):
        term = values.astype(BF16)
        terms.append(term)
        values = values - term.astype(F32)
    return terms


def sigmoid(values):
    return 1.0 / (1.0 + jnp.exp(-values))


def softplus(values):
    return jnp.maximum(values, 0.0) + jnp.log1p(jnp.exp(-jnp.abs(values)))


def lane_ids(shape):
    return lax.broadcasted_iota(jnp.int32, shape, 1)


def row_ids(shape):
    return lax.broadcasted_iota(jnp.int32, shape, 0)


def repeat_lanes(column, count):
    return jnp.concatenate([column] * count, axis=1) if count > 1 else column


def column_of(row):
    ones = jnp.where(row_ids((16, LANES)) == 0, 1.0, 0.0).astype(BF16)
    total = None
    for term in pieces(row, 3):
        part = mm_tn(term, ones)
        total = part if total is None else total + part
    return total


def row_sums(values):
    ones = jnp.ones((16, values.shape[1]), BF16)
    high, low = pieces(values, 2)
    return mm_nt(ones, high) + mm_nt(ones, low)


def causal_shift(values, steps):
    if steps == 0:
        return values
    rolled = pltpu.roll(values, steps, 0)
    return jnp.where(row_ids(values.shape) >= steps, rolled, 0.0)


def anti_shift(values, steps):
    if steps == 0:
        return values
    length = values.shape[0]
    rolled = pltpu.roll(values, length - steps, 0)
    return jnp.where(row_ids(values.shape) < length - steps, rolled, 0.0)


def conv(values, weight, bias):
    taps = weight.shape[0]
    total = bias + weight[taps - 1 : taps] * values
    for offset in range(taps - 1):
        total = total + weight[offset : offset + 1] * causal_shift(values, taps - 1 - offset)
    return total


def conv_back(grad, values, weight):
    taps = weight.shape[0]
    total, rows = None, []
    for offset in range(taps):
        steps = taps - 1 - offset
        moved = anti_shift(grad, steps)
        part = weight[offset : offset + 1] * moved
        total = part if total is None else total + part
        rows.append(jnp.sum(moved * values, axis=0, keepdims=True))
    rows.append(jnp.sum(grad, axis=0, keepdims=True))
    return total, rows


def rope(values, cosine, sine_first, sine_second):
    ahead = pltpu.roll(values, LANES - HEAD_DIM // 2, 1)
    behind = pltpu.roll(values, HEAD_DIM // 2, 1)
    return values * cosine + ahead * sine_first + behind * sine_second


def lower_mask():
    return row_ids((SPAN, SPAN)) >= lane_ids((SPAN, SPAN))


def span_sums(values):
    lower = jnp.where(lower_mask(), 1.0, 0.0).astype(BF16)
    out = []
    for start in range(0, values.shape[0], SPAN):
        total = None
        for term in pieces(values[start : start + SPAN], 3):
            part = mm(lower, term)
            total = part if total is None else total + part
        out.append(total)
    return jnp.concatenate(out, axis=0)


def span_sums_rows(values):
    upper = jnp.where(row_ids((SPAN, SPAN)) <= lane_ids((SPAN, SPAN)), 1.0, 0.0).astype(BF16)
    out = []
    for start in range(0, values.shape[1], SPAN):
        total = None
        for term in pieces(values[:, start : start + SPAN], 3):
            part = mm(term, upper)
            total = part if total is None else total + part
        out.append(total)
    return jnp.concatenate(out, axis=1)


def span_sums_back(values):
    upper = jnp.where(row_ids((SPAN, SPAN)) <= lane_ids((SPAN, SPAN)), 1.0, 0.0).astype(BF16)
    out = []
    for start in range(0, values.shape[0], SPAN):
        total = None
        for term in pieces(values[start : start + SPAN], 3):
            part = mm(upper, term)
            total = part if total is None else total + part
        out.append(total)
    return jnp.concatenate(out, axis=0)


def steps_of(tp, tp_row, bias, bias_col, rate, rate_col, length):
    seq_len = tp.shape[0]
    valid = jnp.where(row_ids((seq_len, 1)) < length, 1.0, 0.0)
    valid_row = jnp.where(lane_ids((1, seq_len)) < length, 1.0, 0.0)
    dt = softplus(tp + bias) * valid
    dt_row = softplus(tp_row + bias_col) * valid_row
    cum = span_sums(-(dt * rate))
    cum_row = span_sums_rows(-(dt_row * rate_col))
    return valid, dt, cum, cum_row


def spread(values, head):
    return jnp.broadcast_to(values[:, head : head + 1], (values.shape[0], LANES))


def decays(cum_first, cum_second, cum_row, pair, span):
    rows = slice(span * SPAN, (span + 1) * SPAN)
    lower = lower_mask()
    out = []
    for head, column in ((2 * pair, cum_first), (2 * pair + 1, cum_second)):
        differ = column[rows] - cum_row[head : head + 1, rows]
        out.append(jnp.exp(jnp.where(lower, differ, -1e30)))
    return out


def split_heads(values):
    first = lane_ids(values.shape) < HEAD_DIM
    zero = jnp.zeros_like(values)
    return jnp.concatenate([jnp.where(first, values, zero), jnp.where(first, zero, values)], axis=0)


def state_of(in_map, weighted_first, cum_pair_first):
    to_end = jnp.exp(cum_pair_first[SPAN - 1 : SPAN] - cum_pair_first)
    ending = (weighted_first * to_end).astype(BF16)
    return to_end, ending, mm_tn(in_map[:SPAN], ending)


def mixer_forward_kernel(
    len_ref, h_ref, wq_ref, wkv_ref, wz_ref, wx_ref, wb_ref, wc_ref, wt_ref, cxw_ref, cxb_ref,
    cbw_ref, cbb_ref, bias_ref, rate_ref, bias_col_ref, rate_col_ref, skip_ref, cos_ref, sa_ref,
    sb_ref, q_ref, kd_ref, vd_ref, z_ref, x_ref, bcp_ref, bc_ref, tp_ref, tpr_ref, y_ref, ss_ref,
):
    h = h_ref[...]
    pairs = wx_ref.shape[1] // LANES
    z_ref[...] = mm(h, wz_ref[...])
    x_ref[...] = mm(h, wx_ref[...])
    bcp_ref[:, :STATE] = mm(h, wb_ref[...])
    bcp_ref[:, STATE:] = mm(h, wc_ref[...])
    tp = mm_nt(h, wt_ref[...])
    tp_row = mm_nt(wt_ref[...], h)
    tp_ref[...] = tp
    tpr_ref[...] = tp_row
    cosine, sine_first, sine_second = cos_ref[...], sa_ref[...], sb_ref[...]
    for pair in range(wq_ref.shape[1] // LANES):
        lanes = slice(pair * LANES, (pair + 1) * LANES)
        q_ref[:, lanes] = rope(mm(h, wq_ref[:, lanes]), cosine, sine_first, sine_second).astype(BF16)
    kv = mm(h, wkv_ref[...])
    turned = pltpu.roll(kv, HEAD_DIM, 1)
    first = lane_ids(kv.shape) < HEAD_DIM
    kd_ref[...] = rope(jnp.where(first, kv, turned), cosine, sine_first, sine_second).astype(BF16)
    vd_ref[...] = jnp.where(first, turned, kv).astype(BF16)

    mapped = conv(bcp_ref[...], cbw_ref[...], cbb_ref[...])
    bc = (mapped * sigmoid(mapped)).astype(BF16)
    bc_ref[...] = bc
    in_map, out_map = bc[:, :STATE], bc[:, STATE:]
    affinity = [
        mm_nt(out_map[s * SPAN : (s + 1) * SPAN], in_map[s * SPAN : (s + 1) * SPAN]) for s in range(2)
    ]
    _, dt, cum, cum_row = steps_of(
        tp, tp_row, bias_ref[...], bias_col_ref[...], rate_ref[...], rate_col_ref[...], len_ref[0]
    )
    squares = None
    for pair in range(pairs):
        lanes = slice(pair * LANES, (pair + 1) * LANES)
        cx = conv(x_ref[:, lanes], cxw_ref[:, lanes], cxb_ref[:, lanes])
        xc = cx * sigmoid(cx)
        dt_pair = jnp.where(first, spread(dt, 2 * pair), spread(dt, 2 * pair + 1))
        cum_first, cum_second = spread(cum, 2 * pair), spread(cum, 2 * pair + 1)
        cum_pair = jnp.where(first, cum_first, cum_second)
        weighted = xc * dt_pair
        low = weighted.astype(BF16)
        _, _, state = state_of(in_map, weighted[:SPAN], cum_pair[:SPAN])
        parts = []
        for s in range(2):
            rows = slice(s * SPAN, (s + 1) * SPAN)
            mats = [
                (affinity[s] * decay).astype(BF16)
                for decay in decays(cum_first, cum_second, cum_row, pair, s)
            ]
            part = mm(jnp.concatenate(mats, axis=1), split_heads(low[rows]))
            if s:
                part = part + mm(out_map[rows], state.astype(BF16)) * jnp.exp(cum_pair[rows])
            parts.append(part)
        y = jnp.concatenate(parts, axis=0)
        y_ref[:, lanes] = y
        z = z_ref[:, lanes]
        gated = (y + skip_ref[:, lanes] * xc) * (z * sigmoid(z))
        square = gated * gated
        squares = square if squares is None else squares + square
    ss_ref[...] = row_sums(squares)


def masked_probs(queries, kd, length, scale):
    seq_len = kd.shape[0]
    scores = mm_nt(split_heads(queries), kd) * scale
    rows = row_ids(scores.shape)
    rows = jnp.where(rows >= seq_len, rows - seq_len, rows)
    columns = lane_ids(scores.shape)
    scores = jnp.where((rows >= columns) & (columns < length), scores, -1e30)
    weights = jnp.exp(scores - jnp.max(scores, axis=1, keepdims=True))
    return weights / jnp.sum(weights, axis=1, keepdims=True)


def attend_kernel(len_ref, q_ref, kd_ref, vd_ref, out_ref):
    seq_len = q_ref.shape[0]
    values = split_heads(vd_ref[...])
    for pair in range(q_ref.shape[1] // LANES):
        lanes = slice(pair * LANES, (pair + 1) * LANES)
        probs = masked_probs(q_ref[:, lanes], kd_ref[...], len_ref[0], HEAD_DIM ** (-0.5)).astype(BF16)
        both = jnp.concatenate([probs[:seq_len], probs[seq_len:]], axis=1)
        out_ref[:, lanes] = mm(both, values).astype(BF16)


def join_halves(values):
    return values + pltpu.roll(values, HEAD_DIM, 1)


def attend_back_kernel(len_ref, q_ref, kd_ref, vd_ref, da_ref, cos_ref, sa_ref, sb_ref, dq_ref, dkv_ref):
    seq_len = q_ref.shape[0]
    scale = HEAD_DIM ** (-0.5)
    cosine, sine_first, sine_second = cos_ref[...], -sa_ref[...], -sb_ref[...]
    kd, vd = kd_ref[...], vd_ref[...]
    keys = split_heads(kd)
    grad_k, grad_v = None, None
    for pair in range(q_ref.shape[1] // LANES):
        lanes = slice(pair * LANES, (pair + 1) * LANES)
        probs = masked_probs(q_ref[:, lanes], kd, len_ref[0], scale)
        da = split_heads(da_ref[:, lanes])
        dprob = mm_nt(da, vd)
        dscore = (probs * (dprob - jnp.sum(probs * dprob, axis=1, keepdims=True))).astype(BF16)
        both = jnp.concatenate([dscore[:seq_len], dscore[seq_len:]], axis=1)
        dq = mm(both, keys) * scale
        dq_ref[:, lanes] = rope(dq, cosine, sine_first, sine_second).astype(BF16)
        part_k = mm_tn(dscore, split_heads(q_ref[:, lanes]))
        part_v = mm_tn(probs.astype(BF16), da)
        grad_k = part_k if grad_k is None else grad_k + part_k
        grad_v = part_v if grad_v is None else grad_v + part_v
    dk = rope(join_halves(grad_k) * scale, cosine, sine_first, sine_second)
    first = lane_ids(dk.shape) < HEAD_DIM
    dkv_ref[...] = jnp.where(first, dk, join_halves(grad_v)).astype(BF16)


def out_kernel(att_ref, y_ref, x_ref, z_ref, ss_ref, cxw_ref, cxb_ref, skip_ref, gain_ref, wa_ref, ws_ref,
               part_ref, mix_ref, *, width):
    total = mm(att_ref[...], wa_ref[...])
    inv = column_of(lax.rsqrt(ss_ref[...] / width + EPSILON))
    for pair in range(y_ref.shape[1] // LANES):
        lanes = slice(pair * LANES, (pair + 1) * LANES)
        cx = conv(x_ref[:, lanes], cxw_ref[:, lanes], cxb_ref[:, lanes])
        z = z_ref[:, lanes]
        gated = (y_ref[:, lanes] + skip_ref[:, lanes] * (cx * sigmoid(cx))) * (z * sigmoid(z))
        mix_ref[:, lanes] = (gated * inv * gain_ref[:, lanes]).astype(BF16)
    part_ref[...] = (total + mm(mix_ref[...], ws_ref[...])).astype(part_ref.dtype)


def mix_grad_kernel(db_ref, y_ref, x_ref, z_ref, cxw_ref, cxb_ref, skip_ref, gain_ref, wa_ref, ws_ref,
                    da_ref, dm_ref, bs_ref):
    db = db_ref[...]
    da_ref[...] = mm_nt(db, wa_ref[...]).astype(BF16)
    dm_ref[...] = mm_nt(db, ws_ref[...]).astype(BF16)
    total = None
    for pair in range(y_ref.shape[1] // LANES):
        lanes = slice(pair * LANES, (pair + 1) * LANES)
        cx = conv(x_ref[:, lanes], cxw_ref[:, lanes], cxb_ref[:, lanes])
        z = z_ref[:, lanes]
        gated = (y_ref[:, lanes] + skip_ref[:, lanes] * (cx * sigmoid(cx))) * (z * sigmoid(z))
        part = gated * (gain_ref[:, lanes] * dm_ref[:, lanes].astype(F32))
        total = part if total is None else total + part
    bs_ref[...] = row_sums(total)


def head_sums(values, pair):
    rows, columns = row_ids((LANES, 16)), lane_ids((LANES, 16))
    chosen = jnp.where(columns == 2 * pair + jnp.where(rows < HEAD_DIM, 0, 1), 1.0, 0.0).astype(BF16)
    high, low = pieces(values, 2)
    return mm(jnp.concatenate([high, low], axis=1), jnp.concatenate([chosen, chosen], axis=0))


def mixer_back_kernel(
    len_ref, dm_ref, y_ref, x_ref, z_ref, bcp_ref, bc_ref, tp_ref, tpr_ref, ss_ref, bs_ref, dq_ref,
    dkv_ref, wq_ref, wkv_ref, wz_ref, wx_ref, wb_ref, wc_ref, wt_ref, cxw_ref, cxb_ref, cbw_ref,
    cbb_ref, bias_ref, rate_ref, bias_col_ref, rate_col_ref, skip_ref, gain_ref,
    dh_ref, dx_ref, dz_ref, dbc_ref, dt_ref, wide_ref, bcg_ref, small_ref, *, width, tick=lambda: None,
):
    pairs = x_ref.shape[1] // LANES
    bc = bc_ref[...]
    in_map, out_map = bc[:, :STATE], bc[:, STATE:]
    affinity = [
        mm_nt(out_map[s * SPAN : (s + 1) * SPAN], in_map[s * SPAN : (s + 1) * SPAN]) for s in range(2)
    ]
    valid, dt, cum, cum_row = steps_of(
        tp_ref[...], tpr_ref[...], bias_ref[...], bias_col_ref[...], rate_ref[...], rate_col_ref[...], len_ref[0]
    )
    inv_row = lax.rsqrt(ss_ref[...] / width + EPSILON)
    inv = column_of(inv_row)
    back = column_of(inv_row * inv_row * inv_row * bs_ref[...] / width)
    first = lane_ids((x_ref.shape[0], LANES)) < HEAD_DIM
    last_row = row_ids((SPAN, LANES)) == SPAN - 1
    d_cum, d_step, d_skip = None, None, None
    wide_ref[7:8, :] = jnp.zeros((1, wide_ref.shape[1]), F32)
    d_aff, d_out, d_in = [None, None], None, None

    def plus(total, part):
        return part if total is None else total + part

    for pair in range(pairs):
        lanes = slice(pair * LANES, (pair + 1) * LANES)
        x = x_ref[:, lanes]
        cxw = cxw_ref[:, lanes]
        cx = conv(x, cxw, cxb_ref[:, lanes])
        sx = sigmoid(cx)
        xc = cx * sx
        z = z_ref[:, lanes]
        sz = sigmoid(z)
        silu_z = z * sz
        scanned = y_ref[:, lanes]
        y = scanned + skip_ref[:, lanes] * xc
        gated = y * silu_z
        d_mix = dm_ref[:, lanes].astype(F32)
        d_gated = inv * (gain_ref[:, lanes] * d_mix) - gated * back
        wide_ref[6:7, lanes] = jnp.sum(d_mix * gated * inv, axis=0, keepdims=True)
        dy = d_gated * silu_z
        dz_ref[:, lanes] = (d_gated * y * (sz * (1.0 + z * (1.0 - sz)))).astype(BF16)
        wide_ref[5:6, lanes] = jnp.sum(dy * xc, axis=0, keepdims=True)
        dt_pair = jnp.where(first, spread(dt, 2 * pair), spread(dt, 2 * pair + 1))
        cum_first, cum_second = spread(cum, 2 * pair), spread(cum, 2 * pair + 1)
        cum_pair = jnp.where(first, cum_first, cum_second)
        weighted = xc * dt_pair
        low = weighted.astype(BF16)
        dy_low = dy.astype(BF16)
        to_end, ending, state = state_of(in_map, weighted[:SPAN], cum_pair[:SPAN])
        d_weighted = []
        for s in range(2):
            rows = slice(s * SPAN, (s + 1) * SPAN)
            decay = decays(cum_first, cum_second, cum_row, pair, s)
            mats = jnp.concatenate([(affinity[s] * one).astype(BF16) for one in decay], axis=0)
            both = split_heads(dy_low[rows])
            d_mats = mm_nt(both, low[rows])
            d_aff[s] = plus(d_aff[s], d_mats[:SPAN] * decay[0] + d_mats[SPAN:] * decay[1])
            d_weighted.append(mm_tn(mats, both))
        reached = (dy[SPAN:] * jnp.exp(cum_pair[SPAN:])).astype(BF16)
        d_out = plus(d_out, mm_nt(reached, state.astype(BF16)))
        d_state = mm_tn(out_map[SPAN:], reached).astype(BF16)
        d_in = plus(d_in, mm_nt(ending, d_state))
        d_ending = mm(in_map[:SPAN], d_state)
        through = ending.astype(F32) * d_ending
        low_f, dy_f = low.astype(F32), dy_low.astype(F32)
        change = dy_f * scanned - low_f * jnp.concatenate(d_weighted, axis=0)
        ended = jnp.where(last_row, jnp.sum(through, axis=0, keepdims=True), 0.0) - through
        change = jnp.concatenate([change[:SPAN] + ended, change[SPAN:]], axis=0)
        d_weight = jnp.concatenate([d_weighted[0] + d_ending * to_end, d_weighted[1]], axis=0)
        d_cum = plus(d_cum, head_sums(change, pair))
        d_step = plus(d_step, head_sums(d_weight * xc, pair))
        d_xc = dy * skip_ref[:, lanes] + d_weight * dt_pair
        d_cx = d_xc * (sx * (1.0 + cx * (1.0 - sx)))
        d_x, rows_x = conv_back(d_cx, x, cxw)
        dx_ref[:, lanes] = d_x.astype(BF16)
        for index, row in enumerate(rows_x):
            wide_ref[index : index + 1, lanes] = row
        d_skip = plus(d_skip, head_sums(wide_ref[:, lanes], pair))
        tick()

    rate = rate_ref[...]
    d_log = span_sums_back(d_cum)
    d_dt = d_step - rate * d_log
    d_tp = d_dt * valid * sigmoid(tp_ref[...] + bias_ref[...])
    small_ref[...] = jnp.zeros(small_ref.shape, F32)
    small_ref[0:1, :] = jnp.sum(d_tp, axis=0, keepdims=True)
    small_ref[1:2, :] = -rate * jnp.sum(dt * d_log, axis=0, keepdims=True)
    small_ref[2:3, :] = d_skip[5:6]
    dt_ref[...] = d_tp.astype(BF16)

    d_maps = []
    low_aff = [part.astype(BF16) for part in d_aff]
    d_ins, d_outs = [], []
    for s in range(2):
        rows = slice(s * SPAN, (s + 1) * SPAN)
        d_outs.append(mm(low_aff[s], in_map[rows]))
        d_ins.append(mm_tn(low_aff[s], out_map[rows]))
    d_outs[1] = d_outs[1] + d_out
    d_ins[0] = d_ins[0] + d_in
    d_maps = jnp.concatenate(
        [jnp.concatenate(d_ins, axis=0), jnp.concatenate(d_outs, axis=0)], axis=1
    )
    mapped = conv(bcp_ref[...], cbw_ref[...], cbb_ref[...])
    sm = sigmoid(mapped)
    d_bc, rows_bc = conv_back(d_maps * (sm * (1.0 + mapped * (1.0 - sm))), bcp_ref[...], cbw_ref[...])
    bcg_ref[...] = jnp.zeros(bcg_ref.shape, F32)
    for index, row in enumerate(rows_bc):
        bcg_ref[index : index + 1, :] = row
    d_bc = d_bc.astype(BF16)
    dbc_ref[...] = d_bc
    total = mm_nt(dx_ref[...], wx_ref[...]) + mm_nt(dz_ref[...], wz_ref[...])
    total = total + mm_nt(dq_ref[...], wq_ref[...]) + mm_nt(dkv_ref[...], wkv_ref[...])
    total = total + mm_nt(d_bc[:, :STATE], wb_ref[...]) + mm_nt(d_bc[:, STATE:], wc_ref[...])
    total = total + mm(dt_ref[...], wt_ref[...])
    dh_ref[...] = total.astype(dh_ref.dtype)


def ffn_kernel(h_ref, ct_ref, wg_ref, wu_ref, wd_ref, *refs):
    base_ref = refs[0] if len(refs) == 9 else None
    hid_ref, dg_ref, du_ref, ff_ref, dh_ref, ht_ref, ff_acc, dh_acc = refs[-8:]
    step = pl.program_id(0)
    h = h_ref[...]
    gate = mm(h, wg_ref[...])
    up = mm(h, wu_ref[...])
    d_hidden = mm_nt(ct_ref[...], wd_ref[...]).astype(BF16).astype(F32)
    sg = sigmoid(gate)
    silu = gate * sg
    hidden = silu * up
    hid_ref[...] = hidden.T.astype(BF16)
    hidden = hidden.astype(BF16)
    d_gate = (d_hidden * up * (sg * (1.0 + gate * (1.0 - sg)))).astype(BF16)
    d_up = (d_hidden * silu).astype(BF16)
    dg_ref[...] = d_gate
    du_ref[...] = d_up
    ff_part = mm(hidden, wd_ref[...])
    dh_part = mm_nt(d_gate, wg_ref[...]) + mm_nt(d_up, wu_ref[...])

    @pl.when(step == 0)
    def _():
        ht_ref[...] = h.astype(F32).T.astype(BF16)
        ff_acc[...] = ff_part if base_ref is None else ff_part + base_ref[...]
        dh_acc[...] = dh_part

    @pl.when(step > 0)
    def _():
        ff_acc[...] += ff_part
        dh_acc[...] += dh_part

    @pl.when(step == pl.num_programs(0) - 1)
    def _():
        ff_ref[...] = ff_acc[...].astype(ff_ref.dtype)
        dh_ref[...] = dh_acc[...].astype(dh_ref.dtype)


class Entry:
    def __init__(self, ref):
        self.ref = ref

    def __getitem__(self, index):
        return self.ref[0]


PARTS = 9
GATE, UP, DOWN, SHARED, STEP, QUERY, ZED, EX, OUT = range(PARTS)
KV_AT, B_AT, C_AT, MISC_AT = 0, LANES, 2 * LANES, 3 * LANES
SHARED_WIDTH = 4 * LANES


def chunk_order(widths):
    wide = 2 * LANES
    order = [(part, column, wide) for part in (GATE, UP, DOWN, OUT, QUERY) for column in range(0, widths[part], wide)]
    order += [(SHARED, column, LANES) for column in (KV_AT, B_AT, C_AT)]
    order += [(EX, column, wide) for column in range(0, widths[EX], wide)]
    order += [(STEP, 0, LANES), (SHARED, MISC_AT, LANES)]
    order += [(ZED, column, wide) for column in range(0, widths[ZED] - wide, wide)]
    order += [(ZED, column, LANES) for column in range(widths[ZED] - wide, widths[ZED], LANES)]
    return [item + ("P" if item[0] == SHARED or index % 2 else "Q",) for index, item in enumerate(order)]


SLOTS = 6


def back_kernel(*refs, small_names, big_names, widths, width, lag, pace):
    it = iter(refs)
    lens = [Entry(next(it)), Entry(next(it))]
    s = {name: next(it) for name in small_names}
    big_in = {name: next(it) for name in big_names}
    dh2_peer, ff_peer = next(it), next(it)
    outs = [next(it) for _ in range(PARTS)]
    xout, grad_in, layer_out = next(it), next(it), next(it)
    b = {name: next(it) for name in big_names}
    (db, bs, bsr, da, dm, dq, dkv, dx, dz, dbc, dt, dt_cat, dh_own, dh_peer, dh_got, ff_got, wide, bcg, small, misc,
     acc, rc, res, ry, zin_p, zin_q, zmid, in_sem, out_sem, xs, xr, send_sem, recv_sem) = it
    rows = outs[GATE].shape[0]
    half, quarter = rows // 2, rows // 4
    seq_len = db.shape[0] // 2
    me = lax.axis_index("dp")
    core, y, z = me % 2, (me // 2) % 2, me // 4
    side = lax.axis_index("tensor")
    sibling = {"dp": me + 1 - 2 * core}
    across = {"dp": me + 2 - 4 * y}
    outer = {"dp": (z + 1 - 2 * (z % 2)) * 4 + y * 2 + core}
    inner = {"dp": (3 - z) * 4 + y * 2 + core}
    pair = {"tensor": 1 - side}
    is_mid = (z == 1) | (z == 2)
    is_end = (z == 0) | (z == 3)

    def at(offset, size):
        return pl.ds(pl.multiple_of(offset, quarter), size)

    mine, other = at(core * half, half), at((1 - core) * half, half)
    my_y, other_y = at(y * quarter, quarter), at((1 - y) * quarter, quarter)
    zq = jnp.where(z <= 1, 0, 1)
    my_z, other_z = at(zq * quarter, quarter), at((1 - zq) * quarter, quarter)

    loads = {}
    for index, name in enumerate(big_names):
        loads[name] = pltpu.make_async_copy(big_in[name], b[name], in_sem.at[index])
        loads[name].start()
    ready = set()

    def need(*names):
        for name in names:
            if name not in ready:
                loads[name].wait()
                ready.add(name)

    barrier = pltpu.get_barrier_semaphore()
    for device in (sibling, across, outer, pair):
        pl.semaphore_signal(barrier, inc=1, device_id=device, device_id_type=MESH)

    @pl.when(is_mid)
    def _():
        pl.semaphore_signal(barrier, inc=1, device_id=inner, device_id_type=MESH)
        pl.semaphore_wait(barrier, 5)

    @pl.when(is_end)
    def _():
        pl.semaphore_wait(barrier, 4)

    ends = []

    def remote(src, dst, send, recv, device):
        return pltpu.make_async_remote_copy(
            src_ref=src, dst_ref=dst, send_sem=send, recv_sem=recv, device_id=device, device_id_type=MESH
        )

    def exchange(src, dst, slot):
        copy = remote(src, dst, xs.at[slot], xr.at[slot], pair)
        copy.start()
        return copy

    def make(part, column, size, span):
        lanes = slice(column, column + size)
        if part == SHARED and column == MISC_AT:
            return misc[span, :].astype(F32)
        total = None
        for k in range(2):
            left, right = {
                GATE: ("h2t", "dg"), UP: ("h2t", "du"), DOWN: ("hid", "ct"), OUT: ("mix", db), SHARED: ("ht", dbc),
                STEP: ("ht", dt_cat), QUERY: ("ht", dq), ZED: ("ht", dz), EX: ("ht", dx),
            }[part]
            need(f"{left}{k}")
            values = b[f"{left}{k}"][span, :]
            if isinstance(right, str):
                need(f"{right}{k}")
                right = b[f"{right}{k}"][:, lanes]
            elif part == SHARED:
                right = dkv[seq(k), :] if column == KV_AT else dbc[seq(k), column - LANES : column]
            else:
                right = right[seq(k), lanes]
            part_k = mm(values, right)
            total = part_k if total is None else total + part_k
        return total

    def add(dst, first, second):
        dst[...] = (first[...].astype(F32) + second[...].astype(F32)).astype(BF16)

    order = chunk_order(widths)
    starts = [sum(item[2] for item in order[:index]) for index in range(len(order))]
    made = set()
    sending = {}

    def chunk_steps(index):
        part, column, size, kind = order[index]
        start = starts[index]
        place = sum(item[2] for item in order[:index] if item[3] == kind)
        cols = slice(start, start + size)
        local = slice(column, column + size)
        tight = slice(place, place + size)
        out = outs[part]

        def own(src, dst, slot, device):
            return remote(src, dst, send_sem.at[slot, index], recv_sem.at[slot, index], device)

        source = acc.at[index % SLOTS, :, :size]
        to_core = own(source, rc.at[:, cols], 0, sibling)
        back_core = own(res.at[:, cols], out.at[mine, local], 6, sibling)
        wait_core = own(res.at[:, cols], out.at[other, local], 6, sibling)
        store = pltpu.make_async_copy(res.at[:, cols], out.at[mine, local], out_sem.at[index])

        def step0():
            assert part < SHARED or (part, column) in made
            if index - SLOTS in sending:
                sending.pop(index - SLOTS)()
            source[...] = make(part, column, size, other).astype(BF16)
            to_core.start()
            sending[index] = to_core.wait_send

        def merge_core():
            term = make(part, column, size, mine)
            to_core.wait_recv()
            rc[:, cols] = (rc[:, cols].astype(F32) + term).astype(BF16)

        def send_core():
            back_core.start()
            store.start()

        def last():
            wait_core.wait_recv()

        ends.append((None, back_core.wait_send))
        ends.append((None, store.wait))

        if kind == "P":
            zin = zin_p.at[:, tight]
            to_y = own(rc.at[other_y, cols], ry.at[:, cols], 1, across)
            to_mid = own(rc.at[my_y, cols], zin, 2, outer)
            swap = own(rc.at[my_y, cols], zmid.at[:, cols], 3, inner)
            to_end = own(res.at[my_y, cols], res.at[my_y, cols], 4, outer)
            back_y = own(res.at[my_y, cols], res.at[my_y, cols], 5, across)
            wait_y = own(res.at[my_y, cols], res.at[other_y, cols], 5, across)

            def step1():
                merge_core()
                to_y.start()
                ends.append((None, to_y.wait_send))

            def step2():
                to_y.wait_recv()
                add(rc.at[my_y, cols], rc.at[my_y, cols], ry.at[:, cols])
                pl.when(is_end)(to_mid.start)
                ends.append((is_end, to_mid.wait_send))

            def step3():
                @pl.when(is_mid)
                def _():
                    to_mid.wait_recv()
                    add(rc.at[my_y, cols], rc.at[my_y, cols], zin)
                    swap.start()

                ends.append((is_mid, swap.wait_send))

            def step4():
                @pl.when(is_mid)
                def _():
                    swap.wait_recv()
                    add(res.at[my_y, cols], rc.at[my_y, cols], zmid.at[:, cols])
                    to_end.start()
                    back_y.start()

                ends.append((is_mid, to_end.wait_send))

            def step5():
                @pl.when(is_end)
                def _():
                    to_end.wait_recv()
                    back_y.start()

                ends.append((None, back_y.wait_send))

            def step6():
                wait_y.wait_recv()
                send_core()

            steps = [step0, step1, step2, step3, step4, step5, step6, last]
            if part == SHARED:
                to_x = own(res.at[:, cols], xout.at[mine, local], 7, pair)
                x_core = own(xout.at[mine, local], xout.at[mine, local], 8, sibling)
                wait_x = own(xout.at[mine, local], xout.at[other, local], 8, sibling)

                def step6x():
                    step6()
                    to_x.start()
                    ends.append((None, to_x.wait_send))

                def step7x():
                    last()
                    to_x.wait_recv()
                    x_core.start()
                    ends.append((None, x_core.wait_send))

                steps[6:] = [step6x, step7x, wait_x.wait_recv]
            return steps

        zin = zin_q.at[:, tight]
        to_mid = own(rc.at[:, cols], zin, 1, outer)
        swap = own(rc.at[other_z, cols], zmid.at[:, cols], 2, inner)
        to_y = own(rc.at[my_z, cols], ry.at[:, cols], 3, across)
        to_inner = own(res.at[my_z, cols], res.at[my_z, cols], 4, inner)
        wait_inner = own(res.at[my_z, cols], res.at[other_z, cols], 4, inner)
        to_end = own(res.at[my_z, cols], res.at[my_z, cols], 5, outer)
        pass_end = own(res.at[other_z, cols], res.at[other_z, cols], 7, outer)

        def step1():
            merge_core()
            pl.when(is_end)(to_mid.start)
            ends.append((is_end, to_mid.wait_send))

        def step2():
            @pl.when(is_mid)
            def _():
                to_mid.wait_recv()
                add(rc.at[:, cols], rc.at[:, cols], zin)
                swap.start()

            ends.append((is_mid, swap.wait_send))

        def step3():
            @pl.when(is_mid)
            def _():
                swap.wait_recv()
                add(rc.at[my_z, cols], rc.at[my_z, cols], zmid.at[:, cols])
                to_y.start()

            ends.append((is_mid, to_y.wait_send))

        def step4():
            @pl.when(is_mid)
            def _():
                to_y.wait_recv()
                add(res.at[my_z, cols], rc.at[my_z, cols], ry.at[:, cols])
                to_inner.start()
                to_end.start()

            ends.append((is_mid, to_inner.wait_send))
            ends.append((is_mid, to_end.wait_send))

        def step5():
            @pl.when(is_mid)
            def _():
                wait_inner.wait_recv()
                pass_end.start()
                send_core()

            ends.append((is_mid, pass_end.wait_send))

        def step6():
            @pl.when(is_end)
            def _():
                to_end.wait_recv()
                pass_end.wait_recv()
                send_core()

        return [step0, step1, step2, step3, step4, step5, step6, last]

    plan = [
        (index + 2 * lag * number, -number, index, step)
        for index in range(len(order))
        for number, step in enumerate(chunk_steps(index))
    ]
    plan.sort(key=lambda item: item[:3])
    clock, done = [0.0], [0]

    def tick(time=pace):
        clock[0] += time
        while done[0] < len(plan) and plan[done[0]][0] <= clock[0]:
            plan[done[0]][3]()
            done[0] += 1

    def seq(k):
        return pl.ds(k * seq_len, seq_len)

    got_second_norm = exchange(dh2_peer, dh_got, 4)
    tick(0.0)
    tick()
    tick()
    tick()
    need("dh2", "rhat", "ct0")
    got_second_norm.wait()
    model = grad_in.shape[1]
    d_second = b["dh2"][...] + dh_got[...].astype(F32)
    scaled = d_second * s["gain2"][...]
    rhat = b["rhat"][...]
    mean = jnp.sum(scaled * rhat, axis=1, keepdims=True) / model
    d_resid = b["ct0"][...].astype(F32) + s["inv2"][...] * (scaled - rhat * mean)
    grad_in[...] = d_resid
    db[:seq_len, :] = d_resid.astype(BF16)
    norm_second = jnp.sum(d_second * rhat, axis=0, keepdims=True)
    got_db = exchange(db.at[:seq_len], db.at[seq_len:], 0)
    tick()

    def mix(k):
        need("wa", "ws", f"y{k}", f"x{k}", f"z{k}")
        mix_grad_kernel(
            db.at[seq(k)], b[f"y{k}"], b[f"x{k}"], b[f"z{k}"], s["cxw"], s["cxb"], s["skip"], s["gain"], b["wa"],
            b["ws"], da.at[k], dm.at[k], bs.at[k],
        )
        return exchange(bs.at[k], bsr.at[1 - k], 1 + k)

    def attend(k):
        need(f"q{k}", f"kd{k}", f"vd{k}")
        attend_back_kernel(
            lens[k], b[f"q{k}"], b[f"kd{k}"], b[f"vd{k}"], da.at[k], s["cos"], s["sa"], s["sb"], dq.at[seq(k)],
            dkv.at[seq(k)],
        )

    def mixer(k, dh):
        need("wq", "wkv", "wz", "wx", "wb", "wc", f"bcp{k}", f"bc{k}")
        bs[k] = bs[k] + bsr[k]
        mixer_back_kernel(
            lens[k], dm.at[k], b[f"y{k}"], b[f"x{k}"], b[f"z{k}"], b[f"bcp{k}"], b[f"bc{k}"], s[f"tp{k}"],
            s[f"tpr{k}"], s[f"ss{k}"], bs.at[k], dq.at[seq(k)], dkv.at[seq(k)], b["wq"], b["wkv"], b["wz"],
            b["wx"], b["wb"], b["wc"], s["wt"], s["cxw"], s["cxb"], s["cbw"], s["cbb"], s["bias"], s["rate"],
            s["bias_col"], s["rate_col"], s["skip"], s["gain"], dh, dx.at[seq(k)], dz.at[seq(k)],
            dbc.at[seq(k)], dt.at[k], wide.at[k], bcg.at[k], small.at[k], width=width, tick=tick,
        )
        tick()

    got_first = mix(0)
    tick()
    attend(0)
    tick()
    got_db.wait_recv()
    got_second = mix(1)
    tick()
    attend(1)
    tick()
    for part in (OUT, QUERY):
        made.update([(part, column) for column in range(0, widths[part], LANES)])
    made.add((SHARED, KV_AT))
    got_first.wait_recv()
    got_second.wait_recv()
    got_first.wait_send()
    got_second.wait_send()
    mixer(1, dh_peer)
    got_dh = exchange(dh_peer, dh_got, 3)
    got_ff = exchange(ff_peer, ff_got, 5)
    mixer(0, dh_own)
    dt_cat[...] = jnp.zeros(dt_cat.shape, BF16)
    dt_cat[:seq_len, :16] = dt[0]
    dt_cat[seq_len:, :16] = dt[1]
    for part in (ZED, EX, STEP):
        made.update([(part, column) for column in range(0, widths[part], LANES)])
    made.update([(SHARED, B_AT), (SHARED, C_AT)])
    misc_key = [item[:2] for item in order].index((SHARED, MISC_AT))
    tick(max(0.0, misc_key - 4 - clock[0]))
    got_dh.wait()
    d_first = dh_own[...] + dh_got[...].astype(F32)
    need("xhat")
    xhat = b["xhat"][...]
    scaled = d_first * s["gain1"][...]
    mean = jnp.sum(scaled * xhat, axis=1, keepdims=True) / model
    grad_in[...] += s["inv1"][...] * (scaled - xhat * mean)
    norm = jnp.sum(d_first * xhat, axis=0, keepdims=True)
    wide_sum, bcg_sum, small_sum = wide[0] + wide[1], bcg[0] + bcg[1], small[0] + small[1]
    first_row = row_ids((8, model)) == 0
    second_row = row_ids((8, model)) == 1
    norms = jnp.where(first_row, norm, jnp.where(second_row, norm_second, 0.0))
    blocks = [array[:, i : i + LANES] for array in (wide_sum, bcg_sum) for i in range(0, array.shape[1], LANES)]
    blocks.append(jnp.concatenate([small_sum, jnp.zeros((8, LANES - 16), F32)], axis=1))
    blocks += [norms[:, i : i + LANES] for i in range(0, model, LANES)]
    if len(blocks) % 2:
        blocks.append(jnp.zeros((8, LANES), F32))
    misc[...] = jnp.zeros(misc.shape, BF16)
    misc[: 8 * len(blocks), :] = jnp.concatenate(blocks, axis=0).astype(BF16)
    made.add((SHARED, MISC_AT))
    tick(max(0.0, len(order) + 2 - clock[0]))
    got_ff.wait()
    need("ff")
    layer_out[...] = (b["ff"][...] + ff_got[...].astype(F32)).astype(BF16)
    got_db.wait_send()
    tick(1e6)
    for wait in sending.values():
        wait()
    for devices, wait in ends:
        if devices is None:
            wait()
        else:
            pl.when(devices)(wait)


def back_call(lens, smalls, bigs, dh2_peer, ff_peer, widths, width, lag=1, pace=0.8):
    rows, (seq_len, model) = bigs["h2t0"].shape[0], dh2_peer.shape
    order = chunk_order(widths)
    columns = sum(item[2] for item in order)
    ones = sum(item[2] for item in order if item[3] == "P")
    count = len(order)
    half, quarter = rows // 2, rows // 4
    ssm_pad, att_pad = bigs["x0"].shape[1], bigs["q0"].shape[1]
    anywhere, vmem = pl.BlockSpec(memory_space=pl.ANY), pl.BlockSpec(memory_space=pltpu.VMEM)
    outs = [shaped((rows, w), BF16) for w in widths] + [shaped((rows, SHARED_WIDTH), BF16), shaped((seq_len, model))]
    outs.append(shaped((seq_len, model), BF16))
    scratch = [pltpu.VMEM(array.shape, array.dtype) for array in bigs.values()]
    both = 2 * seq_len
    scratch += [
        pltpu.VMEM((both, model), BF16),
        pltpu.VMEM((2, 16, seq_len), F32), pltpu.VMEM((2, 16, seq_len), F32),
        pltpu.VMEM((2, seq_len, att_pad), BF16), pltpu.VMEM((2, seq_len, ssm_pad), BF16),
        pltpu.VMEM((both, att_pad), BF16), pltpu.VMEM((both, LANES), BF16), pltpu.VMEM((both, ssm_pad), BF16),
        pltpu.VMEM((both, ssm_pad), BF16), pltpu.VMEM((both, 2 * STATE), BF16), pltpu.VMEM((2, seq_len, 16), BF16),
        pltpu.VMEM((both, LANES), BF16),
        pltpu.VMEM((seq_len, model), F32), pltpu.VMEM((seq_len, model), BF16), pltpu.VMEM((seq_len, model), BF16),
        pltpu.VMEM((seq_len, model), BF16),
        pltpu.VMEM((2, 8, ssm_pad), F32), pltpu.VMEM((2, 8, 2 * STATE), F32), pltpu.VMEM((2, 8, 16), F32),
        pltpu.VMEM((rows, LANES), BF16), pltpu.VMEM((SLOTS, half, 2 * LANES), BF16),
        pltpu.VMEM((half, columns), BF16), pltpu.VMEM((half, columns), BF16),
        pltpu.VMEM((quarter, columns), BF16), pltpu.VMEM((quarter, ones), BF16),
        pltpu.VMEM((half, columns - ones), BF16), pltpu.VMEM((quarter, columns), BF16),
        pltpu.SemaphoreType.DMA((len(bigs),)), pltpu.SemaphoreType.DMA((count,)),
        pltpu.SemaphoreType.DMA((6,)), pltpu.SemaphoreType.DMA((6,)),
        pltpu.SemaphoreType.DMA((9, count)), pltpu.SemaphoreType.DMA((9, count)),
    ]
    return pl.pallas_call(
        functools.partial(
            back_kernel, small_names=tuple(smalls), big_names=tuple(bigs), widths=tuple(widths), width=width,
            lag=lag, pace=pace,
        ),
        out_shape=outs,
        in_specs=[pl.BlockSpec(memory_space=pltpu.SMEM)] * 2 + [vmem] * len(smalls) + [anywhere] * (len(bigs) + 2),
        out_specs=[anywhere] * (PARTS + 1) + [vmem] * 2,
        scratch_shapes=scratch,
        compiler_params=pltpu.CompilerParams(
            collective_id=0, has_side_effects=True, vmem_limit_bytes=REDUCE_LIMIT
        ),
        name="back_and_reduce",
    )(*lens, *smalls.values(), *bigs.values(), dh2_peer, ff_peer)


def finish_kernel(own_ref, peer_ref, own_misc_ref, peer_misc_ref, *refs, split):
    step = pl.program_id(0)
    sums, refs = refs[:8], refs[8:]
    step_ref, out_ref = sums[6:]
    for source, target in zip(sums[:6], refs[:6]):
        target[...] = source[...].astype(F32)
    (att_ref, ssm_ref, key_ref, value_ref, b_ref, c_ref, stp_ref, cxw_ref, cxb_ref, cbw_ref, cbb_ref, bias_ref,
     decay_ref, skip_ref, sgain_ref, norm_ref, ffn_ref) = refs[6:]

    @pl.when(step < split)
    def _():
        att_ref[...] = out_ref[...].astype(F32)

    @pl.when(step >= split)
    def _():
        ssm_ref[...] = out_ref[...].astype(F32)

    even = lax.axis_index("tensor") == 0
    kv, kv_peer = own_ref[:, :LANES].astype(F32), peer_ref[:, :LANES].astype(F32)
    low, high = jnp.where(even, kv, kv_peer), jnp.where(even, kv_peer, kv)
    first = lane_ids(kv.shape) < HEAD_DIM
    key_ref[...] = jnp.where(first, low, pltpu.roll(high, HEAD_DIM, 1))
    value_ref[...] = jnp.where(first, pltpu.roll(low, HEAD_DIM, 1), high)
    for ref, column in ((b_ref, B_AT), (c_ref, C_AT)):
        lanes = slice(column, column + LANES)
        ref[...] = own_ref[:, lanes].astype(F32) + peer_ref[:, lanes].astype(F32)
    stp_ref[...] = step_ref[...].astype(F32)[:, : stp_ref.shape[1]]

    @pl.when(step == 0)
    def _():
        wide_blocks, model_blocks = cxw_ref.shape[1] // LANES, norm_ref.shape[1] // LANES
        mine = own_misc_ref[...].astype(F32)
        both = mine + peer_misc_ref[...].astype(F32)

        def rows(values, block, row, length=1):
            return values[8 * block + row : 8 * block + row + length]

        for block in range(wide_blocks):
            lanes = slice(block * LANES, (block + 1) * LANES)
            cxw_ref[:, lanes] = rows(mine, block, 0, 4)
            cxb_ref[:, lanes] = rows(mine, block, 4)
            sgain_ref[:, lanes] = rows(mine, block, 6)
        for block in range(2):
            lanes = slice(block * LANES, (block + 1) * LANES)
            cbw_ref[:, lanes] = rows(both, wide_blocks + block, 0, 4)
            cbb_ref[:, lanes] = rows(both, wide_blocks + block, 4)
        heads = bias_ref.shape[1]
        for row, ref in enumerate((bias_ref, decay_ref, skip_ref)):
            ref[...] = rows(mine, wide_blocks + 2, row)[:, :heads]
        for block in range(model_blocks):
            lanes = slice(block * LANES, (block + 1) * LANES)
            norm_ref[:, lanes] = rows(both, wide_blocks + 3 + block, 0)
            ffn_ref[:, lanes] = rows(both, wide_blocks + 3 + block, 1)


def finish_call(results, peer, att_width, heads):
    model, block = results[OUT].shape[0], 128
    ssm_pad = results[ZED].shape[1]
    shared = results[SHARED]
    misc_rows = 8 * (ssm_pad // LANES + 3 + model // LANES)
    misc_rows += -misc_rows % 16
    sums = [results[part] for part in (GATE, UP, DOWN, QUERY, ZED, EX, STEP, OUT)]
    split = att_width // block

    def by_rows(width):
        return pl.BlockSpec((block, width), lambda i: (i, 0))

    def fixed(height, width):
        return pl.BlockSpec((height, width), lambda i: (0, 0))

    misc = pl.BlockSpec((misc_rows, LANES), lambda i: (0, MISC_AT // LANES))
    shapes = [(model, part.shape[1]) for part in sums[:6]]
    specs = [by_rows(part.shape[1]) for part in sums[:6]]
    shapes += [(att_width, model), (model - att_width, model)]
    specs += [
        pl.BlockSpec((block, model), lambda i: (jnp.minimum(i, split - 1), 0)),
        pl.BlockSpec((block, model), lambda i: (jnp.maximum(i - split, 0), 0)),
    ]
    shapes += [(model, LANES)] * 4 + [(model, heads)]
    specs += [by_rows(LANES)] * 4 + [by_rows(heads)]
    tiny = [
        (4, ssm_pad), (1, ssm_pad), (4, 2 * STATE), (1, 2 * STATE), (1, heads), (1, heads), (1, heads), (1, ssm_pad),
        (1, model), (1, model),
    ]
    shapes += tiny
    specs += [fixed(*shape) for shape in tiny]
    return pl.pallas_call(
        functools.partial(finish_kernel, split=split),
        grid=(model // block,),
        out_shape=[shaped(shape) for shape in shapes],
        in_specs=[by_rows(SHARED_WIDTH)] * 2 + [misc] * 2 + [by_rows(part.shape[1]) for part in sums],
        out_specs=specs,
        compiler_params=pltpu.CompilerParams(vmem_limit_bytes=VMEM_LIMIT),
        name="finish",
    )(shared, peer, shared, peer, *sums)


def shaped(shape, dtype=F32):
    return jax.ShapeDtypeStruct(shape, dtype)


def whole_call(kernel, outs, scalars, args, flops, name):
    specs = [pl.BlockSpec(memory_space=pltpu.SMEM)] * scalars
    specs += [pl.BlockSpec(memory_space=pltpu.VMEM)] * (len(args) - scalars)
    moved = sum(arg.size * arg.dtype.itemsize for arg in args)
    return pl.pallas_call(
        kernel,
        out_shape=outs,
        in_specs=specs,
        out_specs=[pl.BlockSpec(memory_space=pltpu.VMEM)] * len(outs),
        compiler_params=pltpu.CompilerParams(vmem_limit_bytes=VMEM_LIMIT),
        cost_estimate=pl.CostEstimate(flops=flops, bytes_accessed=moved, transcendentals=0),
        name=name,
    )(*args)


def pad_columns(values, width):
    return jnp.pad(values, ((0, 0), (0, width - values.shape[1]))) if width != values.shape[1] else values


def pad_rows(values, height):
    return jnp.pad(values, ((0, height - values.shape[0]), (0, 0))) if height != values.shape[0] else values


def contract_rows(left, right):
    return mm_tn(jnp.concatenate(left, axis=0), jnp.concatenate(right, axis=0))


def on_device(
    tokens, lengths, cotangent, norm_gain, w_query, w_key, w_value, w_gate_z, w_ssm_x, w_ssm_b, w_ssm_c,
    w_step, conv_x_weight, conv_x_bias, conv_bc_weight, conv_bc_bias, step_bias, decay_log, skip_gain,
    ssm_norm_gain, w_out_att, w_out_ssm, ffn_norm_gain, w_gate, w_up, w_down,
):
    seq_len, model = tokens.shape
    groups = lax.axis_size("tensor")
    position = lax.axis_index("tensor")
    att_width, ssm_width = w_query.shape[1], w_gate_z.shape[1]
    att_pad = -(-att_width // LANES) * LANES
    ssm_pad = -(-ssm_width // LANES) * LANES
    ssm_heads = ssm_width // SSM_DIM
    ssm_width_all = SSM_HEADS * SSM_DIM
    ff_width = w_gate.shape[1]

    def fetch(values, shift):
        return lax.ppermute(values, "tensor", [((i + shift) % groups, i) for i in range(groups)])

    def deliver(values, shift):
        return lax.ppermute(values, "tensor", [(i, (i + shift) % groups) for i in range(groups)])

    def gather(values):
        return [values] + [fetch(values, k) for k in range(1, groups)]

    def scatter_sum(own, others):
        total = own
        for k in range(1, groups):
            total = total + deliver(others[k - 1], k).astype(F32)
        return total

    kv_head = position * (att_width // HEAD_DIM) // (HEADS // KV_HEADS)
    w_kv = jnp.concatenate(
        [lax.dynamic_slice_in_dim(w, kv_head * HEAD_DIM, HEAD_DIM, 1) for w in (w_key, w_value)], axis=1
    )
    wq = pad_columns(w_query, att_pad)
    wz, wx = pad_columns(w_gate_z, ssm_pad), pad_columns(w_ssm_x, ssm_pad)
    wt = pad_rows(w_step.T, 16)
    wa, ws = pad_rows(w_out_att, att_pad), pad_rows(w_out_ssm, ssm_pad)
    cxw, cxb = pad_columns(conv_x_weight, ssm_pad), pad_columns(conv_x_bias[None], ssm_pad)
    cbb = conv_bc_bias[None]
    gain = pad_columns(ssm_norm_gain[None], ssm_pad)
    skip = pad_columns(jnp.repeat(skip_gain, SSM_DIM)[None], ssm_pad)
    bias = pad_columns(step_bias[None], 16)
    rate = pad_columns(jnp.exp(decay_log)[None], 16)
    bias_col, rate_col = bias.T, rate.T
    half = HEAD_DIM // 2
    freqs = ROPE_BASE ** (-(jnp.arange(half).astype(F32) * 2.0 / HEAD_DIM))
    angles = jnp.arange(seq_len).astype(F32)[:, None] * freqs[None, :]
    cosine, sine, none = jnp.cos(angles), jnp.sin(angles), jnp.zeros_like(angles)
    cos_table = jnp.concatenate([cosine] * 4, axis=1)
    sine_first = jnp.concatenate([-sine, none] * 2, axis=1)
    sine_second = jnp.concatenate([none, sine] * 2, axis=1)

    inputs = tokens.astype(F32)
    inv1 = lax.rsqrt(jnp.mean(inputs * inputs, axis=1, keepdims=True) + EPSILON)
    h_own = (inputs * inv1 * norm_gain).astype(BF16)
    own_mask = jnp.arange(seq_len) < lengths[0]
    ct_own = jnp.where(own_mask[:, None], cotangent, jnp.zeros_like(cotangent))
    h_all = gather(h_own)
    len_all = gather(lax.optimization_barrier((lengths, h_own))[0])
    ct_all = gather(lax.optimization_barrier((ct_own, h_all[1]))[0] if groups > 1 else ct_own)

    def forward(k):
        outs = [
            shaped((seq_len, att_pad), BF16), shaped((seq_len, LANES), BF16), shaped((seq_len, LANES), BF16),
            shaped((seq_len, ssm_pad)), shaped((seq_len, ssm_pad)), shaped((seq_len, 2 * STATE)),
            shaped((seq_len, 2 * STATE), BF16), shaped((seq_len, 16)), shaped((16, seq_len)),
            shaped((seq_len, ssm_pad)), shaped((16, seq_len)),
        ]
        args = [
            len_all[k], h_all[k], wq, w_kv, wz, wx, w_ssm_b, w_ssm_c, wt, cxw, cxb, conv_bc_weight, cbb,
            bias, rate, bias_col, rate_col, skip, cos_table, sine_first, sine_second,
        ]
        return whole_call(mixer_forward_kernel, outs, 1, args, 8 * 10**9, "mixer_forward")

    def attend(k):
        q, kd, vd = kept[k][:3]
        return whole_call(
            attend_kernel, [shaped((seq_len, att_pad), BF16)], 1, [len_all[k], q, kd, vd], 2 * 10**9, "attend"
        )[0]

    kept = [forward(k) for k in range(groups)]
    squares_part = [one[10] for one in kept]
    squares = [squares_part[k] for k in range(groups)]
    for shift in range(1, groups):
        for k in range(groups):
            squares[k] = squares[k] + fetch(squares_part[(k - shift) % groups], shift)
    mix_att = [attend(k) for k in range(groups)]

    def project(k, dtype):
        q, kd, vd, z, x, bcp, bc, tp, tpr, y, _ = kept[k]
        return whole_call(
            functools.partial(out_kernel, width=ssm_width_all),
            [shaped((seq_len, model), dtype), shaped((seq_len, ssm_pad), BF16)],
            0,
            [mix_att[k], y, x, z, squares[k], cxw, cxb, skip, gain, wa, ws],
            4 * 10**9,
            "out_project",
        )

    projected = [project(k, F32 if k == 0 else BF16) for k in range(groups)]
    mix_ssm = [one[1] for one in projected]
    branch = scatter_sum(projected[0][0], [one[0] for one in projected[1:]])
    resid = inputs + branch
    inv2 = lax.rsqrt(jnp.mean(resid * resid, axis=1, keepdims=True) + EPSILON)
    h2_own = (resid * inv2 * ffn_norm_gain).astype(BF16)
    h2_all = gather(h2_own)

    def feed(k, rows2):
        dtype = F32 if k == 0 else BF16
        block = min(256, ff_width)
        full = pl.BlockSpec((seq_len, model), lambda i: (0, 0))
        columns = pl.BlockSpec((model, block), lambda i: (0, i))
        rows = pl.BlockSpec((block, model), lambda i: (i, 0))
        tall = pl.BlockSpec((seq_len, block), lambda i: (0, i))
        return pl.pallas_call(
            ffn_kernel,
            grid=(ff_width // block,),
            out_shape=[shaped((ff_width, seq_len), BF16)] + [shaped((seq_len, ff_width), BF16)] * 2
            + [shaped((seq_len, model), dtype)] * 2 + [shaped((model, seq_len), BF16)],
            in_specs=[full, full, columns, columns, rows] + ([full] if k == 0 else []),
            out_specs=[pl.BlockSpec((block, seq_len), lambda i: (i, 0))] + [tall] * 2 + [full] * 2
            + [pl.BlockSpec((model, seq_len), lambda i: (0, 0))],
            scratch_shapes=[pltpu.VMEM((seq_len, model), F32)] * 2,
            compiler_params=pltpu.CompilerParams(vmem_limit_bytes=VMEM_LIMIT),
            cost_estimate=pl.CostEstimate(flops=8 * 10**9, bytes_accessed=10**7, transcendentals=0),
            name="feed_forward",
        )(rows2, ct_all[k], w_gate, w_up, w_down, *([resid] if k == 0 else []))

    fed = [feed(0, h2_own)]
    for k in range(1, groups):
        fed.append(feed(k, lax.optimization_barrier((h2_all[k], fed[0][0]))[0]))
    if lax.axis_size("dp") == 16 and groups == 2:
        smalls = {
            "wt": wt, "cxw": cxw, "cxb": cxb, "cbw": conv_bc_weight, "cbb": cbb, "bias": bias, "rate": rate,
            "bias_col": bias_col, "rate_col": rate_col, "skip": skip, "gain": gain, "cos": cos_table,
            "sa": sine_first, "sb": sine_second, "gain1": norm_gain[None], "gain2": ffn_norm_gain[None],
            "inv1": inv1, "inv2": inv2,
        }
        bigs = {}
        for k in range(groups):
            bigs[f"h2t{k}"] = fed[k][5]
            bigs[f"dg{k}"] = fed[k][1]
        bigs.update({"dh2": fed[0][4], "rhat": resid * inv2})
        for k in range(groups):
            bigs.update({f"du{k}": fed[k][2], f"hid{k}": fed[k][0], f"ct{k}": ct_all[k]})
        bigs.update({"wa": wa, "ws": ws})
        for k in range(groups):
            q, kd, vd, z, x, bcp, bc, tp, tpr, y, _ = kept[k]
            smalls.update({f"tp{k}": tp, f"tpr{k}": tpr, f"ss{k}": squares[k]})
            bigs.update({f"y{k}": y, f"x{k}": x, f"z{k}": z, f"q{k}": q, f"kd{k}": kd, f"vd{k}": vd})
        bigs.update({"wq": wq, "wkv": w_kv, "wz": wz, "wx": wx, "wb": w_ssm_b, "wc": w_ssm_c})
        for k in range(groups):
            bigs.update({f"bcp{k}": kept[k][5], f"bc{k}": kept[k][6]})
        for k in range(groups):
            bigs[f"mix{k}"] = jnp.concatenate([mix_att[k].T, mix_ssm[k].T], axis=0)
            bigs[f"ht{k}"] = h_all[k].T
        bigs["xhat"] = inputs * inv1
        bigs["ff"] = fed[0][3]
        tail_widths = (SHARED_WIDTH, LANES, att_pad, ssm_pad, ssm_pad, model)
        results = back_call(len_all, smalls, bigs, fed[1][4], fed[1][3], (ff_width, ff_width, model) + tail_widths, ssm_width_all)
        peer, grad_input, layer_output = results[PARTS:]
        (grad_gate, grad_up, grad_down, grad_q, grad_z, grad_x, grad_att, grad_ssm, grad_key, grad_value, grad_b,
         grad_c, grad_step, grad_cxw, grad_cxb, grad_cbw, grad_cbb, grad_bias, grad_decay, grad_skip, grad_sgain,
         grad_norm_gain, grad_ffn_gain) = finish_call(results, peer, att_pad, ssm_heads)
    else:
        d_second = scatter_sum(fed[0][4], [one[4] for one in fed[1:]])
        layer_output = scatter_sum(fed[0][3], [one[3] for one in fed[1:]]).astype(BF16)
        h2_turned = jnp.concatenate([one[5] for one in fed], axis=1)
        grad_gate = mm(h2_turned, jnp.concatenate([one[1] for one in fed], axis=0))
        grad_up = mm(h2_turned, jnp.concatenate([one[2] for one in fed], axis=0))
        grad_down = mm(jnp.concatenate([one[0] for one in fed], axis=1), jnp.concatenate(ct_all, axis=0))
        scaled = d_second * ffn_norm_gain
        d_resid = (
            ct_own.astype(F32)
            + inv2 * scaled
            - resid * (inv2**3) * jnp.mean(scaled * resid, axis=1, keepdims=True)
        )
        grad_ffn_gain = jnp.sum(d_second * resid * inv2, axis=0)
        db_all = gather(d_resid.astype(BF16))

        def mix_grad(k):
            q, kd, vd, z, x, bcp, bc, tp, tpr, y, _ = kept[k]
            return whole_call(
                mix_grad_kernel,
                [shaped((seq_len, att_pad), BF16), shaped((seq_len, ssm_pad), BF16), shaped((16, seq_len))],
                0,
                [db_all[k], y, x, z, cxw, cxb, skip, gain, wa, ws],
                4 * 10**9,
                "mix_grad",
            )

        mixed = [mix_grad(k) for k in range(groups)]
        backs_part = [one[2] for one in mixed]
        backs = [backs_part[k] for k in range(groups)]
        for shift in range(1, groups):
            for k in range(groups):
                backs[k] = backs[k] + fetch(backs_part[(k - shift) % groups], shift)

        def attend_back(k):
            q, kd, vd = kept[k][:3]
            return whole_call(
                attend_back_kernel,
                [shaped((seq_len, att_pad), BF16), shaped((seq_len, LANES), BF16)],
                1,
                [len_all[k], q, kd, vd, mixed[k][0], cos_table, sine_first, sine_second],
                4 * 10**9,
                "attend_back",
            )

        turned = [attend_back(k) for k in range(groups)]

        def backward(k):
            q, kd, vd, z, x, bcp, bc, tp, tpr, y, _ = kept[k]
            outs = [
                shaped((seq_len, model), F32 if k == 0 else BF16), shaped((seq_len, ssm_pad), BF16),
                shaped((seq_len, ssm_pad), BF16), shaped((seq_len, 2 * STATE), BF16), shaped((seq_len, 16), BF16),
                shaped((8, ssm_pad)), shaped((8, 2 * STATE)), shaped((8, 16)),
            ]
            args = [
                len_all[k], mixed[k][1], y, x, z, bcp, bc, tp, tpr, squares[k], backs[k], turned[k][0], turned[k][1],
                wq, w_kv, wz, wx, w_ssm_b, w_ssm_c, wt, cxw, cxb, conv_bc_weight, cbb, bias, rate, bias_col, rate_col,
                skip, gain,
            ]
            return whole_call(
                functools.partial(mixer_back_kernel, width=ssm_width_all), outs, 1, args, 16 * 10**9, "mixer_back"
            )

        gone = [None] * groups
        for k in list(range(1, groups)) + [0]:
            gone[k] = backward(k)
        d_first = scatter_sum(gone[0][0], [one[0] for one in gone[1:]])
        grad_norm_gain = jnp.sum(d_first * inputs * inv1, axis=0)

        wide, bcg, small = (sum(one[i] for one in gone) for i in (5, 6, 7))
        grad_q = contract_rows(h_all, [one[0] for one in turned])
        grad_kv = contract_rows(h_all, [one[1] for one in turned])
        grad_bc = contract_rows(h_all, [one[3] for one in gone])
        grad_x = contract_rows(h_all, [one[1] for one in gone])
        grad_z = contract_rows(h_all, [one[2] for one in gone])
        grad_step = contract_rows(h_all, [one[4] for one in gone])
        grad_att = contract_rows(mix_att, db_all)
        grad_ssm = contract_rows(mix_ssm, db_all)
        norms = jnp.concatenate([bcg[:5].reshape(-1), grad_norm_gain, grad_ffn_gain])
        zeros = jnp.zeros((model, KV_HEADS * HEAD_DIM), F32)
        grad_key = lax.dynamic_update_slice(zeros, grad_kv[:, :HEAD_DIM], (0, kv_head * HEAD_DIM))
        grad_value = lax.dynamic_update_slice(zeros, grad_kv[:, HEAD_DIM:], (0, kv_head * HEAD_DIM))
        grad_key, grad_value, grad_bc, norms = lax.psum((grad_key, grad_value, grad_bc, norms), ("dp", "tensor"))
        grad_b, grad_c = grad_bc[:, :STATE], grad_bc[:, STATE:]
        grad_q, grad_z, grad_x, grad_step, grad_att, grad_ssm, wide, small = (
            lax.psum(part.astype(BF16), "dp").astype(F32)
            for part in (grad_q, grad_z, grad_x, grad_step, grad_att, grad_ssm, wide, small)
        )
        grad_gate, grad_up, grad_down = (
            lax.psum(part.astype(BF16), "dp").astype(F32) for part in (grad_gate, grad_up, grad_down)
        )
        grad_step = grad_step[:, :ssm_heads]
        grad_cxw, grad_cxb, grad_sgain = wide[:4], wide[4:5], wide[6:7]
        bcg = norms[: 10 * STATE].reshape(5, 2 * STATE)
        grad_cbw, grad_cbb = bcg[:4], bcg[4:]
        grad_bias, grad_decay, grad_skip = small[0:1, :ssm_heads], small[1:2, :ssm_heads], small[2:3, :ssm_heads]
        grad_norm_gain = norms[10 * STATE : 10 * STATE + model]
        grad_ffn_gain = norms[10 * STATE + model :]

        scaled = d_first * norm_gain
        grad_input = d_resid + inv1 * scaled - inputs * (inv1**3) * jnp.mean(scaled * inputs, axis=1, keepdims=True)

    return (
        layer_output,
        grad_input,
        grad_norm_gain.reshape(-1),
        grad_q[:, :att_width],
        grad_key,
        grad_value,
        grad_z[:, :ssm_width],
        grad_x[:, :ssm_width],
        grad_b,
        grad_c,
        grad_step,
        grad_cxw[:, :ssm_width],
        grad_cxb.reshape(-1)[:ssm_width],
        grad_cbw,
        grad_cbb.reshape(-1),
        grad_bias.reshape(-1),
        grad_decay.reshape(-1),
        grad_skip.reshape(-1),
        grad_sgain.reshape(-1)[:ssm_width],
        grad_att[:att_width],
        grad_ssm[:ssm_width],
        grad_ffn_gain.reshape(-1),
        grad_gate,
        grad_up,
        grad_down,
    )


def solution(mesh):
    rows, split, tall = P(("dp", "tensor"), None), P(None, "tensor"), P("tensor", None)
    vector, copied = P("tensor"), P()
    return jax.shard_map(
        on_device,
        mesh=mesh,
        in_specs=(
            rows, P(("dp", "tensor")), rows, copied, split, copied, copied, split, split, copied, copied, split,
            split, vector, copied, copied, vector, vector, vector, vector, tall, tall, copied, split, split, tall,
        ),
        out_specs=(
            rows, rows, copied, split, copied, copied, split, split, copied, copied, split, split, vector, copied,
            copied, vector, vector, vector, vector, tall, tall, copied, split, split, tall,
        ),
        check_vma=False,
    )
```

```python
import functools

import jax
import jax.numpy as jnp
import numpy as np
from jax import lax
from jax.experimental import pallas as pl
from jax.experimental.pallas import tpu as pltpu
from jax.sharding import PartitionSpec as P

HEADS = 8
KV_HEADS = 2
HEAD_DIM = 64
SSM_HEADS = 24
SSM_DIM = 64
STATE = 128
SPAN = 128
LANES = 128

EPSILON = 1e-05
ROPE_BASE = 100000000000.0
F32 = jnp.float32
BF16 = jnp.bfloat16
VMEM_LIMIT = 62 * 1024 * 1024
REDUCE_LIMIT = 62 * 1024 * 1024
MESH = pl.DeviceIdType.MESH


def mm(left, right):
    return jnp.dot(left, right, preferred_element_type=F32)


def mm_nt(left, right):
    return lax.dot_general(left, right, (((1,), (1,)), ((), ())), preferred_element_type=F32)


def mm_tn(left, right):
    return lax.dot_general(left, right, (((0,), (0,)), ((), ())), preferred_element_type=F32)


def pieces(values, count):
    terms = []
    for _ in range(count):
        term = values.astype(BF16)
        terms.append(term)
        values = values - term.astype(F32)
    return terms


def sigmoid(values):
    return 1.0 / (1.0 + jnp.exp(-values))


def softplus(values):
    return jnp.maximum(values, 0.0) + jnp.log1p(jnp.exp(-jnp.abs(values)))


def lane_ids(shape):
    return lax.broadcasted_iota(jnp.int32, shape, 1)


def row_ids(shape):
    return lax.broadcasted_iota(jnp.int32, shape, 0)


def repeat_lanes(column, count):
    return jnp.concatenate([column] * count, axis=1) if count > 1 else column


def column_of(row):
    ones = jnp.where(row_ids((16, LANES)) == 0, 1.0, 0.0).astype(BF16)
    total = None
    for term in pieces(row, 3):
        part = mm_tn(term, ones)
        total = part if total is None else total + part
    return total


def row_sums(values):
    ones = jnp.ones((16, values.shape[1]), BF16)
    high, low = pieces(values, 2)
    return mm_nt(ones, high) + mm_nt(ones, low)


def causal_shift(values, steps):
    if steps == 0:
        return values
    rolled = pltpu.roll(values, steps, 0)
    return jnp.where(row_ids(values.shape) >= steps, rolled, 0.0)


def anti_shift(values, steps):
    if steps == 0:
        return values
    length = values.shape[0]
    rolled = pltpu.roll(values, length - steps, 0)
    return jnp.where(row_ids(values.shape) < length - steps, rolled, 0.0)


def conv(values, weight, bias):
    taps = weight.shape[0]
    total = bias + weight[taps - 1 : taps] * values
    for offset in range(taps - 1):
        total = total + weight[offset : offset + 1] * causal_shift(values, taps - 1 - offset)
    return total


def conv_back(grad, values, weight):
    taps = weight.shape[0]
    total, rows = None, []
    for offset in range(taps):
        steps = taps - 1 - offset
        moved = anti_shift(grad, steps)
        part = weight[offset : offset + 1] * moved
        total = part if total is None else total + part
        rows.append(jnp.sum(moved * values, axis=0, keepdims=True))
    rows.append(jnp.sum(grad, axis=0, keepdims=True))
    return total, rows


def rope(values, cosine, sine_first, sine_second):
    ahead = pltpu.roll(values, LANES - HEAD_DIM // 2, 1)
    behind = pltpu.roll(values, HEAD_DIM // 2, 1)
    return values * cosine + ahead * sine_first + behind * sine_second


def lower_mask():
    return row_ids((SPAN, SPAN)) >= lane_ids((SPAN, SPAN))


def span_sums(values):
    lower = jnp.where(lower_mask(), 1.0, 0.0).astype(BF16)
    out = []
    for start in range(0, values.shape[0], SPAN):
        total = None
        for term in pieces(values[start : start + SPAN], 3):
            part = mm(lower, term)
            total = part if total is None else total + part
        out.append(total)
    return jnp.concatenate(out, axis=0)


def span_sums_rows(values):
    upper = jnp.where(row_ids((SPAN, SPAN)) <= lane_ids((SPAN, SPAN)), 1.0, 0.0).astype(BF16)
    out = []
    for start in range(0, values.shape[1], SPAN):
        total = None
        for term in pieces(values[:, start : start + SPAN], 3):
            part = mm(term, upper)
            total = part if total is None else total + part
        out.append(total)
    return jnp.concatenate(out, axis=1)


def span_sums_back(values):
    upper = jnp.where(row_ids((SPAN, SPAN)) <= lane_ids((SPAN, SPAN)), 1.0, 0.0).astype(BF16)
    out = []
    for start in range(0, values.shape[0], SPAN):
        total = None
        for term in pieces(values[start : start + SPAN], 3):
            part = mm(upper, term)
            total = part if total is None else total + part
        out.append(total)
    return jnp.concatenate(out, axis=0)


def steps_of(tp, tp_row, bias, bias_col, rate, rate_col, length):
    seq_len = tp.shape[0]
    valid = jnp.where(row_ids((seq_len, 1)) < length, 1.0, 0.0)
    valid_row = jnp.where(lane_ids((1, seq_len)) < length, 1.0, 0.0)
    dt = softplus(tp + bias) * valid
    dt_row = softplus(tp_row + bias_col) * valid_row
    cum = span_sums(-(dt * rate))
    cum_row = span_sums_rows(-(dt_row * rate_col))
    return valid, dt, cum, cum_row


def spread(values, head):
    return jnp.broadcast_to(values[:, head : head + 1], (values.shape[0], LANES))


def decays(cum_first, cum_second, cum_row, pair, span):
    rows = slice(span * SPAN, (span + 1) * SPAN)
    lower = lower_mask()
    out = []
    for head, column in ((2 * pair, cum_first), (2 * pair + 1, cum_second)):
        differ = column[rows] - cum_row[head : head + 1, rows]
        out.append(jnp.exp(jnp.where(lower, differ, -1e30)))
    return out


def split_heads(values):
    first = lane_ids(values.shape) < HEAD_DIM
    zero = jnp.zeros_like(values)
    return jnp.concatenate([jnp.where(first, values, zero), jnp.where(first, zero, values)], axis=0)


def state_of(in_map, weighted_first, cum_pair_first):
    to_end = jnp.exp(cum_pair_first[SPAN - 1 : SPAN] - cum_pair_first)
    ending = (weighted_first * to_end).astype(BF16)
    return to_end, ending, mm_tn(in_map[:SPAN], ending)


def mixer_forward_kernel(
    len_ref, h_ref, wq_ref, wkv_ref, wz_ref, wx_ref, wb_ref, wc_ref, wt_ref, cxw_ref, cxb_ref,
    cbw_ref, cbb_ref, bias_ref, rate_ref, bias_col_ref, rate_col_ref, skip_ref, cos_ref, sa_ref,
    sb_ref, q_ref, kd_ref, vd_ref, z_ref, x_ref, bcp_ref, bc_ref, tp_ref, tpr_ref, y_ref, ss_ref,
):
    h = h_ref[...]
    pairs = wx_ref.shape[1] // LANES
    z_ref[...] = mm(h, wz_ref[...])
    x_ref[...] = mm(h, wx_ref[...])
    bcp_ref[:, :STATE] = mm(h, wb_ref[...])
    bcp_ref[:, STATE:] = mm(h, wc_ref[...])
    tp = mm_nt(h, wt_ref[...])
    tp_row = mm_nt(wt_ref[...], h)
    tp_ref[...] = tp
    tpr_ref[...] = tp_row
    cosine, sine_first, sine_second = cos_ref[...], sa_ref[...], sb_ref[...]
    for pair in range(wq_ref.shape[1] // LANES):
        lanes = slice(pair * LANES, (pair + 1) * LANES)
        q_ref[:, lanes] = rope(mm(h, wq_ref[:, lanes]), cosine, sine_first, sine_second).astype(BF16)
    kv = mm(h, wkv_ref[...])
    turned = pltpu.roll(kv, HEAD_DIM, 1)
    first = lane_ids(kv.shape) < HEAD_DIM
    kd_ref[...] = rope(jnp.where(first, kv, turned), cosine, sine_first, sine_second).astype(BF16)
    vd_ref[...] = jnp.where(first, turned, kv).astype(BF16)

    mapped = conv(bcp_ref[...], cbw_ref[...], cbb_ref[...])
    bc = (mapped * sigmoid(mapped)).astype(BF16)
    bc_ref[...] = bc
    in_map, out_map = bc[:, :STATE], bc[:, STATE:]
    affinity = [
        mm_nt(out_map[s * SPAN : (s + 1) * SPAN], in_map[s * SPAN : (s + 1) * SPAN]) for s in range(2)
    ]
    _, dt, cum, cum_row = steps_of(
        tp, tp_row, bias_ref[...], bias_col_ref[...], rate_ref[...], rate_col_ref[...], len_ref[0]
    )
    squares = None
    for pair in range(pairs):
        lanes = slice(pair * LANES, (pair + 1) * LANES)
        cx = conv(x_ref[:, lanes], cxw_ref[:, lanes], cxb_ref[:, lanes])
        xc = cx * sigmoid(cx)
        dt_pair = jnp.where(first, spread(dt, 2 * pair), spread(dt, 2 * pair + 1))
        cum_first, cum_second = spread(cum, 2 * pair), spread(cum, 2 * pair + 1)
        cum_pair = jnp.where(first, cum_first, cum_second)
        weighted = xc * dt_pair
        low = weighted.astype(BF16)
        _, _, state = state_of(in_map, weighted[:SPAN], cum_pair[:SPAN])
        parts = []
        for s in range(2):
            rows = slice(s * SPAN, (s + 1) * SPAN)
            mats = [
                (affinity[s] * decay).astype(BF16)
                for decay in decays(cum_first, cum_second, cum_row, pair, s)
            ]
            part = mm(jnp.concatenate(mats, axis=1), split_heads(low[rows]))
            if s:
                part = part + mm(out_map[rows], state.astype(BF16)) * jnp.exp(cum_pair[rows])
            parts.append(part)
        y = jnp.concatenate(parts, axis=0)
        y_ref[:, lanes] = y
        z = z_ref[:, lanes]
        gated = (y + skip_ref[:, lanes] * xc) * (z * sigmoid(z))
        square = gated * gated
        squares = square if squares is None else squares + square
    ss_ref[...] = row_sums(squares)


def masked_probs(queries, kd, length, scale):
    seq_len = kd.shape[0]
    scores = mm_nt(split_heads(queries), kd) * scale
    rows = row_ids(scores.shape)
    rows = jnp.where(rows >= seq_len, rows - seq_len, rows)
    padding = jnp.where(lane_ids((1, seq_len)) < length, 0.0, -1e30)
    scores = jnp.where(rows >= lane_ids(scores.shape), scores + padding, -1e30)
    weights = jnp.exp(scores - jnp.max(scores, axis=1, keepdims=True))
    return weights / jnp.sum(weights, axis=1, keepdims=True)


def attend_kernel(len_ref, q_ref, kd_ref, vd_ref, out_ref):
    seq_len = q_ref.shape[0]
    values = split_heads(vd_ref[...])
    for pair in range(q_ref.shape[1] // LANES):
        lanes = slice(pair * LANES, (pair + 1) * LANES)
        probs = masked_probs(q_ref[:, lanes], kd_ref[...], len_ref[0], HEAD_DIM ** (-0.5)).astype(BF16)
        both = jnp.concatenate([probs[:seq_len], probs[seq_len:]], axis=1)
        out_ref[:, lanes] = mm(both, values).astype(BF16)


def join_halves(values):
    return values + pltpu.roll(values, HEAD_DIM, 1)


def attend_back_kernel(len_ref, q_ref, kd_ref, vd_ref, da_ref, cos_ref, sa_ref, sb_ref, dq_ref, dkv_ref):
    seq_len = q_ref.shape[0]
    scale = HEAD_DIM ** (-0.5)
    cosine, sine_first, sine_second = cos_ref[...], -sa_ref[...], -sb_ref[...]
    kd, vd = kd_ref[...], vd_ref[...]
    keys = split_heads(kd)
    grad_k, grad_v = None, None
    for pair in range(q_ref.shape[1] // LANES):
        lanes = slice(pair * LANES, (pair + 1) * LANES)
        probs = masked_probs(q_ref[:, lanes], kd, len_ref[0], scale)
        da = split_heads(da_ref[:, lanes])
        dprob = mm_nt(da, vd)
        dscore = (probs * (dprob - jnp.sum(probs * dprob, axis=1, keepdims=True))).astype(BF16)
        both = jnp.concatenate([dscore[:seq_len], dscore[seq_len:]], axis=1)
        dq = mm(both, keys) * scale
        dq_ref[:, lanes] = rope(dq, cosine, sine_first, sine_second).astype(BF16)
        part_k = mm_tn(dscore, split_heads(q_ref[:, lanes]))
        part_v = mm_tn(probs.astype(BF16), da)
        grad_k = part_k if grad_k is None else grad_k + part_k
        grad_v = part_v if grad_v is None else grad_v + part_v
    dk = rope(join_halves(grad_k) * scale, cosine, sine_first, sine_second)
    first = lane_ids(dk.shape) < HEAD_DIM
    dkv_ref[...] = jnp.where(first, dk, join_halves(grad_v)).astype(BF16)


def out_kernel(att_ref, y_ref, x_ref, z_ref, ss_ref, cxw_ref, cxb_ref, skip_ref, gain_ref, wa_ref, ws_ref,
               part_ref, mix_ref, *, width):
    total = mm(att_ref[...], wa_ref[...])
    inv = column_of(lax.rsqrt(ss_ref[...] / width + EPSILON))
    for pair in range(y_ref.shape[1] // LANES):
        lanes = slice(pair * LANES, (pair + 1) * LANES)
        cx = conv(x_ref[:, lanes], cxw_ref[:, lanes], cxb_ref[:, lanes])
        z = z_ref[:, lanes]
        gated = (y_ref[:, lanes] + skip_ref[:, lanes] * (cx * sigmoid(cx))) * (z * sigmoid(z))
        mix_ref[:, lanes] = (gated * inv * gain_ref[:, lanes]).astype(BF16)
    part_ref[...] = (total + mm(mix_ref[...], ws_ref[...])).astype(part_ref.dtype)


def mix_grad_kernel(db_ref, y_ref, x_ref, z_ref, cxw_ref, cxb_ref, skip_ref, gain_ref, wa_ref, ws_ref,
                    da_ref, dm_ref, bs_ref):
    db = db_ref[...]
    da_ref[...] = mm_nt(db, wa_ref[...]).astype(BF16)
    dm_ref[...] = mm_nt(db, ws_ref[...]).astype(BF16)
    total = None
    for pair in range(y_ref.shape[1] // LANES):
        lanes = slice(pair * LANES, (pair + 1) * LANES)
        cx = conv(x_ref[:, lanes], cxw_ref[:, lanes], cxb_ref[:, lanes])
        z = z_ref[:, lanes]
        gated = (y_ref[:, lanes] + skip_ref[:, lanes] * (cx * sigmoid(cx))) * (z * sigmoid(z))
        part = gated * (gain_ref[:, lanes] * dm_ref[:, lanes].astype(F32))
        total = part if total is None else total + part
    bs_ref[...] = row_sums(total)


def head_sums(values, pair):
    rows, columns = row_ids((LANES, 16)), lane_ids((LANES, 16))
    chosen = jnp.where(columns == 2 * pair + jnp.where(rows < HEAD_DIM, 0, 1), 1.0, 0.0).astype(BF16)
    high, low = pieces(values, 2)
    return mm(jnp.concatenate([high, low], axis=1), jnp.concatenate([chosen, chosen], axis=0))


def mixer_back_kernel(
    len_ref, dm_ref, y_ref, x_ref, z_ref, bcp_ref, bc_ref, tp_ref, tpr_ref, ss_ref, bs_ref, dq_ref,
    dkv_ref, wq_ref, wkv_ref, wz_ref, wx_ref, wb_ref, wc_ref, wt_ref, cxw_ref, cxb_ref, cbw_ref,
    cbb_ref, bias_ref, rate_ref, bias_col_ref, rate_col_ref, skip_ref, gain_ref,
    dh_ref, dx_ref, dz_ref, dbc_ref, dt_ref, wide_ref, bcg_ref, small_ref, *, width, tick=lambda: None,
):
    pairs = x_ref.shape[1] // LANES
    bc = bc_ref[...]
    in_map, out_map = bc[:, :STATE], bc[:, STATE:]
    affinity = [
        mm_nt(out_map[s * SPAN : (s + 1) * SPAN], in_map[s * SPAN : (s + 1) * SPAN]) for s in range(2)
    ]
    valid, dt, cum, cum_row = steps_of(
        tp_ref[...], tpr_ref[...], bias_ref[...], bias_col_ref[...], rate_ref[...], rate_col_ref[...], len_ref[0]
    )
    inv_row = lax.rsqrt(ss_ref[...] / width + EPSILON)
    inv = column_of(inv_row)
    back = column_of(inv_row * inv_row * inv_row * bs_ref[...] / width)
    first = lane_ids((x_ref.shape[0], LANES)) < HEAD_DIM
    last_row = row_ids((SPAN, LANES)) == SPAN - 1
    d_cum, d_step, d_skip = None, None, None
    wide_ref[7:8, :] = jnp.zeros((1, wide_ref.shape[1]), F32)
    d_aff, d_out, d_in = [None, None], None, None

    def plus(total, part):
        return part if total is None else total + part

    for pair in range(pairs):
        lanes = slice(pair * LANES, (pair + 1) * LANES)
        x = x_ref[:, lanes]
        cxw = cxw_ref[:, lanes]
        cx = conv(x, cxw, cxb_ref[:, lanes])
        sx = sigmoid(cx)
        xc = cx * sx
        z = z_ref[:, lanes]
        sz = sigmoid(z)
        silu_z = z * sz
        scanned = y_ref[:, lanes]
        y = scanned + skip_ref[:, lanes] * xc
        gated = y * silu_z
        d_mix = dm_ref[:, lanes].astype(F32)
        d_gated = inv * (gain_ref[:, lanes] * d_mix) - gated * back
        wide_ref[6:7, lanes] = jnp.sum(d_mix * gated * inv, axis=0, keepdims=True)
        dy = d_gated * silu_z
        dz_ref[:, lanes] = (d_gated * y * (sz * (1.0 + z * (1.0 - sz)))).astype(BF16)
        wide_ref[5:6, lanes] = jnp.sum(dy * xc, axis=0, keepdims=True)
        dt_pair = jnp.where(first, spread(dt, 2 * pair), spread(dt, 2 * pair + 1))
        cum_first, cum_second = spread(cum, 2 * pair), spread(cum, 2 * pair + 1)
        cum_pair = jnp.where(first, cum_first, cum_second)
        weighted = xc * dt_pair
        low = weighted.astype(BF16)
        dy_low = dy.astype(BF16)
        to_end, ending, state = state_of(in_map, weighted[:SPAN], cum_pair[:SPAN])
        d_weighted = []
        for s in range(2):
            rows = slice(s * SPAN, (s + 1) * SPAN)
            decay = decays(cum_first, cum_second, cum_row, pair, s)
            mats = jnp.concatenate([(affinity[s] * one).astype(BF16) for one in decay], axis=0)
            both = split_heads(dy_low[rows])
            d_mats = mm_nt(both, low[rows])
            d_aff[s] = plus(d_aff[s], d_mats[:SPAN] * decay[0] + d_mats[SPAN:] * decay[1])
            d_weighted.append(mm_tn(mats, both))
        reached = (dy[SPAN:] * jnp.exp(cum_pair[SPAN:])).astype(BF16)
        d_out = plus(d_out, mm_nt(reached, state.astype(BF16)))
        d_state = mm_tn(out_map[SPAN:], reached).astype(BF16)
        d_in = plus(d_in, mm_nt(ending, d_state))
        d_ending = mm(in_map[:SPAN], d_state)
        through = ending.astype(F32) * d_ending
        low_f, dy_f = low.astype(F32), dy_low.astype(F32)
        change = dy_f * scanned - low_f * jnp.concatenate(d_weighted, axis=0)
        ended = jnp.where(last_row, jnp.sum(through, axis=0, keepdims=True), 0.0) - through
        change = jnp.concatenate([change[:SPAN] + ended, change[SPAN:]], axis=0)
        d_weight = jnp.concatenate([d_weighted[0] + d_ending * to_end, d_weighted[1]], axis=0)
        d_cum = plus(d_cum, head_sums(change, pair))
        d_step = plus(d_step, head_sums(d_weight * xc, pair))
        d_xc = dy * skip_ref[:, lanes] + d_weight * dt_pair
        d_cx = d_xc * (sx * (1.0 + cx * (1.0 - sx)))
        d_x, rows_x = conv_back(d_cx, x, cxw)
        dx_ref[:, lanes] = d_x.astype(BF16)
        for index, row in enumerate(rows_x):
            wide_ref[index : index + 1, lanes] = row
        d_skip = plus(d_skip, head_sums(wide_ref[:, lanes], pair))
        tick()

    rate = rate_ref[...]
    d_log = span_sums_back(d_cum)
    d_dt = d_step - rate * d_log
    d_tp = d_dt * valid * sigmoid(tp_ref[...] + bias_ref[...])
    small_ref[...] = jnp.zeros(small_ref.shape, F32)
    small_ref[0:1, :] = jnp.sum(d_tp, axis=0, keepdims=True)
    small_ref[1:2, :] = -rate * jnp.sum(dt * d_log, axis=0, keepdims=True)
    small_ref[2:3, :] = d_skip[5:6]
    dt_ref[...] = d_tp.astype(BF16)

    d_maps = []
    low_aff = [part.astype(BF16) for part in d_aff]
    d_ins, d_outs = [], []
    for s in range(2):
        rows = slice(s * SPAN, (s + 1) * SPAN)
        d_outs.append(mm(low_aff[s], in_map[rows]))
        d_ins.append(mm_tn(low_aff[s], out_map[rows]))
    d_outs[1] = d_outs[1] + d_out
    d_ins[0] = d_ins[0] + d_in
    d_maps = jnp.concatenate(
        [jnp.concatenate(d_ins, axis=0), jnp.concatenate(d_outs, axis=0)], axis=1
    )
    mapped = conv(bcp_ref[...], cbw_ref[...], cbb_ref[...])
    sm = sigmoid(mapped)
    d_bc, rows_bc = conv_back(d_maps * (sm * (1.0 + mapped * (1.0 - sm))), bcp_ref[...], cbw_ref[...])
    bcg_ref[...] = jnp.zeros(bcg_ref.shape, F32)
    for index, row in enumerate(rows_bc):
        bcg_ref[index : index + 1, :] = row
    d_bc = d_bc.astype(BF16)
    dbc_ref[...] = d_bc
    total = mm_nt(dx_ref[...], wx_ref[...]) + mm_nt(dz_ref[...], wz_ref[...])
    total = total + mm_nt(dq_ref[...], wq_ref[...]) + mm_nt(dkv_ref[...], wkv_ref[...])
    total = total + mm_nt(d_bc[:, :STATE], wb_ref[...]) + mm_nt(d_bc[:, STATE:], wc_ref[...])
    total = total + mm(dt_ref[...], wt_ref[...])
    dh_ref[...] = total.astype(dh_ref.dtype)


def ffn_kernel(h_ref, ct_ref, wg_ref, wu_ref, wd_ref, *refs):
    base_ref = refs[0] if len(refs) == 9 else None
    hid_ref, dg_ref, du_ref, ff_ref, dh_ref, ht_ref, ff_acc, dh_acc = refs[-8:]
    step = pl.program_id(0)
    h = h_ref[...]
    gate = mm(h, wg_ref[...])
    up = mm(h, wu_ref[...])
    d_hidden = mm_nt(ct_ref[...], wd_ref[...]).astype(BF16).astype(F32)
    sg = sigmoid(gate)
    silu = gate * sg
    hidden = silu * up
    hid_ref[...] = hidden.T.astype(BF16)
    hidden = hidden.astype(BF16)
    d_gate = (d_hidden * up * (sg * (1.0 + gate * (1.0 - sg)))).astype(BF16)
    d_up = (d_hidden * silu).astype(BF16)
    dg_ref[...] = d_gate
    du_ref[...] = d_up
    ff_part = mm(hidden, wd_ref[...])
    dh_part = mm_nt(d_gate, wg_ref[...]) + mm_nt(d_up, wu_ref[...])

    @pl.when(step == 0)
    def _():
        ht_ref[...] = h.astype(F32).T.astype(BF16)
        ff_acc[...] = ff_part if base_ref is None else ff_part + base_ref[...]
        dh_acc[...] = dh_part

    @pl.when(step > 0)
    def _():
        ff_acc[...] += ff_part
        dh_acc[...] += dh_part

    @pl.when(step == pl.num_programs(0) - 1)
    def _():
        ff_ref[...] = ff_acc[...].astype(ff_ref.dtype)
        dh_ref[...] = dh_acc[...].astype(dh_ref.dtype)


class Entry:
    def __init__(self, ref):
        self.ref = ref

    def __getitem__(self, index):
        return self.ref[0:1, 0:1]


PARTS = 8
GATE, UP, DOWN, SHARED, QUERY, ZED, EX, OUT = range(PARTS)
KV_AT, B_AT, C_AT, MISC_AT = 0, LANES, 2 * LANES, 3 * LANES
SHARED_WIDTH = 4 * LANES


def chunk_order(widths):
    wide = 2 * LANES
    order = [(part, column, wide) for part in (GATE, UP, DOWN, OUT, QUERY) for column in range(0, widths[part], wide)]
    order += [(SHARED, column, LANES) for column in (KV_AT, B_AT, C_AT)]
    order += [(EX, column, wide) for column in range(0, widths[EX], wide)]
    order += [(SHARED, MISC_AT, LANES)]
    order += [(ZED, column, wide) for column in range(0, widths[ZED] - wide, wide)]
    order += [(ZED, column, LANES) for column in range(widths[ZED] - wide, widths[ZED], LANES)]
    return [item + ("P" if item[0] == SHARED or index % 2 else "Q",) for index, item in enumerate(order)]


SLOTS = 6


def unit_matrix(size):
    return jnp.where(row_ids((size, size)) == lane_ids((size, size)), 1.0, 0.0)


def turned_small(values):
    unit = unit_matrix(16).astype(BF16)
    total = None
    for term in pieces(values, 3):
        part = mm_nt(unit, term)
        total = part if total is None else total + part
    return total


def back_kernel(*refs, small_names, big_names, widths, width, lag, pace):
    it = iter(refs)
    s = {name: next(it) for name in small_names}
    lens = [Entry(s["len0"]), Entry(s["len1"])]
    big_in = {name: next(it) for name in big_names}
    dh2_peer, ff_peer = next(it), next(it)
    outs = [next(it) for _ in range(PARTS)]
    xout, grad_in, layer_out = next(it), next(it), next(it)
    b = {name: next(it) for name in big_names}
    (db, bs, bsr, da, dm, dq, dkv, dx, dz, dbc, dt, dh_own, dh_peer, dh_got, ff_got, wide, bcg, small, misc,
     acc, rc, res, ry, zin_p, zin_q, zmid, in_sem, out_sem, xs, xr, send_sem, recv_sem) = it
    rows = outs[GATE].shape[0]
    half, quarter = rows // 2, rows // 4
    seq_len = db.shape[0] // 2
    me = lax.axis_index("dp")
    core, y, z = me % 2, (me // 2) % 2, me // 4
    side = lax.axis_index("tensor")
    sibling = {"dp": me + 1 - 2 * core}
    across = {"dp": me + 2 - 4 * y}
    outer = {"dp": (z + 1 - 2 * (z % 2)) * 4 + y * 2 + core}
    inner = {"dp": (3 - z) * 4 + y * 2 + core}
    pair = {"tensor": 1 - side}
    is_mid = (z == 1) | (z == 2)
    is_end = (z == 0) | (z == 3)

    def at(offset, size):
        return pl.ds(pl.multiple_of(offset, quarter), size)

    mine, other = at(core * half, half), at((1 - core) * half, half)
    my_y, other_y = at(y * quarter, quarter), at((1 - y) * quarter, quarter)
    zq = jnp.where(z <= 1, 0, 1)
    my_z, other_z = at(zq * quarter, quarter), at((1 - zq) * quarter, quarter)

    loads = {}
    for index, name in enumerate(big_names):
        loads[name] = pltpu.make_async_copy(big_in[name], b[name], in_sem.at[index])
        loads[name].start()
    ready = set()

    def need(*names):
        for name in names:
            if name not in ready:
                loads[name].wait()
                ready.add(name)

    barrier = pltpu.get_barrier_semaphore()
    for device in (sibling, across, outer, pair):
        pl.semaphore_signal(barrier, inc=1, device_id=device, device_id_type=MESH)

    @pl.when(is_mid)
    def _():
        pl.semaphore_signal(barrier, inc=1, device_id=inner, device_id_type=MESH)
        pl.semaphore_wait(barrier, 5)

    @pl.when(is_end)
    def _():
        pl.semaphore_wait(barrier, 4)

    ends = []

    def remote(src, dst, send, recv, device):
        return pltpu.make_async_remote_copy(
            src_ref=src, dst_ref=dst, send_sem=send, recv_sem=recv, device_id=device, device_id_type=MESH
        )

    def exchange(src, dst, slot):
        copy = remote(src, dst, xs.at[slot], xr.at[slot], pair)
        copy.start()
        return copy

    def make(part, column, size, span):
        lanes = slice(column, column + size)
        if part == SHARED and column == MISC_AT:
            return misc[span, :].astype(F32)
        total = None
        for k in range(2):
            left, right = {
                GATE: ("h2t", "dg"), UP: ("h2t", "du"), DOWN: ("hid", "ct"), OUT: ("mix", db), SHARED: ("ht", dbc),
                QUERY: ("ht", dq), ZED: ("ht", dz), EX: ("ht", dx),
            }[part]
            need(f"{left}{k}")
            values = b[f"{left}{k}"][span, :]
            if isinstance(right, str):
                need(f"{right}{k}")
                right = b[f"{right}{k}"][:, lanes]
            elif part == SHARED:
                right = dkv[seq(k), :] if column == KV_AT else dbc[seq(k), column - LANES : column]
            else:
                right = right[seq(k), lanes]
            part_k = mm(values, right)
            total = part_k if total is None else total + part_k
        return total

    def add(dst, first, second):
        dst[...] = (first[...].astype(F32) + second[...].astype(F32)).astype(BF16)

    order = chunk_order(widths)
    starts = [sum(item[2] for item in order[:index]) for index in range(len(order))]
    made = set()
    sending = {}

    def chunk_steps(index):
        part, column, size, kind = order[index]
        start = starts[index]
        place = sum(item[2] for item in order[:index] if item[3] == kind)
        cols = slice(start, start + size)
        local = slice(column, column + size)
        tight = slice(place, place + size)
        out = outs[part]

        def own(src, dst, slot, device):
            return remote(src, dst, send_sem.at[slot, index], recv_sem.at[slot, index], device)

        source = acc.at[index % SLOTS, :, :size]
        to_core = own(source, rc.at[:, cols], 0, sibling)
        back_core = own(res.at[:, cols], out.at[mine, local], 6, sibling)
        wait_core = own(res.at[:, cols], out.at[other, local], 6, sibling)
        store = pltpu.make_async_copy(res.at[:, cols], out.at[mine, local], out_sem.at[index])

        def step0():
            assert part < SHARED or (part, column) in made
            if index - SLOTS in sending:
                sending.pop(index - SLOTS)()
            source[...] = make(part, column, size, other).astype(BF16)
            to_core.start()
            sending[index] = to_core.wait_send

        def merge_core():
            term = make(part, column, size, mine)
            to_core.wait_recv()
            rc[:, cols] = (rc[:, cols].astype(F32) + term).astype(BF16)

        def send_core():
            back_core.start()
            store.start()

        def last():
            wait_core.wait_recv()

        ends.append((None, back_core.wait_send))
        ends.append((None, store.wait))

        if kind == "P":
            zin = zin_p.at[:, tight]
            to_y = own(rc.at[other_y, cols], ry.at[:, cols], 1, across)
            to_mid = own(rc.at[my_y, cols], zin, 2, outer)
            swap = own(rc.at[my_y, cols], zmid.at[:, cols], 3, inner)
            to_end = own(res.at[my_y, cols], res.at[my_y, cols], 4, outer)
            back_y = own(res.at[my_y, cols], res.at[my_y, cols], 5, across)
            wait_y = own(res.at[my_y, cols], res.at[other_y, cols], 5, across)

            def step1():
                merge_core()
                to_y.start()
                ends.append((None, to_y.wait_send))

            def step2():
                to_y.wait_recv()
                add(rc.at[my_y, cols], rc.at[my_y, cols], ry.at[:, cols])
                pl.when(is_end)(to_mid.start)
                ends.append((is_end, to_mid.wait_send))

            def step3():
                @pl.when(is_mid)
                def _():
                    to_mid.wait_recv()
                    add(rc.at[my_y, cols], rc.at[my_y, cols], zin)
                    swap.start()

                ends.append((is_mid, swap.wait_send))

            def step4():
                @pl.when(is_mid)
                def _():
                    swap.wait_recv()
                    add(res.at[my_y, cols], rc.at[my_y, cols], zmid.at[:, cols])
                    to_end.start()
                    back_y.start()

                ends.append((is_mid, to_end.wait_send))

            def step5():
                @pl.when(is_end)
                def _():
                    to_end.wait_recv()
                    back_y.start()

                ends.append((None, back_y.wait_send))

            def step6():
                wait_y.wait_recv()
                send_core()

            steps = [step0, step1, step2, step3, step4, step5, step6, last]
            if part == SHARED:
                to_x = own(res.at[:, cols], xout.at[mine, local], 7, pair)
                x_core = own(xout.at[mine, local], xout.at[mine, local], 8, sibling)
                wait_x = own(xout.at[mine, local], xout.at[other, local], 8, sibling)

                def step6x():
                    step6()
                    to_x.start()
                    ends.append((None, to_x.wait_send))

                def step7x():
                    last()
                    to_x.wait_recv()
                    x_core.start()
                    ends.append((None, x_core.wait_send))

                steps[6:] = [step6x, step7x, wait_x.wait_recv]
            return steps

        zin = zin_q.at[:, tight]
        to_mid = own(rc.at[:, cols], zin, 1, outer)
        swap = own(rc.at[other_z, cols], zmid.at[:, cols], 2, inner)
        to_y = own(rc.at[my_z, cols], ry.at[:, cols], 3, across)
        to_inner = own(res.at[my_z, cols], res.at[my_z, cols], 4, inner)
        wait_inner = own(res.at[my_z, cols], res.at[other_z, cols], 4, inner)
        to_end = own(res.at[my_z, cols], res.at[my_z, cols], 5, outer)
        pass_end = own(res.at[other_z, cols], res.at[other_z, cols], 7, outer)

        def step1():
            merge_core()
            pl.when(is_end)(to_mid.start)
            ends.append((is_end, to_mid.wait_send))

        def step2():
            @pl.when(is_mid)
            def _():
                to_mid.wait_recv()
                add(rc.at[:, cols], rc.at[:, cols], zin)
                swap.start()

            ends.append((is_mid, swap.wait_send))

        def step3():
            @pl.when(is_mid)
            def _():
                swap.wait_recv()
                add(rc.at[my_z, cols], rc.at[my_z, cols], zmid.at[:, cols])
                to_y.start()

            ends.append((is_mid, to_y.wait_send))

        def step4():
            @pl.when(is_mid)
            def _():
                to_y.wait_recv()
                add(res.at[my_z, cols], rc.at[my_z, cols], ry.at[:, cols])
                to_inner.start()
                to_end.start()

            ends.append((is_mid, to_inner.wait_send))
            ends.append((is_mid, to_end.wait_send))

        def step5():
            @pl.when(is_mid)
            def _():
                wait_inner.wait_recv()
                pass_end.start()
                send_core()

            ends.append((is_mid, pass_end.wait_send))

        def step6():
            @pl.when(is_end)
            def _():
                to_end.wait_recv()
                pass_end.wait_recv()
                send_core()

        return [step0, step1, step2, step3, step4, step5, step6, last]

    plan = [
        (index + 2 * lag * number, -number, index, step)
        for index in range(len(order))
        for number, step in enumerate(chunk_steps(index))
    ]
    plan.sort(key=lambda item: item[:3])
    clock, done = [0.0], [0]

    def tick(time=pace):
        clock[0] += time
        while done[0] < len(plan) and plan[done[0]][0] <= clock[0]:
            plan[done[0]][3]()
            done[0] += 1

    def seq(k):
        return pl.ds(k * seq_len, seq_len)

    got_second_norm = exchange(dh2_peer, dh_got, 4)
    tick(0.0)
    tick()
    tick()
    tick()
    need("dh2", "rhat", "ct0")
    got_second_norm.wait()
    model = grad_in.shape[1]
    d_second = b["dh2"][...] + dh_got[...].astype(F32)
    scaled = d_second * s["gain2"][...]
    rhat = b["rhat"][...]
    mean = jnp.sum(scaled * rhat, axis=1, keepdims=True) / model
    d_resid = b["ct0"][...].astype(F32) + s["inv2"][...] * (scaled - rhat * mean)
    grad_in[...] = d_resid
    db[:seq_len, :] = d_resid.astype(BF16)
    norm_second = jnp.sum(d_second * rhat, axis=0, keepdims=True)
    got_db = exchange(db.at[:seq_len], db.at[seq_len:], 0)
    tick()

    def mix(k):
        need("wa", "ws", f"y{k}", f"x{k}", f"z{k}")
        mix_grad_kernel(
            db.at[seq(k)], b[f"y{k}"], b[f"x{k}"], b[f"z{k}"], s["cxw"], s["cxb"], s["skip"], s["gain"], b["wa"],
            b["ws"], da.at[k], dm.at[k], bs.at[k],
        )
        return exchange(bs.at[k], bsr.at[1 - k], 1 + k)

    def attend(k):
        need(f"q{k}", f"kd{k}", f"vd{k}")
        attend_back_kernel(
            lens[k], b[f"q{k}"], b[f"kd{k}"], b[f"vd{k}"], da.at[k], s["cos"], s["sa"], s["sb"], dq.at[seq(k)],
            dkv.at[seq(k)],
        )

    def mixer(k, dh):
        need("wq", "wkv", "wz", "wx", "wb", "wc", f"bcp{k}", f"bc{k}")
        bs[k] = bs[k] + bsr[k]
        mixer_back_kernel(
            lens[k], dm.at[k], b[f"y{k}"], b[f"x{k}"], b[f"z{k}"], b[f"bcp{k}"], b[f"bc{k}"], s[f"tp{k}"],
            s[f"tpr{k}"], s[f"ss{k}"], bs.at[k], dq.at[seq(k)], dkv.at[seq(k)], b["wq"], b["wkv"], b["wz"],
            b["wx"], b["wb"], b["wc"], s["wt"], s["cxw"], s["cxb"], s["cbw"], s["cbb"], s["bias"], s["rate"],
            s["bias_col"], s["rate_col"], s["skip"], s["gain"], dh, dx.at[seq(k)], dz.at[seq(k)],
            dbc.at[seq(k)], dt.at[k], wide.at[k], bcg.at[k], small.at[k], width=width, tick=tick,
        )
        tick()

    got_first = mix(0)
    tick()
    attend(0)
    tick()
    got_db.wait_recv()
    got_second = mix(1)
    tick()
    attend(1)
    tick()
    for part in (OUT, QUERY):
        made.update([(part, column) for column in range(0, widths[part], LANES)])
    made.add((SHARED, KV_AT))
    got_first.wait_recv()
    got_second.wait_recv()
    got_first.wait_send()
    got_second.wait_send()
    mixer(1, dh_peer)
    got_dh = exchange(dh_peer, dh_got, 3)
    got_ff = exchange(ff_peer, ff_got, 5)
    mixer(0, dh_own)
    for part in (ZED, EX):
        made.update([(part, column) for column in range(0, widths[part], LANES)])
    made.update([(SHARED, B_AT), (SHARED, C_AT)])
    misc_key = [item[:2] for item in order].index((SHARED, MISC_AT))
    tick(max(0.0, misc_key - 4 - clock[0]))
    got_dh.wait()
    d_first = dh_own[...] + dh_got[...].astype(F32)
    need("xhat")
    xhat = b["xhat"][...]
    scaled = d_first * s["gain1"][...]
    mean = jnp.sum(scaled * xhat, axis=1, keepdims=True) / model
    grad_in[...] += s["inv1"][...] * (scaled - xhat * mean)
    norm = jnp.sum(d_first * xhat, axis=0, keepdims=True)
    wide_sum, bcg_sum, small_sum = wide[0] + wide[1], bcg[0] + bcg[1], small[0] + small[1]
    first_row = row_ids((8, model)) == 0
    second_row = row_ids((8, model)) == 1
    norms = jnp.where(first_row, norm, jnp.where(second_row, norm_second, 0.0))
    blocks = [array[:, i : i + LANES] for array in (wide_sum, bcg_sum) for i in range(0, array.shape[1], LANES)]
    blocks.append(jnp.concatenate([small_sum, jnp.zeros((8, LANES - 16), F32)], axis=1))
    blocks += [norms[:, i : i + LANES] for i in range(0, model, LANES)]
    if len(blocks) % 2:
        blocks.append(jnp.zeros((8, LANES), F32))
    misc[...] = jnp.zeros(misc.shape, BF16)
    misc[: 8 * len(blocks), :] = jnp.concatenate(blocks, axis=0).astype(BF16)
    need("ht0", "ht1")
    step_grad = turned_small(mm(b["ht0"][...], dt[0]) + mm(b["ht1"][...], dt[1])).astype(BF16)
    for i in range(0, model, LANES):
        place = 8 * len(blocks) + 16 * (i // LANES)
        misc[place : place + 16, :] = step_grad[:, i : i + LANES]
    made.add((SHARED, MISC_AT))
    tick(max(0.0, len(order) + 2 - clock[0]))
    got_ff.wait()
    need("ff")
    layer_out[...] = (b["ff"][...] + ff_got[...].astype(F32)).astype(BF16)
    got_db.wait_send()
    tick(1e6)
    for wait in sending.values():
        wait()
    for devices, wait in ends:
        if devices is None:
            wait()
        else:
            pl.when(devices)(wait)


def back_call(smalls, bigs, dh2_peer, ff_peer, widths, width, lag=0.75, pace=0.8):
    rows, (seq_len, model) = bigs["h2t0"].shape[0], dh2_peer.shape
    order = chunk_order(widths)
    columns = sum(item[2] for item in order)
    ones = sum(item[2] for item in order if item[3] == "P")
    count = len(order)
    half, quarter = rows // 2, rows // 4
    ssm_pad, att_pad = bigs["x0"].shape[1], bigs["q0"].shape[1]
    anywhere, vmem = pl.BlockSpec(memory_space=pl.ANY), pl.BlockSpec(memory_space=pltpu.VMEM)
    outs = [shaped((rows, w), BF16) for w in widths] + [shaped((rows, SHARED_WIDTH), BF16), shaped((seq_len, model))]
    outs.append(shaped((seq_len, model), BF16))
    scratch = [pltpu.VMEM(array.shape, array.dtype) for array in bigs.values()]
    both = 2 * seq_len
    scratch += [
        pltpu.VMEM((both, model), BF16),
        pltpu.VMEM((2, 16, seq_len), F32), pltpu.VMEM((2, 16, seq_len), F32),
        pltpu.VMEM((2, seq_len, att_pad), BF16), pltpu.VMEM((2, seq_len, ssm_pad), BF16),
        pltpu.VMEM((both, att_pad), BF16), pltpu.VMEM((both, LANES), BF16), pltpu.VMEM((both, ssm_pad), BF16),
        pltpu.VMEM((both, ssm_pad), BF16), pltpu.VMEM((both, 2 * STATE), BF16), pltpu.VMEM((2, seq_len, 16), BF16),
        pltpu.VMEM((seq_len, model), F32), pltpu.VMEM((seq_len, model), BF16), pltpu.VMEM((seq_len, model), BF16),
        pltpu.VMEM((seq_len, model), BF16),
        pltpu.VMEM((2, 8, ssm_pad), F32), pltpu.VMEM((2, 8, 2 * STATE), F32), pltpu.VMEM((2, 8, 16), F32),
        pltpu.VMEM((rows, LANES), BF16), pltpu.VMEM((SLOTS, half, 2 * LANES), BF16),
        pltpu.VMEM((half, columns), BF16), pltpu.VMEM((half, columns), BF16),
        pltpu.VMEM((quarter, columns), BF16), pltpu.VMEM((quarter, ones), BF16),
        pltpu.VMEM((half, columns - ones), BF16), pltpu.VMEM((quarter, columns), BF16),
        pltpu.SemaphoreType.DMA((len(bigs),)), pltpu.SemaphoreType.DMA((count,)),
        pltpu.SemaphoreType.DMA((6,)), pltpu.SemaphoreType.DMA((6,)),
        pltpu.SemaphoreType.DMA((9, count)), pltpu.SemaphoreType.DMA((9, count)),
    ]
    return pl.pallas_call(
        functools.partial(
            back_kernel, small_names=tuple(smalls), big_names=tuple(bigs), widths=tuple(widths), width=width,
            lag=lag, pace=pace,
        ),
        out_shape=outs,
        in_specs=[vmem] * len(smalls) + [anywhere] * (len(bigs) + 2),
        out_specs=[anywhere] * (PARTS + 1) + [vmem] * 2,
        scratch_shapes=scratch,
        compiler_params=pltpu.CompilerParams(
            collective_id=0, has_side_effects=True, vmem_limit_bytes=REDUCE_LIMIT
        ),
        name="back_and_reduce",
    )(*smalls.values(), *bigs.values(), dh2_peer, ff_peer)


FORMS = ("wt", "cxb", "cbb", "gain", "skip", "bias", "rate", "bias_col", "rate_col")


def write_forms(raw, forms):
    for name, source in (("cxb", "conv_x_bias"), ("cbb", "conv_bc_bias"), ("gain", "gain")):
        forms[name][...] = raw[source][...].reshape(forms[name].shape)
    heads = raw["bias"].shape[0]
    for name, values in (("bias", raw["bias"][...]), ("rate", jnp.exp(raw["decay"][...].reshape(1, heads)))):
        forms[name][...] = jnp.zeros(forms[name].shape, F32)
        forms[name][:, :heads] = values.reshape(1, heads)
        forms[f"{name}_col"][...] = jnp.sum(unit_matrix(16) * forms[name][...], axis=1, keepdims=True)
    skip = raw["skip"][...].reshape(1, heads)
    first = lane_ids((1, LANES)) < HEAD_DIM
    for pair in range(heads // 2):
        lanes = slice(pair * LANES, (pair + 1) * LANES)
        forms["skip"][:, lanes] = jnp.where(first, skip[:, 2 * pair : 2 * pair + 1], skip[:, 2 * pair + 1 : 2 * pair + 2])
    chosen = jnp.where(row_ids((16, heads)) == lane_ids((16, heads)), 1.0, 0.0).astype(BF16)
    forms["wt"][...] = mm_nt(chosen, raw["step"][...]).astype(BF16)


def turned_low(values):
    return values.astype(F32).T.astype(BF16)


def front_kernel(*refs, small_names, raw_names, big_names, out_names, tiny_names, width):
    it = iter(refs)
    len_ref = next(it)
    s = {name: next(it) for name in small_names}
    raw = {name: next(it) for name in raw_names}
    big_in = {name: next(it) for name in big_names}
    outs = {name: next(it) for name in out_names}
    tiny = {name: next(it) for name in tiny_names}
    b = {name: next(it) for name in big_names}
    o = {name: next(it) for name in out_names}
    (h, h2, att, ssm, hid, ssp, ssr, part_own, part_peer, part_got, in_sem, out_sem, xs, xr) = it
    seq_len, model = part_own.shape
    s.update({name: tiny[name] for name in FORMS})
    side = lax.axis_index("tensor")
    pair = {"tensor": 1 - side}
    loads = {}
    for index, name in enumerate(big_names):
        loads[name] = pltpu.make_async_copy(big_in[name], b[name], in_sem.at[index])
        loads[name].start()
    barrier = pltpu.get_barrier_semaphore()
    pl.semaphore_signal(barrier, inc=1, device_id=pair, device_id_type=MESH)
    pl.semaphore_wait(barrier, 1)
    ready, stores = set(), []

    def need(*names):
        for name in names:
            if name not in ready:
                loads[name].wait()
                ready.add(name)

    def emit(*names):
        for name in names:
            store = pltpu.make_async_copy(o[name], outs[name], out_sem.at[out_names.index(name)])
            store.start()
            stores.append(store)

    def exchange(src, dst, slot):
        copy = pltpu.make_async_remote_copy(
            src_ref=src, dst_ref=dst, send_sem=xs.at[slot], recv_sem=xr.at[slot], device_id=pair,
            device_id_type=MESH,
        )
        copy.start()
        return copy

    tiny["len0"][...] = jnp.full((8, LANES), len_ref[0], jnp.int32)
    need("tok")
    x = b["tok"][...].astype(F32)
    inv1 = lax.rsqrt(jnp.mean(x * x, axis=1, keepdims=True) + EPSILON)
    tiny["inv1"][...] = inv1
    xhat = x * inv1
    o["xhat"][...] = xhat
    h[0] = (xhat * s["gain1"][...]).astype(BF16)
    got_h = exchange(h.at[0], h.at[1], 0)
    got_len = exchange(tiny["len0"], tiny["len1"], 1)
    emit("xhat")
    need("cot")
    cot = b["cot"][...]
    o["ct0"][...] = jnp.where(row_ids((seq_len, 1)) < len_ref[0], cot.astype(F32), 0.0).astype(BF16)
    emit("ct0")
    write_forms(raw, tiny)
    need("w_key", "w_value")
    key, value = b["w_key"][...].astype(F32), b["w_value"][...].astype(F32)
    key = jnp.where(side == 0, key, pltpu.roll(key, HEAD_DIM, 1))
    value = jnp.where(side == 0, pltpu.roll(value, HEAD_DIM, 1), value)
    o["wkv"][...] = jnp.where(lane_ids(key.shape) < HEAD_DIM, key, value).astype(BF16)
    emit("wkv")

    def mixer(k):
        need("wz", "wx", "wb", "wc", "wq")
        mixer_forward_kernel(
            Entry(tiny[f"len{k}"]), h.at[k], b["wq"], o["wkv"], b["wz"], b["wx"], b["wb"], b["wc"], s["wt"], s["cxw"],
            s["cxb"], s["cbw"], s["cbb"], s["bias"], s["rate"], s["bias_col"], s["rate_col"], s["skip"], s["cos"],
            s["sa"], s["sb"], o[f"q{k}"], o[f"kd{k}"], o[f"vd{k}"], o[f"z{k}"], o[f"x{k}"], o[f"bcp{k}"], o[f"bc{k}"],
            tiny[f"tp{k}"], tiny[f"tpr{k}"], o[f"y{k}"], ssp.at[k],
        )
        emit(f"q{k}", f"kd{k}", f"vd{k}", f"z{k}", f"x{k}", f"bcp{k}", f"bc{k}", f"y{k}")
        return exchange(ssp.at[k], ssr.at[1 - k], 2 + k)

    def attend(k):
        attend_kernel(Entry(tiny[f"len{k}"]), o[f"q{k}"], o[f"kd{k}"], o[f"vd{k}"], att.at[k])

    def project(k, part):
        need("wa", "ws")
        out_kernel(
            att.at[k], o[f"y{k}"], o[f"x{k}"], o[f"z{k}"], tiny[f"ss{k}"], s["cxw"], s["cxb"], s["skip"], s["gain"],
            b["wa"], b["ws"], part, ssm.at[k], width=width,
        )

    def turn_mix(k):
        width_att = att.shape[2]
        o[f"mix{k}"][:width_att, :] = turned_low(att[k])
        o[f"mix{k}"][width_att:, :] = turned_low(ssm[k])
        emit(f"mix{k}")

    def feed(k, base):
        need("wg", "wu", "wd")
        rows, ct = h2[k], o[f"ct{k}"][...]
        total = hid.shape[1]
        for first in range(0, total, 256):
            lanes = slice(first, min(first + 256, total))
            gate, up = mm(rows, b["wg"][:, lanes]), mm(rows, b["wu"][:, lanes])
            d_hidden = mm_nt(ct, b["wd"][lanes, :]).astype(BF16).astype(F32)
            sg = sigmoid(gate)
            silu = gate * sg
            hidden = silu * up
            hid[:, lanes] = hidden.astype(BF16)
            o[f"hid{k}"][lanes, :] = hidden.T.astype(BF16)
            o[f"dg{k}"][:, lanes] = (d_hidden * up * (sg * (1.0 + gate * (1.0 - sg)))).astype(BF16)
            o[f"du{k}"][:, lanes] = (d_hidden * silu).astype(BF16)
        emit(f"dg{k}", f"du{k}", f"hid{k}")
        dh, ff = o["dh2" if k == 0 else "dh2p"], o["ff" if k == 0 else "ffp"]
        dh[...] = (mm_nt(o[f"dg{k}"][...], b["wg"][...]) + mm_nt(o[f"du{k}"][...], b["wu"][...])).astype(dh.dtype)
        ff_part = mm(hid[...], b["wd"][...])
        ff[...] = (ff_part if base is None else ff_part + base).astype(ff.dtype)
        emit(*(("dh2", "ff") if k == 0 else ("dh2p", "ffp")))

    got_first = mixer(0)
    attend(0)
    o["ht0"][...] = turned_low(h[0])
    emit("ht0")
    got_h.wait()
    got_len.wait()
    got_ct = exchange(o["ct0"], o["ct1"], 4)
    got_second = mixer(1)
    attend(1)
    got_first.wait()
    got_second.wait()
    for k in range(2):
        tiny[f"ss{k}"][...] = ssp[k] + ssr[k]
    project(1, part_peer)
    got_part = exchange(part_peer, part_got, 5)
    project(0, part_own)
    o["ht1"][...] = turned_low(h[1])
    emit("ht1")
    turn_mix(0)
    turn_mix(1)
    got_part.wait()
    resid = b["tok"][...].astype(F32) + part_own[...] + part_got[...].astype(F32)
    part_own[...] = resid
    inv2 = lax.rsqrt(jnp.mean(resid * resid, axis=1, keepdims=True) + EPSILON)
    tiny["inv2"][...] = inv2
    rhat = resid * inv2
    o["rhat"][...] = rhat
    h2[0] = (rhat * s["gain2"][...]).astype(BF16)
    got_h2 = exchange(h2.at[0], h2.at[1], 6)
    emit("rhat")
    feed(0, part_own[...])
    o["h2t0"][...] = turned_low(h2[0])
    emit("h2t0")
    got_ct.wait()
    emit("ct1")
    got_h2.wait()
    feed(1, None)
    o["h2t1"][...] = turned_low(h2[1])
    emit("h2t1")
    for store in stores:
        store.wait()


def front_call(length, smalls, raw, bigs, width):
    seq_len, model = bigs["tok"].shape
    att_pad, ssm_pad, ff_width = bigs["wq"].shape[1], bigs["wz"].shape[1], bigs["wg"].shape[1]
    outs = {"xhat": shaped((seq_len, model)), "rhat": shaped((seq_len, model))}
    outs.update({"dh2": shaped((seq_len, model)), "ff": shaped((seq_len, model))})
    outs.update({"dh2p": shaped((seq_len, model), BF16), "ffp": shaped((seq_len, model), BF16)})
    outs["wkv"] = shaped((model, LANES), BF16)
    tiny = {"inv1": shaped((seq_len, 1)), "inv2": shaped((seq_len, 1))}
    tiny.update({
        "wt": shaped((16, model), BF16), "cxb": shaped((1, ssm_pad)), "cbb": shaped((1, 2 * STATE)),
        "gain": shaped((1, ssm_pad)), "skip": shaped((1, ssm_pad)), "bias": shaped((1, 16)), "rate": shaped((1, 16)),
        "bias_col": shaped((16, 1)), "rate_col": shaped((16, 1)),
    })
    for k in range(2):
        outs.update({f"{name}{k}": shaped((seq_len, ssm_pad)) for name in ("x", "y", "z")})
        outs.update({
            f"q{k}": shaped((seq_len, att_pad), BF16), f"kd{k}": shaped((seq_len, LANES), BF16),
            f"vd{k}": shaped((seq_len, LANES), BF16), f"bcp{k}": shaped((seq_len, 2 * STATE)),
            f"bc{k}": shaped((seq_len, 2 * STATE), BF16), f"ct{k}": shaped((seq_len, model), BF16),
            f"dg{k}": shaped((seq_len, ff_width), BF16), f"du{k}": shaped((seq_len, ff_width), BF16),
            f"hid{k}": shaped((ff_width, seq_len), BF16), f"h2t{k}": shaped((model, seq_len), BF16),
            f"ht{k}": shaped((model, seq_len), BF16), f"mix{k}": shaped((att_pad + ssm_pad, seq_len), BF16),
        })
        tiny.update({
            f"tp{k}": shaped((seq_len, 16)), f"tpr{k}": shaped((16, seq_len)), f"ss{k}": shaped((16, seq_len)),
            f"len{k}": shaped((8, LANES), jnp.int32),
        })
    anywhere, vmem = pl.BlockSpec(memory_space=pl.ANY), pl.BlockSpec(memory_space=pltpu.VMEM)
    scratch = [pltpu.VMEM(array.shape, array.dtype) for array in list(bigs.values()) + list(outs.values())]
    scratch += [
        pltpu.VMEM((2, seq_len, model), BF16), pltpu.VMEM((2, seq_len, model), BF16),
        pltpu.VMEM((2, seq_len, att_pad), BF16), pltpu.VMEM((2, seq_len, ssm_pad), BF16),
        pltpu.VMEM((seq_len, ff_width), BF16), pltpu.VMEM((2, 16, seq_len), F32), pltpu.VMEM((2, 16, seq_len), F32),
        pltpu.VMEM((seq_len, model), F32), pltpu.VMEM((seq_len, model), BF16), pltpu.VMEM((seq_len, model), BF16),
        pltpu.SemaphoreType.DMA((len(bigs),)), pltpu.SemaphoreType.DMA((len(outs),)),
        pltpu.SemaphoreType.DMA((7,)), pltpu.SemaphoreType.DMA((7,)),
    ]
    results = pl.pallas_call(
        functools.partial(
            front_kernel, small_names=tuple(smalls), raw_names=tuple(raw), big_names=tuple(bigs), out_names=tuple(outs),
            tiny_names=tuple(tiny), width=width,
        ),
        out_shape=list(outs.values()) + list(tiny.values()),
        in_specs=[pl.BlockSpec(memory_space=pltpu.SMEM)] + [vmem] * (len(smalls) + len(raw)) + [anywhere] * len(bigs),
        out_specs=[anywhere] * len(outs) + [vmem] * len(tiny),
        scratch_shapes=scratch,
        compiler_params=pltpu.CompilerParams(
            collective_id=1, has_side_effects=True, vmem_limit_bytes=REDUCE_LIMIT
        ),
        name="front",
    )(length, *smalls.values(), *raw.values(), *bigs.values())
    return dict(zip(list(outs) + list(tiny), results))


def finish_kernel(own_ref, peer_ref, own_misc_ref, peer_misc_ref, *refs, split):
    step = pl.program_id(0)
    sums, refs = refs[:7], refs[7:]
    out_ref = sums[6]
    for source, target in zip(sums[:6], refs[:6]):
        target[...] = source[...].astype(F32)
    (att_ref, ssm_ref, key_ref, value_ref, b_ref, c_ref, stp_ref, cxw_ref, cxb_ref, cbw_ref, cbb_ref, bias_ref,
     decay_ref, skip_ref, sgain_ref, norm_ref, ffn_ref) = refs[6:]

    @pl.when(step < split)
    def _():
        att_ref[...] = out_ref[...].astype(F32)

    @pl.when(step >= split)
    def _():
        ssm_ref[...] = out_ref[...].astype(F32)

    even = lax.axis_index("tensor") == 0
    kv, kv_peer = own_ref[:, :LANES].astype(F32), peer_ref[:, :LANES].astype(F32)
    low, high = jnp.where(even, kv, kv_peer), jnp.where(even, kv_peer, kv)
    first = lane_ids(kv.shape) < HEAD_DIM
    key_ref[...] = jnp.where(first, low, pltpu.roll(high, HEAD_DIM, 1))
    value_ref[...] = jnp.where(first, pltpu.roll(low, HEAD_DIM, 1), high)
    for ref, column in ((b_ref, B_AT), (c_ref, C_AT)):
        lanes = slice(column, column + LANES)
        ref[...] = own_ref[:, lanes].astype(F32) + peer_ref[:, lanes].astype(F32)
    @pl.when(step == 0)
    def _():
        wide_blocks, model_blocks = cxw_ref.shape[1] // LANES, norm_ref.shape[0] // LANES
        mine = own_misc_ref[...].astype(F32)
        both = mine + peer_misc_ref[...].astype(F32)

        def rows(values, block, row, length=1):
            return values[8 * block + row : 8 * block + row + length]

        def flat(values, first, blocks, row):
            parts = [rows(values, first + block, row) for block in range(blocks)]
            return jnp.concatenate(parts, axis=1).reshape(blocks * LANES)

        for block in range(wide_blocks):
            cxw_ref[:, block * LANES : (block + 1) * LANES] = rows(mine, block, 0, 4)
        for block in range(2):
            cbw_ref[:, block * LANES : (block + 1) * LANES] = rows(both, wide_blocks + block, 0, 4)
        cxb_ref[...] = flat(mine, 0, wide_blocks, 4)
        sgain_ref[...] = flat(mine, 0, wide_blocks, 6)
        cbb_ref[...] = flat(both, wide_blocks, 2, 4)
        norm_ref[...] = flat(both, wide_blocks + 3, model_blocks, 0)
        ffn_ref[...] = flat(both, wide_blocks + 3, model_blocks, 1)
        heads = bias_ref.shape[0]
        for row, ref in enumerate((bias_ref, decay_ref, skip_ref)):
            ref[...] = rows(mine, wide_blocks + 2, row)[:, :heads].reshape(heads)
        place = mine.shape[0] - 16 * model_blocks
        for block in range(model_blocks):
            values = mine[place + 16 * block : place + 16 * block + 16]
            stp_ref[:, block * LANES : (block + 1) * LANES] = values[: stp_ref.shape[0]]


def finish_call(results, peer, att_width, heads):
    model, block = results[OUT].shape[0], 128
    ssm_pad = results[ZED].shape[1]
    shared = results[SHARED]
    misc_rows = 8 * (ssm_pad // LANES + 3 + model // LANES)
    misc_rows += -misc_rows % 16 + 16 * (model // LANES)
    sums = [results[part] for part in (GATE, UP, DOWN, QUERY, ZED, EX, OUT)]
    split = att_width // block

    def by_rows(width):
        return pl.BlockSpec((block, width), lambda i: (i, 0))

    def fixed(*shape):
        return pl.BlockSpec(shape, lambda i: (0,) * len(shape))

    misc = pl.BlockSpec((misc_rows, LANES), lambda i: (0, MISC_AT // LANES))
    shapes = [(model, part.shape[1]) for part in sums[:6]]
    specs = [by_rows(part.shape[1]) for part in sums[:6]]
    shapes += [(att_width, model), (model - att_width, model)]
    specs += [
        pl.BlockSpec((block, model), lambda i: (jnp.minimum(i, split - 1), 0)),
        pl.BlockSpec((block, model), lambda i: (jnp.maximum(i - split, 0), 0)),
    ]
    shapes += [(model, LANES)] * 4
    specs += [by_rows(LANES)] * 4
    tiny = [
        (heads, model), (4, ssm_pad), (ssm_pad,), (4, 2 * STATE), (2 * STATE,), (heads,), (heads,), (heads,), (ssm_pad,),
        (model,), (model,),
    ]
    shapes += tiny
    specs += [fixed(*shape) for shape in tiny]
    return pl.pallas_call(
        functools.partial(finish_kernel, split=split),
        grid=(model // block,),
        out_shape=[shaped(shape) for shape in shapes],
        in_specs=[by_rows(SHARED_WIDTH)] * 2 + [misc] * 2 + [by_rows(part.shape[1]) for part in sums],
        out_specs=specs,
        compiler_params=pltpu.CompilerParams(vmem_limit_bytes=VMEM_LIMIT),
        name="finish",
    )(shared, peer, shared, peer, *sums)


def shaped(shape, dtype=F32):
    return jax.ShapeDtypeStruct(shape, dtype)


def whole_call(kernel, outs, scalars, args, flops, name):
    specs = [pl.BlockSpec(memory_space=pltpu.SMEM)] * scalars
    specs += [pl.BlockSpec(memory_space=pltpu.VMEM)] * (len(args) - scalars)
    moved = sum(arg.size * arg.dtype.itemsize for arg in args)
    return pl.pallas_call(
        kernel,
        out_shape=outs,
        in_specs=specs,
        out_specs=[pl.BlockSpec(memory_space=pltpu.VMEM)] * len(outs),
        compiler_params=pltpu.CompilerParams(vmem_limit_bytes=VMEM_LIMIT),
        cost_estimate=pl.CostEstimate(flops=flops, bytes_accessed=moved, transcendentals=0),
        name=name,
    )(*args)


def pad_columns(values, width):
    return jnp.pad(values, ((0, 0), (0, width - values.shape[1]))) if width != values.shape[1] else values


def pad_rows(values, height):
    return jnp.pad(values, ((0, height - values.shape[0]), (0, 0))) if height != values.shape[0] else values


def contract_rows(left, right):
    return mm_tn(jnp.concatenate(left, axis=0), jnp.concatenate(right, axis=0))


def on_device(
    tokens, lengths, cotangent, norm_gain, w_query, w_key, w_value, w_gate_z, w_ssm_x, w_ssm_b, w_ssm_c,
    w_step, conv_x_weight, conv_x_bias, conv_bc_weight, conv_bc_bias, step_bias, decay_log, skip_gain,
    ssm_norm_gain, w_out_att, w_out_ssm, ffn_norm_gain, w_gate, w_up, w_down,
):
    seq_len, model = tokens.shape
    groups = lax.axis_size("tensor")
    position = lax.axis_index("tensor")
    att_width, ssm_width = w_query.shape[1], w_gate_z.shape[1]
    att_pad = -(-att_width // LANES) * LANES
    ssm_pad = -(-ssm_width // LANES) * LANES
    ssm_heads = ssm_width // SSM_DIM
    ssm_width_all = SSM_HEADS * SSM_DIM
    ff_width = w_gate.shape[1]

    def fetch(values, shift):
        return lax.ppermute(values, "tensor", [((i + shift) % groups, i) for i in range(groups)])

    def deliver(values, shift):
        return lax.ppermute(values, "tensor", [(i, (i + shift) % groups) for i in range(groups)])

    def gather(values):
        return [values] + [fetch(values, k) for k in range(1, groups)]

    def scatter_sum(own, others):
        total = own
        for k in range(1, groups):
            total = total + deliver(others[k - 1], k).astype(F32)
        return total

    kv_head = position * (att_width // HEAD_DIM) // (HEADS // KV_HEADS)
    w_kv = jnp.concatenate(
        [lax.dynamic_slice_in_dim(w, kv_head * HEAD_DIM, HEAD_DIM, 1) for w in (w_key, w_value)], axis=1
    )
    wq = pad_columns(w_query, att_pad)
    wz, wx = pad_columns(w_gate_z, ssm_pad), pad_columns(w_ssm_x, ssm_pad)
    wt = pad_rows(w_step.T, 16)
    wa, ws = pad_rows(w_out_att, att_pad), pad_rows(w_out_ssm, ssm_pad)
    cxw, cxb = pad_columns(conv_x_weight, ssm_pad), pad_columns(conv_x_bias[None], ssm_pad)
    cbb = conv_bc_bias[None]
    gain = pad_columns(ssm_norm_gain[None], ssm_pad)
    skip = pad_columns(jnp.repeat(skip_gain, SSM_DIM)[None], ssm_pad)
    bias = pad_columns(step_bias[None], 16)
    rate = pad_columns(jnp.exp(decay_log)[None], 16)
    bias_col, rate_col = bias.T, rate.T
    half = HEAD_DIM // 2
    freqs = np.float64(ROPE_BASE) ** (-np.arange(half) * 2.0 / HEAD_DIM)
    angles = np.arange(seq_len, dtype=np.float32)[:, None] * freqs.astype(np.float32)[None, :]
    cosine, sine = np.cos(angles.astype(np.float64)), np.sin(angles.astype(np.float64))
    cos_table = jnp.asarray(np.concatenate([cosine] * 4, axis=1), F32)
    sine_first = jnp.asarray(np.concatenate([-sine, 0.0 * sine] * 2, axis=1), F32)
    sine_second = jnp.asarray(np.concatenate([0.0 * sine, sine] * 2, axis=1), F32)

    if lax.axis_size("dp") == 16 and groups == 2:
        smalls = {
            "cxw": conv_x_weight, "cbw": conv_bc_weight, "cos": cos_table, "sa": sine_first, "sb": sine_second,
            "gain1": norm_gain[None], "gain2": ffn_norm_gain[None],
        }
        raw = {
            "conv_x_bias": conv_x_bias, "conv_bc_bias": conv_bc_bias, "gain": ssm_norm_gain, "skip": skip_gain,
            "bias": step_bias, "decay": decay_log, "step": w_step,
        }
        bigs = {
            "tok": tokens, "cot": cotangent, "w_key": w_key, "w_value": w_value, "wz": w_gate_z, "wx": w_ssm_x,
            "wb": w_ssm_b, "wc": w_ssm_c, "wq": w_query, "wa": w_out_att, "ws": w_out_ssm, "wg": w_gate, "wu": w_up,
            "wd": w_down,
        }
        kept = front_call(lengths, smalls, raw, bigs, ssm_width_all)
        wq, wz, wx, wa, ws = w_query, w_gate_z, w_ssm_x, w_out_att, w_out_ssm
        for name in FORMS:
            smalls[name] = kept[name]

        def both(*names):
            return {f"{name}{k}": kept[f"{name}{k}"] for k in range(2) for name in names}

        smalls.update(both("tp", "tpr", "ss", "len"))
        smalls.update({"inv1": kept["inv1"], "inv2": kept["inv2"]})
        order = both("h2t", "dg")
        order.update({"dh2": kept["dh2"], "rhat": kept["rhat"]})
        order.update(both("du", "hid", "ct"))
        order.update({"wa": wa, "ws": ws})
        order.update(both("y", "x", "z", "q", "kd", "vd"))
        order.update({"wq": wq, "wkv": kept["wkv"], "wz": wz, "wx": wx, "wb": w_ssm_b, "wc": w_ssm_c})
        order.update(both("bcp", "bc", "mix", "ht"))
        order.update({"xhat": kept["xhat"], "ff": kept["ff"]})
        widths = (ff_width, ff_width, model, SHARED_WIDTH, att_pad, ssm_pad, ssm_pad, model)
        results = back_call(smalls, order, kept["dh2p"], kept["ffp"], widths, ssm_width_all)
        peer, grad_input, layer_output = results[PARTS:]
        (grad_gate, grad_up, grad_down, grad_q, grad_z, grad_x, grad_att, grad_ssm, grad_key, grad_value, grad_b,
         grad_c, grad_step, grad_cxw, grad_cxb, grad_cbw, grad_cbb, grad_bias, grad_decay, grad_skip, grad_sgain,
         grad_norm_gain, grad_ffn_gain) = finish_call(results, peer, att_pad, ssm_heads)
        return (
            layer_output, grad_input, grad_norm_gain, grad_q, grad_key, grad_value, grad_z, grad_x, grad_b, grad_c,
            grad_step.T, grad_cxw, grad_cxb, grad_cbw, grad_cbb, grad_bias, grad_decay, grad_skip, grad_sgain, grad_att,
            grad_ssm, grad_ffn_gain, grad_gate, grad_up, grad_down,
        )

    inputs = tokens.astype(F32)
    inv1 = lax.rsqrt(jnp.mean(inputs * inputs, axis=1, keepdims=True) + EPSILON)
    h_own = (inputs * inv1 * norm_gain).astype(BF16)
    own_mask = jnp.arange(seq_len) < lengths[0]
    ct_own = jnp.where(own_mask[:, None], cotangent, jnp.zeros_like(cotangent))
    h_all = gather(h_own)
    len_all = gather(lax.optimization_barrier((lengths, h_own))[0])
    ct_all = gather(lax.optimization_barrier((ct_own, h_all[1]))[0] if groups > 1 else ct_own)

    def forward(k):
        outs = [
            shaped((seq_len, att_pad), BF16), shaped((seq_len, LANES), BF16), shaped((seq_len, LANES), BF16),
            shaped((seq_len, ssm_pad)), shaped((seq_len, ssm_pad)), shaped((seq_len, 2 * STATE)),
            shaped((seq_len, 2 * STATE), BF16), shaped((seq_len, 16)), shaped((16, seq_len)),
            shaped((seq_len, ssm_pad)), shaped((16, seq_len)),
        ]
        args = [
            len_all[k], h_all[k], wq, w_kv, wz, wx, w_ssm_b, w_ssm_c, wt, cxw, cxb, conv_bc_weight, cbb,
            bias, rate, bias_col, rate_col, skip, cos_table, sine_first, sine_second,
        ]
        return whole_call(mixer_forward_kernel, outs, 1, args, 8 * 10**9, "mixer_forward")

    def attend(k):
        q, kd, vd = kept[k][:3]
        return whole_call(
            attend_kernel, [shaped((seq_len, att_pad), BF16)], 1, [len_all[k], q, kd, vd], 2 * 10**9, "attend"
        )[0]

    kept = [forward(k) for k in range(groups)]
    squares_part = [one[10] for one in kept]
    squares = [squares_part[k] for k in range(groups)]
    for shift in range(1, groups):
        for k in range(groups):
            squares[k] = squares[k] + fetch(squares_part[(k - shift) % groups], shift)
    mix_att = [attend(k) for k in range(groups)]

    def project(k, dtype):
        q, kd, vd, z, x, bcp, bc, tp, tpr, y, _ = kept[k]
        return whole_call(
            functools.partial(out_kernel, width=ssm_width_all),
            [shaped((seq_len, model), dtype), shaped((seq_len, ssm_pad), BF16)],
            0,
            [mix_att[k], y, x, z, squares[k], cxw, cxb, skip, gain, wa, ws],
            4 * 10**9,
            "out_project",
        )

    projected = [project(k, F32 if k == 0 else BF16) for k in range(groups)]
    mix_ssm = [one[1] for one in projected]
    branch = scatter_sum(projected[0][0], [one[0] for one in projected[1:]])
    resid = inputs + branch
    inv2 = lax.rsqrt(jnp.mean(resid * resid, axis=1, keepdims=True) + EPSILON)
    h2_own = (resid * inv2 * ffn_norm_gain).astype(BF16)
    h2_all = gather(h2_own)

    def feed(k, rows2):
        dtype = F32 if k == 0 else BF16
        block = min(256, ff_width)
        full = pl.BlockSpec((seq_len, model), lambda i: (0, 0))
        columns = pl.BlockSpec((model, block), lambda i: (0, i))
        rows = pl.BlockSpec((block, model), lambda i: (i, 0))
        tall = pl.BlockSpec((seq_len, block), lambda i: (0, i))
        return pl.pallas_call(
            ffn_kernel,
            grid=(ff_width // block,),
            out_shape=[shaped((ff_width, seq_len), BF16)] + [shaped((seq_len, ff_width), BF16)] * 2
            + [shaped((seq_len, model), dtype)] * 2 + [shaped((model, seq_len), BF16)],
            in_specs=[full, full, columns, columns, rows] + ([full] if k == 0 else []),
            out_specs=[pl.BlockSpec((block, seq_len), lambda i: (i, 0))] + [tall] * 2 + [full] * 2
            + [pl.BlockSpec((model, seq_len), lambda i: (0, 0))],
            scratch_shapes=[pltpu.VMEM((seq_len, model), F32)] * 2,
            compiler_params=pltpu.CompilerParams(vmem_limit_bytes=VMEM_LIMIT),
            cost_estimate=pl.CostEstimate(flops=8 * 10**9, bytes_accessed=10**7, transcendentals=0),
            name="feed_forward",
        )(rows2, ct_all[k], w_gate, w_up, w_down, *([resid] if k == 0 else []))

    fed = [feed(0, h2_own)]
    for k in range(1, groups):
        fed.append(feed(k, lax.optimization_barrier((h2_all[k], fed[0][0]))[0]))
    d_second = scatter_sum(fed[0][4], [one[4] for one in fed[1:]])
    layer_output = scatter_sum(fed[0][3], [one[3] for one in fed[1:]]).astype(BF16)
    h2_turned = jnp.concatenate([one[5] for one in fed], axis=1)
    grad_gate = mm(h2_turned, jnp.concatenate([one[1] for one in fed], axis=0))
    grad_up = mm(h2_turned, jnp.concatenate([one[2] for one in fed], axis=0))
    grad_down = mm(jnp.concatenate([one[0] for one in fed], axis=1), jnp.concatenate(ct_all, axis=0))
    scaled = d_second * ffn_norm_gain
    d_resid = (
        ct_own.astype(F32)
        + inv2 * scaled
        - resid * (inv2**3) * jnp.mean(scaled * resid, axis=1, keepdims=True)
    )
    grad_ffn_gain = jnp.sum(d_second * resid * inv2, axis=0)
    db_all = gather(d_resid.astype(BF16))

    def mix_grad(k):
        q, kd, vd, z, x, bcp, bc, tp, tpr, y, _ = kept[k]
        return whole_call(
            mix_grad_kernel,
            [shaped((seq_len, att_pad), BF16), shaped((seq_len, ssm_pad), BF16), shaped((16, seq_len))],
            0,
            [db_all[k], y, x, z, cxw, cxb, skip, gain, wa, ws],
            4 * 10**9,
            "mix_grad",
        )

    mixed = [mix_grad(k) for k in range(groups)]
    backs_part = [one[2] for one in mixed]
    backs = [backs_part[k] for k in range(groups)]
    for shift in range(1, groups):
        for k in range(groups):
            backs[k] = backs[k] + fetch(backs_part[(k - shift) % groups], shift)

    def attend_back(k):
        q, kd, vd = kept[k][:3]
        return whole_call(
            attend_back_kernel,
            [shaped((seq_len, att_pad), BF16), shaped((seq_len, LANES), BF16)],
            1,
            [len_all[k], q, kd, vd, mixed[k][0], cos_table, sine_first, sine_second],
            4 * 10**9,
            "attend_back",
        )

    turned = [attend_back(k) for k in range(groups)]

    def backward(k):
        q, kd, vd, z, x, bcp, bc, tp, tpr, y, _ = kept[k]
        outs = [
            shaped((seq_len, model), F32 if k == 0 else BF16), shaped((seq_len, ssm_pad), BF16),
            shaped((seq_len, ssm_pad), BF16), shaped((seq_len, 2 * STATE), BF16), shaped((seq_len, 16), BF16),
            shaped((8, ssm_pad)), shaped((8, 2 * STATE)), shaped((8, 16)),
        ]
        args = [
            len_all[k], mixed[k][1], y, x, z, bcp, bc, tp, tpr, squares[k], backs[k], turned[k][0], turned[k][1],
            wq, w_kv, wz, wx, w_ssm_b, w_ssm_c, wt, cxw, cxb, conv_bc_weight, cbb, bias, rate, bias_col, rate_col,
            skip, gain,
        ]
        return whole_call(
            functools.partial(mixer_back_kernel, width=ssm_width_all), outs, 1, args, 16 * 10**9, "mixer_back"
        )

    gone = [None] * groups
    for k in list(range(1, groups)) + [0]:
        gone[k] = backward(k)
    d_first = scatter_sum(gone[0][0], [one[0] for one in gone[1:]])
    grad_norm_gain = jnp.sum(d_first * inputs * inv1, axis=0)

    wide, bcg, small = (sum(one[i] for one in gone) for i in (5, 6, 7))
    grad_q = contract_rows(h_all, [one[0] for one in turned])
    grad_kv = contract_rows(h_all, [one[1] for one in turned])
    grad_bc = contract_rows(h_all, [one[3] for one in gone])
    grad_x = contract_rows(h_all, [one[1] for one in gone])
    grad_z = contract_rows(h_all, [one[2] for one in gone])
    grad_step = contract_rows(h_all, [one[4] for one in gone])
    grad_att = contract_rows(mix_att, db_all)
    grad_ssm = contract_rows(mix_ssm, db_all)
    norms = jnp.concatenate([bcg[:5].reshape(-1), grad_norm_gain, grad_ffn_gain])
    zeros = jnp.zeros((model, KV_HEADS * HEAD_DIM), F32)
    grad_key = lax.dynamic_update_slice(zeros, grad_kv[:, :HEAD_DIM], (0, kv_head * HEAD_DIM))
    grad_value = lax.dynamic_update_slice(zeros, grad_kv[:, HEAD_DIM:], (0, kv_head * HEAD_DIM))
    grad_key, grad_value, grad_bc, norms = lax.psum((grad_key, grad_value, grad_bc, norms), ("dp", "tensor"))
    grad_b, grad_c = grad_bc[:, :STATE], grad_bc[:, STATE:]
    grad_q, grad_z, grad_x, grad_step, grad_att, grad_ssm, wide, small = (
        lax.psum(part.astype(BF16), "dp").astype(F32)
        for part in (grad_q, grad_z, grad_x, grad_step, grad_att, grad_ssm, wide, small)
    )
    grad_gate, grad_up, grad_down = (
        lax.psum(part.astype(BF16), "dp").astype(F32) for part in (grad_gate, grad_up, grad_down)
    )
    grad_step = grad_step[:, :ssm_heads]
    grad_cxw, grad_cxb, grad_sgain = wide[:4], wide[4:5], wide[6:7]
    bcg = norms[: 10 * STATE].reshape(5, 2 * STATE)
    grad_cbw, grad_cbb = bcg[:4], bcg[4:]
    grad_bias, grad_decay, grad_skip = small[0:1, :ssm_heads], small[1:2, :ssm_heads], small[2:3, :ssm_heads]
    grad_norm_gain = norms[10 * STATE : 10 * STATE + model]
    grad_ffn_gain = norms[10 * STATE + model :]

    scaled = d_first * norm_gain
    grad_input = d_resid + inv1 * scaled - inputs * (inv1**3) * jnp.mean(scaled * inputs, axis=1, keepdims=True)

    return (
        layer_output,
        grad_input,
        grad_norm_gain.reshape(-1),
        grad_q[:, :att_width],
        grad_key,
        grad_value,
        grad_z[:, :ssm_width],
        grad_x[:, :ssm_width],
        grad_b,
        grad_c,
        grad_step,
        grad_cxw[:, :ssm_width],
        grad_cxb.reshape(-1)[:ssm_width],
        grad_cbw,
        grad_cbb.reshape(-1),
        grad_bias.reshape(-1),
        grad_decay.reshape(-1),
        grad_skip.reshape(-1),
        grad_sgain.reshape(-1)[:ssm_width],
        grad_att[:att_width],
        grad_ssm[:ssm_width],
        grad_ffn_gain.reshape(-1),
        grad_gate,
        grad_up,
        grad_down,
    )


def solution(mesh):
    rows, split, tall = P(("dp", "tensor"), None), P(None, "tensor"), P("tensor", None)
    vector, copied = P("tensor"), P()
    return jax.shard_map(
        on_device,
        mesh=mesh,
        in_specs=(
            rows, P(("dp", "tensor")), rows, copied, split, copied, copied, split, split, copied, copied, split,
            split, vector, copied, copied, vector, vector, vector, vector, tall, tall, copied, split, split, tall,
        ),
        out_specs=(
            rows, rows, copied, split, copied, copied, split, split, copied, copied, split, split, vector, copied,
            copied, vector, vector, vector, vector, tall, tall, copied, split, split, tall,
        ),
        check_vma=False,
    )
```

```python
import functools

import jax
import jax.numpy as jnp
import numpy as np
from jax import lax
from jax.experimental import pallas as pl
from jax.experimental.pallas import tpu as pltpu
from jax.sharding import PartitionSpec as P

HEADS = 8
KV_HEADS = 2
HEAD_DIM = 64
SSM_HEADS = 24
SSM_DIM = 64
STATE = 128
SPAN = 128
LANES = 128

EPSILON = 1e-05
ROPE_BASE = 100000000000.0
F32 = jnp.float32
BF16 = jnp.bfloat16
VMEM_LIMIT = 62 * 1024 * 1024
REDUCE_LIMIT = 62 * 1024 * 1024
MESH = pl.DeviceIdType.MESH


def mm(left, right):
    return jnp.dot(left, right, preferred_element_type=F32)


def mm_nt(left, right):
    return lax.dot_general(left, right, (((1,), (1,)), ((), ())), preferred_element_type=F32)


def mm_tn(left, right):
    return lax.dot_general(left, right, (((0,), (0,)), ((), ())), preferred_element_type=F32)


def pieces(values, count):
    terms = []
    for _ in range(count):
        term = values.astype(BF16)
        terms.append(term)
        values = values - term.astype(F32)
    return terms


def sigmoid(values):
    return 1.0 / (1.0 + jnp.exp(-values))


def softplus(values):
    return jnp.maximum(values, 0.0) + jnp.log1p(jnp.exp(-jnp.abs(values)))


def lane_ids(shape):
    return lax.broadcasted_iota(jnp.int32, shape, 1)


def row_ids(shape):
    return lax.broadcasted_iota(jnp.int32, shape, 0)


def repeat_lanes(column, count):
    return jnp.concatenate([column] * count, axis=1) if count > 1 else column


def column_of(row):
    ones = jnp.where(row_ids((16, LANES)) == 0, 1.0, 0.0).astype(BF16)
    total = None
    for term in pieces(row, 3):
        part = mm_tn(term, ones)
        total = part if total is None else total + part
    return total


def row_sums(values):
    ones = jnp.ones((16, values.shape[1]), BF16)
    high, low = pieces(values, 2)
    return mm_nt(ones, high) + mm_nt(ones, low)


def causal_shift(values, steps):
    if steps == 0:
        return values
    rolled = pltpu.roll(values, steps, 0)
    return jnp.where(row_ids(values.shape) >= steps, rolled, 0.0)


def anti_shift(values, steps):
    if steps == 0:
        return values
    length = values.shape[0]
    rolled = pltpu.roll(values, length - steps, 0)
    return jnp.where(row_ids(values.shape) < length - steps, rolled, 0.0)


def conv(values, weight, bias):
    taps = weight.shape[0]
    total = bias + weight[taps - 1 : taps] * values
    for offset in range(taps - 1):
        total = total + weight[offset : offset + 1] * causal_shift(values, taps - 1 - offset)
    return total


def conv_back(grad, values, weight):
    taps = weight.shape[0]
    total, rows = None, []
    for offset in range(taps):
        steps = taps - 1 - offset
        moved = anti_shift(grad, steps)
        part = weight[offset : offset + 1] * moved
        total = part if total is None else total + part
        rows.append(jnp.sum(moved * values, axis=0, keepdims=True))
    rows.append(jnp.sum(grad, axis=0, keepdims=True))
    return total, rows


def rope(values, cosine, sine_first, sine_second):
    ahead = pltpu.roll(values, LANES - HEAD_DIM // 2, 1)
    behind = pltpu.roll(values, HEAD_DIM // 2, 1)
    return values * cosine + ahead * sine_first + behind * sine_second


def lower_mask():
    return row_ids((SPAN, SPAN)) >= lane_ids((SPAN, SPAN))


def span_sums(values):
    lower = jnp.where(lower_mask(), 1.0, 0.0).astype(BF16)
    out = []
    for start in range(0, values.shape[0], SPAN):
        total = None
        for term in pieces(values[start : start + SPAN], 3):
            part = mm(lower, term)
            total = part if total is None else total + part
        out.append(total)
    return jnp.concatenate(out, axis=0)


def span_sums_rows(values):
    upper = jnp.where(row_ids((SPAN, SPAN)) <= lane_ids((SPAN, SPAN)), 1.0, 0.0).astype(BF16)
    out = []
    for start in range(0, values.shape[1], SPAN):
        total = None
        for term in pieces(values[:, start : start + SPAN], 3):
            part = mm(term, upper)
            total = part if total is None else total + part
        out.append(total)
    return jnp.concatenate(out, axis=1)


def span_sums_back(values):
    upper = jnp.where(row_ids((SPAN, SPAN)) <= lane_ids((SPAN, SPAN)), 1.0, 0.0).astype(BF16)
    out = []
    for start in range(0, values.shape[0], SPAN):
        total = None
        for term in pieces(values[start : start + SPAN], 3):
            part = mm(upper, term)
            total = part if total is None else total + part
        out.append(total)
    return jnp.concatenate(out, axis=0)


def steps_of(tp, tp_row, bias, bias_col, rate, rate_col, length):
    seq_len = tp.shape[0]
    valid = jnp.where(row_ids((seq_len, 1)) < length, 1.0, 0.0)
    valid_row = jnp.where(lane_ids((1, seq_len)) < length, 1.0, 0.0)
    dt = softplus(tp + bias) * valid
    dt_row = softplus(tp_row + bias_col) * valid_row
    cum = span_sums(-(dt * rate))
    cum_row = span_sums_rows(-(dt_row * rate_col))
    return valid, dt, cum, cum_row


def spread(values, head):
    return jnp.broadcast_to(values[:, head : head + 1], (values.shape[0], LANES))


def decays(cum_first, cum_second, cum_row, pair, span):
    rows = slice(span * SPAN, (span + 1) * SPAN)
    lower = lower_mask()
    out = []
    for head, column in ((2 * pair, cum_first), (2 * pair + 1, cum_second)):
        differ = column[rows] - cum_row[head : head + 1, rows]
        out.append(jnp.exp(jnp.where(lower, differ, -1e30)))
    return out


def split_heads(values):
    first = lane_ids(values.shape) < HEAD_DIM
    zero = jnp.zeros_like(values)
    return jnp.concatenate([jnp.where(first, values, zero), jnp.where(first, zero, values)], axis=0)


def state_of(in_map, weighted_first, cum_pair_first):
    to_end = jnp.exp(cum_pair_first[SPAN - 1 : SPAN] - cum_pair_first)
    ending = (weighted_first * to_end).astype(BF16)
    return to_end, ending, mm_tn(in_map[:SPAN], ending)


def mixer_forward_kernel(
    len_ref, h_ref, wq_ref, wkv_ref, wz_ref, wx_ref, wb_ref, wc_ref, wt_ref, cxw_ref, cxb_ref,
    cbw_ref, cbb_ref, bias_ref, rate_ref, bias_col_ref, rate_col_ref, skip_ref, cos_ref, sa_ref,
    sb_ref, q_ref, kd_ref, vd_ref, z_ref, x_ref, bcp_ref, bc_ref, tp_ref, tpr_ref, y_ref, ss_ref,
):
    h = h_ref[...]
    pairs = wx_ref.shape[1] // LANES
    z_ref[...] = mm(h, wz_ref[...])
    x_ref[...] = mm(h, wx_ref[...])
    bcp_ref[:, :STATE] = mm(h, wb_ref[...])
    bcp_ref[:, STATE:] = mm(h, wc_ref[...])
    tp = mm_nt(h, wt_ref[...])
    tp_row = mm_nt(wt_ref[...], h)
    tp_ref[...] = tp
    tpr_ref[...] = tp_row
    cosine, sine_first, sine_second = cos_ref[...], sa_ref[...], sb_ref[...]
    for pair in range(wq_ref.shape[1] // LANES):
        lanes = slice(pair * LANES, (pair + 1) * LANES)
        q_ref[:, lanes] = rope(mm(h, wq_ref[:, lanes]), cosine, sine_first, sine_second).astype(BF16)
    kv = mm(h, wkv_ref[...])
    turned = pltpu.roll(kv, HEAD_DIM, 1)
    first = lane_ids(kv.shape) < HEAD_DIM
    kd_ref[...] = rope(jnp.where(first, kv, turned), cosine, sine_first, sine_second).astype(BF16)
    vd_ref[...] = jnp.where(first, turned, kv).astype(BF16)

    mapped = conv(bcp_ref[...], cbw_ref[...], cbb_ref[...])
    bc = (mapped * sigmoid(mapped)).astype(BF16)
    bc_ref[...] = bc
    in_map, out_map = bc[:, :STATE], bc[:, STATE:]
    affinity = [
        mm_nt(out_map[s * SPAN : (s + 1) * SPAN], in_map[s * SPAN : (s + 1) * SPAN]) for s in range(2)
    ]
    _, dt, cum, cum_row = steps_of(
        tp, tp_row, bias_ref[...], bias_col_ref[...], rate_ref[...], rate_col_ref[...], len_ref[0]
    )
    squares = None
    for pair in range(pairs):
        lanes = slice(pair * LANES, (pair + 1) * LANES)
        cx = conv(x_ref[:, lanes], cxw_ref[:, lanes], cxb_ref[:, lanes])
        xc = cx * sigmoid(cx)
        dt_pair = jnp.where(first, spread(dt, 2 * pair), spread(dt, 2 * pair + 1))
        cum_first, cum_second = spread(cum, 2 * pair), spread(cum, 2 * pair + 1)
        cum_pair = jnp.where(first, cum_first, cum_second)
        weighted = xc * dt_pair
        low = weighted.astype(BF16)
        _, _, state = state_of(in_map, weighted[:SPAN], cum_pair[:SPAN])
        parts = []
        for s in range(2):
            rows = slice(s * SPAN, (s + 1) * SPAN)
            mats = [
                (affinity[s] * decay).astype(BF16)
                for decay in decays(cum_first, cum_second, cum_row, pair, s)
            ]
            part = mm(jnp.concatenate(mats, axis=1), split_heads(low[rows]))
            if s:
                part = part + mm(out_map[rows], state.astype(BF16)) * jnp.exp(cum_pair[rows])
            parts.append(part)
        y = jnp.concatenate(parts, axis=0)
        y_ref[:, lanes] = y
        z = z_ref[:, lanes]
        gated = (y + skip_ref[:, lanes] * xc) * (z * sigmoid(z))
        square = gated * gated
        squares = square if squares is None else squares + square
    ss_ref[...] = row_sums(squares)


def masked_probs(queries, kd, length, scale):
    seq_len = kd.shape[0]
    scores = mm_nt(split_heads(queries), kd) * scale
    rows = row_ids(scores.shape)
    rows = jnp.where(rows >= seq_len, rows - seq_len, rows)
    padding = jnp.where(lane_ids((1, seq_len)) < length, 0.0, -1e30)
    scores = jnp.where(rows >= lane_ids(scores.shape), scores + padding, -1e30)
    weights = jnp.exp(scores - jnp.max(scores, axis=1, keepdims=True))
    return weights / jnp.sum(weights, axis=1, keepdims=True)


def attend_kernel(len_ref, q_ref, kd_ref, vd_ref, out_ref):
    seq_len = q_ref.shape[0]
    values = split_heads(vd_ref[...])
    for pair in range(q_ref.shape[1] // LANES):
        lanes = slice(pair * LANES, (pair + 1) * LANES)
        probs = masked_probs(q_ref[:, lanes], kd_ref[...], len_ref[0], HEAD_DIM ** (-0.5)).astype(BF16)
        both = jnp.concatenate([probs[:seq_len], probs[seq_len:]], axis=1)
        out_ref[:, lanes] = mm(both, values).astype(BF16)


def join_halves(values):
    return values + pltpu.roll(values, HEAD_DIM, 1)


def attend_back_kernel(len_ref, q_ref, kd_ref, vd_ref, da_ref, cos_ref, sa_ref, sb_ref, dq_ref, dkv_ref):
    seq_len = q_ref.shape[0]
    scale = HEAD_DIM ** (-0.5)
    cosine, sine_first, sine_second = cos_ref[...], -sa_ref[...], -sb_ref[...]
    kd, vd = kd_ref[...], vd_ref[...]
    keys = split_heads(kd)
    grad_k, grad_v = None, None
    for pair in range(q_ref.shape[1] // LANES):
        lanes = slice(pair * LANES, (pair + 1) * LANES)
        probs = masked_probs(q_ref[:, lanes], kd, len_ref[0], scale)
        da = split_heads(da_ref[:, lanes])
        dprob = mm_nt(da, vd)
        dscore = (probs * (dprob - jnp.sum(probs * dprob, axis=1, keepdims=True))).astype(BF16)
        both = jnp.concatenate([dscore[:seq_len], dscore[seq_len:]], axis=1)
        dq = mm(both, keys) * scale
        dq_ref[:, lanes] = rope(dq, cosine, sine_first, sine_second).astype(BF16)
        part_k = mm_tn(dscore, split_heads(q_ref[:, lanes]))
        part_v = mm_tn(probs.astype(BF16), da)
        grad_k = part_k if grad_k is None else grad_k + part_k
        grad_v = part_v if grad_v is None else grad_v + part_v
    dk = rope(join_halves(grad_k) * scale, cosine, sine_first, sine_second)
    first = lane_ids(dk.shape) < HEAD_DIM
    dkv_ref[...] = jnp.where(first, dk, join_halves(grad_v)).astype(BF16)


def out_kernel(att_ref, y_ref, x_ref, z_ref, ss_ref, cxw_ref, cxb_ref, skip_ref, gain_ref, wa_ref, ws_ref,
               part_ref, mix_ref, *, width):
    total = mm(att_ref[...], wa_ref[...])
    inv = column_of(lax.rsqrt(ss_ref[...] / width + EPSILON))
    for pair in range(y_ref.shape[1] // LANES):
        lanes = slice(pair * LANES, (pair + 1) * LANES)
        cx = conv(x_ref[:, lanes], cxw_ref[:, lanes], cxb_ref[:, lanes])
        z = z_ref[:, lanes]
        gated = (y_ref[:, lanes] + skip_ref[:, lanes] * (cx * sigmoid(cx))) * (z * sigmoid(z))
        mix_ref[:, lanes] = (gated * inv * gain_ref[:, lanes]).astype(BF16)
    part_ref[...] = (total + mm(mix_ref[...], ws_ref[...])).astype(part_ref.dtype)


def mix_grad_kernel(db_ref, y_ref, x_ref, z_ref, cxw_ref, cxb_ref, skip_ref, gain_ref, wa_ref, ws_ref,
                    da_ref, dm_ref, bs_ref):
    db = db_ref[...]
    da_ref[...] = mm_nt(db, wa_ref[...]).astype(BF16)
    dm_ref[...] = mm_nt(db, ws_ref[...]).astype(BF16)
    total = None
    for pair in range(y_ref.shape[1] // LANES):
        lanes = slice(pair * LANES, (pair + 1) * LANES)
        cx = conv(x_ref[:, lanes], cxw_ref[:, lanes], cxb_ref[:, lanes])
        z = z_ref[:, lanes]
        gated = (y_ref[:, lanes] + skip_ref[:, lanes] * (cx * sigmoid(cx))) * (z * sigmoid(z))
        part = gated * (gain_ref[:, lanes] * dm_ref[:, lanes].astype(F32))
        total = part if total is None else total + part
    bs_ref[...] = row_sums(total)


def head_sums(values, pair):
    rows, columns = row_ids((LANES, 16)), lane_ids((LANES, 16))
    chosen = jnp.where(columns == 2 * pair + jnp.where(rows < HEAD_DIM, 0, 1), 1.0, 0.0).astype(BF16)
    high, low = pieces(values, 2)
    return mm(jnp.concatenate([high, low], axis=1), jnp.concatenate([chosen, chosen], axis=0))


def mixer_back_kernel(
    len_ref, dm_ref, y_ref, x_ref, z_ref, bcp_ref, bc_ref, tp_ref, tpr_ref, ss_ref, bs_ref, dq_ref,
    dkv_ref, wq_ref, wkv_ref, wz_ref, wx_ref, wb_ref, wc_ref, wt_ref, cxw_ref, cxb_ref, cbw_ref,
    cbb_ref, bias_ref, rate_ref, bias_col_ref, rate_col_ref, skip_ref, gain_ref,
    dh_ref, dx_ref, dz_ref, dbc_ref, dt_ref, wide_ref, bcg_ref, small_ref, *, width, tick=lambda: None,
):
    pairs = x_ref.shape[1] // LANES
    bc = bc_ref[...]
    in_map, out_map = bc[:, :STATE], bc[:, STATE:]
    affinity = [
        mm_nt(out_map[s * SPAN : (s + 1) * SPAN], in_map[s * SPAN : (s + 1) * SPAN]) for s in range(2)
    ]
    valid, dt, cum, cum_row = steps_of(
        tp_ref[...], tpr_ref[...], bias_ref[...], bias_col_ref[...], rate_ref[...], rate_col_ref[...], len_ref[0]
    )
    inv_row = lax.rsqrt(ss_ref[...] / width + EPSILON)
    inv = column_of(inv_row)
    back = column_of(inv_row * inv_row * inv_row * bs_ref[...] / width)
    first = lane_ids((x_ref.shape[0], LANES)) < HEAD_DIM
    last_row = row_ids((SPAN, LANES)) == SPAN - 1
    d_cum, d_step, d_skip = None, None, None
    wide_ref[7:8, :] = jnp.zeros((1, wide_ref.shape[1]), F32)
    d_aff, d_out, d_in = [None, None], None, None

    def plus(total, part):
        return part if total is None else total + part

    for pair in range(pairs):
        lanes = slice(pair * LANES, (pair + 1) * LANES)
        x = x_ref[:, lanes]
        cxw = cxw_ref[:, lanes]
        cx = conv(x, cxw, cxb_ref[:, lanes])
        sx = sigmoid(cx)
        xc = cx * sx
        z = z_ref[:, lanes]
        sz = sigmoid(z)
        silu_z = z * sz
        scanned = y_ref[:, lanes]
        y = scanned + skip_ref[:, lanes] * xc
        gated = y * silu_z
        d_mix = dm_ref[:, lanes].astype(F32)
        d_gated = inv * (gain_ref[:, lanes] * d_mix) - gated * back
        wide_ref[6:7, lanes] = jnp.sum(d_mix * gated * inv, axis=0, keepdims=True)
        dy = d_gated * silu_z
        dz_ref[:, lanes] = (d_gated * y * (sz * (1.0 + z * (1.0 - sz)))).astype(BF16)
        wide_ref[5:6, lanes] = jnp.sum(dy * xc, axis=0, keepdims=True)
        dt_pair = jnp.where(first, spread(dt, 2 * pair), spread(dt, 2 * pair + 1))
        cum_first, cum_second = spread(cum, 2 * pair), spread(cum, 2 * pair + 1)
        cum_pair = jnp.where(first, cum_first, cum_second)
        weighted = xc * dt_pair
        low = weighted.astype(BF16)
        dy_low = dy.astype(BF16)
        to_end, ending, state = state_of(in_map, weighted[:SPAN], cum_pair[:SPAN])
        d_weighted = []
        for s in range(2):
            rows = slice(s * SPAN, (s + 1) * SPAN)
            decay = decays(cum_first, cum_second, cum_row, pair, s)
            mats = jnp.concatenate([(affinity[s] * one).astype(BF16) for one in decay], axis=0)
            both = split_heads(dy_low[rows])
            d_mats = mm_nt(both, low[rows])
            d_aff[s] = plus(d_aff[s], d_mats[:SPAN] * decay[0] + d_mats[SPAN:] * decay[1])
            d_weighted.append(mm_tn(mats, both))
        reached = (dy[SPAN:] * jnp.exp(cum_pair[SPAN:])).astype(BF16)
        d_out = plus(d_out, mm_nt(reached, state.astype(BF16)))
        d_state = mm_tn(out_map[SPAN:], reached).astype(BF16)
        d_in = plus(d_in, mm_nt(ending, d_state))
        d_ending = mm(in_map[:SPAN], d_state)
        through = ending.astype(F32) * d_ending
        low_f, dy_f = low.astype(F32), dy_low.astype(F32)
        change = dy_f * scanned - low_f * jnp.concatenate(d_weighted, axis=0)
        ended = jnp.where(last_row, jnp.sum(through, axis=0, keepdims=True), 0.0) - through
        change = jnp.concatenate([change[:SPAN] + ended, change[SPAN:]], axis=0)
        d_weight = jnp.concatenate([d_weighted[0] + d_ending * to_end, d_weighted[1]], axis=0)
        d_cum = plus(d_cum, head_sums(change, pair))
        d_step = plus(d_step, head_sums(d_weight * xc, pair))
        d_xc = dy * skip_ref[:, lanes] + d_weight * dt_pair
        d_cx = d_xc * (sx * (1.0 + cx * (1.0 - sx)))
        d_x, rows_x = conv_back(d_cx, x, cxw)
        dx_ref[:, lanes] = d_x.astype(BF16)
        for index, row in enumerate(rows_x):
            wide_ref[index : index + 1, lanes] = row
        d_skip = plus(d_skip, head_sums(wide_ref[:, lanes], pair))
        tick()

    rate = rate_ref[...]
    d_log = span_sums_back(d_cum)
    d_dt = d_step - rate * d_log
    d_tp = d_dt * valid * sigmoid(tp_ref[...] + bias_ref[...])
    small_ref[...] = jnp.zeros(small_ref.shape, F32)
    small_ref[0:1, :] = jnp.sum(d_tp, axis=0, keepdims=True)
    small_ref[1:2, :] = -rate * jnp.sum(dt * d_log, axis=0, keepdims=True)
    small_ref[2:3, :] = d_skip[5:6]
    dt_ref[...] = d_tp.astype(BF16)

    d_maps = []
    low_aff = [part.astype(BF16) for part in d_aff]
    d_ins, d_outs = [], []
    for s in range(2):
        rows = slice(s * SPAN, (s + 1) * SPAN)
        d_outs.append(mm(low_aff[s], in_map[rows]))
        d_ins.append(mm_tn(low_aff[s], out_map[rows]))
    d_outs[1] = d_outs[1] + d_out
    d_ins[0] = d_ins[0] + d_in
    d_maps = jnp.concatenate(
        [jnp.concatenate(d_ins, axis=0), jnp.concatenate(d_outs, axis=0)], axis=1
    )
    mapped = conv(bcp_ref[...], cbw_ref[...], cbb_ref[...])
    sm = sigmoid(mapped)
    d_bc, rows_bc = conv_back(d_maps * (sm * (1.0 + mapped * (1.0 - sm))), bcp_ref[...], cbw_ref[...])
    bcg_ref[...] = jnp.zeros(bcg_ref.shape, F32)
    for index, row in enumerate(rows_bc):
        bcg_ref[index : index + 1, :] = row
    d_bc = d_bc.astype(BF16)
    dbc_ref[...] = d_bc
    total = mm_nt(dx_ref[...], wx_ref[...]) + mm_nt(dz_ref[...], wz_ref[...])
    total = total + mm_nt(dq_ref[...], wq_ref[...]) + mm_nt(dkv_ref[...], wkv_ref[...])
    total = total + mm_nt(d_bc[:, :STATE], wb_ref[...]) + mm_nt(d_bc[:, STATE:], wc_ref[...])
    total = total + mm(dt_ref[...], wt_ref[...])
    dh_ref[...] = total.astype(dh_ref.dtype)


def ffn_kernel(h_ref, ct_ref, wg_ref, wu_ref, wd_ref, *refs):
    base_ref = refs[0] if len(refs) == 9 else None
    hid_ref, dg_ref, du_ref, ff_ref, dh_ref, ht_ref, ff_acc, dh_acc = refs[-8:]
    step = pl.program_id(0)
    h = h_ref[...]
    gate = mm(h, wg_ref[...])
    up = mm(h, wu_ref[...])
    d_hidden = mm_nt(ct_ref[...], wd_ref[...]).astype(BF16).astype(F32)
    sg = sigmoid(gate)
    silu = gate * sg
    hidden = silu * up
    hid_ref[...] = hidden.T.astype(BF16)
    hidden = hidden.astype(BF16)
    d_gate = (d_hidden * up * (sg * (1.0 + gate * (1.0 - sg)))).astype(BF16)
    d_up = (d_hidden * silu).astype(BF16)
    dg_ref[...] = d_gate
    du_ref[...] = d_up
    ff_part = mm(hidden, wd_ref[...])
    dh_part = mm_nt(d_gate, wg_ref[...]) + mm_nt(d_up, wu_ref[...])

    @pl.when(step == 0)
    def _():
        ht_ref[...] = h.astype(F32).T.astype(BF16)
        ff_acc[...] = ff_part if base_ref is None else ff_part + base_ref[...]
        dh_acc[...] = dh_part

    @pl.when(step > 0)
    def _():
        ff_acc[...] += ff_part
        dh_acc[...] += dh_part

    @pl.when(step == pl.num_programs(0) - 1)
    def _():
        ff_ref[...] = ff_acc[...].astype(ff_ref.dtype)
        dh_ref[...] = dh_acc[...].astype(dh_ref.dtype)


class Names(dict):
    __getattr__ = dict.__getitem__


class Entry:
    def __init__(self, ref):
        self.ref = ref

    def __getitem__(self, index):
        return self.ref[0:1, 0:1]


PARTS = 8
GATE, UP, DOWN, SHARED, QUERY, ZED, EX, OUT = range(PARTS)
KV_AT, B_AT, C_AT, MISC_AT = 0, LANES, 2 * LANES, 3 * LANES
SHARED_WIDTH = 4 * LANES


def chunk_order(widths):
    wide = 2 * LANES
    order = [(part, column, wide) for part in (GATE, UP, DOWN, OUT, QUERY) for column in range(0, widths[part], wide)]
    order += [(SHARED, column, LANES) for column in (KV_AT, B_AT, C_AT)]
    order += [(EX, column, wide) for column in range(0, widths[EX], wide)]
    order += [(SHARED, MISC_AT, LANES)]
    order += [(ZED, column, wide) for column in range(0, widths[ZED] - wide, wide)]
    order += [(ZED, column, LANES) for column in range(widths[ZED] - wide, widths[ZED], LANES)]
    return [item + ("P" if item[0] == SHARED or index % 2 else "Q",) for index, item in enumerate(order)]


SLOTS = 6
STAGE_AT = (0.0, 1.5, 3.0, 5.0, 7.0, 9.0, 11.0, 12.5, 14.0)


def unit_matrix(size):
    return jnp.where(row_ids((size, size)) == lane_ids((size, size)), 1.0, 0.0)


def turned_small(values):
    unit = unit_matrix(16).astype(BF16)
    total = None
    for term in pieces(values, 3):
        part = mm_nt(unit, term)
        total = part if total is None else total + part
    return total


def back_kernel(*refs, small_names, big_names, widths, width, pace):
    it = iter(refs)
    s = Names({name: next(it) for name in small_names})
    lens = [Entry(s.len0), Entry(s.len1)]
    big_in = Names({name: next(it) for name in big_names})
    dh2_peer, ff_peer = next(it), next(it)
    outs = [next(it) for _ in range(PARTS)]
    xout, grad_in, layer_out = next(it), next(it), next(it)
    b = Names({name: next(it) for name in big_names})
    (db, bs, bsr, da, dm, dq, dkv, dx, dz, dbc, dt, dh_own, dh_peer, dh_got, ff_got, wide, bcg, small, misc,
     acc, rc, res, ry, zin_p, zin_q, zmid, in_sem, out_sem, xs, xr, send_sem, recv_sem) = it
    rows = outs[GATE].shape[0]
    half, quarter = rows // 2, rows // 4
    seq_len = db.shape[0] // 2
    me = lax.axis_index("dp")
    core, y, z = me % 2, (me // 2) % 2, me // 4
    side = lax.axis_index("tensor")
    sibling = dict(dp=me + 1 - 2 * core)
    across = dict(dp=me + 2 - 4 * y)
    outer = dict(dp=(z + 1 - 2 * (z % 2)) * 4 + y * 2 + core)
    inner = dict(dp=(3 - z) * 4 + y * 2 + core)
    pair = dict(tensor=1 - side)
    is_mid = (z == 1) | (z == 2)
    is_end = (z == 0) | (z == 3)

    def at(offset, size):
        return pl.ds(pl.multiple_of(offset, quarter), size)

    mine, other = at(core * half, half), at((1 - core) * half, half)
    my_y, other_y = at(y * quarter, quarter), at((1 - y) * quarter, quarter)
    zq = jnp.where(z <= 1, 0, 1)
    my_z, other_z = at(zq * quarter, quarter), at((1 - zq) * quarter, quarter)

    loads = {}
    for index, name in enumerate(big_names):
        loads[name] = pltpu.make_async_copy(big_in[name], b[name], in_sem.at[index])
        loads[name].start()
    ready = set()

    def need(*names):
        for name in names:
            if name not in ready:
                loads[name].wait()
                ready.add(name)

    barrier = pltpu.get_barrier_semaphore()
    for device in (sibling, across, outer, pair):
        pl.semaphore_signal(barrier, inc=1, device_id=device, device_id_type=MESH)

    @pl.when(is_mid)
    def _():
        pl.semaphore_signal(barrier, inc=1, device_id=inner, device_id_type=MESH)
        pl.semaphore_wait(barrier, 5)

    @pl.when(is_end)
    def _():
        pl.semaphore_wait(barrier, 4)

    ends = []

    def remote(src, dst, send, recv, device):
        return pltpu.make_async_remote_copy(
            src_ref=src, dst_ref=dst, send_sem=send, recv_sem=recv, device_id=device, device_id_type=MESH
        )

    def exchange(src, dst, slot):
        copy = remote(src, dst, xs.at[slot], xr.at[slot], pair)
        copy.start()
        return copy

    def make(part, column, size, span):
        lanes = slice(column, column + size)
        if part == SHARED and column == MISC_AT:
            return misc[span, :].astype(F32)
        total = None
        for k in range(2):
            left, right = {
                GATE: ("h2t", "dg"), UP: ("h2t", "du"), DOWN: ("hid", "ct"), OUT: ("mix", db), SHARED: ("ht", dbc),
                QUERY: ("ht", dq), ZED: ("ht", dz), EX: ("ht", dx),
            }[part]
            need(f"{left}{k}")
            values = b[f"{left}{k}"][span, :]
            if isinstance(right, str):
                need(f"{right}{k}")
                right = b[f"{right}{k}"][:, lanes]
            elif part == SHARED:
                right = dkv[seq(k), :] if column == KV_AT else dbc[seq(k), column - LANES : column]
            else:
                right = right[seq(k), lanes]
            part_k = mm(values, right)
            total = part_k if total is None else total + part_k
        return total

    def add(dst, first, second):
        dst[...] = (first[...].astype(F32) + second[...].astype(F32)).astype(BF16)

    order = chunk_order(widths)
    starts = [sum(item[2] for item in order[:index]) for index in range(len(order))]
    made = set()
    sending = {}

    def chunk_steps(index):
        part, column, size, kind = order[index]
        start = starts[index]
        place = sum(item[2] for item in order[:index] if item[3] == kind)
        cols = slice(start, start + size)
        local = slice(column, column + size)
        tight = slice(place, place + size)
        out = outs[part]

        def own(src, dst, slot, device):
            return remote(src, dst, send_sem.at[slot, index], recv_sem.at[slot, index], device)

        source = acc.at[index % SLOTS, :, :size]
        to_core = own(source, rc.at[:, cols], 0, sibling)
        back_core = own(res.at[:, cols], out.at[mine, local], 6, sibling)
        wait_core = own(res.at[:, cols], out.at[other, local], 6, sibling)
        store = pltpu.make_async_copy(res.at[:, cols], out.at[mine, local], out_sem.at[index])

        def step0():
            assert part < SHARED or (part, column) in made
            if index - SLOTS in sending:
                sending.pop(index - SLOTS)()
            source[...] = make(part, column, size, other).astype(BF16)
            to_core.start()
            sending[index] = to_core.wait_send

        def merge_core():
            term = make(part, column, size, mine)
            to_core.wait_recv()
            rc[:, cols] = (rc[:, cols].astype(F32) + term).astype(BF16)

        def send_core():
            back_core.start()
            store.start()

        def last():
            wait_core.wait_recv()

        ends.append((None, back_core.wait_send))
        ends.append((None, store.wait))

        if kind == "P":
            zin = zin_p.at[:, tight]
            to_y = own(rc.at[other_y, cols], ry.at[:, cols], 1, across)
            to_mid = own(rc.at[my_y, cols], zin, 2, outer)
            swap = own(rc.at[my_y, cols], zmid.at[:, cols], 3, inner)
            to_end = own(res.at[my_y, cols], res.at[my_y, cols], 4, outer)
            back_y = own(res.at[my_y, cols], res.at[my_y, cols], 5, across)
            wait_y = own(res.at[my_y, cols], res.at[other_y, cols], 5, across)

            def step1():
                merge_core()
                to_y.start()
                ends.append((None, to_y.wait_send))

            def step2():
                to_y.wait_recv()
                add(rc.at[my_y, cols], rc.at[my_y, cols], ry.at[:, cols])
                pl.when(is_end)(to_mid.start)
                ends.append((is_end, to_mid.wait_send))

            def step3():
                @pl.when(is_mid)
                def _():
                    to_mid.wait_recv()
                    add(rc.at[my_y, cols], rc.at[my_y, cols], zin)
                    swap.start()

                ends.append((is_mid, swap.wait_send))

            def step4():
                @pl.when(is_mid)
                def _():
                    swap.wait_recv()
                    add(res.at[my_y, cols], rc.at[my_y, cols], zmid.at[:, cols])
                    to_end.start()
                    back_y.start()

                ends.append((is_mid, to_end.wait_send))

            def step5():
                @pl.when(is_end)
                def _():
                    to_end.wait_recv()
                    back_y.start()

                ends.append((None, back_y.wait_send))

            def step6():
                wait_y.wait_recv()
                send_core()

            steps = [step0, step1, step2, step3, step4, step5, step6, last]
            if part == SHARED:
                to_x = own(res.at[:, cols], xout.at[mine, local], 7, pair)
                x_core = own(xout.at[mine, local], xout.at[mine, local], 8, sibling)
                wait_x = own(xout.at[mine, local], xout.at[other, local], 8, sibling)

                def step6x():
                    step6()
                    to_x.start()
                    ends.append((None, to_x.wait_send))

                def step7x():
                    last()
                    to_x.wait_recv()
                    x_core.start()
                    ends.append((None, x_core.wait_send))

                steps[6:] = [step6x, step7x, wait_x.wait_recv]
            return steps

        zin = zin_q.at[:, tight]
        to_mid = own(rc.at[:, cols], zin, 1, outer)
        swap = own(rc.at[other_z, cols], zmid.at[:, cols], 2, inner)
        to_y = own(rc.at[my_z, cols], ry.at[:, cols], 3, across)
        to_inner = own(res.at[my_z, cols], res.at[my_z, cols], 4, inner)
        wait_inner = own(res.at[my_z, cols], res.at[other_z, cols], 4, inner)
        to_end = own(res.at[my_z, cols], res.at[my_z, cols], 5, outer)
        pass_end = own(res.at[other_z, cols], res.at[other_z, cols], 7, outer)

        def step1():
            merge_core()
            pl.when(is_end)(to_mid.start)
            ends.append((is_end, to_mid.wait_send))

        def step2():
            @pl.when(is_mid)
            def _():
                to_mid.wait_recv()
                add(rc.at[:, cols], rc.at[:, cols], zin)
                swap.start()

            ends.append((is_mid, swap.wait_send))

        def step3():
            @pl.when(is_mid)
            def _():
                swap.wait_recv()
                add(rc.at[my_z, cols], rc.at[my_z, cols], zmid.at[:, cols])
                to_y.start()

            ends.append((is_mid, to_y.wait_send))

        def step4():
            @pl.when(is_mid)
            def _():
                to_y.wait_recv()
                add(res.at[my_z, cols], rc.at[my_z, cols], ry.at[:, cols])
                to_inner.start()
                to_end.start()

            ends.append((is_mid, to_inner.wait_send))
            ends.append((is_mid, to_end.wait_send))

        def step5():
            @pl.when(is_mid)
            def _():
                wait_inner.wait_recv()
                pass_end.start()
                send_core()

            ends.append((is_mid, pass_end.wait_send))

        def step6():
            @pl.when(is_end)
            def _():
                to_end.wait_recv()
                pass_end.wait_recv()
                send_core()

        return [step0, step1, step2, step3, step4, step5, step6, last]

    plan = [
        (index + STAGE_AT[number], -number, index, step)
        for index in range(len(order))
        for number, step in enumerate(chunk_steps(index))
    ]
    plan.sort(key=lambda item: item[:3])
    clock, done = [0.0], [0]

    def tick(time=pace):
        clock[0] += time
        while done[0] < len(plan) and plan[done[0]][0] <= clock[0]:
            plan[done[0]][3]()
            done[0] += 1

    def seq(k):
        return pl.ds(k * seq_len, seq_len)

    got_second_norm = exchange(dh2_peer, dh_got, 4)
    tick(0.0)
    tick(1.3)
    tick(1.3)
    tick(1.3)
    need("dh2", "rhat", "ct0")
    got_second_norm.wait()
    model = grad_in.shape[1]
    d_second = b.dh2[...] + dh_got[...].astype(F32)
    scaled = d_second * s.gain2[...]
    rhat = b.rhat[...]
    mean = jnp.sum(scaled * rhat, axis=1, keepdims=True) / model
    d_resid = b.ct0[...].astype(F32) + s.inv2[...] * (scaled - rhat * mean)
    grad_in[...] = d_resid
    db[:seq_len, :] = d_resid.astype(BF16)
    norm_second = jnp.sum(d_second * rhat, axis=0, keepdims=True)
    got_db = exchange(db.at[:seq_len], db.at[seq_len:], 0)
    tick()

    def mix(k):
        need("wa", "ws", f"y{k}", f"x{k}", f"z{k}")
        mix_grad_kernel(
            db.at[seq(k)], b[f"y{k}"], b[f"x{k}"], b[f"z{k}"], s.cxw, s.cxb, s.skip, s.gain, b.wa,
            b.ws, da.at[k], dm.at[k], bs.at[k],
        )
        return exchange(bs.at[k], bsr.at[1 - k], 1 + k)

    def attend(k):
        need(f"q{k}", f"kd{k}", f"vd{k}")
        attend_back_kernel(
            lens[k], b[f"q{k}"], b[f"kd{k}"], b[f"vd{k}"], da.at[k], s.cos, s.sa, s.sb, dq.at[seq(k)],
            dkv.at[seq(k)],
        )

    def mixer(k, dh):
        need("wq", "wkv", "wz", "wx", "wb", "wc", f"bcp{k}", f"bc{k}")
        bs[k] = bs[k] + bsr[k]
        mixer_back_kernel(
            lens[k], dm.at[k], b[f"y{k}"], b[f"x{k}"], b[f"z{k}"], b[f"bcp{k}"], b[f"bc{k}"], s[f"tp{k}"],
            s[f"tpr{k}"], s[f"ss{k}"], bs.at[k], dq.at[seq(k)], dkv.at[seq(k)], b.wq, b.wkv, b.wz,
            b.wx, b.wb, b.wc, s.wt, s.cxw, s.cxb, s.cbw, s.cbb, s.bias, s.rate,
            s.bias_col, s.rate_col, s.skip, s.gain, dh, dx.at[seq(k)], dz.at[seq(k)],
            dbc.at[seq(k)], dt.at[k], wide.at[k], bcg.at[k], small.at[k], width=width, tick=tick,
        )
        tick()

    got_first = mix(0)
    tick()
    attend(0)
    tick()
    got_db.wait_recv()
    got_second = mix(1)
    tick()
    attend(1)
    tick()
    for part in (OUT, QUERY):
        made.update([(part, column) for column in range(0, widths[part], LANES)])
    made.add((SHARED, KV_AT))
    got_first.wait_recv()
    got_second.wait_recv()
    got_first.wait_send()
    got_second.wait_send()
    mixer(1, dh_peer)
    got_dh = exchange(dh_peer, dh_got, 3)
    got_ff = exchange(ff_peer, ff_got, 5)
    mixer(0, dh_own)
    for part in (ZED, EX):
        made.update([(part, column) for column in range(0, widths[part], LANES)])
    made.update([(SHARED, B_AT), (SHARED, C_AT)])
    misc_key = [item[:2] for item in order].index((SHARED, MISC_AT))
    tick(max(0.0, misc_key - 4 - clock[0]))
    got_dh.wait()
    d_first = dh_own[...] + dh_got[...].astype(F32)
    need("xhat")
    xhat = b.xhat[...]
    scaled = d_first * s.gain1[...]
    mean = jnp.sum(scaled * xhat, axis=1, keepdims=True) / model
    grad_in[...] += s.inv1[...] * (scaled - xhat * mean)
    norm = jnp.sum(d_first * xhat, axis=0, keepdims=True)
    wide_sum, bcg_sum, small_sum = wide[0] + wide[1], bcg[0] + bcg[1], small[0] + small[1]
    first_row = row_ids((8, model)) == 0
    second_row = row_ids((8, model)) == 1
    norms = jnp.where(first_row, norm, jnp.where(second_row, norm_second, 0.0))
    blocks = [array[:, i : i + LANES] for array in (wide_sum, bcg_sum) for i in range(0, array.shape[1], LANES)]
    blocks.append(jnp.concatenate([small_sum, jnp.zeros((8, LANES - 16), F32)], axis=1))
    blocks += [norms[:, i : i + LANES] for i in range(0, model, LANES)]
    if len(blocks) % 2:
        blocks.append(jnp.zeros((8, LANES), F32))
    misc[...] = jnp.zeros(misc.shape, BF16)
    misc[: 8 * len(blocks), :] = jnp.concatenate(blocks, axis=0).astype(BF16)
    need("ht0", "ht1")
    step_grad = turned_small(mm(b.ht0[...], dt[0]) + mm(b.ht1[...], dt[1])).astype(BF16)
    for i in range(0, model, LANES):
        place = 8 * len(blocks) + 16 * (i // LANES)
        misc[place : place + 16, :] = step_grad[:, i : i + LANES]
    made.add((SHARED, MISC_AT))
    tick(max(0.0, len(order) + 2 - clock[0]))
    got_ff.wait()
    need("ff")
    layer_out[...] = (b.ff[...] + ff_got[...].astype(F32)).astype(BF16)
    got_db.wait_send()
    tick(1e6)
    for wait in sending.values():
        wait()
    for devices, wait in ends:
        if devices is None:
            wait()
        else:
            pl.when(devices)(wait)


def back_call(smalls, bigs, dh2_peer, ff_peer, widths, width, pace=0.74):
    rows, (seq_len, model) = bigs["h2t0"].shape[0], dh2_peer.shape
    order = chunk_order(widths)
    columns = sum(item[2] for item in order)
    ones = sum(item[2] for item in order if item[3] == "P")
    count = len(order)
    half, quarter = rows // 2, rows // 4
    ssm_pad, att_pad = bigs["x0"].shape[1], bigs["q0"].shape[1]
    anywhere, vmem = pl.BlockSpec(memory_space=pl.ANY), pl.BlockSpec(memory_space=pltpu.VMEM)
    outs = [shaped((rows, w), BF16) for w in widths] + [shaped((rows, SHARED_WIDTH), BF16), shaped((seq_len, model))]
    outs.append(shaped((seq_len, model), BF16))
    scratch = [pltpu.VMEM(array.shape, array.dtype) for array in bigs.values()]
    both = 2 * seq_len
    scratch += [
        pltpu.VMEM((both, model), BF16),
        pltpu.VMEM((2, 16, seq_len), F32), pltpu.VMEM((2, 16, seq_len), F32),
        pltpu.VMEM((2, seq_len, att_pad), BF16), pltpu.VMEM((2, seq_len, ssm_pad), BF16),
        pltpu.VMEM((both, att_pad), BF16), pltpu.VMEM((both, LANES), BF16), pltpu.VMEM((both, ssm_pad), BF16),
        pltpu.VMEM((both, ssm_pad), BF16), pltpu.VMEM((both, 2 * STATE), BF16), pltpu.VMEM((2, seq_len, 16), BF16),
        pltpu.VMEM((seq_len, model), F32), pltpu.VMEM((seq_len, model), BF16), pltpu.VMEM((seq_len, model), BF16),
        pltpu.VMEM((seq_len, model), BF16),
        pltpu.VMEM((2, 8, ssm_pad), F32), pltpu.VMEM((2, 8, 2 * STATE), F32), pltpu.VMEM((2, 8, 16), F32),
        pltpu.VMEM((rows, LANES), BF16), pltpu.VMEM((SLOTS, half, 2 * LANES), BF16),
        pltpu.VMEM((half, columns), BF16), pltpu.VMEM((half, columns), BF16),
        pltpu.VMEM((quarter, columns), BF16), pltpu.VMEM((quarter, ones), BF16),
        pltpu.VMEM((half, columns - ones), BF16), pltpu.VMEM((quarter, columns), BF16),
        pltpu.SemaphoreType.DMA((len(bigs),)), pltpu.SemaphoreType.DMA((count,)),
        pltpu.SemaphoreType.DMA((6,)), pltpu.SemaphoreType.DMA((6,)),
        pltpu.SemaphoreType.DMA((9, count)), pltpu.SemaphoreType.DMA((9, count)),
    ]
    return pl.pallas_call(
        functools.partial(
            back_kernel, small_names=tuple(smalls), big_names=tuple(bigs), widths=tuple(widths), width=width,
            pace=pace,
        ),
        out_shape=outs,
        in_specs=[vmem] * len(smalls) + [anywhere] * (len(bigs) + 2),
        out_specs=[anywhere] * (PARTS + 1) + [vmem] * 2,
        scratch_shapes=scratch,
        compiler_params=pltpu.CompilerParams(
            collective_id=0, has_side_effects=True, vmem_limit_bytes=REDUCE_LIMIT
        ),
        name="back_and_reduce",
    )(*smalls.values(), *bigs.values(), dh2_peer, ff_peer)


FORMS = ("wt", "cxb", "cbb", "gain", "skip", "bias", "rate", "bias_col", "rate_col")


def write_forms(raw, forms):
    for form, source in ((forms.cxb, raw.cxb), (forms.cbb, raw.cbb), (forms.gain, raw.gain)):
        form[...] = source[...].reshape(form.shape)
    heads = raw.bias.shape[0]
    for form, column, values in (
        (forms.bias, forms.bias_col, raw.bias[...].reshape(1, heads)),
        (forms.rate, forms.rate_col, jnp.exp(raw.decay[...].reshape(1, heads))),
    ):
        form[...] = jnp.zeros(form.shape, F32)
        form[:, :heads] = values
        column[...] = jnp.sum(unit_matrix(16) * form[...], axis=1, keepdims=True)
    skip = raw.skip[...].reshape(1, heads)
    first = lane_ids((1, LANES)) < HEAD_DIM
    for pair in range(heads // 2):
        lanes = slice(pair * LANES, (pair + 1) * LANES)
        forms.skip[:, lanes] = jnp.where(first, skip[:, 2 * pair : 2 * pair + 1], skip[:, 2 * pair + 1 : 2 * pair + 2])
    chosen = jnp.where(row_ids((16, heads)) == lane_ids((16, heads)), 1.0, 0.0).astype(BF16)
    forms.wt[...] = mm(chosen, raw.step[...]).astype(BF16)


def turned_low(values):
    return values.astype(F32).T.astype(BF16)


def front_kernel(*refs, small_names, raw_names, big_names, out_names, tiny_names, width):
    it = iter(refs)
    len_ref = next(it)
    s = Names({name: next(it) for name in small_names})
    raw = Names({name: next(it) for name in raw_names})
    big_in = Names({name: next(it) for name in big_names})
    outs = Names({name: next(it) for name in out_names})
    tiny = Names({name: next(it) for name in tiny_names})
    b = Names({name: next(it) for name in big_names})
    o = Names({name: next(it) for name in out_names})
    (h, h2, att, ssm, hid, ssp, ssr, part_own, part_peer, part_got, in_sem, out_sem, xs, xr) = it
    seq_len, model = part_own.shape
    s.update({name: tiny[name] for name in FORMS})
    side = lax.axis_index("tensor")
    pair = dict(tensor=1 - side)
    loads = {}
    for index, name in enumerate(big_names):
        loads[name] = pltpu.make_async_copy(big_in[name], b[name], in_sem.at[index])
        loads[name].start()
    barrier = pltpu.get_barrier_semaphore()
    pl.semaphore_signal(barrier, inc=1, device_id=pair, device_id_type=MESH)
    pl.semaphore_wait(barrier, 1)
    ready, stores = set(), []

    def need(*names):
        for name in names:
            if name not in ready:
                loads[name].wait()
                ready.add(name)

    def emit(*names):
        for name in names:
            store = pltpu.make_async_copy(o[name], outs[name], out_sem.at[out_names.index(name)])
            store.start()
            stores.append(store)

    def exchange(src, dst, slot):
        copy = pltpu.make_async_remote_copy(
            src_ref=src, dst_ref=dst, send_sem=xs.at[slot], recv_sem=xr.at[slot], device_id=pair,
            device_id_type=MESH,
        )
        copy.start()
        return copy

    tiny.len0[...] = jnp.full((8, LANES), len_ref[0], jnp.int32)
    need("tok")
    x = b.tok[...].astype(F32)
    inv1 = lax.rsqrt(jnp.mean(x * x, axis=1, keepdims=True) + EPSILON)
    tiny.inv1[...] = inv1
    xhat = x * inv1
    o.xhat[...] = xhat
    h[0] = (xhat * s.gain1[...]).astype(BF16)
    got_h = exchange(h.at[0], h.at[1], 0)
    got_len = exchange(tiny.len0, tiny.len1, 1)
    emit("xhat")
    need("cot")
    cot = b.cot[...]
    o.ct0[...] = jnp.where(row_ids((seq_len, 1)) < len_ref[0], cot.astype(F32), 0.0).astype(BF16)
    emit("ct0")
    write_forms(raw, tiny)
    need("w_key", "w_value")
    key, value = b.w_key[...].astype(F32), b.w_value[...].astype(F32)
    key = jnp.where(side == 0, key, pltpu.roll(key, HEAD_DIM, 1))
    value = jnp.where(side == 0, pltpu.roll(value, HEAD_DIM, 1), value)
    o.wkv[...] = jnp.where(lane_ids(key.shape) < HEAD_DIM, key, value).astype(BF16)
    emit("wkv")

    def mixer(k):
        need("wz", "wx", "wb", "wc", "wq")
        mixer_forward_kernel(
            Entry(tiny[f"len{k}"]), h.at[k], b.wq, o.wkv, b.wz, b.wx, b.wb, b.wc, s.wt, s.cxw,
            s.cxb, s.cbw, s.cbb, s.bias, s.rate, s.bias_col, s.rate_col, s.skip, s.cos,
            s.sa, s.sb, o[f"q{k}"], o[f"kd{k}"], o[f"vd{k}"], o[f"z{k}"], o[f"x{k}"], o[f"bcp{k}"], o[f"bc{k}"],
            tiny[f"tp{k}"], tiny[f"tpr{k}"], o[f"y{k}"], ssp.at[k],
        )
        emit(f"q{k}", f"kd{k}", f"vd{k}", f"z{k}", f"x{k}", f"bcp{k}", f"bc{k}", f"y{k}")
        return exchange(ssp.at[k], ssr.at[1 - k], 2 + k)

    def attend(k):
        attend_kernel(Entry(tiny[f"len{k}"]), o[f"q{k}"], o[f"kd{k}"], o[f"vd{k}"], att.at[k])

    def project(k, part):
        need("wa", "ws")
        out_kernel(
            att.at[k], o[f"y{k}"], o[f"x{k}"], o[f"z{k}"], tiny[f"ss{k}"], s.cxw, s.cxb, s.skip, s.gain,
            b.wa, b.ws, part, ssm.at[k], width=width,
        )

    def turn_mix(k):
        width_att = att.shape[2]
        o[f"mix{k}"][:width_att, :] = turned_low(att[k])
        o[f"mix{k}"][width_att:, :] = turned_low(ssm[k])
        emit(f"mix{k}")

    def feed(k, base):
        need("wg", "wu", "wd")
        rows, ct = h2[k], o[f"ct{k}"][...]
        total = hid.shape[1]
        for first in range(0, total, 256):
            lanes = slice(first, min(first + 256, total))
            gate, up = mm(rows, b.wg[:, lanes]), mm(rows, b.wu[:, lanes])
            d_hidden = mm_nt(ct, b.wd[lanes, :]).astype(BF16).astype(F32)
            sg = sigmoid(gate)
            silu = gate * sg
            hidden = silu * up
            hid[:, lanes] = hidden.astype(BF16)
            o[f"hid{k}"][lanes, :] = hidden.T.astype(BF16)
            o[f"dg{k}"][:, lanes] = (d_hidden * up * (sg * (1.0 + gate * (1.0 - sg)))).astype(BF16)
            o[f"du{k}"][:, lanes] = (d_hidden * silu).astype(BF16)
        emit(f"dg{k}", f"du{k}", f"hid{k}")
        dh, ff = o["dh2" if k == 0 else "dh2p"], o["ff" if k == 0 else "ffp"]
        dh[...] = (mm_nt(o[f"dg{k}"][...], b.wg[...]) + mm_nt(o[f"du{k}"][...], b.wu[...])).astype(dh.dtype)
        ff_part = mm(hid[...], b.wd[...])
        ff[...] = (ff_part if base is None else ff_part + base).astype(ff.dtype)
        emit(*(("dh2", "ff") if k == 0 else ("dh2p", "ffp")))

    got_first = mixer(0)
    attend(0)
    o.ht0[...] = turned_low(h[0])
    emit("ht0")
    got_h.wait()
    got_len.wait()
    got_ct = exchange(o.ct0, o.ct1, 4)
    got_second = mixer(1)
    attend(1)
    got_first.wait()
    got_second.wait()
    for k in range(2):
        tiny[f"ss{k}"][...] = ssp[k] + ssr[k]
    project(1, part_peer)
    got_part = exchange(part_peer, part_got, 5)
    project(0, part_own)
    o.ht1[...] = turned_low(h[1])
    emit("ht1")
    turn_mix(0)
    turn_mix(1)
    got_part.wait()
    resid = b.tok[...].astype(F32) + part_own[...] + part_got[...].astype(F32)
    part_own[...] = resid
    inv2 = lax.rsqrt(jnp.mean(resid * resid, axis=1, keepdims=True) + EPSILON)
    tiny.inv2[...] = inv2
    rhat = resid * inv2
    o.rhat[...] = rhat
    h2[0] = (rhat * s.gain2[...]).astype(BF16)
    got_h2 = exchange(h2.at[0], h2.at[1], 6)
    emit("rhat")
    feed(0, part_own[...])
    o.h2t0[...] = turned_low(h2[0])
    emit("h2t0")
    got_ct.wait()
    emit("ct1")
    got_h2.wait()
    feed(1, None)
    o.h2t1[...] = turned_low(h2[1])
    emit("h2t1")
    for store in stores:
        store.wait()


def front_call(length, smalls, raw, bigs, width):
    seq_len, model = bigs["tok"].shape
    att_pad, ssm_pad, ff_width = bigs["wq"].shape[1], bigs["wz"].shape[1], bigs["wg"].shape[1]
    outs = dict(xhat=shaped((seq_len, model)), rhat=shaped((seq_len, model)))
    outs.update(dict(dh2=shaped((seq_len, model)), ff=shaped((seq_len, model))))
    outs.update(dict(dh2p=shaped((seq_len, model), BF16), ffp=shaped((seq_len, model), BF16)))
    outs["wkv"] = shaped((model, LANES), BF16)
    tiny = dict(inv1=shaped((seq_len, 1)), inv2=shaped((seq_len, 1)))
    tiny.update(dict(
        wt=shaped((16, model), BF16), cxb=shaped((1, ssm_pad)), cbb=shaped((1, 2 * STATE)),
        gain=shaped((1, ssm_pad)), skip=shaped((1, ssm_pad)), bias=shaped((1, 16)), rate=shaped((1, 16)),
        bias_col=shaped((16, 1)), rate_col=shaped((16, 1)),
    ))
    for k in range(2):
        outs.update({f"{name}{k}": shaped((seq_len, ssm_pad)) for name in ("x", "y", "z")})
        outs.update({
            f"q{k}": shaped((seq_len, att_pad), BF16), f"kd{k}": shaped((seq_len, LANES), BF16),
            f"vd{k}": shaped((seq_len, LANES), BF16), f"bcp{k}": shaped((seq_len, 2 * STATE)),
            f"bc{k}": shaped((seq_len, 2 * STATE), BF16), f"ct{k}": shaped((seq_len, model), BF16),
            f"dg{k}": shaped((seq_len, ff_width), BF16), f"du{k}": shaped((seq_len, ff_width), BF16),
            f"hid{k}": shaped((ff_width, seq_len), BF16), f"h2t{k}": shaped((model, seq_len), BF16),
            f"ht{k}": shaped((model, seq_len), BF16), f"mix{k}": shaped((att_pad + ssm_pad, seq_len), BF16),
        })
        tiny.update({
            f"tp{k}": shaped((seq_len, 16)), f"tpr{k}": shaped((16, seq_len)), f"ss{k}": shaped((16, seq_len)),
            f"len{k}": shaped((8, LANES), jnp.int32),
        })
    anywhere, vmem = pl.BlockSpec(memory_space=pl.ANY), pl.BlockSpec(memory_space=pltpu.VMEM)
    scratch = [pltpu.VMEM(array.shape, array.dtype) for array in list(bigs.values()) + list(outs.values())]
    scratch += [
        pltpu.VMEM((2, seq_len, model), BF16), pltpu.VMEM((2, seq_len, model), BF16),
        pltpu.VMEM((2, seq_len, att_pad), BF16), pltpu.VMEM((2, seq_len, ssm_pad), BF16),
        pltpu.VMEM((seq_len, ff_width), BF16), pltpu.VMEM((2, 16, seq_len), F32), pltpu.VMEM((2, 16, seq_len), F32),
        pltpu.VMEM((seq_len, model), F32), pltpu.VMEM((seq_len, model), BF16), pltpu.VMEM((seq_len, model), BF16),
        pltpu.SemaphoreType.DMA((len(bigs),)), pltpu.SemaphoreType.DMA((len(outs),)),
        pltpu.SemaphoreType.DMA((7,)), pltpu.SemaphoreType.DMA((7,)),
    ]
    results = pl.pallas_call(
        functools.partial(
            front_kernel, small_names=tuple(smalls), raw_names=tuple(raw), big_names=tuple(bigs), out_names=tuple(outs),
            tiny_names=tuple(tiny), width=width,
        ),
        out_shape=list(outs.values()) + list(tiny.values()),
        in_specs=[pl.BlockSpec(memory_space=pltpu.SMEM)] + [vmem] * (len(smalls) + len(raw)) + [anywhere] * len(bigs),
        out_specs=[anywhere] * len(outs) + [vmem] * len(tiny),
        scratch_shapes=scratch,
        compiler_params=pltpu.CompilerParams(
            collective_id=1, has_side_effects=True, vmem_limit_bytes=REDUCE_LIMIT
        ),
        name="front",
    )(length, *smalls.values(), *raw.values(), *bigs.values())
    return Names(zip(list(outs) + list(tiny), results))


def finish_kernel(own_ref, peer_ref, own_misc_ref, peer_misc_ref, *refs, split):
    step = pl.program_id(0)
    sums, refs = refs[:7], refs[7:]
    out_ref = sums[6]
    for source, target in zip(sums[:6], refs[:6]):
        target[...] = source[...].astype(F32)
    (att_ref, ssm_ref, key_ref, value_ref, b_ref, c_ref, stp_ref, cxw_ref, cxb_ref, cbw_ref, cbb_ref, bias_ref,
     decay_ref, skip_ref, sgain_ref, norm_ref, ffn_ref) = refs[6:]

    @pl.when(step < split)
    def _():
        att_ref[...] = out_ref[...].astype(F32)

    @pl.when(step >= split)
    def _():
        ssm_ref[...] = out_ref[...].astype(F32)

    even = lax.axis_index("tensor") == 0
    kv, kv_peer = own_ref[:, :LANES].astype(F32), peer_ref[:, :LANES].astype(F32)
    low, high = jnp.where(even, kv, kv_peer), jnp.where(even, kv_peer, kv)
    first = lane_ids(kv.shape) < HEAD_DIM
    key_ref[...] = jnp.where(first, low, pltpu.roll(high, HEAD_DIM, 1))
    value_ref[...] = jnp.where(first, pltpu.roll(low, HEAD_DIM, 1), high)
    for ref, column in ((b_ref, B_AT), (c_ref, C_AT)):
        lanes = slice(column, column + LANES)
        ref[...] = own_ref[:, lanes].astype(F32) + peer_ref[:, lanes].astype(F32)
    @pl.when(step == 0)
    def _():
        wide_blocks, model_blocks = cxw_ref.shape[1] // LANES, norm_ref.shape[0] // LANES
        mine = own_misc_ref[...].astype(F32)
        both = mine + peer_misc_ref[...].astype(F32)

        def rows(values, block, row, length=1):
            return values[8 * block + row : 8 * block + row + length]

        def flat(values, first, blocks, row):
            parts = [rows(values, first + block, row) for block in range(blocks)]
            return jnp.concatenate(parts, axis=1).reshape(blocks * LANES)

        for block in range(wide_blocks):
            cxw_ref[:, block * LANES : (block + 1) * LANES] = rows(mine, block, 0, 4)
        for block in range(2):
            cbw_ref[:, block * LANES : (block + 1) * LANES] = rows(both, wide_blocks + block, 0, 4)
        cxb_ref[...] = flat(mine, 0, wide_blocks, 4)
        sgain_ref[...] = flat(mine, 0, wide_blocks, 6)
        cbb_ref[...] = flat(both, wide_blocks, 2, 4)
        norm_ref[...] = flat(both, wide_blocks + 3, model_blocks, 0)
        ffn_ref[...] = flat(both, wide_blocks + 3, model_blocks, 1)
        heads = bias_ref.shape[0]
        for row, ref in enumerate((bias_ref, decay_ref, skip_ref)):
            ref[...] = rows(mine, wide_blocks + 2, row)[:, :heads].reshape(heads)
        place = mine.shape[0] - 16 * model_blocks
        for block in range(model_blocks):
            values = mine[place + 16 * block : place + 16 * block + 16]
            stp_ref[:, block * LANES : (block + 1) * LANES] = values[: stp_ref.shape[0]]


def finish_call(results, peer, att_width, heads):
    model, block = results[OUT].shape[0], 128
    ssm_pad = results[ZED].shape[1]
    shared = results[SHARED]
    misc_rows = 8 * (ssm_pad // LANES + 3 + model // LANES)
    misc_rows += -misc_rows % 16 + 16 * (model // LANES)
    sums = [results[part] for part in (GATE, UP, DOWN, QUERY, ZED, EX, OUT)]
    split = att_width // block

    def by_rows(width):
        return pl.BlockSpec((block, width), lambda i: (i, 0))

    def fixed(*shape):
        return pl.BlockSpec(shape, lambda i: (0,) * len(shape))

    misc = pl.BlockSpec((misc_rows, LANES), lambda i: (0, MISC_AT // LANES))
    shapes = [(model, part.shape[1]) for part in sums[:6]]
    specs = [by_rows(part.shape[1]) for part in sums[:6]]
    shapes += [(att_width, model), (model - att_width, model)]
    specs += [
        pl.BlockSpec((block, model), lambda i: (jnp.minimum(i, split - 1), 0)),
        pl.BlockSpec((block, model), lambda i: (jnp.maximum(i - split, 0), 0)),
    ]
    shapes += [(model, LANES)] * 4
    specs += [by_rows(LANES)] * 4
    tiny = [
        (heads, model), (4, ssm_pad), (ssm_pad,), (4, 2 * STATE), (2 * STATE,), (heads,), (heads,), (heads,), (ssm_pad,),
        (model,), (model,),
    ]
    shapes += tiny
    specs += [fixed(*shape) for shape in tiny]
    return pl.pallas_call(
        functools.partial(finish_kernel, split=split),
        grid=(model // block,),
        out_shape=[shaped(shape) for shape in shapes],
        in_specs=[by_rows(SHARED_WIDTH)] * 2 + [misc] * 2 + [by_rows(part.shape[1]) for part in sums],
        out_specs=specs,
        compiler_params=pltpu.CompilerParams(vmem_limit_bytes=VMEM_LIMIT),
        name="finish",
    )(shared, peer, shared, peer, *sums)


def shaped(shape, dtype=F32):
    return jax.ShapeDtypeStruct(shape, dtype)


def whole_call(kernel, outs, scalars, args, flops, name):
    specs = [pl.BlockSpec(memory_space=pltpu.SMEM)] * scalars
    specs += [pl.BlockSpec(memory_space=pltpu.VMEM)] * (len(args) - scalars)
    moved = sum(arg.size * arg.dtype.itemsize for arg in args)
    return pl.pallas_call(
        kernel,
        out_shape=outs,
        in_specs=specs,
        out_specs=[pl.BlockSpec(memory_space=pltpu.VMEM)] * len(outs),
        compiler_params=pltpu.CompilerParams(vmem_limit_bytes=VMEM_LIMIT),
        cost_estimate=pl.CostEstimate(flops=flops, bytes_accessed=moved, transcendentals=0),
        name=name,
    )(*args)


def pad_columns(values, width):
    return jnp.pad(values, ((0, 0), (0, width - values.shape[1]))) if width != values.shape[1] else values


def pad_rows(values, height):
    return jnp.pad(values, ((0, height - values.shape[0]), (0, 0))) if height != values.shape[0] else values


def contract_rows(left, right):
    return mm_tn(jnp.concatenate(left, axis=0), jnp.concatenate(right, axis=0))


def on_device(
    tokens, lengths, cotangent, norm_gain, w_query, w_key, w_value, w_gate_z, w_ssm_x, w_ssm_b, w_ssm_c,
    w_step, conv_x_weight, conv_x_bias, conv_bc_weight, conv_bc_bias, step_bias, decay_log, skip_gain,
    ssm_norm_gain, w_out_att, w_out_ssm, ffn_norm_gain, w_gate, w_up, w_down,
):
    seq_len, model = tokens.shape
    groups = lax.axis_size("tensor")
    position = lax.axis_index("tensor")
    att_width, ssm_width = w_query.shape[1], w_gate_z.shape[1]
    att_pad = -(-att_width // LANES) * LANES
    ssm_pad = -(-ssm_width // LANES) * LANES
    ssm_heads = ssm_width // SSM_DIM
    ssm_width_all = SSM_HEADS * SSM_DIM
    ff_width = w_gate.shape[1]

    def fetch(values, shift):
        return lax.ppermute(values, "tensor", [((i + shift) % groups, i) for i in range(groups)])

    def deliver(values, shift):
        return lax.ppermute(values, "tensor", [(i, (i + shift) % groups) for i in range(groups)])

    def gather(values):
        return [values] + [fetch(values, k) for k in range(1, groups)]

    def scatter_sum(own, others):
        total = own
        for k in range(1, groups):
            total = total + deliver(others[k - 1], k).astype(F32)
        return total

    kv_head = position * (att_width // HEAD_DIM) // (HEADS // KV_HEADS)
    w_kv = jnp.concatenate(
        [lax.dynamic_slice_in_dim(w, kv_head * HEAD_DIM, HEAD_DIM, 1) for w in (w_key, w_value)], axis=1
    )
    wq = pad_columns(w_query, att_pad)
    wz, wx = pad_columns(w_gate_z, ssm_pad), pad_columns(w_ssm_x, ssm_pad)
    wt = pad_rows(w_step.T, 16)
    wa, ws = pad_rows(w_out_att, att_pad), pad_rows(w_out_ssm, ssm_pad)
    cxw, cxb = pad_columns(conv_x_weight, ssm_pad), pad_columns(conv_x_bias[None], ssm_pad)
    cbb = conv_bc_bias[None]
    gain = pad_columns(ssm_norm_gain[None], ssm_pad)
    skip = pad_columns(jnp.repeat(skip_gain, SSM_DIM)[None], ssm_pad)
    bias = pad_columns(step_bias[None], 16)
    rate = pad_columns(jnp.exp(decay_log)[None], 16)
    bias_col, rate_col = bias.T, rate.T
    half = HEAD_DIM // 2
    freqs = np.float64(ROPE_BASE) ** (-np.arange(half) * 2.0 / HEAD_DIM)
    angles = np.arange(seq_len, dtype=np.float32)[:, None] * freqs.astype(np.float32)[None, :]
    cosine, sine = np.cos(angles.astype(np.float64)), np.sin(angles.astype(np.float64))
    cos_table = jnp.asarray(np.concatenate([cosine] * 4, axis=1), F32)
    sine_first = jnp.asarray(np.concatenate([-sine, 0.0 * sine] * 2, axis=1), F32)
    sine_second = jnp.asarray(np.concatenate([0.0 * sine, sine] * 2, axis=1), F32)

    if lax.axis_size("dp") == 16 and groups == 2:
        smalls = dict(
            cxw=conv_x_weight, cbw=conv_bc_weight, cos=cos_table, sa=sine_first, sb=sine_second,
            gain1=norm_gain[None], gain2=ffn_norm_gain[None],
        )
        raw = dict(
            cxb=conv_x_bias, cbb=conv_bc_bias, gain=ssm_norm_gain, skip=skip_gain,
            bias=step_bias, decay=decay_log, step=w_step.T,
        )
        bigs = dict(
            tok=tokens, cot=cotangent, w_key=w_key, w_value=w_value, wz=w_gate_z, wx=w_ssm_x,
            wb=w_ssm_b, wc=w_ssm_c, wq=w_query, wa=w_out_att, ws=w_out_ssm, wg=w_gate, wu=w_up,
            wd=w_down,
        )
        kept = front_call(lengths, smalls, raw, bigs, ssm_width_all)
        wq, wz, wx, wa, ws = w_query, w_gate_z, w_ssm_x, w_out_att, w_out_ssm
        for name in FORMS:
            smalls[name] = kept[name]

        def both(*names):
            return {f"{name}{k}": kept[f"{name}{k}"] for k in range(2) for name in names}

        smalls.update(both("tp", "tpr", "ss", "len"))
        smalls.update(dict(inv1=kept.inv1, inv2=kept.inv2))
        order = both("h2t", "dg")
        order.update(dict(dh2=kept.dh2, rhat=kept.rhat))
        order.update(both("du", "hid", "ct"))
        order.update(dict(wa=wa, ws=ws))
        order.update(both("y", "x", "z", "q", "kd", "vd"))
        order.update(dict(wq=wq, wkv=kept.wkv, wz=wz, wx=wx, wb=w_ssm_b, wc=w_ssm_c))
        order.update(both("bcp", "bc", "mix", "ht"))
        order.update(dict(xhat=kept.xhat, ff=kept.ff))
        widths = (ff_width, ff_width, model, SHARED_WIDTH, att_pad, ssm_pad, ssm_pad, model)
        results = back_call(smalls, order, kept.dh2p, kept.ffp, widths, ssm_width_all)
        peer, grad_input, layer_output = results[PARTS:]
        (grad_gate, grad_up, grad_down, grad_q, grad_z, grad_x, grad_att, grad_ssm, grad_key, grad_value, grad_b,
         grad_c, grad_step, grad_cxw, grad_cxb, grad_cbw, grad_cbb, grad_bias, grad_decay, grad_skip, grad_sgain,
         grad_norm_gain, grad_ffn_gain) = finish_call(results, peer, att_pad, ssm_heads)
        return (
            layer_output, grad_input, grad_norm_gain, grad_q, grad_key, grad_value, grad_z, grad_x, grad_b, grad_c,
            grad_step.T, grad_cxw, grad_cxb, grad_cbw, grad_cbb, grad_bias, grad_decay, grad_skip, grad_sgain, grad_att,
            grad_ssm, grad_ffn_gain, grad_gate, grad_up, grad_down,
        )

    inputs = tokens.astype(F32)
    inv1 = lax.rsqrt(jnp.mean(inputs * inputs, axis=1, keepdims=True) + EPSILON)
    h_own = (inputs * inv1 * norm_gain).astype(BF16)
    own_mask = jnp.arange(seq_len) < lengths[0]
    ct_own = jnp.where(own_mask[:, None], cotangent, jnp.zeros_like(cotangent))
    h_all = gather(h_own)
    len_all = gather(lax.optimization_barrier((lengths, h_own))[0])
    ct_all = gather(lax.optimization_barrier((ct_own, h_all[1]))[0] if groups > 1 else ct_own)

    def forward(k):
        outs = [
            shaped((seq_len, att_pad), BF16), shaped((seq_len, LANES), BF16), shaped((seq_len, LANES), BF16),
            shaped((seq_len, ssm_pad)), shaped((seq_len, ssm_pad)), shaped((seq_len, 2 * STATE)),
            shaped((seq_len, 2 * STATE), BF16), shaped((seq_len, 16)), shaped((16, seq_len)),
            shaped((seq_len, ssm_pad)), shaped((16, seq_len)),
        ]
        args = [
            len_all[k], h_all[k], wq, w_kv, wz, wx, w_ssm_b, w_ssm_c, wt, cxw, cxb, conv_bc_weight, cbb,
            bias, rate, bias_col, rate_col, skip, cos_table, sine_first, sine_second,
        ]
        return whole_call(mixer_forward_kernel, outs, 1, args, 8 * 10**9, "mixer_forward")

    def attend(k):
        q, kd, vd = kept[k][:3]
        return whole_call(
            attend_kernel, [shaped((seq_len, att_pad), BF16)], 1, [len_all[k], q, kd, vd], 2 * 10**9, "attend"
        )[0]

    kept = [forward(k) for k in range(groups)]
    squares_part = [one[10] for one in kept]
    squares = [squares_part[k] for k in range(groups)]
    for shift in range(1, groups):
        for k in range(groups):
            squares[k] = squares[k] + fetch(squares_part[(k - shift) % groups], shift)
    mix_att = [attend(k) for k in range(groups)]

    def project(k, dtype):
        q, kd, vd, z, x, bcp, bc, tp, tpr, y, _ = kept[k]
        return whole_call(
            functools.partial(out_kernel, width=ssm_width_all),
            [shaped((seq_len, model), dtype), shaped((seq_len, ssm_pad), BF16)],
            0,
            [mix_att[k], y, x, z, squares[k], cxw, cxb, skip, gain, wa, ws],
            4 * 10**9,
            "out_project",
        )

    projected = [project(k, F32 if k == 0 else BF16) for k in range(groups)]
    mix_ssm = [one[1] for one in projected]
    branch = scatter_sum(projected[0][0], [one[0] for one in projected[1:]])
    resid = inputs + branch
    inv2 = lax.rsqrt(jnp.mean(resid * resid, axis=1, keepdims=True) + EPSILON)
    h2_own = (resid * inv2 * ffn_norm_gain).astype(BF16)
    h2_all = gather(h2_own)

    def feed(k, rows2):
        dtype = F32 if k == 0 else BF16
        block = min(256, ff_width)
        full = pl.BlockSpec((seq_len, model), lambda i: (0, 0))
        columns = pl.BlockSpec((model, block), lambda i: (0, i))
        rows = pl.BlockSpec((block, model), lambda i: (i, 0))
        tall = pl.BlockSpec((seq_len, block), lambda i: (0, i))
        return pl.pallas_call(
            ffn_kernel,
            grid=(ff_width // block,),
            out_shape=[shaped((ff_width, seq_len), BF16)] + [shaped((seq_len, ff_width), BF16)] * 2
            + [shaped((seq_len, model), dtype)] * 2 + [shaped((model, seq_len), BF16)],
            in_specs=[full, full, columns, columns, rows] + ([full] if k == 0 else []),
            out_specs=[pl.BlockSpec((block, seq_len), lambda i: (i, 0))] + [tall] * 2 + [full] * 2
            + [pl.BlockSpec((model, seq_len), lambda i: (0, 0))],
            scratch_shapes=[pltpu.VMEM((seq_len, model), F32)] * 2,
            compiler_params=pltpu.CompilerParams(vmem_limit_bytes=VMEM_LIMIT),
            cost_estimate=pl.CostEstimate(flops=8 * 10**9, bytes_accessed=10**7, transcendentals=0),
            name="feed_forward",
        )(rows2, ct_all[k], w_gate, w_up, w_down, *([resid] if k == 0 else []))

    fed = [feed(0, h2_own)]
    for k in range(1, groups):
        fed.append(feed(k, lax.optimization_barrier((h2_all[k], fed[0][0]))[0]))
    d_second = scatter_sum(fed[0][4], [one[4] for one in fed[1:]])
    layer_output = scatter_sum(fed[0][3], [one[3] for one in fed[1:]]).astype(BF16)
    h2_turned = jnp.concatenate([one[5] for one in fed], axis=1)
    grad_gate = mm(h2_turned, jnp.concatenate([one[1] for one in fed], axis=0))
    grad_up = mm(h2_turned, jnp.concatenate([one[2] for one in fed], axis=0))
    grad_down = mm(jnp.concatenate([one[0] for one in fed], axis=1), jnp.concatenate(ct_all, axis=0))
    scaled = d_second * ffn_norm_gain
    d_resid = (
        ct_own.astype(F32)
        + inv2 * scaled
        - resid * (inv2**3) * jnp.mean(scaled * resid, axis=1, keepdims=True)
    )
    grad_ffn_gain = jnp.sum(d_second * resid * inv2, axis=0)
    db_all = gather(d_resid.astype(BF16))

    def mix_grad(k):
        q, kd, vd, z, x, bcp, bc, tp, tpr, y, _ = kept[k]
        return whole_call(
            mix_grad_kernel,
            [shaped((seq_len, att_pad), BF16), shaped((seq_len, ssm_pad), BF16), shaped((16, seq_len))],
            0,
            [db_all[k], y, x, z, cxw, cxb, skip, gain, wa, ws],
            4 * 10**9,
            "mix_grad",
        )

    mixed = [mix_grad(k) for k in range(groups)]
    backs_part = [one[2] for one in mixed]
    backs = [backs_part[k] for k in range(groups)]
    for shift in range(1, groups):
        for k in range(groups):
            backs[k] = backs[k] + fetch(backs_part[(k - shift) % groups], shift)

    def attend_back(k):
        q, kd, vd = kept[k][:3]
        return whole_call(
            attend_back_kernel,
            [shaped((seq_len, att_pad), BF16), shaped((seq_len, LANES), BF16)],
            1,
            [len_all[k], q, kd, vd, mixed[k][0], cos_table, sine_first, sine_second],
            4 * 10**9,
            "attend_back",
        )

    turned = [attend_back(k) for k in range(groups)]

    def backward(k):
        q, kd, vd, z, x, bcp, bc, tp, tpr, y, _ = kept[k]
        outs = [
            shaped((seq_len, model), F32 if k == 0 else BF16), shaped((seq_len, ssm_pad), BF16),
            shaped((seq_len, ssm_pad), BF16), shaped((seq_len, 2 * STATE), BF16), shaped((seq_len, 16), BF16),
            shaped((8, ssm_pad)), shaped((8, 2 * STATE)), shaped((8, 16)),
        ]
        args = [
            len_all[k], mixed[k][1], y, x, z, bcp, bc, tp, tpr, squares[k], backs[k], turned[k][0], turned[k][1],
            wq, w_kv, wz, wx, w_ssm_b, w_ssm_c, wt, cxw, cxb, conv_bc_weight, cbb, bias, rate, bias_col, rate_col,
            skip, gain,
        ]
        return whole_call(
            functools.partial(mixer_back_kernel, width=ssm_width_all), outs, 1, args, 16 * 10**9, "mixer_back"
        )

    gone = [None] * groups
    for k in list(range(1, groups)) + [0]:
        gone[k] = backward(k)
    d_first = scatter_sum(gone[0][0], [one[0] for one in gone[1:]])
    grad_norm_gain = jnp.sum(d_first * inputs * inv1, axis=0)

    wide, bcg, small = (sum(one[i] for one in gone) for i in (5, 6, 7))
    grad_q = contract_rows(h_all, [one[0] for one in turned])
    grad_kv = contract_rows(h_all, [one[1] for one in turned])
    grad_bc = contract_rows(h_all, [one[3] for one in gone])
    grad_x = contract_rows(h_all, [one[1] for one in gone])
    grad_z = contract_rows(h_all, [one[2] for one in gone])
    grad_step = contract_rows(h_all, [one[4] for one in gone])
    grad_att = contract_rows(mix_att, db_all)
    grad_ssm = contract_rows(mix_ssm, db_all)
    norms = jnp.concatenate([bcg[:5].reshape(-1), grad_norm_gain, grad_ffn_gain])
    zeros = jnp.zeros((model, KV_HEADS * HEAD_DIM), F32)
    grad_key = lax.dynamic_update_slice(zeros, grad_kv[:, :HEAD_DIM], (0, kv_head * HEAD_DIM))
    grad_value = lax.dynamic_update_slice(zeros, grad_kv[:, HEAD_DIM:], (0, kv_head * HEAD_DIM))
    grad_key, grad_value, grad_bc, norms = lax.psum((grad_key, grad_value, grad_bc, norms), ("dp", "tensor"))
    grad_b, grad_c = grad_bc[:, :STATE], grad_bc[:, STATE:]
    grad_q, grad_z, grad_x, grad_step, grad_att, grad_ssm, wide, small = (
        lax.psum(part.astype(BF16), "dp").astype(F32)
        for part in (grad_q, grad_z, grad_x, grad_step, grad_att, grad_ssm, wide, small)
    )
    grad_gate, grad_up, grad_down = (
        lax.psum(part.astype(BF16), "dp").astype(F32) for part in (grad_gate, grad_up, grad_down)
    )
    grad_step = grad_step[:, :ssm_heads]
    grad_cxw, grad_cxb, grad_sgain = wide[:4], wide[4:5], wide[6:7]
    bcg = norms[: 10 * STATE].reshape(5, 2 * STATE)
    grad_cbw, grad_cbb = bcg[:4], bcg[4:]
    grad_bias, grad_decay, grad_skip = small[0:1, :ssm_heads], small[1:2, :ssm_heads], small[2:3, :ssm_heads]
    grad_norm_gain = norms[10 * STATE : 10 * STATE + model]
    grad_ffn_gain = norms[10 * STATE + model :]

    scaled = d_first * norm_gain
    grad_input = d_resid + inv1 * scaled - inputs * (inv1**3) * jnp.mean(scaled * inputs, axis=1, keepdims=True)

    return (
        layer_output,
        grad_input,
        grad_norm_gain.reshape(-1),
        grad_q[:, :att_width],
        grad_key,
        grad_value,
        grad_z[:, :ssm_width],
        grad_x[:, :ssm_width],
        grad_b,
        grad_c,
        grad_step,
        grad_cxw[:, :ssm_width],
        grad_cxb.reshape(-1)[:ssm_width],
        grad_cbw,
        grad_cbb.reshape(-1),
        grad_bias.reshape(-1),
        grad_decay.reshape(-1),
        grad_skip.reshape(-1),
        grad_sgain.reshape(-1)[:ssm_width],
        grad_att[:att_width],
        grad_ssm[:ssm_width],
        grad_ffn_gain.reshape(-1),
        grad_gate,
        grad_up,
        grad_down,
    )


def solution(mesh):
    rows, split, tall = P(("dp", "tensor"), None), P(None, "tensor"), P("tensor", None)
    vector, copied = P("tensor"), P()
    return jax.shard_map(
        on_device,
        mesh=mesh,
        in_specs=(
            rows, P(("dp", "tensor")), rows, copied, split, copied, copied, split, split, copied, copied, split,
            split, vector, copied, copied, vector, vector, vector, vector, tall, tall, copied, split, split, tall,
        ),
        out_specs=(
            rows, rows, copied, split, copied, copied, split, split, copied, copied, split, split, vector, copied,
            copied, vector, vector, vector, vector, tall, tall, copied, split, split, tall,
        ),
        check_vma=False,
    )
```

```python
import functools

import jax
import jax.numpy as jnp
import numpy as np
from jax import lax
from jax.experimental import pallas as pl
from jax.experimental.pallas import tpu as pltpu
from jax.sharding import PartitionSpec as P

HEADS = 8
KV_HEADS = 2
HEAD_DIM = 64
SSM_HEADS = 24
SSM_DIM = 64
STATE = 128
SPAN = 128
LANES = 128

EPSILON = 1e-05
ROPE_BASE = 100000000000.0
F32 = jnp.float32
BF16 = jnp.bfloat16
VMEM_LIMIT = 62 * 1024 * 1024
REDUCE_LIMIT = 62 * 1024 * 1024
MESH = pl.DeviceIdType.MESH


def mm(left, right):
    return jnp.dot(left, right, preferred_element_type=F32)


def mm_nt(left, right):
    return lax.dot_general(left, right, (((1,), (1,)), ((), ())), preferred_element_type=F32)


def mm_tn(left, right):
    return lax.dot_general(left, right, (((0,), (0,)), ((), ())), preferred_element_type=F32)


def pieces(values, count):
    terms = []
    for _ in range(count):
        term = values.astype(BF16)
        terms.append(term)
        values = values - term.astype(F32)
    return terms


def sigmoid(values):
    return 1.0 / (1.0 + jnp.exp(-values))


def softplus(values):
    return jnp.maximum(values, 0.0) + jnp.log1p(jnp.exp(-jnp.abs(values)))


def lane_ids(shape):
    return lax.broadcasted_iota(jnp.int32, shape, 1)


def row_ids(shape):
    return lax.broadcasted_iota(jnp.int32, shape, 0)


def repeat_lanes(column, count):
    return jnp.concatenate([column] * count, axis=1) if count > 1 else column


def column_of(row):
    ones = jnp.where(row_ids((16, LANES)) == 0, 1.0, 0.0).astype(BF16)
    total = None
    for term in pieces(row, 3):
        part = mm_tn(term, ones)
        total = part if total is None else total + part
    return total


def row_sums(values):
    ones = jnp.ones((16, values.shape[1]), BF16)
    high, low = pieces(values, 2)
    return mm_nt(ones, high) + mm_nt(ones, low)


def causal_shift(values, steps):
    if steps == 0:
        return values
    rolled = pltpu.roll(values, steps, 0)
    return jnp.where(row_ids(values.shape) >= steps, rolled, 0.0)


def anti_shift(values, steps):
    if steps == 0:
        return values
    length = values.shape[0]
    rolled = pltpu.roll(values, length - steps, 0)
    return jnp.where(row_ids(values.shape) < length - steps, rolled, 0.0)


def conv(values, weight, bias):
    taps = weight.shape[0]
    total = bias + weight[taps - 1 : taps] * values
    for offset in range(taps - 1):
        total = total + weight[offset : offset + 1] * causal_shift(values, taps - 1 - offset)
    return total


def conv_back(grad, values, weight):
    taps = weight.shape[0]
    total, rows = None, []
    for offset in range(taps):
        steps = taps - 1 - offset
        moved = anti_shift(grad, steps)
        part = weight[offset : offset + 1] * moved
        total = part if total is None else total + part
        rows.append(jnp.sum(moved * values, axis=0, keepdims=True))
    rows.append(jnp.sum(grad, axis=0, keepdims=True))
    return total, rows


def rope(values, cosine, sine_first, sine_second):
    ahead = pltpu.roll(values, LANES - HEAD_DIM // 2, 1)
    behind = pltpu.roll(values, HEAD_DIM // 2, 1)
    return values * cosine + ahead * sine_first + behind * sine_second


def lower_mask():
    return row_ids((SPAN, SPAN)) >= lane_ids((SPAN, SPAN))


def span_sums(values):
    lower = jnp.where(lower_mask(), 1.0, 0.0).astype(BF16)
    out = []
    for start in range(0, values.shape[0], SPAN):
        total = None
        for term in pieces(values[start : start + SPAN], 3):
            part = mm(lower, term)
            total = part if total is None else total + part
        out.append(total)
    return jnp.concatenate(out, axis=0)


def span_sums_rows(values):
    upper = jnp.where(row_ids((SPAN, SPAN)) <= lane_ids((SPAN, SPAN)), 1.0, 0.0).astype(BF16)
    out = []
    for start in range(0, values.shape[1], SPAN):
        total = None
        for term in pieces(values[:, start : start + SPAN], 3):
            part = mm(term, upper)
            total = part if total is None else total + part
        out.append(total)
    return jnp.concatenate(out, axis=1)


def span_sums_back(values):
    upper = jnp.where(row_ids((SPAN, SPAN)) <= lane_ids((SPAN, SPAN)), 1.0, 0.0).astype(BF16)
    out = []
    for start in range(0, values.shape[0], SPAN):
        total = None
        for term in pieces(values[start : start + SPAN], 3):
            part = mm(upper, term)
            total = part if total is None else total + part
        out.append(total)
    return jnp.concatenate(out, axis=0)


def steps_of(tp, tp_row, bias, bias_col, rate, rate_col, length):
    seq_len = tp.shape[0]
    valid = jnp.where(row_ids((seq_len, 1)) < length, 1.0, 0.0)
    valid_row = jnp.where(lane_ids((1, seq_len)) < length, 1.0, 0.0)
    dt = softplus(tp + bias) * valid
    dt_row = softplus(tp_row + bias_col) * valid_row
    cum = span_sums(-(dt * rate))
    cum_row = span_sums_rows(-(dt_row * rate_col))
    return valid, dt, cum, cum_row


def spread(values, head):
    return jnp.broadcast_to(values[:, head : head + 1], (values.shape[0], LANES))


def decays(cum_first, cum_second, cum_row, pair, span):
    rows = slice(span * SPAN, (span + 1) * SPAN)
    lower = lower_mask()
    out = []
    for head, column in ((2 * pair, cum_first), (2 * pair + 1, cum_second)):
        differ = column[rows] - cum_row[head : head + 1, rows]
        out.append(jnp.exp(jnp.where(lower, differ, -1e30)))
    return out


def split_heads(values):
    first = lane_ids(values.shape) < HEAD_DIM
    zero = jnp.zeros_like(values)
    return jnp.concatenate([jnp.where(first, values, zero), jnp.where(first, zero, values)], axis=0)


def state_of(in_map, weighted_first, cum_pair_first):
    to_end = jnp.exp(cum_pair_first[SPAN - 1 : SPAN] - cum_pair_first)
    ending = (weighted_first * to_end).astype(BF16)
    return to_end, ending, mm_tn(in_map[:SPAN], ending)


def mixer_forward_kernel(
    len_ref, h_ref, wq_ref, wkv_ref, wz_ref, wx_ref, wb_ref, wc_ref, wt_ref, cxw_ref, cxb_ref,
    cbw_ref, cbb_ref, bias_ref, rate_ref, bias_col_ref, rate_col_ref, skip_ref, cos_ref, sa_ref,
    sb_ref, q_ref, kd_ref, vd_ref, z_ref, x_ref, bcp_ref, bc_ref, tp_ref, tpr_ref, y_ref, ss_ref,
):
    h = h_ref[...]
    pairs = wx_ref.shape[1] // LANES
    z_ref[...] = mm(h, wz_ref[...])
    x_ref[...] = mm(h, wx_ref[...])
    bcp_ref[:, :STATE] = mm(h, wb_ref[...])
    bcp_ref[:, STATE:] = mm(h, wc_ref[...])
    tp = mm_nt(h, wt_ref[...])
    tp_row = mm_nt(wt_ref[...], h)
    tp_ref[...] = tp
    tpr_ref[...] = tp_row
    cosine, sine_first, sine_second = cos_ref[...], sa_ref[...], sb_ref[...]
    for pair in range(wq_ref.shape[1] // LANES):
        lanes = slice(pair * LANES, (pair + 1) * LANES)
        q_ref[:, lanes] = rope(mm(h, wq_ref[:, lanes]), cosine, sine_first, sine_second).astype(BF16)
    kv = mm(h, wkv_ref[...])
    turned = pltpu.roll(kv, HEAD_DIM, 1)
    first = lane_ids(kv.shape) < HEAD_DIM
    kd_ref[...] = rope(jnp.where(first, kv, turned), cosine, sine_first, sine_second).astype(BF16)
    vd_ref[...] = jnp.where(first, turned, kv).astype(BF16)

    mapped = conv(bcp_ref[...], cbw_ref[...], cbb_ref[...])
    bc = (mapped * sigmoid(mapped)).astype(BF16)
    bc_ref[...] = bc
    in_map, out_map = bc[:, :STATE], bc[:, STATE:]
    affinity = [
        mm_nt(out_map[s * SPAN : (s + 1) * SPAN], in_map[s * SPAN : (s + 1) * SPAN]) for s in range(2)
    ]
    _, dt, cum, cum_row = steps_of(
        tp, tp_row, bias_ref[...], bias_col_ref[...], rate_ref[...], rate_col_ref[...], len_ref[0]
    )
    squares = None
    for pair in range(pairs):
        lanes = slice(pair * LANES, (pair + 1) * LANES)
        cx = conv(x_ref[:, lanes], cxw_ref[:, lanes], cxb_ref[:, lanes])
        xc = cx * sigmoid(cx)
        dt_pair = jnp.where(first, spread(dt, 2 * pair), spread(dt, 2 * pair + 1))
        cum_first, cum_second = spread(cum, 2 * pair), spread(cum, 2 * pair + 1)
        cum_pair = jnp.where(first, cum_first, cum_second)
        weighted = xc * dt_pair
        low = weighted.astype(BF16)
        _, _, state = state_of(in_map, weighted[:SPAN], cum_pair[:SPAN])
        parts = []
        for s in range(2):
            rows = slice(s * SPAN, (s + 1) * SPAN)
            mats = [
                (affinity[s] * decay).astype(BF16)
                for decay in decays(cum_first, cum_second, cum_row, pair, s)
            ]
            part = mm(jnp.concatenate(mats, axis=1), split_heads(low[rows]))
            if s:
                part = part + mm(out_map[rows], state.astype(BF16)) * jnp.exp(cum_pair[rows])
            parts.append(part)
        y = jnp.concatenate(parts, axis=0)
        y_ref[:, lanes] = y
        z = z_ref[:, lanes]
        gated = (y + skip_ref[:, lanes] * xc) * (z * sigmoid(z))
        square = gated * gated
        squares = square if squares is None else squares + square
    ss_ref[...] = row_sums(squares)


def masked_probs(queries, kd, length, scale):
    seq_len = kd.shape[0]
    scores = mm_nt(split_heads(queries), kd) * scale
    rows = row_ids(scores.shape)
    rows = jnp.where(rows >= seq_len, rows - seq_len, rows)
    padding = jnp.where(lane_ids((1, seq_len)) < length, 0.0, -1e30)
    scores = jnp.where(rows >= lane_ids(scores.shape), scores + padding, -1e30)
    weights = jnp.exp(scores - jnp.max(scores, axis=1, keepdims=True))
    return weights / jnp.sum(weights, axis=1, keepdims=True)


def attend_kernel(len_ref, q_ref, kd_ref, vd_ref, out_ref):
    seq_len = q_ref.shape[0]
    values = split_heads(vd_ref[...])
    for pair in range(q_ref.shape[1] // LANES):
        lanes = slice(pair * LANES, (pair + 1) * LANES)
        probs = masked_probs(q_ref[:, lanes], kd_ref[...], len_ref[0], HEAD_DIM ** (-0.5)).astype(BF16)
        both = jnp.concatenate([probs[:seq_len], probs[seq_len:]], axis=1)
        out_ref[:, lanes] = mm(both, values).astype(BF16)


def join_halves(values):
    return values + pltpu.roll(values, HEAD_DIM, 1)


def attend_back_kernel(len_ref, q_ref, kd_ref, vd_ref, da_ref, cos_ref, sa_ref, sb_ref, dq_ref, dkv_ref):
    seq_len = q_ref.shape[0]
    scale = HEAD_DIM ** (-0.5)
    cosine, sine_first, sine_second = cos_ref[...], -sa_ref[...], -sb_ref[...]
    kd, vd = kd_ref[...], vd_ref[...]
    keys = split_heads(kd)
    grad_k, grad_v = None, None
    for pair in range(q_ref.shape[1] // LANES):
        lanes = slice(pair * LANES, (pair + 1) * LANES)
        probs = masked_probs(q_ref[:, lanes], kd, len_ref[0], scale)
        da = split_heads(da_ref[:, lanes])
        dprob = mm_nt(da, vd)
        dscore = (probs * (dprob - jnp.sum(probs * dprob, axis=1, keepdims=True))).astype(BF16)
        both = jnp.concatenate([dscore[:seq_len], dscore[seq_len:]], axis=1)
        dq = mm(both, keys) * scale
        dq_ref[:, lanes] = rope(dq, cosine, sine_first, sine_second).astype(BF16)
        part_k = mm_tn(dscore, split_heads(q_ref[:, lanes]))
        part_v = mm_tn(probs.astype(BF16), da)
        grad_k = part_k if grad_k is None else grad_k + part_k
        grad_v = part_v if grad_v is None else grad_v + part_v
    dk = rope(join_halves(grad_k) * scale, cosine, sine_first, sine_second)
    first = lane_ids(dk.shape) < HEAD_DIM
    dkv_ref[...] = jnp.where(first, dk, join_halves(grad_v)).astype(BF16)


def out_kernel(att_ref, y_ref, x_ref, z_ref, ss_ref, cxw_ref, cxb_ref, skip_ref, gain_ref, wa_ref, ws_ref,
               part_ref, mix_ref, *, width, splits=1, send=lambda index, rows: None):
    inv = column_of(lax.rsqrt(ss_ref[...] / width + EPSILON))
    for pair in range(y_ref.shape[1] // LANES):
        lanes = slice(pair * LANES, (pair + 1) * LANES)
        cx = conv(x_ref[:, lanes], cxw_ref[:, lanes], cxb_ref[:, lanes])
        z = z_ref[:, lanes]
        gated = (y_ref[:, lanes] + skip_ref[:, lanes] * (cx * sigmoid(cx))) * (z * sigmoid(z))
        mix_ref[:, lanes] = (gated * inv * gain_ref[:, lanes]).astype(BF16)
    size = part_ref.shape[0] // splits
    for index in range(splits):
        rows = slice(index * size, (index + 1) * size)
        part = mm(att_ref[rows, :], wa_ref[...]) + mm(mix_ref[rows, :], ws_ref[...])
        part_ref[rows, :] = part.astype(part_ref.dtype)
        send(index, rows)


def mix_grad_kernel(db_ref, y_ref, x_ref, z_ref, cxw_ref, cxb_ref, skip_ref, gain_ref, wa_ref, ws_ref,
                    da_ref, dm_ref, bs_ref):
    db = db_ref[...]
    da_ref[...] = mm_nt(db, wa_ref[...]).astype(BF16)
    dm_ref[...] = mm_nt(db, ws_ref[...]).astype(BF16)
    total = None
    for pair in range(y_ref.shape[1] // LANES):
        lanes = slice(pair * LANES, (pair + 1) * LANES)
        cx = conv(x_ref[:, lanes], cxw_ref[:, lanes], cxb_ref[:, lanes])
        z = z_ref[:, lanes]
        gated = (y_ref[:, lanes] + skip_ref[:, lanes] * (cx * sigmoid(cx))) * (z * sigmoid(z))
        part = gated * (gain_ref[:, lanes] * dm_ref[:, lanes].astype(F32))
        total = part if total is None else total + part
    bs_ref[...] = row_sums(total)


def head_sums(values, pair):
    rows, columns = row_ids((LANES, 16)), lane_ids((LANES, 16))
    chosen = jnp.where(columns == 2 * pair + jnp.where(rows < HEAD_DIM, 0, 1), 1.0, 0.0).astype(BF16)
    high, low = pieces(values, 2)
    return mm(jnp.concatenate([high, low], axis=1), jnp.concatenate([chosen, chosen], axis=0))


def mixer_back_kernel(
    len_ref, dm_ref, y_ref, x_ref, z_ref, bcp_ref, bc_ref, tp_ref, tpr_ref, ss_ref, bs_ref, dq_ref,
    dkv_ref, wq_ref, wkv_ref, wz_ref, wx_ref, wb_ref, wc_ref, wt_ref, cxw_ref, cxb_ref, cbw_ref,
    cbb_ref, bias_ref, rate_ref, bias_col_ref, rate_col_ref, skip_ref, gain_ref,
    dh_ref, dx_ref, dz_ref, dbc_ref, dt_ref, wide_ref, bcg_ref, small_ref, *, width, tick=lambda: None,
):
    pairs = x_ref.shape[1] // LANES
    bc = bc_ref[...]
    in_map, out_map = bc[:, :STATE], bc[:, STATE:]
    affinity = [
        mm_nt(out_map[s * SPAN : (s + 1) * SPAN], in_map[s * SPAN : (s + 1) * SPAN]) for s in range(2)
    ]
    valid, dt, cum, cum_row = steps_of(
        tp_ref[...], tpr_ref[...], bias_ref[...], bias_col_ref[...], rate_ref[...], rate_col_ref[...], len_ref[0]
    )
    inv_row = lax.rsqrt(ss_ref[...] / width + EPSILON)
    inv = column_of(inv_row)
    back = column_of(inv_row * inv_row * inv_row * bs_ref[...] / width)
    first = lane_ids((x_ref.shape[0], LANES)) < HEAD_DIM
    last_row = row_ids((SPAN, LANES)) == SPAN - 1
    d_cum, d_step, d_skip = None, None, None
    wide_ref[7:8, :] = jnp.zeros((1, wide_ref.shape[1]), F32)
    d_aff, d_out, d_in = [None, None], None, None

    def plus(total, part):
        return part if total is None else total + part

    for pair in range(pairs):
        lanes = slice(pair * LANES, (pair + 1) * LANES)
        x = x_ref[:, lanes]
        cxw = cxw_ref[:, lanes]
        cx = conv(x, cxw, cxb_ref[:, lanes])
        sx = sigmoid(cx)
        xc = cx * sx
        z = z_ref[:, lanes]
        sz = sigmoid(z)
        silu_z = z * sz
        scanned = y_ref[:, lanes]
        y = scanned + skip_ref[:, lanes] * xc
        gated = y * silu_z
        d_mix = dm_ref[:, lanes].astype(F32)
        d_gated = inv * (gain_ref[:, lanes] * d_mix) - gated * back
        wide_ref[6:7, lanes] = jnp.sum(d_mix * gated * inv, axis=0, keepdims=True)
        dy = d_gated * silu_z
        dz_ref[:, lanes] = (d_gated * y * (sz * (1.0 + z * (1.0 - sz)))).astype(BF16)
        wide_ref[5:6, lanes] = jnp.sum(dy * xc, axis=0, keepdims=True)
        dt_pair = jnp.where(first, spread(dt, 2 * pair), spread(dt, 2 * pair + 1))
        cum_first, cum_second = spread(cum, 2 * pair), spread(cum, 2 * pair + 1)
        cum_pair = jnp.where(first, cum_first, cum_second)
        weighted = xc * dt_pair
        low = weighted.astype(BF16)
        dy_low = dy.astype(BF16)
        to_end, ending, state = state_of(in_map, weighted[:SPAN], cum_pair[:SPAN])
        d_weighted = []
        for s in range(2):
            rows = slice(s * SPAN, (s + 1) * SPAN)
            decay = decays(cum_first, cum_second, cum_row, pair, s)
            mats = jnp.concatenate([(affinity[s] * one).astype(BF16) for one in decay], axis=0)
            both = split_heads(dy_low[rows])
            d_mats = mm_nt(both, low[rows])
            d_aff[s] = plus(d_aff[s], d_mats[:SPAN] * decay[0] + d_mats[SPAN:] * decay[1])
            d_weighted.append(mm_tn(mats, both))
        reached = (dy[SPAN:] * jnp.exp(cum_pair[SPAN:])).astype(BF16)
        d_out = plus(d_out, mm_nt(reached, state.astype(BF16)))
        d_state = mm_tn(out_map[SPAN:], reached).astype(BF16)
        d_in = plus(d_in, mm_nt(ending, d_state))
        d_ending = mm(in_map[:SPAN], d_state)
        through = ending.astype(F32) * d_ending
        low_f, dy_f = low.astype(F32), dy_low.astype(F32)
        change = dy_f * scanned - low_f * jnp.concatenate(d_weighted, axis=0)
        ended = jnp.where(last_row, jnp.sum(through, axis=0, keepdims=True), 0.0) - through
        change = jnp.concatenate([change[:SPAN] + ended, change[SPAN:]], axis=0)
        d_weight = jnp.concatenate([d_weighted[0] + d_ending * to_end, d_weighted[1]], axis=0)
        d_cum = plus(d_cum, head_sums(change, pair))
        d_step = plus(d_step, head_sums(d_weight * xc, pair))
        d_xc = dy * skip_ref[:, lanes] + d_weight * dt_pair
        d_cx = d_xc * (sx * (1.0 + cx * (1.0 - sx)))
        d_x, rows_x = conv_back(d_cx, x, cxw)
        dx_ref[:, lanes] = d_x.astype(BF16)
        for index, row in enumerate(rows_x):
            wide_ref[index : index + 1, lanes] = row
        d_skip = plus(d_skip, head_sums(wide_ref[:, lanes], pair))
        tick()

    rate = rate_ref[...]
    d_log = span_sums_back(d_cum)
    d_dt = d_step - rate * d_log
    d_tp = d_dt * valid * sigmoid(tp_ref[...] + bias_ref[...])
    small_ref[...] = jnp.zeros(small_ref.shape, F32)
    small_ref[0:1, :] = jnp.sum(d_tp, axis=0, keepdims=True)
    small_ref[1:2, :] = -rate * jnp.sum(dt * d_log, axis=0, keepdims=True)
    small_ref[2:3, :] = d_skip[5:6]
    dt_ref[...] = d_tp.astype(BF16)

    d_maps = []
    low_aff = [part.astype(BF16) for part in d_aff]
    d_ins, d_outs = [], []
    for s in range(2):
        rows = slice(s * SPAN, (s + 1) * SPAN)
        d_outs.append(mm(low_aff[s], in_map[rows]))
        d_ins.append(mm_tn(low_aff[s], out_map[rows]))
    d_outs[1] = d_outs[1] + d_out
    d_ins[0] = d_ins[0] + d_in
    d_maps = jnp.concatenate(
        [jnp.concatenate(d_ins, axis=0), jnp.concatenate(d_outs, axis=0)], axis=1
    )
    mapped = conv(bcp_ref[...], cbw_ref[...], cbb_ref[...])
    sm = sigmoid(mapped)
    d_bc, rows_bc = conv_back(d_maps * (sm * (1.0 + mapped * (1.0 - sm))), bcp_ref[...], cbw_ref[...])
    bcg_ref[...] = jnp.zeros(bcg_ref.shape, F32)
    for index, row in enumerate(rows_bc):
        bcg_ref[index : index + 1, :] = row
    d_bc = d_bc.astype(BF16)
    dbc_ref[...] = d_bc
    total = mm_nt(dx_ref[...], wx_ref[...]) + mm_nt(dz_ref[...], wz_ref[...])
    total = total + mm_nt(dq_ref[...], wq_ref[...]) + mm_nt(dkv_ref[...], wkv_ref[...])
    total = total + mm_nt(d_bc[:, :STATE], wb_ref[...]) + mm_nt(d_bc[:, STATE:], wc_ref[...])
    total = total + mm(dt_ref[...], wt_ref[...])
    dh_ref[...] = total.astype(dh_ref.dtype)


def ffn_kernel(h_ref, ct_ref, wg_ref, wu_ref, wd_ref, *refs):
    base_ref = refs[0] if len(refs) == 9 else None
    hid_ref, dg_ref, du_ref, ff_ref, dh_ref, ht_ref, ff_acc, dh_acc = refs[-8:]
    step = pl.program_id(0)
    h = h_ref[...]
    gate = mm(h, wg_ref[...])
    up = mm(h, wu_ref[...])
    d_hidden = mm_nt(ct_ref[...], wd_ref[...]).astype(BF16).astype(F32)
    sg = sigmoid(gate)
    silu = gate * sg
    hidden = silu * up
    hid_ref[...] = hidden.T.astype(BF16)
    hidden = hidden.astype(BF16)
    d_gate = (d_hidden * up * (sg * (1.0 + gate * (1.0 - sg)))).astype(BF16)
    d_up = (d_hidden * silu).astype(BF16)
    dg_ref[...] = d_gate
    du_ref[...] = d_up
    ff_part = mm(hidden, wd_ref[...])
    dh_part = mm_nt(d_gate, wg_ref[...]) + mm_nt(d_up, wu_ref[...])

    @pl.when(step == 0)
    def _():
        ht_ref[...] = h.astype(F32).T.astype(BF16)
        ff_acc[...] = ff_part if base_ref is None else ff_part + base_ref[...]
        dh_acc[...] = dh_part

    @pl.when(step > 0)
    def _():
        ff_acc[...] += ff_part
        dh_acc[...] += dh_part

    @pl.when(step == pl.num_programs(0) - 1)
    def _():
        ff_ref[...] = ff_acc[...].astype(ff_ref.dtype)
        dh_ref[...] = dh_acc[...].astype(dh_ref.dtype)


class Names(dict):
    __getattr__ = dict.__getitem__


class Entry:
    def __init__(self, ref):
        self.ref = ref

    def __getitem__(self, index):
        return self.ref[0:1, 0:1]


PARTS = 8
GATE, UP, DOWN, SHARED, QUERY, ZED, EX, OUT = range(PARTS)
KV_AT, B_AT, C_AT, MISC_AT = 0, LANES, 2 * LANES, 3 * LANES
SHARED_WIDTH = 4 * LANES


def chunk_order(widths):
    wide = 2 * LANES
    order = [(part, column, wide) for part in (GATE, UP, DOWN, OUT, QUERY) for column in range(0, widths[part], wide)]
    order += [(SHARED, column, LANES) for column in (KV_AT, B_AT, C_AT)]
    order += [(EX, column, wide) for column in range(0, widths[EX], wide)]
    order += [(SHARED, MISC_AT, LANES)]
    order += [(ZED, column, wide) for column in range(0, widths[ZED] - wide, wide)]
    order += [(ZED, column, LANES) for column in range(widths[ZED] - wide, widths[ZED], LANES)]
    return [item + ("P" if item[0] == SHARED or index % 2 else "Q",) for index, item in enumerate(order)]


SLOTS = 6
STAGE_AT = (0.0, 1.5, 3.0, 5.0, 7.0, 9.0, 11.0, 12.5, 14.0)


def unit_matrix(size):
    return jnp.where(row_ids((size, size)) == lane_ids((size, size)), 1.0, 0.0)


def turned_small(values):
    unit = unit_matrix(16).astype(BF16)
    total = None
    for term in pieces(values, 3):
        part = mm_nt(unit, term)
        total = part if total is None else total + part
    return total


def back_kernel(*refs, small_names, big_names, widths, width, pace):
    it = iter(refs)
    s = Names({name: next(it) for name in small_names})
    lens = [Entry(s.len0), Entry(s.len1)]
    big_in = Names({name: next(it) for name in big_names})
    dh2_peer, ff_peer = next(it), next(it)
    outs = [next(it) for _ in range(PARTS)]
    xout, grad_in, layer_out = next(it), next(it), next(it)
    b = Names({name: next(it) for name in big_names})
    (db, bs, bsr, da, dm, dq, dkv, dx, dz, dbc, dt, dh_own, dh_peer, dh_got, ff_got, wide, bcg, small, misc,
     acc, rc, res, ry, zin_p, zin_q, zmid, in_sem, out_sem, xs, xr, send_sem, recv_sem) = it
    rows = outs[GATE].shape[0]
    half, quarter = rows // 2, rows // 4
    seq_len = db.shape[0] // 2
    me = lax.axis_index("dp")
    core, y, z = me % 2, (me // 2) % 2, me // 4
    side = lax.axis_index("tensor")
    sibling = dict(dp=me + 1 - 2 * core)
    across = dict(dp=me + 2 - 4 * y)
    outer = dict(dp=(z + 1 - 2 * (z % 2)) * 4 + y * 2 + core)
    inner = dict(dp=(3 - z) * 4 + y * 2 + core)
    pair = dict(tensor=1 - side)
    is_mid = (z == 1) | (z == 2)
    is_end = (z == 0) | (z == 3)

    def at(offset, size):
        return pl.ds(pl.multiple_of(offset, quarter), size)

    mine, other = at(core * half, half), at((1 - core) * half, half)
    my_y, other_y = at(y * quarter, quarter), at((1 - y) * quarter, quarter)
    zq = jnp.where(z <= 1, 0, 1)
    my_z, other_z = at(zq * quarter, quarter), at((1 - zq) * quarter, quarter)

    loads = {}
    for index, name in enumerate(big_names):
        loads[name] = pltpu.make_async_copy(big_in[name], b[name], in_sem.at[index])
        loads[name].start()
    ready = set()

    def need(*names):
        for name in names:
            if name not in ready:
                loads[name].wait()
                ready.add(name)

    barrier = pltpu.get_barrier_semaphore()
    for device in (sibling, across, outer, pair):
        pl.semaphore_signal(barrier, inc=1, device_id=device, device_id_type=MESH)

    @pl.when(is_mid)
    def _():
        pl.semaphore_signal(barrier, inc=1, device_id=inner, device_id_type=MESH)
        pl.semaphore_wait(barrier, 5)

    @pl.when(is_end)
    def _():
        pl.semaphore_wait(barrier, 4)

    ends = []

    def remote(src, dst, send, recv, device):
        return pltpu.make_async_remote_copy(
            src_ref=src, dst_ref=dst, send_sem=send, recv_sem=recv, device_id=device, device_id_type=MESH
        )

    def exchange(src, dst, slot):
        copy = remote(src, dst, xs.at[slot], xr.at[slot], pair)
        copy.start()
        return copy

    def make(part, column, size, span):
        lanes = slice(column, column + size)
        if part == SHARED and column == MISC_AT:
            return misc[span, :].astype(F32)
        total = None
        for k in range(2):
            left, right = {
                GATE: ("h2t", "dg"), UP: ("h2t", "du"), DOWN: ("hid", "ct"), OUT: ("mix", db), SHARED: ("ht", dbc),
                QUERY: ("ht", dq), ZED: ("ht", dz), EX: ("ht", dx),
            }[part]
            need(f"{left}{k}")
            values = b[f"{left}{k}"][span, :]
            if isinstance(right, str):
                need(f"{right}{k}")
                right = b[f"{right}{k}"][:, lanes]
            elif part == SHARED:
                right = dkv[seq(k), :] if column == KV_AT else dbc[seq(k), column - LANES : column]
            else:
                right = right[seq(k), lanes]
            part_k = mm(values, right)
            total = part_k if total is None else total + part_k
        return total

    def add(dst, first, second):
        dst[...] = (first[...].astype(F32) + second[...].astype(F32)).astype(BF16)

    order = chunk_order(widths)
    starts = [sum(item[2] for item in order[:index]) for index in range(len(order))]
    made = set()
    sending = {}

    def chunk_steps(index):
        part, column, size, kind = order[index]
        start = starts[index]
        place = sum(item[2] for item in order[:index] if item[3] == kind)
        cols = slice(start, start + size)
        local = slice(column, column + size)
        tight = slice(place, place + size)
        out = outs[part]

        def own(src, dst, slot, device):
            return remote(src, dst, send_sem.at[slot, index], recv_sem.at[slot, index], device)

        source = acc.at[index % SLOTS, :, :size]
        to_core = own(source, rc.at[:, cols], 0, sibling)
        back_core = own(res.at[:, cols], out.at[mine, local], 6, sibling)
        wait_core = own(res.at[:, cols], out.at[other, local], 6, sibling)
        store = pltpu.make_async_copy(res.at[:, cols], out.at[mine, local], out_sem.at[index])

        def step0():
            assert part < SHARED or (part, column) in made
            if index - SLOTS in sending:
                sending.pop(index - SLOTS)()
            source[...] = make(part, column, size, other).astype(BF16)
            to_core.start()
            sending[index] = to_core.wait_send

        def merge_core():
            term = make(part, column, size, mine)
            to_core.wait_recv()
            rc[:, cols] = (rc[:, cols].astype(F32) + term).astype(BF16)

        def send_core():
            back_core.start()
            store.start()

        def last():
            wait_core.wait_recv()

        ends.append((None, back_core.wait_send))
        ends.append((None, store.wait))

        if kind == "P":
            zin = zin_p.at[:, tight]
            to_y = own(rc.at[other_y, cols], ry.at[:, cols], 1, across)
            to_mid = own(rc.at[my_y, cols], zin, 2, outer)
            swap = own(rc.at[my_y, cols], zmid.at[:, cols], 3, inner)
            to_end = own(res.at[my_y, cols], res.at[my_y, cols], 4, outer)
            back_y = own(res.at[my_y, cols], res.at[my_y, cols], 5, across)
            wait_y = own(res.at[my_y, cols], res.at[other_y, cols], 5, across)

            def step1():
                merge_core()
                to_y.start()
                ends.append((None, to_y.wait_send))

            def step2():
                to_y.wait_recv()
                add(rc.at[my_y, cols], rc.at[my_y, cols], ry.at[:, cols])
                pl.when(is_end)(to_mid.start)
                ends.append((is_end, to_mid.wait_send))

            def step3():
                @pl.when(is_mid)
                def _():
                    to_mid.wait_recv()
                    add(rc.at[my_y, cols], rc.at[my_y, cols], zin)
                    swap.start()

                ends.append((is_mid, swap.wait_send))

            def step4():
                @pl.when(is_mid)
                def _():
                    swap.wait_recv()
                    add(res.at[my_y, cols], rc.at[my_y, cols], zmid.at[:, cols])
                    to_end.start()
                    back_y.start()

                ends.append((is_mid, to_end.wait_send))

            def step5():
                @pl.when(is_end)
                def _():
                    to_end.wait_recv()
                    back_y.start()

                ends.append((None, back_y.wait_send))

            def step6():
                wait_y.wait_recv()
                send_core()

            steps = [step0, step1, step2, step3, step4, step5, step6, last]
            if part == SHARED:
                to_x = own(res.at[:, cols], xout.at[mine, local], 7, pair)
                x_core = own(xout.at[mine, local], xout.at[mine, local], 8, sibling)
                wait_x = own(xout.at[mine, local], xout.at[other, local], 8, sibling)

                def step6x():
                    step6()
                    to_x.start()
                    ends.append((None, to_x.wait_send))

                def step7x():
                    last()
                    to_x.wait_recv()
                    x_core.start()
                    ends.append((None, x_core.wait_send))

                steps[6:] = [step6x, step7x, wait_x.wait_recv]
            return steps

        zin = zin_q.at[:, tight]
        to_mid = own(rc.at[:, cols], zin, 1, outer)
        swap = own(rc.at[other_z, cols], zmid.at[:, cols], 2, inner)
        to_y = own(rc.at[my_z, cols], ry.at[:, cols], 3, across)
        to_inner = own(res.at[my_z, cols], res.at[my_z, cols], 4, inner)
        wait_inner = own(res.at[my_z, cols], res.at[other_z, cols], 4, inner)
        to_end = own(res.at[my_z, cols], res.at[my_z, cols], 5, outer)
        pass_end = own(res.at[other_z, cols], res.at[other_z, cols], 7, outer)

        def step1():
            merge_core()
            pl.when(is_end)(to_mid.start)
            ends.append((is_end, to_mid.wait_send))

        def step2():
            @pl.when(is_mid)
            def _():
                to_mid.wait_recv()
                add(rc.at[:, cols], rc.at[:, cols], zin)
                swap.start()

            ends.append((is_mid, swap.wait_send))

        def step3():
            @pl.when(is_mid)
            def _():
                swap.wait_recv()
                add(rc.at[my_z, cols], rc.at[my_z, cols], zmid.at[:, cols])
                to_y.start()

            ends.append((is_mid, to_y.wait_send))

        def step4():
            @pl.when(is_mid)
            def _():
                to_y.wait_recv()
                add(res.at[my_z, cols], rc.at[my_z, cols], ry.at[:, cols])
                to_inner.start()
                to_end.start()

            ends.append((is_mid, to_inner.wait_send))
            ends.append((is_mid, to_end.wait_send))

        def step5():
            @pl.when(is_mid)
            def _():
                wait_inner.wait_recv()
                pass_end.start()
                send_core()

            ends.append((is_mid, pass_end.wait_send))

        def step6():
            @pl.when(is_end)
            def _():
                to_end.wait_recv()
                pass_end.wait_recv()
                send_core()

        return [step0, step1, step2, step3, step4, step5, step6, last]

    plan = [
        (index + STAGE_AT[number], -number, index, step)
        for index in range(len(order))
        for number, step in enumerate(chunk_steps(index))
    ]
    plan.sort(key=lambda item: item[:3])
    clock, done = [0.0], [0]

    def tick(time=pace):
        clock[0] += time
        while done[0] < len(plan) and plan[done[0]][0] <= clock[0]:
            plan[done[0]][3]()
            done[0] += 1

    def seq(k):
        return pl.ds(k * seq_len, seq_len)

    got_second_norm = exchange(dh2_peer, dh_got, 4)
    tick(0.0)
    tick(1.3)
    tick(1.3)
    tick(1.3)
    need("dh2", "rhat", "ct0")
    got_second_norm.wait()
    model = grad_in.shape[1]
    d_second = b.dh2[...] + dh_got[...].astype(F32)
    scaled = d_second * s.gain2[...]
    rhat = b.rhat[...]
    mean = jnp.sum(scaled * rhat, axis=1, keepdims=True) / model
    d_resid = b.ct0[...].astype(F32) + s.inv2[...] * (scaled - rhat * mean)
    grad_in[...] = d_resid
    db[:seq_len, :] = d_resid.astype(BF16)
    norm_second = jnp.sum(d_second * rhat, axis=0, keepdims=True)
    got_db = exchange(db.at[:seq_len], db.at[seq_len:], 0)
    tick()

    def mix(k):
        need("wa", "ws", f"y{k}", f"x{k}", f"z{k}")
        mix_grad_kernel(
            db.at[seq(k)], b[f"y{k}"], b[f"x{k}"], b[f"z{k}"], s.cxw, s.cxb, s.skip, s.gain, b.wa,
            b.ws, da.at[k], dm.at[k], bs.at[k],
        )
        return exchange(bs.at[k], bsr.at[1 - k], 1 + k)

    def attend(k):
        need(f"q{k}", f"kd{k}", f"vd{k}")
        attend_back_kernel(
            lens[k], b[f"q{k}"], b[f"kd{k}"], b[f"vd{k}"], da.at[k], s.cos, s.sa, s.sb, dq.at[seq(k)],
            dkv.at[seq(k)],
        )

    def mixer(k, dh):
        need("wq", "wkv", "wz", "wx", "wb", "wc", f"bcp{k}", f"bc{k}")
        bs[k] = bs[k] + bsr[k]
        mixer_back_kernel(
            lens[k], dm.at[k], b[f"y{k}"], b[f"x{k}"], b[f"z{k}"], b[f"bcp{k}"], b[f"bc{k}"], s[f"tp{k}"],
            s[f"tpr{k}"], s[f"ss{k}"], bs.at[k], dq.at[seq(k)], dkv.at[seq(k)], b.wq, b.wkv, b.wz,
            b.wx, b.wb, b.wc, s.wt, s.cxw, s.cxb, s.cbw, s.cbb, s.bias, s.rate,
            s.bias_col, s.rate_col, s.skip, s.gain, dh, dx.at[seq(k)], dz.at[seq(k)],
            dbc.at[seq(k)], dt.at[k], wide.at[k], bcg.at[k], small.at[k], width=width, tick=tick,
        )
        tick()

    got_first = mix(0)
    tick()
    attend(0)
    tick()
    got_db.wait_recv()
    got_second = mix(1)
    tick()
    attend(1)
    tick()
    for part in (OUT, QUERY):
        made.update([(part, column) for column in range(0, widths[part], LANES)])
    made.add((SHARED, KV_AT))
    got_first.wait_recv()
    got_second.wait_recv()
    got_first.wait_send()
    got_second.wait_send()
    mixer(1, dh_peer)
    got_dh = exchange(dh_peer, dh_got, 3)
    got_ff = exchange(ff_peer, ff_got, 5)
    mixer(0, dh_own)
    for part in (ZED, EX):
        made.update([(part, column) for column in range(0, widths[part], LANES)])
    made.update([(SHARED, B_AT), (SHARED, C_AT)])
    misc_key = [item[:2] for item in order].index((SHARED, MISC_AT))
    tick(max(0.0, misc_key - 4 - clock[0]))
    got_dh.wait()
    d_first = dh_own[...] + dh_got[...].astype(F32)
    need("xhat")
    xhat = b.xhat[...]
    scaled = d_first * s.gain1[...]
    mean = jnp.sum(scaled * xhat, axis=1, keepdims=True) / model
    grad_in[...] += s.inv1[...] * (scaled - xhat * mean)
    norm = jnp.sum(d_first * xhat, axis=0, keepdims=True)
    wide_sum, bcg_sum, small_sum = wide[0] + wide[1], bcg[0] + bcg[1], small[0] + small[1]
    first_row = row_ids((8, model)) == 0
    second_row = row_ids((8, model)) == 1
    norms = jnp.where(first_row, norm, jnp.where(second_row, norm_second, 0.0))
    blocks = [array[:, i : i + LANES] for array in (wide_sum, bcg_sum) for i in range(0, array.shape[1], LANES)]
    blocks.append(jnp.concatenate([small_sum, jnp.zeros((8, LANES - 16), F32)], axis=1))
    blocks += [norms[:, i : i + LANES] for i in range(0, model, LANES)]
    if len(blocks) % 2:
        blocks.append(jnp.zeros((8, LANES), F32))
    misc[...] = jnp.zeros(misc.shape, BF16)
    misc[: 8 * len(blocks), :] = jnp.concatenate(blocks, axis=0).astype(BF16)
    need("ht0", "ht1")
    step_grad = turned_small(mm(b.ht0[...], dt[0]) + mm(b.ht1[...], dt[1])).astype(BF16)
    for i in range(0, model, LANES):
        place = 8 * len(blocks) + 16 * (i // LANES)
        misc[place : place + 16, :] = step_grad[:, i : i + LANES]
    made.add((SHARED, MISC_AT))
    tick(max(0.0, len(order) + 2 - clock[0]))
    got_ff.wait()
    need("ff")
    layer_out[...] = (b.ff[...] + ff_got[...].astype(F32)).astype(BF16)
    got_db.wait_send()
    tick(1e6)
    for wait in sending.values():
        wait()
    for devices, wait in ends:
        if devices is None:
            wait()
        else:
            pl.when(devices)(wait)


def back_call(smalls, bigs, dh2_peer, ff_peer, widths, width, pace=0.74):
    rows, (seq_len, model) = bigs["h2t0"].shape[0], dh2_peer.shape
    order = chunk_order(widths)
    columns = sum(item[2] for item in order)
    ones = sum(item[2] for item in order if item[3] == "P")
    count = len(order)
    half, quarter = rows // 2, rows // 4
    ssm_pad, att_pad = bigs["x0"].shape[1], bigs["q0"].shape[1]
    anywhere, vmem = pl.BlockSpec(memory_space=pl.ANY), pl.BlockSpec(memory_space=pltpu.VMEM)
    outs = [shaped((rows, w), BF16) for w in widths] + [shaped((rows, SHARED_WIDTH), BF16), shaped((seq_len, model))]
    outs.append(shaped((seq_len, model), BF16))
    scratch = [pltpu.VMEM(array.shape, array.dtype) for array in bigs.values()]
    both = 2 * seq_len
    scratch += [
        pltpu.VMEM((both, model), BF16),
        pltpu.VMEM((2, 16, seq_len), F32), pltpu.VMEM((2, 16, seq_len), F32),
        pltpu.VMEM((2, seq_len, att_pad), BF16), pltpu.VMEM((2, seq_len, ssm_pad), BF16),
        pltpu.VMEM((both, att_pad), BF16), pltpu.VMEM((both, LANES), BF16), pltpu.VMEM((both, ssm_pad), BF16),
        pltpu.VMEM((both, ssm_pad), BF16), pltpu.VMEM((both, 2 * STATE), BF16), pltpu.VMEM((2, seq_len, 16), BF16),
        pltpu.VMEM((seq_len, model), F32), pltpu.VMEM((seq_len, model), BF16), pltpu.VMEM((seq_len, model), BF16),
        pltpu.VMEM((seq_len, model), BF16),
        pltpu.VMEM((2, 8, ssm_pad), F32), pltpu.VMEM((2, 8, 2 * STATE), F32), pltpu.VMEM((2, 8, 16), F32),
        pltpu.VMEM((rows, LANES), BF16), pltpu.VMEM((SLOTS, half, 2 * LANES), BF16),
        pltpu.VMEM((half, columns), BF16), pltpu.VMEM((half, columns), BF16),
        pltpu.VMEM((quarter, columns), BF16), pltpu.VMEM((quarter, ones), BF16),
        pltpu.VMEM((half, columns - ones), BF16), pltpu.VMEM((quarter, columns), BF16),
        pltpu.SemaphoreType.DMA((len(bigs),)), pltpu.SemaphoreType.DMA((count,)),
        pltpu.SemaphoreType.DMA((6,)), pltpu.SemaphoreType.DMA((6,)),
        pltpu.SemaphoreType.DMA((9, count)), pltpu.SemaphoreType.DMA((9, count)),
    ]
    return pl.pallas_call(
        functools.partial(
            back_kernel, small_names=tuple(smalls), big_names=tuple(bigs), widths=tuple(widths), width=width,
            pace=pace,
        ),
        out_shape=outs,
        in_specs=[vmem] * len(smalls) + [anywhere] * (len(bigs) + 2),
        out_specs=[anywhere] * (PARTS + 1) + [vmem] * 2,
        scratch_shapes=scratch,
        compiler_params=pltpu.CompilerParams(
            collective_id=0, has_side_effects=True, vmem_limit_bytes=REDUCE_LIMIT
        ),
        name="back_and_reduce",
    )(*smalls.values(), *bigs.values(), dh2_peer, ff_peer)


FORMS = ("wt", "cxb", "cbb", "gain", "skip", "bias", "rate", "bias_col", "rate_col")


def write_forms(raw, forms):
    for form, source in ((forms.cxb, raw.cxb), (forms.cbb, raw.cbb), (forms.gain, raw.gain)):
        form[...] = source[...].reshape(form.shape)
    heads = raw.bias.shape[0]
    for form, column, values in (
        (forms.bias, forms.bias_col, raw.bias[...].reshape(1, heads)),
        (forms.rate, forms.rate_col, jnp.exp(raw.decay[...].reshape(1, heads))),
    ):
        form[...] = jnp.zeros(form.shape, F32)
        form[:, :heads] = values
        column[...] = jnp.sum(unit_matrix(16) * form[...], axis=1, keepdims=True)
    skip = raw.skip[...].reshape(1, heads)
    first = lane_ids((1, LANES)) < HEAD_DIM
    for pair in range(heads // 2):
        lanes = slice(pair * LANES, (pair + 1) * LANES)
        forms.skip[:, lanes] = jnp.where(first, skip[:, 2 * pair : 2 * pair + 1], skip[:, 2 * pair + 1 : 2 * pair + 2])
    chosen = jnp.where(row_ids((16, heads)) == lane_ids((16, heads)), 1.0, 0.0).astype(BF16)
    forms.wt[...] = mm(chosen, raw.step[...]).astype(BF16)


def turned_low(values):
    return values.astype(F32).T.astype(BF16)


def front_kernel(*refs, small_names, raw_names, big_names, out_names, tiny_names, width):
    it = iter(refs)
    len_ref = next(it)
    s = Names({name: next(it) for name in small_names})
    raw = Names({name: next(it) for name in raw_names})
    big_in = Names({name: next(it) for name in big_names})
    outs = Names({name: next(it) for name in out_names})
    tiny = Names({name: next(it) for name in tiny_names})
    b = Names({name: next(it) for name in big_names})
    o = Names({name: next(it) for name in out_names})
    (h, h2, att, ssm, hid, dhid, ssp, ssr, part_own, part_peer, part_got, in_sem, out_sem, xs, xr) = it
    seq_len, model = part_own.shape
    s.update({name: tiny[name] for name in FORMS})
    side = lax.axis_index("tensor")
    pair = dict(tensor=1 - side)
    loads = {}
    for index, name in enumerate(big_names):
        loads[name] = pltpu.make_async_copy(big_in[name], b[name], in_sem.at[index])
        loads[name].start()
    barrier = pltpu.get_barrier_semaphore()
    pl.semaphore_signal(barrier, inc=1, device_id=pair, device_id_type=MESH)
    pl.semaphore_wait(barrier, 1)
    ready, stores = set(), []

    def need(*names):
        for name in names:
            if name not in ready:
                loads[name].wait()
                ready.add(name)

    def emit(*names):
        for name in names:
            store = pltpu.make_async_copy(o[name], outs[name], out_sem.at[out_names.index(name)])
            store.start()
            stores.append(store)

    def exchange(src, dst, slot):
        copy = pltpu.make_async_remote_copy(
            src_ref=src, dst_ref=dst, send_sem=xs.at[slot], recv_sem=xr.at[slot], device_id=pair,
            device_id_type=MESH,
        )
        copy.start()
        return copy

    tiny.len0[...] = jnp.full((8, LANES), len_ref[0], jnp.int32)
    need("tok")
    x = b.tok[...].astype(F32)
    inv1 = lax.rsqrt(jnp.mean(x * x, axis=1, keepdims=True) + EPSILON)
    tiny.inv1[...] = inv1
    xhat = x * inv1
    o.xhat[...] = xhat
    h[0] = (xhat * s.gain1[...]).astype(BF16)
    got_h = exchange(h.at[0], h.at[1], 0)
    got_len = exchange(tiny.len0, tiny.len1, 1)
    emit("xhat")
    need("cot")
    cot = b.cot[...]
    o.ct0[...] = jnp.where(row_ids((seq_len, 1)) < len_ref[0], cot.astype(F32), 0.0).astype(BF16)
    emit("ct0")
    write_forms(raw, tiny)
    need("w_key", "w_value")
    key, value = b.w_key[...].astype(F32), b.w_value[...].astype(F32)
    key = jnp.where(side == 0, key, pltpu.roll(key, HEAD_DIM, 1))
    value = jnp.where(side == 0, pltpu.roll(value, HEAD_DIM, 1), value)
    o.wkv[...] = jnp.where(lane_ids(key.shape) < HEAD_DIM, key, value).astype(BF16)
    emit("wkv")

    def mixer(k):
        need("wz", "wx", "wb", "wc", "wq")
        mixer_forward_kernel(
            Entry(tiny[f"len{k}"]), h.at[k], b.wq, o.wkv, b.wz, b.wx, b.wb, b.wc, s.wt, s.cxw,
            s.cxb, s.cbw, s.cbb, s.bias, s.rate, s.bias_col, s.rate_col, s.skip, s.cos,
            s.sa, s.sb, o[f"q{k}"], o[f"kd{k}"], o[f"vd{k}"], o[f"z{k}"], o[f"x{k}"], o[f"bcp{k}"], o[f"bc{k}"],
            tiny[f"tp{k}"], tiny[f"tpr{k}"], o[f"y{k}"], ssp.at[k],
        )
        emit(f"q{k}", f"kd{k}", f"vd{k}", f"z{k}", f"x{k}", f"bcp{k}", f"bc{k}", f"y{k}")
        return exchange(ssp.at[k], ssr.at[1 - k], 2 + k)

    def attend(k):
        attend_kernel(Entry(tiny[f"len{k}"]), o[f"q{k}"], o[f"kd{k}"], o[f"vd{k}"], att.at[k])

    def project(k, part, **split):
        need("wa", "ws")
        out_kernel(
            att.at[k], o[f"y{k}"], o[f"x{k}"], o[f"z{k}"], tiny[f"ss{k}"], s.cxw, s.cxb, s.skip, s.gain,
            b.wa, b.ws, part, ssm.at[k], width=width, **split,
        )

    def turn_mix(k):
        width_att = att.shape[2]
        o[f"mix{k}"][:width_att, :] = turned_low(att[k])
        o[f"mix{k}"][width_att:, :] = turned_low(ssm[k])
        emit(f"mix{k}")

    blocks = [slice(first, min(first + 256, hid.shape[1])) for first in range(0, hid.shape[1], 256)]

    def hidden_grad(k):
        need("wd")
        for lanes in blocks:
            dhid[k, :, lanes] = mm_nt(o[f"ct{k}"][...], b.wd[lanes, :]).astype(BF16)

    def feed(k, base):
        need("wg", "wu", "wd")
        values = h2[k]
        for lanes in blocks:
            gate, up = mm(values, b.wg[:, lanes]), mm(values, b.wu[:, lanes])
            d_hidden = dhid[k, :, lanes].astype(F32)
            sg = sigmoid(gate)
            silu = gate * sg
            hidden = silu * up
            hid[:, lanes] = hidden.astype(BF16)
            o[f"hid{k}"][lanes, :] = hidden.T.astype(BF16)
            o[f"dg{k}"][:, lanes] = (d_hidden * up * (sg * (1.0 + gate * (1.0 - sg)))).astype(BF16)
            o[f"du{k}"][:, lanes] = (d_hidden * silu).astype(BF16)
        emit(f"dg{k}", f"du{k}", f"hid{k}")
        dh, ff = (o.dh2, o.ff) if k == 0 else (o.dh2p, o.ffp)
        dh[...] = (mm_nt(o[f"dg{k}"][...], b.wg[...]) + mm_nt(o[f"du{k}"][...], b.wu[...])).astype(dh.dtype)
        ff_part = mm(hid[...], b.wd[...])
        ff[...] = (ff_part if base is None else ff_part + base).astype(ff.dtype)
        emit(*(("dh2", "ff") if k == 0 else ("dh2p", "ffp")))

    got_first = mixer(0)
    attend(0)
    o.ht0[...] = turned_low(h[0])
    emit("ht0")
    got_h.wait()
    got_len.wait()
    upper, lower = slice(0, seq_len // 2), slice(seq_len // 2, seq_len)
    got_ct = [exchange(o.ct0.at[upper], o.ct1.at[upper], 4)]
    got_second = mixer(1)
    got_ct.append(exchange(o.ct0.at[lower], o.ct1.at[lower], 9))
    attend(1)
    got_first.wait()
    got_second.wait()
    for k in range(2):
        tiny[f"ss{k}"][...] = ssp[k] + ssr[k]
    got_part = []

    def send_part(index, rows):
        got_part.append(exchange(part_peer.at[rows], part_got.at[rows], 5 + index))

    project(1, part_peer, splits=2, send=send_part)
    project(0, part_own)
    hidden_grad(0)
    got_h2, size = [], seq_len // 2
    for index in range(2):
        if index == 1:
            o.ht1[...] = turned_low(h[1])
            emit("ht1")
            turn_mix(0)
        rows = slice(index * size, (index + 1) * size)
        got_part[index].wait()
        resid = b.tok[rows, :].astype(F32) + part_own[rows, :] + part_got[rows, :].astype(F32)
        part_own[rows, :] = resid
        inv2 = lax.rsqrt(jnp.mean(resid * resid, axis=1, keepdims=True) + EPSILON)
        tiny.inv2[rows, :] = inv2
        rhat = resid * inv2
        o.rhat[rows, :] = rhat
        h2[0, rows, :] = (rhat * s.gain2[...]).astype(BF16)
        got_h2.append(exchange(h2.at[0, rows], h2.at[1, rows], 7 + index))
    emit("rhat")
    turn_mix(1)
    for copy in got_ct:
        copy.wait()
    emit("ct1")
    hidden_grad(1)
    feed(0, part_own[...])
    o.h2t0[...] = turned_low(h2[0])
    emit("h2t0")
    for copy in got_h2:
        copy.wait()
    feed(1, None)
    o.h2t1[...] = turned_low(h2[1])
    emit("h2t1")
    for store in stores:
        store.wait()


def front_call(length, smalls, raw, bigs, width):
    seq_len, model = bigs["tok"].shape
    att_pad, ssm_pad, ff_width = bigs["wq"].shape[1], bigs["wz"].shape[1], bigs["wg"].shape[1]
    outs = dict(xhat=shaped((seq_len, model)), rhat=shaped((seq_len, model)))
    outs.update(dict(dh2=shaped((seq_len, model)), ff=shaped((seq_len, model))))
    outs.update(dict(dh2p=shaped((seq_len, model), BF16), ffp=shaped((seq_len, model), BF16)))
    outs["wkv"] = shaped((model, LANES), BF16)
    tiny = dict(inv1=shaped((seq_len, 1)), inv2=shaped((seq_len, 1)))
    tiny.update(dict(
        wt=shaped((16, model), BF16), cxb=shaped((1, ssm_pad)), cbb=shaped((1, 2 * STATE)),
        gain=shaped((1, ssm_pad)), skip=shaped((1, ssm_pad)), bias=shaped((1, 16)), rate=shaped((1, 16)),
        bias_col=shaped((16, 1)), rate_col=shaped((16, 1)),
    ))
    for k in range(2):
        outs.update({f"{name}{k}": shaped((seq_len, ssm_pad)) for name in ("x", "y", "z")})
        outs.update({
            f"q{k}": shaped((seq_len, att_pad), BF16), f"kd{k}": shaped((seq_len, LANES), BF16),
            f"vd{k}": shaped((seq_len, LANES), BF16), f"bcp{k}": shaped((seq_len, 2 * STATE)),
            f"bc{k}": shaped((seq_len, 2 * STATE), BF16), f"ct{k}": shaped((seq_len, model), BF16),
            f"dg{k}": shaped((seq_len, ff_width), BF16), f"du{k}": shaped((seq_len, ff_width), BF16),
            f"hid{k}": shaped((ff_width, seq_len), BF16), f"h2t{k}": shaped((model, seq_len), BF16),
            f"ht{k}": shaped((model, seq_len), BF16), f"mix{k}": shaped((att_pad + ssm_pad, seq_len), BF16),
        })
        tiny.update({
            f"tp{k}": shaped((seq_len, 16)), f"tpr{k}": shaped((16, seq_len)), f"ss{k}": shaped((16, seq_len)),
            f"len{k}": shaped((8, LANES), jnp.int32),
        })
    anywhere, vmem = pl.BlockSpec(memory_space=pl.ANY), pl.BlockSpec(memory_space=pltpu.VMEM)
    scratch = [pltpu.VMEM(array.shape, array.dtype) for array in list(bigs.values()) + list(outs.values())]
    scratch += [
        pltpu.VMEM((2, seq_len, model), BF16), pltpu.VMEM((2, seq_len, model), BF16),
        pltpu.VMEM((2, seq_len, att_pad), BF16), pltpu.VMEM((2, seq_len, ssm_pad), BF16),
        pltpu.VMEM((seq_len, ff_width), BF16), pltpu.VMEM((2, seq_len, ff_width), BF16),
        pltpu.VMEM((2, 16, seq_len), F32), pltpu.VMEM((2, 16, seq_len), F32),
        pltpu.VMEM((seq_len, model), F32), pltpu.VMEM((seq_len, model), BF16), pltpu.VMEM((seq_len, model), BF16),
        pltpu.SemaphoreType.DMA((len(bigs),)), pltpu.SemaphoreType.DMA((len(outs),)),
        pltpu.SemaphoreType.DMA((10,)), pltpu.SemaphoreType.DMA((10,)),
    ]
    results = pl.pallas_call(
        functools.partial(
            front_kernel, small_names=tuple(smalls), raw_names=tuple(raw), big_names=tuple(bigs), out_names=tuple(outs),
            tiny_names=tuple(tiny), width=width,
        ),
        out_shape=list(outs.values()) + list(tiny.values()),
        in_specs=[pl.BlockSpec(memory_space=pltpu.SMEM)] + [vmem] * (len(smalls) + len(raw)) + [anywhere] * len(bigs),
        out_specs=[anywhere] * len(outs) + [vmem] * len(tiny),
        scratch_shapes=scratch,
        compiler_params=pltpu.CompilerParams(
            collective_id=1, has_side_effects=True, vmem_limit_bytes=REDUCE_LIMIT
        ),
        name="front",
    )(length, *smalls.values(), *raw.values(), *bigs.values())
    return Names(zip(list(outs) + list(tiny), results))


def finish_kernel(own_ref, peer_ref, own_misc_ref, peer_misc_ref, *refs, split):
    step = pl.program_id(0)
    sums, refs = refs[:7], refs[7:]
    out_ref = sums[6]
    for source, target in zip(sums[:6], refs[:6]):
        target[...] = source[...].astype(F32)
    (att_ref, ssm_ref, key_ref, value_ref, b_ref, c_ref, stp_ref, cxw_ref, cxb_ref, cbw_ref, cbb_ref, bias_ref,
     decay_ref, skip_ref, sgain_ref, norm_ref, ffn_ref) = refs[6:]

    @pl.when(step < split)
    def _():
        att_ref[...] = out_ref[...].astype(F32)

    @pl.when(step >= split)
    def _():
        ssm_ref[...] = out_ref[...].astype(F32)

    even = lax.axis_index("tensor") == 0
    kv, kv_peer = own_ref[:, :LANES].astype(F32), peer_ref[:, :LANES].astype(F32)
    low, high = jnp.where(even, kv, kv_peer), jnp.where(even, kv_peer, kv)
    first = lane_ids(kv.shape) < HEAD_DIM
    key_ref[...] = jnp.where(first, low, pltpu.roll(high, HEAD_DIM, 1))
    value_ref[...] = jnp.where(first, pltpu.roll(low, HEAD_DIM, 1), high)
    for ref, column in ((b_ref, B_AT), (c_ref, C_AT)):
        lanes = slice(column, column + LANES)
        ref[...] = own_ref[:, lanes].astype(F32) + peer_ref[:, lanes].astype(F32)
    @pl.when(step == 0)
    def _():
        wide_blocks, model_blocks = cxw_ref.shape[1] // LANES, norm_ref.shape[0] // LANES
        mine = own_misc_ref[...].astype(F32)
        both = mine + peer_misc_ref[...].astype(F32)

        def rows(values, block, row, length=1):
            return values[8 * block + row : 8 * block + row + length]

        def flat(values, first, blocks, row):
            parts = [rows(values, first + block, row) for block in range(blocks)]
            return jnp.concatenate(parts, axis=1).reshape(blocks * LANES)

        for block in range(wide_blocks):
            cxw_ref[:, block * LANES : (block + 1) * LANES] = rows(mine, block, 0, 4)
        for block in range(2):
            cbw_ref[:, block * LANES : (block + 1) * LANES] = rows(both, wide_blocks + block, 0, 4)
        cxb_ref[...] = flat(mine, 0, wide_blocks, 4)
        sgain_ref[...] = flat(mine, 0, wide_blocks, 6)
        cbb_ref[...] = flat(both, wide_blocks, 2, 4)
        norm_ref[...] = flat(both, wide_blocks + 3, model_blocks, 0)
        ffn_ref[...] = flat(both, wide_blocks + 3, model_blocks, 1)
        heads = bias_ref.shape[0]
        for row, ref in enumerate((bias_ref, decay_ref, skip_ref)):
            ref[...] = rows(mine, wide_blocks + 2, row)[:, :heads].reshape(heads)
        place = mine.shape[0] - 16 * model_blocks
        for block in range(model_blocks):
            values = mine[place + 16 * block : place + 16 * block + 16]
            stp_ref[:, block * LANES : (block + 1) * LANES] = values[: stp_ref.shape[0]]


def finish_call(results, peer, att_width, heads):
    model, block = results[OUT].shape[0], 256
    ssm_pad = results[ZED].shape[1]
    shared = results[SHARED]
    misc_rows = 8 * (ssm_pad // LANES + 3 + model // LANES)
    misc_rows += -misc_rows % 16 + 16 * (model // LANES)
    sums = [results[part] for part in (GATE, UP, DOWN, QUERY, ZED, EX, OUT)]
    split = att_width // block

    def by_rows(width):
        return pl.BlockSpec((block, width), lambda i: (i, 0))

    def fixed(*shape):
        return pl.BlockSpec(shape, lambda i: (0,) * len(shape))

    misc = pl.BlockSpec((misc_rows, LANES), lambda i: (0, MISC_AT // LANES))
    shapes = [(model, part.shape[1]) for part in sums[:6]]
    specs = [by_rows(part.shape[1]) for part in sums[:6]]
    shapes += [(att_width, model), (model - att_width, model)]
    specs += [
        pl.BlockSpec((block, model), lambda i: (jnp.minimum(i, split - 1), 0)),
        pl.BlockSpec((block, model), lambda i: (jnp.maximum(i - split, 0), 0)),
    ]
    shapes += [(model, LANES)] * 4
    specs += [by_rows(LANES)] * 4
    tiny = [
        (heads, model), (4, ssm_pad), (ssm_pad,), (4, 2 * STATE), (2 * STATE,), (heads,), (heads,), (heads,), (ssm_pad,),
        (model,), (model,),
    ]
    shapes += tiny
    specs += [fixed(*shape) for shape in tiny]
    return pl.pallas_call(
        functools.partial(finish_kernel, split=split),
        grid=(model // block,),
        out_shape=[shaped(shape) for shape in shapes],
        in_specs=[by_rows(SHARED_WIDTH)] * 2 + [misc] * 2 + [by_rows(part.shape[1]) for part in sums],
        out_specs=specs,
        compiler_params=pltpu.CompilerParams(vmem_limit_bytes=VMEM_LIMIT),
        name="finish",
    )(shared, peer, shared, peer, *sums)


def shaped(shape, dtype=F32):
    return jax.ShapeDtypeStruct(shape, dtype)


def whole_call(kernel, outs, scalars, args, flops, name):
    specs = [pl.BlockSpec(memory_space=pltpu.SMEM)] * scalars
    specs += [pl.BlockSpec(memory_space=pltpu.VMEM)] * (len(args) - scalars)
    moved = sum(arg.size * arg.dtype.itemsize for arg in args)
    return pl.pallas_call(
        kernel,
        out_shape=outs,
        in_specs=specs,
        out_specs=[pl.BlockSpec(memory_space=pltpu.VMEM)] * len(outs),
        compiler_params=pltpu.CompilerParams(vmem_limit_bytes=VMEM_LIMIT),
        cost_estimate=pl.CostEstimate(flops=flops, bytes_accessed=moved, transcendentals=0),
        name=name,
    )(*args)


def pad_columns(values, width):
    return jnp.pad(values, ((0, 0), (0, width - values.shape[1]))) if width != values.shape[1] else values


def pad_rows(values, height):
    return jnp.pad(values, ((0, height - values.shape[0]), (0, 0))) if height != values.shape[0] else values


def contract_rows(left, right):
    return mm_tn(jnp.concatenate(left, axis=0), jnp.concatenate(right, axis=0))


def on_device(
    tokens, lengths, cotangent, norm_gain, w_query, w_key, w_value, w_gate_z, w_ssm_x, w_ssm_b, w_ssm_c,
    w_step, conv_x_weight, conv_x_bias, conv_bc_weight, conv_bc_bias, step_bias, decay_log, skip_gain,
    ssm_norm_gain, w_out_att, w_out_ssm, ffn_norm_gain, w_gate, w_up, w_down,
):
    seq_len, model = tokens.shape
    groups = lax.axis_size("tensor")
    position = lax.axis_index("tensor")
    att_width, ssm_width = w_query.shape[1], w_gate_z.shape[1]
    att_pad = -(-att_width // LANES) * LANES
    ssm_pad = -(-ssm_width // LANES) * LANES
    ssm_heads = ssm_width // SSM_DIM
    ssm_width_all = SSM_HEADS * SSM_DIM
    ff_width = w_gate.shape[1]

    def fetch(values, shift):
        return lax.ppermute(values, "tensor", [((i + shift) % groups, i) for i in range(groups)])

    def deliver(values, shift):
        return lax.ppermute(values, "tensor", [(i, (i + shift) % groups) for i in range(groups)])

    def gather(values):
        return [values] + [fetch(values, k) for k in range(1, groups)]

    def scatter_sum(own, others):
        total = own
        for k in range(1, groups):
            total = total + deliver(others[k - 1], k).astype(F32)
        return total

    kv_head = position * (att_width // HEAD_DIM) // (HEADS // KV_HEADS)
    w_kv = jnp.concatenate(
        [lax.dynamic_slice_in_dim(w, kv_head * HEAD_DIM, HEAD_DIM, 1) for w in (w_key, w_value)], axis=1
    )
    wq = pad_columns(w_query, att_pad)
    wz, wx = pad_columns(w_gate_z, ssm_pad), pad_columns(w_ssm_x, ssm_pad)
    wt = pad_rows(w_step.T, 16)
    wa, ws = pad_rows(w_out_att, att_pad), pad_rows(w_out_ssm, ssm_pad)
    cxw, cxb = pad_columns(conv_x_weight, ssm_pad), pad_columns(conv_x_bias[None], ssm_pad)
    cbb = conv_bc_bias[None]
    gain = pad_columns(ssm_norm_gain[None], ssm_pad)
    skip = pad_columns(jnp.repeat(skip_gain, SSM_DIM)[None], ssm_pad)
    bias = pad_columns(step_bias[None], 16)
    rate = pad_columns(jnp.exp(decay_log)[None], 16)
    bias_col, rate_col = bias.T, rate.T
    half = HEAD_DIM // 2
    freqs = np.float64(ROPE_BASE) ** (-np.arange(half) * 2.0 / HEAD_DIM)
    angles = np.arange(seq_len, dtype=np.float32)[:, None] * freqs.astype(np.float32)[None, :]
    cosine, sine = np.cos(angles.astype(np.float64)), np.sin(angles.astype(np.float64))
    cos_table = jnp.asarray(np.concatenate([cosine] * 4, axis=1), F32)
    sine_first = jnp.asarray(np.concatenate([-sine, 0.0 * sine] * 2, axis=1), F32)
    sine_second = jnp.asarray(np.concatenate([0.0 * sine, sine] * 2, axis=1), F32)

    if lax.axis_size("dp") == 16 and groups == 2:
        smalls = dict(
            cxw=conv_x_weight, cbw=conv_bc_weight, cos=cos_table, sa=sine_first, sb=sine_second,
            gain1=norm_gain[None], gain2=ffn_norm_gain[None],
        )
        raw = dict(
            cxb=conv_x_bias, cbb=conv_bc_bias, gain=ssm_norm_gain, skip=skip_gain,
            bias=step_bias, decay=decay_log, step=w_step.T,
        )
        bigs = dict(
            tok=tokens, cot=cotangent, w_key=w_key, w_value=w_value, wz=w_gate_z, wx=w_ssm_x,
            wb=w_ssm_b, wc=w_ssm_c, wq=w_query, wa=w_out_att, ws=w_out_ssm, wg=w_gate, wu=w_up,
            wd=w_down,
        )
        kept = front_call(lengths, smalls, raw, bigs, ssm_width_all)
        wq, wz, wx, wa, ws = w_query, w_gate_z, w_ssm_x, w_out_att, w_out_ssm
        for name in FORMS:
            smalls[name] = kept[name]

        def both(*names):
            return {f"{name}{k}": kept[f"{name}{k}"] for k in range(2) for name in names}

        smalls.update(both("tp", "tpr", "ss", "len"))
        smalls.update(dict(inv1=kept.inv1, inv2=kept.inv2))
        order = both("h2t", "dg")
        order.update(dict(dh2=kept.dh2, rhat=kept.rhat))
        order.update(both("du", "hid", "ct"))
        order.update(dict(wa=wa, ws=ws))
        order.update(both("y", "x", "z", "q", "kd", "vd"))
        order.update(dict(wq=wq, wkv=kept.wkv, wz=wz, wx=wx, wb=w_ssm_b, wc=w_ssm_c))
        order.update(both("bcp", "bc", "mix", "ht"))
        order.update(dict(xhat=kept.xhat, ff=kept.ff))
        widths = (ff_width, ff_width, model, SHARED_WIDTH, att_pad, ssm_pad, ssm_pad, model)
        results = back_call(smalls, order, kept.dh2p, kept.ffp, widths, ssm_width_all)
        peer, grad_input, layer_output = results[PARTS:]
        (grad_gate, grad_up, grad_down, grad_q, grad_z, grad_x, grad_att, grad_ssm, grad_key, grad_value, grad_b,
         grad_c, grad_step, grad_cxw, grad_cxb, grad_cbw, grad_cbb, grad_bias, grad_decay, grad_skip, grad_sgain,
         grad_norm_gain, grad_ffn_gain) = finish_call(results, peer, att_pad, ssm_heads)
        return (
            layer_output, grad_input, grad_norm_gain, grad_q, grad_key, grad_value, grad_z, grad_x, grad_b, grad_c,
            grad_step.T, grad_cxw, grad_cxb, grad_cbw, grad_cbb, grad_bias, grad_decay, grad_skip, grad_sgain, grad_att,
            grad_ssm, grad_ffn_gain, grad_gate, grad_up, grad_down,
        )

    inputs = tokens.astype(F32)
    inv1 = lax.rsqrt(jnp.mean(inputs * inputs, axis=1, keepdims=True) + EPSILON)
    h_own = (inputs * inv1 * norm_gain).astype(BF16)
    own_mask = jnp.arange(seq_len) < lengths[0]
    ct_own = jnp.where(own_mask[:, None], cotangent, jnp.zeros_like(cotangent))
    h_all = gather(h_own)
    len_all = gather(lax.optimization_barrier((lengths, h_own))[0])
    ct_all = gather(lax.optimization_barrier((ct_own, h_all[1]))[0] if groups > 1 else ct_own)

    def forward(k):
        outs = [
            shaped((seq_len, att_pad), BF16), shaped((seq_len, LANES), BF16), shaped((seq_len, LANES), BF16),
            shaped((seq_len, ssm_pad)), shaped((seq_len, ssm_pad)), shaped((seq_len, 2 * STATE)),
            shaped((seq_len, 2 * STATE), BF16), shaped((seq_len, 16)), shaped((16, seq_len)),
            shaped((seq_len, ssm_pad)), shaped((16, seq_len)),
        ]
        args = [
            len_all[k], h_all[k], wq, w_kv, wz, wx, w_ssm_b, w_ssm_c, wt, cxw, cxb, conv_bc_weight, cbb,
            bias, rate, bias_col, rate_col, skip, cos_table, sine_first, sine_second,
        ]
        return whole_call(mixer_forward_kernel, outs, 1, args, 8 * 10**9, "mixer_forward")

    def attend(k):
        q, kd, vd = kept[k][:3]
        return whole_call(
            attend_kernel, [shaped((seq_len, att_pad), BF16)], 1, [len_all[k], q, kd, vd], 2 * 10**9, "attend"
        )[0]

    kept = [forward(k) for k in range(groups)]
    squares_part = [one[10] for one in kept]
    squares = [squares_part[k] for k in range(groups)]
    for shift in range(1, groups):
        for k in range(groups):
            squares[k] = squares[k] + fetch(squares_part[(k - shift) % groups], shift)
    mix_att = [attend(k) for k in range(groups)]

    def project(k, dtype):
        q, kd, vd, z, x, bcp, bc, tp, tpr, y, _ = kept[k]
        return whole_call(
            functools.partial(out_kernel, width=ssm_width_all),
            [shaped((seq_len, model), dtype), shaped((seq_len, ssm_pad), BF16)],
            0,
            [mix_att[k], y, x, z, squares[k], cxw, cxb, skip, gain, wa, ws],
            4 * 10**9,
            "out_project",
        )

    projected = [project(k, F32 if k == 0 else BF16) for k in range(groups)]
    mix_ssm = [one[1] for one in projected]
    branch = scatter_sum(projected[0][0], [one[0] for one in projected[1:]])
    resid = inputs + branch
    inv2 = lax.rsqrt(jnp.mean(resid * resid, axis=1, keepdims=True) + EPSILON)
    h2_own = (resid * inv2 * ffn_norm_gain).astype(BF16)
    h2_all = gather(h2_own)

    def feed(k, rows2):
        dtype = F32 if k == 0 else BF16
        block = min(256, ff_width)
        full = pl.BlockSpec((seq_len, model), lambda i: (0, 0))
        columns = pl.BlockSpec((model, block), lambda i: (0, i))
        rows = pl.BlockSpec((block, model), lambda i: (i, 0))
        tall = pl.BlockSpec((seq_len, block), lambda i: (0, i))
        return pl.pallas_call(
            ffn_kernel,
            grid=(ff_width // block,),
            out_shape=[shaped((ff_width, seq_len), BF16)] + [shaped((seq_len, ff_width), BF16)] * 2
            + [shaped((seq_len, model), dtype)] * 2 + [shaped((model, seq_len), BF16)],
            in_specs=[full, full, columns, columns, rows] + ([full] if k == 0 else []),
            out_specs=[pl.BlockSpec((block, seq_len), lambda i: (i, 0))] + [tall] * 2 + [full] * 2
            + [pl.BlockSpec((model, seq_len), lambda i: (0, 0))],
            scratch_shapes=[pltpu.VMEM((seq_len, model), F32)] * 2,
            compiler_params=pltpu.CompilerParams(vmem_limit_bytes=VMEM_LIMIT),
            cost_estimate=pl.CostEstimate(flops=8 * 10**9, bytes_accessed=10**7, transcendentals=0),
            name="feed_forward",
        )(rows2, ct_all[k], w_gate, w_up, w_down, *([resid] if k == 0 else []))

    fed = [feed(0, h2_own)]
    for k in range(1, groups):
        fed.append(feed(k, lax.optimization_barrier((h2_all[k], fed[0][0]))[0]))
    d_second = scatter_sum(fed[0][4], [one[4] for one in fed[1:]])
    layer_output = scatter_sum(fed[0][3], [one[3] for one in fed[1:]]).astype(BF16)
    h2_turned = jnp.concatenate([one[5] for one in fed], axis=1)
    grad_gate = mm(h2_turned, jnp.concatenate([one[1] for one in fed], axis=0))
    grad_up = mm(h2_turned, jnp.concatenate([one[2] for one in fed], axis=0))
    grad_down = mm(jnp.concatenate([one[0] for one in fed], axis=1), jnp.concatenate(ct_all, axis=0))
    scaled = d_second * ffn_norm_gain
    d_resid = (
        ct_own.astype(F32)
        + inv2 * scaled
        - resid * (inv2**3) * jnp.mean(scaled * resid, axis=1, keepdims=True)
    )
    grad_ffn_gain = jnp.sum(d_second * resid * inv2, axis=0)
    db_all = gather(d_resid.astype(BF16))

    def mix_grad(k):
        q, kd, vd, z, x, bcp, bc, tp, tpr, y, _ = kept[k]
        return whole_call(
            mix_grad_kernel,
            [shaped((seq_len, att_pad), BF16), shaped((seq_len, ssm_pad), BF16), shaped((16, seq_len))],
            0,
            [db_all[k], y, x, z, cxw, cxb, skip, gain, wa, ws],
            4 * 10**9,
            "mix_grad",
        )

    mixed = [mix_grad(k) for k in range(groups)]
    backs_part = [one[2] for one in mixed]
    backs = [backs_part[k] for k in range(groups)]
    for shift in range(1, groups):
        for k in range(groups):
            backs[k] = backs[k] + fetch(backs_part[(k - shift) % groups], shift)

    def attend_back(k):
        q, kd, vd = kept[k][:3]
        return whole_call(
            attend_back_kernel,
            [shaped((seq_len, att_pad), BF16), shaped((seq_len, LANES), BF16)],
            1,
            [len_all[k], q, kd, vd, mixed[k][0], cos_table, sine_first, sine_second],
            4 * 10**9,
            "attend_back",
        )

    turned = [attend_back(k) for k in range(groups)]

    def backward(k):
        q, kd, vd, z, x, bcp, bc, tp, tpr, y, _ = kept[k]
        outs = [
            shaped((seq_len, model), F32 if k == 0 else BF16), shaped((seq_len, ssm_pad), BF16),
            shaped((seq_len, ssm_pad), BF16), shaped((seq_len, 2 * STATE), BF16), shaped((seq_len, 16), BF16),
            shaped((8, ssm_pad)), shaped((8, 2 * STATE)), shaped((8, 16)),
        ]
        args = [
            len_all[k], mixed[k][1], y, x, z, bcp, bc, tp, tpr, squares[k], backs[k], turned[k][0], turned[k][1],
            wq, w_kv, wz, wx, w_ssm_b, w_ssm_c, wt, cxw, cxb, conv_bc_weight, cbb, bias, rate, bias_col, rate_col,
            skip, gain,
        ]
        return whole_call(
            functools.partial(mixer_back_kernel, width=ssm_width_all), outs, 1, args, 16 * 10**9, "mixer_back"
        )

    gone = [None] * groups
    for k in list(range(1, groups)) + [0]:
        gone[k] = backward(k)
    d_first = scatter_sum(gone[0][0], [one[0] for one in gone[1:]])
    grad_norm_gain = jnp.sum(d_first * inputs * inv1, axis=0)

    wide, bcg, small = (sum(one[i] for one in gone) for i in (5, 6, 7))
    grad_q = contract_rows(h_all, [one[0] for one in turned])
    grad_kv = contract_rows(h_all, [one[1] for one in turned])
    grad_bc = contract_rows(h_all, [one[3] for one in gone])
    grad_x = contract_rows(h_all, [one[1] for one in gone])
    grad_z = contract_rows(h_all, [one[2] for one in gone])
    grad_step = contract_rows(h_all, [one[4] for one in gone])
    grad_att = contract_rows(mix_att, db_all)
    grad_ssm = contract_rows(mix_ssm, db_all)
    norms = jnp.concatenate([bcg[:5].reshape(-1), grad_norm_gain, grad_ffn_gain])
    zeros = jnp.zeros((model, KV_HEADS * HEAD_DIM), F32)
    grad_key = lax.dynamic_update_slice(zeros, grad_kv[:, :HEAD_DIM], (0, kv_head * HEAD_DIM))
    grad_value = lax.dynamic_update_slice(zeros, grad_kv[:, HEAD_DIM:], (0, kv_head * HEAD_DIM))
    grad_key, grad_value, grad_bc, norms = lax.psum((grad_key, grad_value, grad_bc, norms), ("dp", "tensor"))
    grad_b, grad_c = grad_bc[:, :STATE], grad_bc[:, STATE:]
    grad_q, grad_z, grad_x, grad_step, grad_att, grad_ssm, wide, small = (
        lax.psum(part.astype(BF16), "dp").astype(F32)
        for part in (grad_q, grad_z, grad_x, grad_step, grad_att, grad_ssm, wide, small)
    )
    grad_gate, grad_up, grad_down = (
        lax.psum(part.astype(BF16), "dp").astype(F32) for part in (grad_gate, grad_up, grad_down)
    )
    grad_step = grad_step[:, :ssm_heads]
    grad_cxw, grad_cxb, grad_sgain = wide[:4], wide[4:5], wide[6:7]
    bcg = norms[: 10 * STATE].reshape(5, 2 * STATE)
    grad_cbw, grad_cbb = bcg[:4], bcg[4:]
    grad_bias, grad_decay, grad_skip = small[0:1, :ssm_heads], small[1:2, :ssm_heads], small[2:3, :ssm_heads]
    grad_norm_gain = norms[10 * STATE : 10 * STATE + model]
    grad_ffn_gain = norms[10 * STATE + model :]

    scaled = d_first * norm_gain
    grad_input = d_resid + inv1 * scaled - inputs * (inv1**3) * jnp.mean(scaled * inputs, axis=1, keepdims=True)

    return (
        layer_output,
        grad_input,
        grad_norm_gain.reshape(-1),
        grad_q[:, :att_width],
        grad_key,
        grad_value,
        grad_z[:, :ssm_width],
        grad_x[:, :ssm_width],
        grad_b,
        grad_c,
        grad_step,
        grad_cxw[:, :ssm_width],
        grad_cxb.reshape(-1)[:ssm_width],
        grad_cbw,
        grad_cbb.reshape(-1),
        grad_bias.reshape(-1),
        grad_decay.reshape(-1),
        grad_skip.reshape(-1),
        grad_sgain.reshape(-1)[:ssm_width],
        grad_att[:att_width],
        grad_ssm[:ssm_width],
        grad_ffn_gain.reshape(-1),
        grad_gate,
        grad_up,
        grad_down,
    )


def solution(mesh):
    rows, split, tall = P(("dp", "tensor"), None), P(None, "tensor"), P("tensor", None)
    vector, copied = P("tensor"), P()
    return jax.shard_map(
        on_device,
        mesh=mesh,
        in_specs=(
            rows, P(("dp", "tensor")), rows, copied, split, copied, copied, split, split, copied, copied, split,
            split, vector, copied, copied, vector, vector, vector, vector, tall, tall, copied, split, split, tall,
        ),
        out_specs=(
            rows, rows, copied, split, copied, copied, split, split, copied, copied, split, split, vector, copied,
            copied, vector, vector, vector, vector, tall, tall, copied, split, split, tall,
        ),
        check_vma=False,
    )
```

```python
import functools

import jax
import jax.numpy as jnp
import numpy as np
from jax import lax
from jax.experimental import pallas as pl
from jax.experimental.pallas import tpu as pltpu
from jax.sharding import PartitionSpec as P

HEADS = 8
KV_HEADS = 2
HEAD_DIM = 64
SSM_HEADS = 24
SSM_DIM = 64
STATE = 128
SPAN = 128
LANES = 128

EPSILON = 1e-05
ROPE_BASE = 100000000000.0
F32 = jnp.float32
BF16 = jnp.bfloat16
VMEM_LIMIT = 62 * 1024 * 1024
REDUCE_LIMIT = 62 * 1024 * 1024
MESH = pl.DeviceIdType.MESH


def mm(left, right):
    return jnp.dot(left, right, preferred_element_type=F32)


def mm_nt(left, right):
    return lax.dot_general(left, right, (((1,), (1,)), ((), ())), preferred_element_type=F32)


def mm_tn(left, right):
    return lax.dot_general(left, right, (((0,), (0,)), ((), ())), preferred_element_type=F32)


def pieces(values, count):
    terms = []
    for _ in range(count):
        term = values.astype(BF16)
        terms.append(term)
        values = values - term.astype(F32)
    return terms


def sigmoid(values):
    return 1.0 / (1.0 + jnp.exp(-values))


def softplus(values):
    return jnp.maximum(values, 0.0) + jnp.log1p(jnp.exp(-jnp.abs(values)))


def lane_ids(shape):
    return lax.broadcasted_iota(jnp.int32, shape, 1)


def row_ids(shape):
    return lax.broadcasted_iota(jnp.int32, shape, 0)


def repeat_lanes(column, count):
    return jnp.concatenate([column] * count, axis=1) if count > 1 else column


def column_of(row):
    ones = jnp.where(row_ids((16, LANES)) == 0, 1.0, 0.0).astype(BF16)
    total = None
    for term in pieces(row, 3):
        part = mm_tn(term, ones)
        total = part if total is None else total + part
    return total


def row_sums(values):
    ones = jnp.ones((16, values.shape[1]), BF16)
    high, low = pieces(values, 2)
    return mm_nt(ones, high) + mm_nt(ones, low)


def causal_shift(values, steps):
    if steps == 0:
        return values
    rolled = pltpu.roll(values, steps, 0)
    return jnp.where(row_ids(values.shape) >= steps, rolled, 0.0)


def anti_shift(values, steps):
    if steps == 0:
        return values
    length = values.shape[0]
    rolled = pltpu.roll(values, length - steps, 0)
    return jnp.where(row_ids(values.shape) < length - steps, rolled, 0.0)


def conv(values, weight, bias):
    taps = weight.shape[0]
    total = bias + weight[taps - 1 : taps] * values
    for offset in range(taps - 1):
        total = total + weight[offset : offset + 1] * causal_shift(values, taps - 1 - offset)
    return total


def conv_back(grad, values, weight):
    taps = weight.shape[0]
    total, rows = None, []
    for offset in range(taps):
        steps = taps - 1 - offset
        moved = anti_shift(grad, steps)
        part = weight[offset : offset + 1] * moved
        total = part if total is None else total + part
        rows.append(jnp.sum(moved * values, axis=0, keepdims=True))
    rows.append(jnp.sum(grad, axis=0, keepdims=True))
    return total, rows


def rope(values, cosine, sine_first, sine_second):
    ahead = pltpu.roll(values, LANES - HEAD_DIM // 2, 1)
    behind = pltpu.roll(values, HEAD_DIM // 2, 1)
    return values * cosine + ahead * sine_first + behind * sine_second


def lower_mask():
    return row_ids((SPAN, SPAN)) >= lane_ids((SPAN, SPAN))


def span_sums(values):
    lower = jnp.where(lower_mask(), 1.0, 0.0).astype(BF16)
    out = []
    for start in range(0, values.shape[0], SPAN):
        total = None
        for term in pieces(values[start : start + SPAN], 3):
            part = mm(lower, term)
            total = part if total is None else total + part
        out.append(total)
    return jnp.concatenate(out, axis=0)


def span_sums_rows(values):
    upper = jnp.where(row_ids((SPAN, SPAN)) <= lane_ids((SPAN, SPAN)), 1.0, 0.0).astype(BF16)
    out = []
    for start in range(0, values.shape[1], SPAN):
        total = None
        for term in pieces(values[:, start : start + SPAN], 3):
            part = mm(term, upper)
            total = part if total is None else total + part
        out.append(total)
    return jnp.concatenate(out, axis=1)


def span_sums_back(values):
    upper = jnp.where(row_ids((SPAN, SPAN)) <= lane_ids((SPAN, SPAN)), 1.0, 0.0).astype(BF16)
    out = []
    for start in range(0, values.shape[0], SPAN):
        total = None
        for term in pieces(values[start : start + SPAN], 3):
            part = mm(upper, term)
            total = part if total is None else total + part
        out.append(total)
    return jnp.concatenate(out, axis=0)


def steps_of(tp, tp_row, bias, bias_col, rate, rate_col, length):
    seq_len = tp.shape[0]
    valid = jnp.where(row_ids((seq_len, 1)) < length, 1.0, 0.0)
    valid_row = jnp.where(lane_ids((1, seq_len)) < length, 1.0, 0.0)
    dt = softplus(tp + bias) * valid
    dt_row = softplus(tp_row + bias_col) * valid_row
    cum = span_sums(-(dt * rate))
    cum_row = span_sums_rows(-(dt_row * rate_col))
    return valid, dt, cum, cum_row


def spread(values, head):
    return jnp.broadcast_to(values[:, head : head + 1], (values.shape[0], LANES))


def decays(cum_first, cum_second, cum_row, pair, span):
    rows = slice(span * SPAN, (span + 1) * SPAN)
    lower = lower_mask()
    out = []
    for head, column in ((2 * pair, cum_first), (2 * pair + 1, cum_second)):
        differ = column[rows] - cum_row[head : head + 1, rows]
        out.append(jnp.exp(jnp.where(lower, differ, -1e30)))
    return out


def split_heads(values):
    first = lane_ids(values.shape) < HEAD_DIM
    zero = jnp.zeros_like(values)
    return jnp.concatenate([jnp.where(first, values, zero), jnp.where(first, zero, values)], axis=0)


def state_of(in_map, weighted_first, cum_pair_first):
    to_end = jnp.exp(cum_pair_first[SPAN - 1 : SPAN] - cum_pair_first)
    ending = (weighted_first * to_end).astype(BF16)
    return to_end, ending, mm_tn(in_map[:SPAN], ending)


def mixer_forward_kernel(
    len_ref, h_ref, wq_ref, wkv_ref, wz_ref, wx_ref, wb_ref, wc_ref, wt_ref, cxw_ref, cxb_ref,
    cbw_ref, cbb_ref, bias_ref, rate_ref, bias_col_ref, rate_col_ref, skip_ref, cos_ref, sa_ref,
    sb_ref, q_ref, kd_ref, vd_ref, z_ref, x_ref, bcp_ref, bc_ref, tp_ref, tpr_ref, y_ref, ss_ref,
):
    h = h_ref[...]
    pairs = wx_ref.shape[1] // LANES
    z_ref[...] = mm(h, wz_ref[...])
    x_ref[...] = mm(h, wx_ref[...])
    bcp_ref[:, :STATE] = mm(h, wb_ref[...])
    bcp_ref[:, STATE:] = mm(h, wc_ref[...])
    tp = mm_nt(h, wt_ref[...])
    tp_row = mm_nt(wt_ref[...], h)
    tp_ref[...] = tp
    tpr_ref[...] = tp_row
    cosine, sine_first, sine_second = cos_ref[...], sa_ref[...], sb_ref[...]
    for pair in range(wq_ref.shape[1] // LANES):
        lanes = slice(pair * LANES, (pair + 1) * LANES)
        q_ref[:, lanes] = rope(mm(h, wq_ref[:, lanes]), cosine, sine_first, sine_second).astype(BF16)
    kv = mm(h, wkv_ref[...])
    turned = pltpu.roll(kv, HEAD_DIM, 1)
    first = lane_ids(kv.shape) < HEAD_DIM
    kd_ref[...] = rope(jnp.where(first, kv, turned), cosine, sine_first, sine_second).astype(BF16)
    vd_ref[...] = jnp.where(first, turned, kv).astype(BF16)

    mapped = conv(bcp_ref[...], cbw_ref[...], cbb_ref[...])
    bc = (mapped * sigmoid(mapped)).astype(BF16)
    bc_ref[...] = bc
    in_map, out_map = bc[:, :STATE], bc[:, STATE:]
    affinity = [
        mm_nt(out_map[s * SPAN : (s + 1) * SPAN], in_map[s * SPAN : (s + 1) * SPAN]) for s in range(2)
    ]
    _, dt, cum, cum_row = steps_of(
        tp, tp_row, bias_ref[...], bias_col_ref[...], rate_ref[...], rate_col_ref[...], len_ref[0]
    )
    squares = None
    for pair in range(pairs):
        lanes = slice(pair * LANES, (pair + 1) * LANES)
        cx = conv(x_ref[:, lanes], cxw_ref[:, lanes], cxb_ref[:, lanes])
        xc = cx * sigmoid(cx)
        dt_pair = jnp.where(first, spread(dt, 2 * pair), spread(dt, 2 * pair + 1))
        cum_first, cum_second = spread(cum, 2 * pair), spread(cum, 2 * pair + 1)
        cum_pair = jnp.where(first, cum_first, cum_second)
        weighted = xc * dt_pair
        low = weighted.astype(BF16)
        _, _, state = state_of(in_map, weighted[:SPAN], cum_pair[:SPAN])
        parts = []
        for s in range(2):
            rows = slice(s * SPAN, (s + 1) * SPAN)
            mats = [
                (affinity[s] * decay).astype(BF16)
                for decay in decays(cum_first, cum_second, cum_row, pair, s)
            ]
            part = mm(jnp.concatenate(mats, axis=1), split_heads(low[rows]))
            if s:
                part = part + mm(out_map[rows], state.astype(BF16)) * jnp.exp(cum_pair[rows])
            parts.append(part)
        y = jnp.concatenate(parts, axis=0)
        y_ref[:, lanes] = y
        z = z_ref[:, lanes]
        gated = (y + skip_ref[:, lanes] * xc) * (z * sigmoid(z))
        square = gated * gated
        squares = square if squares is None else squares + square
    ss_ref[...] = row_sums(squares)


def masked_probs(queries, kd, length, scale):
    seq_len = kd.shape[0]
    scores = mm_nt(split_heads(queries), kd) * scale
    rows = row_ids(scores.shape)
    rows = jnp.where(rows >= seq_len, rows - seq_len, rows)
    padding = jnp.where(lane_ids((1, seq_len)) < length, 0.0, -1e30)
    scores = jnp.where(rows >= lane_ids(scores.shape), scores + padding, -1e30)
    weights = jnp.exp(scores - jnp.max(scores, axis=1, keepdims=True))
    return weights / jnp.sum(weights, axis=1, keepdims=True)


def attend_kernel(len_ref, q_ref, kd_ref, vd_ref, out_ref):
    seq_len = q_ref.shape[0]
    values = split_heads(vd_ref[...])
    for pair in range(q_ref.shape[1] // LANES):
        lanes = slice(pair * LANES, (pair + 1) * LANES)
        probs = masked_probs(q_ref[:, lanes], kd_ref[...], len_ref[0], HEAD_DIM ** (-0.5)).astype(BF16)
        both = jnp.concatenate([probs[:seq_len], probs[seq_len:]], axis=1)
        out_ref[:, lanes] = mm(both, values).astype(BF16)


def join_halves(values):
    return values + pltpu.roll(values, HEAD_DIM, 1)


def attend_back_kernel(len_ref, q_ref, kd_ref, vd_ref, da_ref, cos_ref, sa_ref, sb_ref, dq_ref, dkv_ref):
    seq_len = q_ref.shape[0]
    scale = HEAD_DIM ** (-0.5)
    cosine, sine_first, sine_second = cos_ref[...], -sa_ref[...], -sb_ref[...]
    kd, vd = kd_ref[...], vd_ref[...]
    keys = split_heads(kd)
    grad_k, grad_v = None, None
    for pair in range(q_ref.shape[1] // LANES):
        lanes = slice(pair * LANES, (pair + 1) * LANES)
        probs = masked_probs(q_ref[:, lanes], kd, len_ref[0], scale)
        da = split_heads(da_ref[:, lanes])
        dprob = mm_nt(da, vd)
        dscore = (probs * (dprob - jnp.sum(probs * dprob, axis=1, keepdims=True))).astype(BF16)
        both = jnp.concatenate([dscore[:seq_len], dscore[seq_len:]], axis=1)
        dq = mm(both, keys) * scale
        dq_ref[:, lanes] = rope(dq, cosine, sine_first, sine_second).astype(BF16)
        part_k = mm_tn(dscore, split_heads(q_ref[:, lanes]))
        part_v = mm_tn(probs.astype(BF16), da)
        grad_k = part_k if grad_k is None else grad_k + part_k
        grad_v = part_v if grad_v is None else grad_v + part_v
    dk = rope(join_halves(grad_k) * scale, cosine, sine_first, sine_second)
    first = lane_ids(dk.shape) < HEAD_DIM
    dkv_ref[...] = jnp.where(first, dk, join_halves(grad_v)).astype(BF16)


def out_kernel(att_ref, y_ref, x_ref, z_ref, ss_ref, cxw_ref, cxb_ref, skip_ref, gain_ref, wa_ref, ws_ref,
               part_ref, mix_ref, *, width, splits=1, send=lambda index, rows: None):
    inv = column_of(lax.rsqrt(ss_ref[...] / width + EPSILON))
    for pair in range(y_ref.shape[1] // LANES):
        lanes = slice(pair * LANES, (pair + 1) * LANES)
        cx = conv(x_ref[:, lanes], cxw_ref[:, lanes], cxb_ref[:, lanes])
        z = z_ref[:, lanes]
        gated = (y_ref[:, lanes] + skip_ref[:, lanes] * (cx * sigmoid(cx))) * (z * sigmoid(z))
        mix_ref[:, lanes] = (gated * inv * gain_ref[:, lanes]).astype(BF16)
    size = part_ref.shape[0] // splits
    for index in range(splits):
        rows = slice(index * size, (index + 1) * size)
        part = mm(att_ref[rows, :], wa_ref[...]) + mm(mix_ref[rows, :], ws_ref[...])
        part_ref[rows, :] = part.astype(part_ref.dtype)
        send(index, rows)


def mix_grad_kernel(db_ref, y_ref, x_ref, z_ref, cxw_ref, cxb_ref, skip_ref, gain_ref, wa_ref, ws_ref,
                    da_ref, dm_ref, bs_ref):
    db = db_ref[...]
    da_ref[...] = mm_nt(db, wa_ref[...]).astype(BF16)
    dm_ref[...] = mm_nt(db, ws_ref[...]).astype(BF16)
    total = None
    for pair in range(y_ref.shape[1] // LANES):
        lanes = slice(pair * LANES, (pair + 1) * LANES)
        cx = conv(x_ref[:, lanes], cxw_ref[:, lanes], cxb_ref[:, lanes])
        z = z_ref[:, lanes]
        gated = (y_ref[:, lanes] + skip_ref[:, lanes] * (cx * sigmoid(cx))) * (z * sigmoid(z))
        part = gated * (gain_ref[:, lanes] * dm_ref[:, lanes].astype(F32))
        total = part if total is None else total + part
    bs_ref[...] = row_sums(total)


def head_sums(values, pair):
    rows, columns = row_ids((LANES, 16)), lane_ids((LANES, 16))
    chosen = jnp.where(columns == 2 * pair + jnp.where(rows < HEAD_DIM, 0, 1), 1.0, 0.0).astype(BF16)
    high, low = pieces(values, 2)
    return mm(jnp.concatenate([high, low], axis=1), jnp.concatenate([chosen, chosen], axis=0))


def mixer_back_kernel(
    len_ref, dm_ref, y_ref, x_ref, z_ref, bcp_ref, bc_ref, tp_ref, tpr_ref, ss_ref, bs_ref, dq_ref,
    dkv_ref, wq_ref, wkv_ref, wz_ref, wx_ref, wb_ref, wc_ref, wt_ref, cxw_ref, cxb_ref, cbw_ref,
    cbb_ref, bias_ref, rate_ref, bias_col_ref, rate_col_ref, skip_ref, gain_ref,
    dh_ref, dx_ref, dz_ref, dbc_ref, dt_ref, wide_ref, bcg_ref, small_ref, *, width, tick=lambda: None,
):
    pairs = x_ref.shape[1] // LANES
    bc = bc_ref[...]
    in_map, out_map = bc[:, :STATE], bc[:, STATE:]
    affinity = [
        mm_nt(out_map[s * SPAN : (s + 1) * SPAN], in_map[s * SPAN : (s + 1) * SPAN]) for s in range(2)
    ]
    valid, dt, cum, cum_row = steps_of(
        tp_ref[...], tpr_ref[...], bias_ref[...], bias_col_ref[...], rate_ref[...], rate_col_ref[...], len_ref[0]
    )
    inv_row = lax.rsqrt(ss_ref[...] / width + EPSILON)
    inv = column_of(inv_row)
    back = column_of(inv_row * inv_row * inv_row * bs_ref[...] / width)
    first = lane_ids((x_ref.shape[0], LANES)) < HEAD_DIM
    last_row = row_ids((SPAN, LANES)) == SPAN - 1
    d_cum, d_step, d_skip = None, None, None
    wide_ref[7:8, :] = jnp.zeros((1, wide_ref.shape[1]), F32)
    d_aff, d_out, d_in = [None, None], None, None

    def plus(total, part):
        return part if total is None else total + part

    for pair in range(pairs):
        lanes = slice(pair * LANES, (pair + 1) * LANES)
        x = x_ref[:, lanes]
        cxw = cxw_ref[:, lanes]
        cx = conv(x, cxw, cxb_ref[:, lanes])
        sx = sigmoid(cx)
        xc = cx * sx
        z = z_ref[:, lanes]
        sz = sigmoid(z)
        silu_z = z * sz
        scanned = y_ref[:, lanes]
        y = scanned + skip_ref[:, lanes] * xc
        gated = y * silu_z
        d_mix = dm_ref[:, lanes].astype(F32)
        d_gated = inv * (gain_ref[:, lanes] * d_mix) - gated * back
        wide_ref[6:7, lanes] = jnp.sum(d_mix * gated * inv, axis=0, keepdims=True)
        dy = d_gated * silu_z
        dz_ref[:, lanes] = (d_gated * y * (sz * (1.0 + z * (1.0 - sz)))).astype(BF16)
        wide_ref[5:6, lanes] = jnp.sum(dy * xc, axis=0, keepdims=True)
        dt_pair = jnp.where(first, spread(dt, 2 * pair), spread(dt, 2 * pair + 1))
        cum_first, cum_second = spread(cum, 2 * pair), spread(cum, 2 * pair + 1)
        cum_pair = jnp.where(first, cum_first, cum_second)
        weighted = xc * dt_pair
        low = weighted.astype(BF16)
        dy_low = dy.astype(BF16)
        to_end, ending, state = state_of(in_map, weighted[:SPAN], cum_pair[:SPAN])
        d_weighted = []
        for s in range(2):
            rows = slice(s * SPAN, (s + 1) * SPAN)
            decay = decays(cum_first, cum_second, cum_row, pair, s)
            mats = jnp.concatenate([(affinity[s] * one).astype(BF16) for one in decay], axis=0)
            both = split_heads(dy_low[rows])
            d_mats = mm_nt(both, low[rows])
            d_aff[s] = plus(d_aff[s], d_mats[:SPAN] * decay[0] + d_mats[SPAN:] * decay[1])
            d_weighted.append(mm_tn(mats, both))
        reached = (dy[SPAN:] * jnp.exp(cum_pair[SPAN:])).astype(BF16)
        d_out = plus(d_out, mm_nt(reached, state.astype(BF16)))
        d_state = mm_tn(out_map[SPAN:], reached).astype(BF16)
        d_in = plus(d_in, mm_nt(ending, d_state))
        d_ending = mm(in_map[:SPAN], d_state)
        through = ending.astype(F32) * d_ending
        low_f, dy_f = low.astype(F32), dy_low.astype(F32)
        change = dy_f * scanned - low_f * jnp.concatenate(d_weighted, axis=0)
        ended = jnp.where(last_row, jnp.sum(through, axis=0, keepdims=True), 0.0) - through
        change = jnp.concatenate([change[:SPAN] + ended, change[SPAN:]], axis=0)
        d_weight = jnp.concatenate([d_weighted[0] + d_ending * to_end, d_weighted[1]], axis=0)
        d_cum = plus(d_cum, head_sums(change, pair))
        d_step = plus(d_step, head_sums(d_weight * xc, pair))
        d_xc = dy * skip_ref[:, lanes] + d_weight * dt_pair
        d_cx = d_xc * (sx * (1.0 + cx * (1.0 - sx)))
        d_x, rows_x = conv_back(d_cx, x, cxw)
        dx_ref[:, lanes] = d_x.astype(BF16)
        for index, row in enumerate(rows_x):
            wide_ref[index : index + 1, lanes] = row
        d_skip = plus(d_skip, head_sums(wide_ref[:, lanes], pair))
        tick()

    rate = rate_ref[...]
    d_log = span_sums_back(d_cum)
    d_dt = d_step - rate * d_log
    d_tp = d_dt * valid * sigmoid(tp_ref[...] + bias_ref[...])
    small_ref[...] = jnp.zeros(small_ref.shape, F32)
    small_ref[0:1, :] = jnp.sum(d_tp, axis=0, keepdims=True)
    small_ref[1:2, :] = -rate * jnp.sum(dt * d_log, axis=0, keepdims=True)
    small_ref[2:3, :] = d_skip[5:6]
    dt_ref[...] = d_tp.astype(BF16)

    d_maps = []
    low_aff = [part.astype(BF16) for part in d_aff]
    d_ins, d_outs = [], []
    for s in range(2):
        rows = slice(s * SPAN, (s + 1) * SPAN)
        d_outs.append(mm(low_aff[s], in_map[rows]))
        d_ins.append(mm_tn(low_aff[s], out_map[rows]))
    d_outs[1] = d_outs[1] + d_out
    d_ins[0] = d_ins[0] + d_in
    d_maps = jnp.concatenate(
        [jnp.concatenate(d_ins, axis=0), jnp.concatenate(d_outs, axis=0)], axis=1
    )
    mapped = conv(bcp_ref[...], cbw_ref[...], cbb_ref[...])
    sm = sigmoid(mapped)
    d_bc, rows_bc = conv_back(d_maps * (sm * (1.0 + mapped * (1.0 - sm))), bcp_ref[...], cbw_ref[...])
    bcg_ref[...] = jnp.zeros(bcg_ref.shape, F32)
    for index, row in enumerate(rows_bc):
        bcg_ref[index : index + 1, :] = row
    d_bc = d_bc.astype(BF16)
    dbc_ref[...] = d_bc
    total = mm_nt(dx_ref[...], wx_ref[...]) + mm_nt(dz_ref[...], wz_ref[...])
    total = total + mm_nt(dq_ref[...], wq_ref[...]) + mm_nt(dkv_ref[...], wkv_ref[...])
    total = total + mm_nt(d_bc[:, :STATE], wb_ref[...]) + mm_nt(d_bc[:, STATE:], wc_ref[...])
    total = total + mm(dt_ref[...], wt_ref[...])
    dh_ref[...] = total.astype(dh_ref.dtype)


def ffn_kernel(h_ref, ct_ref, wg_ref, wu_ref, wd_ref, *refs):
    base_ref = refs[0] if len(refs) == 9 else None
    hid_ref, dg_ref, du_ref, ff_ref, dh_ref, ht_ref, ff_acc, dh_acc = refs[-8:]
    step = pl.program_id(0)
    h = h_ref[...]
    gate = mm(h, wg_ref[...])
    up = mm(h, wu_ref[...])
    d_hidden = mm_nt(ct_ref[...], wd_ref[...]).astype(BF16).astype(F32)
    sg = sigmoid(gate)
    silu = gate * sg
    hidden = silu * up
    hid_ref[...] = hidden.T.astype(BF16)
    hidden = hidden.astype(BF16)
    d_gate = (d_hidden * up * (sg * (1.0 + gate * (1.0 - sg)))).astype(BF16)
    d_up = (d_hidden * silu).astype(BF16)
    dg_ref[...] = d_gate
    du_ref[...] = d_up
    ff_part = mm(hidden, wd_ref[...])
    dh_part = mm_nt(d_gate, wg_ref[...]) + mm_nt(d_up, wu_ref[...])

    @pl.when(step == 0)
    def _():
        ht_ref[...] = h.astype(F32).T.astype(BF16)
        ff_acc[...] = ff_part if base_ref is None else ff_part + base_ref[...]
        dh_acc[...] = dh_part

    @pl.when(step > 0)
    def _():
        ff_acc[...] += ff_part
        dh_acc[...] += dh_part

    @pl.when(step == pl.num_programs(0) - 1)
    def _():
        ff_ref[...] = ff_acc[...].astype(ff_ref.dtype)
        dh_ref[...] = dh_acc[...].astype(dh_ref.dtype)


class Names(dict):
    __getattr__ = dict.__getitem__


class Entry:
    def __init__(self, ref):
        self.ref = ref

    def __getitem__(self, index):
        return self.ref[0:1, 0:1]


PARTS = 8
GATE, UP, DOWN, SHARED, QUERY, ZED, EX, OUT = range(PARTS)
KV_AT, B_AT, C_AT, MISC_AT = 0, LANES, 2 * LANES, 3 * LANES
SHARED_WIDTH = 4 * LANES


def chunk_order(widths):
    wide = 2 * LANES
    order = [(part, column, wide) for part in (GATE, UP, DOWN, OUT, QUERY) for column in range(0, widths[part], wide)]
    order += [(SHARED, column, LANES) for column in (KV_AT, B_AT, C_AT)]
    order += [(EX, column, wide) for column in range(0, widths[EX], wide)]
    order += [(SHARED, MISC_AT, LANES)]
    order += [(ZED, column, wide) for column in range(0, widths[ZED] - 2 * wide, wide)]
    order += [(ZED, column, LANES) for column in range(widths[ZED] - 2 * wide, widths[ZED], LANES)]
    return [item + ("P" if item[0] == SHARED or index % 2 else "Q",) for index, item in enumerate(order)]


SLOTS = 6
STAGE_AT = (0.0, 1.5, 3.0, 5.0, 7.0, 9.0, 11.0, 12.5, 14.0)


def unit_matrix(size):
    return jnp.where(row_ids((size, size)) == lane_ids((size, size)), 1.0, 0.0)


def turned_small(values):
    unit = unit_matrix(16).astype(BF16)
    total = None
    for term in pieces(values, 3):
        part = mm_nt(unit, term)
        total = part if total is None else total + part
    return total


def back_kernel(*refs, small_names, big_names, widths, width, pace):
    it = iter(refs)
    s = Names({name: next(it) for name in small_names})
    lens = [Entry(s.len0), Entry(s.len1)]
    big_in = Names({name: next(it) for name in big_names})
    dh2_peer, ff_peer = next(it), next(it)
    outs = [next(it) for _ in range(PARTS)]
    xout, grad_in, layer_out = next(it), next(it), next(it)
    b = Names({name: next(it) for name in big_names})
    (db, bs, bsr, da, dm, dq, dkv, dx, dz, dbc, dt, dh_own, dh_peer, dh_got, ff_got, wide, bcg, small, misc,
     acc, rc, res, ry, zin_p, zin_q, zmid, in_sem, out_sem, xs, xr, send_sem, recv_sem) = it
    rows = outs[GATE].shape[0]
    half, quarter = rows // 2, rows // 4
    seq_len = db.shape[0] // 2
    me = lax.axis_index("dp")
    core, y, z = me % 2, (me // 2) % 2, me // 4
    side = lax.axis_index("tensor")
    sibling = dict(dp=me + 1 - 2 * core)
    across = dict(dp=me + 2 - 4 * y)
    outer = dict(dp=(z + 1 - 2 * (z % 2)) * 4 + y * 2 + core)
    inner = dict(dp=(3 - z) * 4 + y * 2 + core)
    pair = dict(tensor=1 - side)
    is_mid = (z == 1) | (z == 2)
    is_end = (z == 0) | (z == 3)

    def at(offset, size):
        return pl.ds(pl.multiple_of(offset, quarter), size)

    mine, other = at(core * half, half), at((1 - core) * half, half)
    my_y, other_y = at(y * quarter, quarter), at((1 - y) * quarter, quarter)
    zq = jnp.where(z <= 1, 0, 1)
    my_z, other_z = at(zq * quarter, quarter), at((1 - zq) * quarter, quarter)

    loads = {}
    for index, name in enumerate(big_names):
        loads[name] = pltpu.make_async_copy(big_in[name], b[name], in_sem.at[index])
        loads[name].start()
    ready = set()

    def need(*names):
        for name in names:
            if name not in ready:
                loads[name].wait()
                ready.add(name)

    barrier = pltpu.get_barrier_semaphore()
    for device in (sibling, across, outer, pair):
        pl.semaphore_signal(barrier, inc=1, device_id=device, device_id_type=MESH)

    @pl.when(is_mid)
    def _():
        pl.semaphore_signal(barrier, inc=1, device_id=inner, device_id_type=MESH)
        pl.semaphore_wait(barrier, 5)

    @pl.when(is_end)
    def _():
        pl.semaphore_wait(barrier, 4)

    ends = []

    def remote(src, dst, send, recv, device):
        return pltpu.make_async_remote_copy(
            src_ref=src, dst_ref=dst, send_sem=send, recv_sem=recv, device_id=device, device_id_type=MESH
        )

    def exchange(src, dst, slot):
        copy = remote(src, dst, xs.at[slot], xr.at[slot], pair)
        copy.start()
        return copy

    def make(part, column, size, span):
        lanes = slice(column, column + size)
        if part == SHARED and column == MISC_AT:
            return misc[span, :].astype(F32)
        total = None
        for k in range(2):
            left, right = {
                GATE: ("h2t", "dg"), UP: ("h2t", "du"), DOWN: ("hid", "ct"), OUT: ("mix", db), SHARED: ("ht", dbc),
                QUERY: ("ht", dq), ZED: ("ht", dz), EX: ("ht", dx),
            }[part]
            need(f"{left}{k}")
            values = b[f"{left}{k}"][span, :]
            if isinstance(right, str):
                need(f"{right}{k}")
                right = b[f"{right}{k}"][:, lanes]
            elif part == SHARED:
                right = dkv[seq(k), :] if column == KV_AT else dbc[seq(k), column - LANES : column]
            else:
                right = right[seq(k), lanes]
            part_k = mm(values, right)
            total = part_k if total is None else total + part_k
        return total

    def add(dst, first, second):
        dst[...] = (first[...].astype(F32) + second[...].astype(F32)).astype(BF16)

    order = chunk_order(widths)
    starts = [sum(item[2] for item in order[:index]) for index in range(len(order))]
    made = set()
    sending = {}

    def chunk_steps(index):
        part, column, size, kind = order[index]
        start = starts[index]
        place = sum(item[2] for item in order[:index] if item[3] == kind)
        cols = slice(start, start + size)
        local = slice(column, column + size)
        tight = slice(place, place + size)
        out = outs[part]

        def own(src, dst, slot, device):
            return remote(src, dst, send_sem.at[slot, index], recv_sem.at[slot, index], device)

        source = acc.at[index % SLOTS, :, :size]
        to_core = own(source, rc.at[:, cols], 0, sibling)
        back_core = own(res.at[:, cols], out.at[mine, local], 6, sibling)
        wait_core = own(res.at[:, cols], out.at[other, local], 6, sibling)
        store = pltpu.make_async_copy(res.at[:, cols], out.at[mine, local], out_sem.at[index])

        def step0():
            assert part < SHARED or (part, column) in made
            if index - SLOTS in sending:
                sending.pop(index - SLOTS)()
            source[...] = make(part, column, size, other).astype(BF16)
            to_core.start()
            sending[index] = to_core.wait_send

        def merge_core():
            term = make(part, column, size, mine)
            to_core.wait_recv()
            rc[:, cols] = (rc[:, cols].astype(F32) + term).astype(BF16)

        def send_core():
            back_core.start()
            store.start()

        def last():
            wait_core.wait_recv()

        ends.append((None, back_core.wait_send))
        ends.append((None, store.wait))

        if kind == "P":
            zin = zin_p.at[:, tight]
            to_y = own(rc.at[other_y, cols], ry.at[:, cols], 1, across)
            to_mid = own(rc.at[my_y, cols], zin, 2, outer)
            swap = own(rc.at[my_y, cols], zmid.at[:, cols], 3, inner)
            to_end = own(res.at[my_y, cols], res.at[my_y, cols], 4, outer)
            back_y = own(res.at[my_y, cols], res.at[my_y, cols], 5, across)
            wait_y = own(res.at[my_y, cols], res.at[other_y, cols], 5, across)

            def step1():
                merge_core()
                to_y.start()
                ends.append((None, to_y.wait_send))

            def step2():
                to_y.wait_recv()
                add(rc.at[my_y, cols], rc.at[my_y, cols], ry.at[:, cols])
                pl.when(is_end)(to_mid.start)
                ends.append((is_end, to_mid.wait_send))

            def step3():
                @pl.when(is_mid)
                def _():
                    to_mid.wait_recv()
                    add(rc.at[my_y, cols], rc.at[my_y, cols], zin)
                    swap.start()

                ends.append((is_mid, swap.wait_send))

            def step4():
                @pl.when(is_mid)
                def _():
                    swap.wait_recv()
                    add(res.at[my_y, cols], rc.at[my_y, cols], zmid.at[:, cols])
                    to_end.start()
                    back_y.start()

                ends.append((is_mid, to_end.wait_send))

            def step5():
                @pl.when(is_end)
                def _():
                    to_end.wait_recv()
                    back_y.start()

                ends.append((None, back_y.wait_send))

            def step6():
                wait_y.wait_recv()
                send_core()

            steps = [step0, step1, step2, step3, step4, step5, step6, last]
            if part == SHARED:
                to_x = own(res.at[:, cols], xout.at[mine, local], 7, pair)
                x_core = own(xout.at[mine, local], xout.at[mine, local], 8, sibling)
                wait_x = own(xout.at[mine, local], xout.at[other, local], 8, sibling)

                def step6x():
                    step6()
                    to_x.start()
                    ends.append((None, to_x.wait_send))

                def step7x():
                    last()
                    to_x.wait_recv()
                    x_core.start()
                    ends.append((None, x_core.wait_send))

                steps[6:] = [step6x, step7x, wait_x.wait_recv]
            return steps

        zin = zin_q.at[:, tight]
        to_mid = own(rc.at[:, cols], zin, 1, outer)
        swap = own(rc.at[other_z, cols], zmid.at[:, cols], 2, inner)
        to_y = own(rc.at[my_z, cols], ry.at[:, cols], 3, across)
        to_inner = own(res.at[my_z, cols], res.at[my_z, cols], 4, inner)
        wait_inner = own(res.at[my_z, cols], res.at[other_z, cols], 4, inner)
        to_end = own(res.at[my_z, cols], res.at[my_z, cols], 5, outer)
        pass_end = own(res.at[other_z, cols], res.at[other_z, cols], 7, outer)

        def step1():
            merge_core()
            pl.when(is_end)(to_mid.start)
            ends.append((is_end, to_mid.wait_send))

        def step2():
            @pl.when(is_mid)
            def _():
                to_mid.wait_recv()
                add(rc.at[:, cols], rc.at[:, cols], zin)
                swap.start()

            ends.append((is_mid, swap.wait_send))

        def step3():
            @pl.when(is_mid)
            def _():
                swap.wait_recv()
                add(rc.at[my_z, cols], rc.at[my_z, cols], zmid.at[:, cols])
                to_y.start()

            ends.append((is_mid, to_y.wait_send))

        def step4():
            @pl.when(is_mid)
            def _():
                to_y.wait_recv()
                add(res.at[my_z, cols], rc.at[my_z, cols], ry.at[:, cols])
                to_inner.start()
                to_end.start()

            ends.append((is_mid, to_inner.wait_send))
            ends.append((is_mid, to_end.wait_send))

        def step5():
            @pl.when(is_mid)
            def _():
                wait_inner.wait_recv()
                pass_end.start()
                send_core()

            ends.append((is_mid, pass_end.wait_send))

        def step6():
            @pl.when(is_end)
            def _():
                to_end.wait_recv()
                pass_end.wait_recv()
                send_core()

        return [step0, step1, step2, step3, step4, step5, step6, last]

    plan = [
        (index + STAGE_AT[number], -number, index, step)
        for index in range(len(order))
        for number, step in enumerate(chunk_steps(index))
    ]
    plan.sort(key=lambda item: item[:3])
    clock, done = [0.0], [0]

    def tick(time=pace):
        clock[0] += time
        while done[0] < len(plan) and plan[done[0]][0] <= clock[0]:
            plan[done[0]][3]()
            done[0] += 1

    def seq(k):
        return pl.ds(k * seq_len, seq_len)

    got_second_norm = exchange(dh2_peer, dh_got, 4)
    tick(0.0)
    tick(1.6)
    tick(1.6)
    tick(1.6)
    need("dh2", "rhat", "ct0")
    got_second_norm.wait()
    model = grad_in.shape[1]
    d_second = b.dh2[...] + dh_got[...].astype(F32)
    scaled = d_second * s.gain2[...]
    rhat = b.rhat[...]
    mean = jnp.sum(scaled * rhat, axis=1, keepdims=True) / model
    d_resid = b.ct0[...].astype(F32) + s.inv2[...] * (scaled - rhat * mean)
    grad_in[...] = d_resid
    db[:seq_len, :] = d_resid.astype(BF16)
    norm_second = jnp.sum(d_second * rhat, axis=0, keepdims=True)
    got_db = exchange(db.at[:seq_len], db.at[seq_len:], 0)
    tick()

    def mix(k):
        need("wa", "ws", f"y{k}", f"x{k}", f"z{k}")
        mix_grad_kernel(
            db.at[seq(k)], b[f"y{k}"], b[f"x{k}"], b[f"z{k}"], s.cxw, s.cxb, s.skip, s.gain, b.wa,
            b.ws, da.at[k], dm.at[k], bs.at[k],
        )
        return exchange(bs.at[k], bsr.at[1 - k], 1 + k)

    def attend(k):
        need(f"q{k}", f"kd{k}", f"vd{k}")
        attend_back_kernel(
            lens[k], b[f"q{k}"], b[f"kd{k}"], b[f"vd{k}"], da.at[k], s.cos, s.sa, s.sb, dq.at[seq(k)],
            dkv.at[seq(k)],
        )

    def mixer(k, dh):
        need("wq", "wkv", "wz", "wx", "wb", "wc", f"bcp{k}", f"bc{k}")
        bs[k] = bs[k] + bsr[k]
        mixer_back_kernel(
            lens[k], dm.at[k], b[f"y{k}"], b[f"x{k}"], b[f"z{k}"], b[f"bcp{k}"], b[f"bc{k}"], s[f"tp{k}"],
            s[f"tpr{k}"], s[f"ss{k}"], bs.at[k], dq.at[seq(k)], dkv.at[seq(k)], b.wq, b.wkv, b.wz,
            b.wx, b.wb, b.wc, s.wt, s.cxw, s.cxb, s.cbw, s.cbb, s.bias, s.rate,
            s.bias_col, s.rate_col, s.skip, s.gain, dh, dx.at[seq(k)], dz.at[seq(k)],
            dbc.at[seq(k)], dt.at[k], wide.at[k], bcg.at[k], small.at[k], width=width, tick=tick,
        )
        tick()

    got_first = mix(0)
    tick()
    attend(0)
    tick()
    got_db.wait_recv()
    got_second = mix(1)
    tick()
    attend(1)
    tick()
    for part in (OUT, QUERY):
        made.update([(part, column) for column in range(0, widths[part], LANES)])
    made.add((SHARED, KV_AT))
    got_first.wait_recv()
    got_second.wait_recv()
    got_first.wait_send()
    got_second.wait_send()
    mixer(1, dh_peer)
    got_dh = exchange(dh_peer, dh_got, 3)
    got_ff = exchange(ff_peer, ff_got, 5)
    mixer(0, dh_own)
    for part in (ZED, EX):
        made.update([(part, column) for column in range(0, widths[part], LANES)])
    made.update([(SHARED, B_AT), (SHARED, C_AT)])
    misc_key = [item[:2] for item in order].index((SHARED, MISC_AT))
    tick(max(0.0, misc_key - 4 - clock[0]))
    got_dh.wait()
    d_first = dh_own[...] + dh_got[...].astype(F32)
    need("xhat")
    xhat = b.xhat[...]
    scaled = d_first * s.gain1[...]
    mean = jnp.sum(scaled * xhat, axis=1, keepdims=True) / model
    grad_in[...] += s.inv1[...] * (scaled - xhat * mean)
    norm = jnp.sum(d_first * xhat, axis=0, keepdims=True)
    wide_sum, bcg_sum, small_sum = wide[0] + wide[1], bcg[0] + bcg[1], small[0] + small[1]
    first_row = row_ids((8, model)) == 0
    second_row = row_ids((8, model)) == 1
    norms = jnp.where(first_row, norm, jnp.where(second_row, norm_second, 0.0))
    blocks = [array[:, i : i + LANES] for array in (wide_sum, bcg_sum) for i in range(0, array.shape[1], LANES)]
    blocks.append(jnp.concatenate([small_sum, jnp.zeros((8, LANES - 16), F32)], axis=1))
    blocks += [norms[:, i : i + LANES] for i in range(0, model, LANES)]
    if len(blocks) % 2:
        blocks.append(jnp.zeros((8, LANES), F32))
    misc[...] = jnp.zeros(misc.shape, BF16)
    misc[: 8 * len(blocks), :] = jnp.concatenate(blocks, axis=0).astype(BF16)
    need("ht0", "ht1")
    step_grad = turned_small(mm(b.ht0[...], dt[0]) + mm(b.ht1[...], dt[1])).astype(BF16)
    for i in range(0, model, LANES):
        place = 8 * len(blocks) + 16 * (i // LANES)
        misc[place : place + 16, :] = step_grad[:, i : i + LANES]
    made.add((SHARED, MISC_AT))
    tick(max(0.0, len(order) + 2 - clock[0]))
    got_ff.wait()
    need("ff")
    layer_out[...] = (b.ff[...] + ff_got[...].astype(F32)).astype(BF16)
    got_db.wait_send()
    tick(1e6)
    for wait in sending.values():
        wait()
    for devices, wait in ends:
        if devices is None:
            wait()
        else:
            pl.when(devices)(wait)


def back_call(smalls, bigs, dh2_peer, ff_peer, widths, width, pace=0.68):
    rows, (seq_len, model) = bigs["h2t0"].shape[0], dh2_peer.shape
    order = chunk_order(widths)
    columns = sum(item[2] for item in order)
    ones = sum(item[2] for item in order if item[3] == "P")
    count = len(order)
    half, quarter = rows // 2, rows // 4
    ssm_pad, att_pad = bigs["x0"].shape[1], bigs["q0"].shape[1]
    anywhere, vmem = pl.BlockSpec(memory_space=pl.ANY), pl.BlockSpec(memory_space=pltpu.VMEM)
    outs = [shaped((rows, w), BF16) for w in widths] + [shaped((rows, SHARED_WIDTH), BF16), shaped((seq_len, model))]
    outs.append(shaped((seq_len, model), BF16))
    scratch = [pltpu.VMEM(array.shape, array.dtype) for array in bigs.values()]
    both = 2 * seq_len
    scratch += [
        pltpu.VMEM((both, model), BF16),
        pltpu.VMEM((2, 16, seq_len), F32), pltpu.VMEM((2, 16, seq_len), F32),
        pltpu.VMEM((2, seq_len, att_pad), BF16), pltpu.VMEM((2, seq_len, ssm_pad), BF16),
        pltpu.VMEM((both, att_pad), BF16), pltpu.VMEM((both, LANES), BF16), pltpu.VMEM((both, ssm_pad), BF16),
        pltpu.VMEM((both, ssm_pad), BF16), pltpu.VMEM((both, 2 * STATE), BF16), pltpu.VMEM((2, seq_len, 16), BF16),
        pltpu.VMEM((seq_len, model), F32), pltpu.VMEM((seq_len, model), BF16), pltpu.VMEM((seq_len, model), BF16),
        pltpu.VMEM((seq_len, model), BF16),
        pltpu.VMEM((2, 8, ssm_pad), F32), pltpu.VMEM((2, 8, 2 * STATE), F32), pltpu.VMEM((2, 8, 16), F32),
        pltpu.VMEM((rows, LANES), BF16), pltpu.VMEM((SLOTS, half, 2 * LANES), BF16),
        pltpu.VMEM((half, columns), BF16), pltpu.VMEM((half, columns), BF16),
        pltpu.VMEM((quarter, columns), BF16), pltpu.VMEM((quarter, ones), BF16),
        pltpu.VMEM((half, columns - ones), BF16), pltpu.VMEM((quarter, columns), BF16),
        pltpu.SemaphoreType.DMA((len(bigs),)), pltpu.SemaphoreType.DMA((count,)),
        pltpu.SemaphoreType.DMA((6,)), pltpu.SemaphoreType.DMA((6,)),
        pltpu.SemaphoreType.DMA((9, count)), pltpu.SemaphoreType.DMA((9, count)),
    ]
    return pl.pallas_call(
        functools.partial(
            back_kernel, small_names=tuple(smalls), big_names=tuple(bigs), widths=tuple(widths), width=width,
            pace=pace,
        ),
        out_shape=outs,
        in_specs=[vmem] * len(smalls) + [anywhere] * (len(bigs) + 2),
        out_specs=[anywhere] * (PARTS + 1) + [vmem] * 2,
        scratch_shapes=scratch,
        compiler_params=pltpu.CompilerParams(
            collective_id=0, has_side_effects=True, vmem_limit_bytes=REDUCE_LIMIT
        ),
        name="back_and_reduce",
    )(*smalls.values(), *bigs.values(), dh2_peer, ff_peer)


FORMS = ("wt", "cxb", "cbb", "gain", "skip", "bias", "rate", "bias_col", "rate_col")


def write_forms(raw, forms):
    for form, source in ((forms.cxb, raw.cxb), (forms.cbb, raw.cbb), (forms.gain, raw.gain)):
        form[...] = source[...].reshape(form.shape)
    heads = raw.bias.shape[0]
    for form, column, values in (
        (forms.bias, forms.bias_col, raw.bias[...].reshape(1, heads)),
        (forms.rate, forms.rate_col, jnp.exp(raw.decay[...].reshape(1, heads))),
    ):
        form[...] = jnp.zeros(form.shape, F32)
        form[:, :heads] = values
        column[...] = jnp.sum(unit_matrix(16) * form[...], axis=1, keepdims=True)
    skip = raw.skip[...].reshape(1, heads)
    first = lane_ids((1, LANES)) < HEAD_DIM
    for pair in range(heads // 2):
        lanes = slice(pair * LANES, (pair + 1) * LANES)
        forms.skip[:, lanes] = jnp.where(first, skip[:, 2 * pair : 2 * pair + 1], skip[:, 2 * pair + 1 : 2 * pair + 2])
    chosen = jnp.where(row_ids((16, heads)) == lane_ids((16, heads)), 1.0, 0.0).astype(BF16)
    forms.wt[...] = mm(chosen, raw.step[...]).astype(BF16)


def turned_low(values):
    return values.astype(F32).T.astype(BF16)


def front_kernel(*refs, small_names, raw_names, big_names, out_names, tiny_names, width):
    it = iter(refs)
    len_ref = next(it)
    s = Names({name: next(it) for name in small_names})
    raw = Names({name: next(it) for name in raw_names})
    big_in = Names({name: next(it) for name in big_names})
    outs = Names({name: next(it) for name in out_names})
    tiny = Names({name: next(it) for name in tiny_names})
    b = Names({name: next(it) for name in big_names})
    o = Names({name: next(it) for name in out_names})
    (h, h2, att, ssm, hid, dhid, ssp, ssr, part_own, part_peer, part_got, in_sem, out_sem, xs, xr) = it
    seq_len, model = part_own.shape
    s.update({name: tiny[name] for name in FORMS})
    side = lax.axis_index("tensor")
    pair = dict(tensor=1 - side)
    loads = {}
    for index, name in enumerate(big_names):
        loads[name] = pltpu.make_async_copy(big_in[name], b[name], in_sem.at[index])
        loads[name].start()
    barrier = pltpu.get_barrier_semaphore()
    pl.semaphore_signal(barrier, inc=1, device_id=pair, device_id_type=MESH)
    pl.semaphore_wait(barrier, 1)
    ready, stores = set(), []

    def need(*names):
        for name in names:
            if name not in ready:
                loads[name].wait()
                ready.add(name)

    def emit(*names):
        for name in names:
            store = pltpu.make_async_copy(o[name], outs[name], out_sem.at[out_names.index(name)])
            store.start()
            stores.append(store)

    def exchange(src, dst, slot):
        copy = pltpu.make_async_remote_copy(
            src_ref=src, dst_ref=dst, send_sem=xs.at[slot], recv_sem=xr.at[slot], device_id=pair,
            device_id_type=MESH,
        )
        copy.start()
        return copy

    tiny.len0[...] = jnp.full((8, LANES), len_ref[0], jnp.int32)
    need("tok")
    x = b.tok[...].astype(F32)
    inv1 = lax.rsqrt(jnp.mean(x * x, axis=1, keepdims=True) + EPSILON)
    tiny.inv1[...] = inv1
    xhat = x * inv1
    o.xhat[...] = xhat
    h[0] = (xhat * s.gain1[...]).astype(BF16)
    got_h = exchange(h.at[0], h.at[1], 0)
    got_len = exchange(tiny.len0, tiny.len1, 1)
    emit("xhat")
    need("cot")
    cot = b.cot[...]
    o.ct0[...] = jnp.where(row_ids((seq_len, 1)) < len_ref[0], cot.astype(F32), 0.0).astype(BF16)
    emit("ct0")
    write_forms(raw, tiny)
    need("w_key", "w_value")
    key, value = b.w_key[...].astype(F32), b.w_value[...].astype(F32)
    key = jnp.where(side == 0, key, pltpu.roll(key, HEAD_DIM, 1))
    value = jnp.where(side == 0, pltpu.roll(value, HEAD_DIM, 1), value)
    o.wkv[...] = jnp.where(lane_ids(key.shape) < HEAD_DIM, key, value).astype(BF16)
    emit("wkv")

    def mixer(k):
        need("wz", "wx", "wb", "wc", "wq")
        mixer_forward_kernel(
            Entry(tiny[f"len{k}"]), h.at[k], b.wq, o.wkv, b.wz, b.wx, b.wb, b.wc, s.wt, s.cxw,
            s.cxb, s.cbw, s.cbb, s.bias, s.rate, s.bias_col, s.rate_col, s.skip, s.cos,
            s.sa, s.sb, o[f"q{k}"], o[f"kd{k}"], o[f"vd{k}"], o[f"z{k}"], o[f"x{k}"], o[f"bcp{k}"], o[f"bc{k}"],
            tiny[f"tp{k}"], tiny[f"tpr{k}"], o[f"y{k}"], ssp.at[k],
        )
        emit(f"q{k}", f"kd{k}", f"vd{k}", f"z{k}", f"x{k}", f"bcp{k}", f"bc{k}", f"y{k}")
        return exchange(ssp.at[k], ssr.at[1 - k], 2 + k)

    def attend(k):
        attend_kernel(Entry(tiny[f"len{k}"]), o[f"q{k}"], o[f"kd{k}"], o[f"vd{k}"], att.at[k])

    def project(k, part, **split):
        need("wa", "ws")
        out_kernel(
            att.at[k], o[f"y{k}"], o[f"x{k}"], o[f"z{k}"], tiny[f"ss{k}"], s.cxw, s.cxb, s.skip, s.gain,
            b.wa, b.ws, part, ssm.at[k], width=width, **split,
        )

    def turn_mix(k):
        width_att = att.shape[2]
        o[f"mix{k}"][:width_att, :] = turned_low(att[k])
        o[f"mix{k}"][width_att:, :] = turned_low(ssm[k])
        emit(f"mix{k}")

    blocks = [slice(first, min(first + 256, hid.shape[1])) for first in range(0, hid.shape[1], 256)]

    def hidden_grad(k):
        need("wd")
        for lanes in blocks:
            dhid[k, :, lanes] = mm_nt(o[f"ct{k}"][...], b.wd[lanes, :]).astype(BF16)

    def feed(k, base):
        need("wg", "wu", "wd")
        values = h2[k]
        for lanes in blocks:
            gate, up = mm(values, b.wg[:, lanes]), mm(values, b.wu[:, lanes])
            d_hidden = dhid[k, :, lanes].astype(F32)
            sg = sigmoid(gate)
            silu = gate * sg
            hidden = silu * up
            hid[:, lanes] = hidden.astype(BF16)
            o[f"hid{k}"][lanes, :] = hidden.T.astype(BF16)
            o[f"dg{k}"][:, lanes] = (d_hidden * up * (sg * (1.0 + gate * (1.0 - sg)))).astype(BF16)
            o[f"du{k}"][:, lanes] = (d_hidden * silu).astype(BF16)
        emit(f"dg{k}", f"du{k}", f"hid{k}")
        dh, ff = (o.dh2, o.ff) if k == 0 else (o.dh2p, o.ffp)
        dh[...] = (mm_nt(o[f"dg{k}"][...], b.wg[...]) + mm_nt(o[f"du{k}"][...], b.wu[...])).astype(dh.dtype)
        ff_part = mm(hid[...], b.wd[...])
        ff[...] = (ff_part if base is None else ff_part + base).astype(ff.dtype)
        emit(*(("dh2", "ff") if k == 0 else ("dh2p", "ffp")))

    got_first = mixer(0)
    attend(0)
    o.ht0[...] = turned_low(h[0])
    emit("ht0")
    got_h.wait()
    got_len.wait()
    upper, lower = slice(0, seq_len // 2), slice(seq_len // 2, seq_len)
    got_ct = [exchange(o.ct0.at[upper], o.ct1.at[upper], 4)]
    got_second = mixer(1)
    got_ct.append(exchange(o.ct0.at[lower], o.ct1.at[lower], 9))
    attend(1)
    got_first.wait()
    got_second.wait()
    for k in range(2):
        tiny[f"ss{k}"][...] = ssp[k] + ssr[k]
    got_part = []

    def send_part(index, rows):
        got_part.append(exchange(part_peer.at[rows], part_got.at[rows], 5 + index))

    project(1, part_peer, splits=2, send=send_part)
    project(0, part_own)
    hidden_grad(0)
    got_h2, size = [], seq_len // 2
    for index in range(2):
        if index == 1:
            o.ht1[...] = turned_low(h[1])
            emit("ht1")
            turn_mix(0)
        rows = slice(index * size, (index + 1) * size)
        got_part[index].wait()
        resid = b.tok[rows, :].astype(F32) + part_own[rows, :] + part_got[rows, :].astype(F32)
        part_own[rows, :] = resid
        inv2 = lax.rsqrt(jnp.mean(resid * resid, axis=1, keepdims=True) + EPSILON)
        tiny.inv2[rows, :] = inv2
        rhat = resid * inv2
        o.rhat[rows, :] = rhat
        h2[0, rows, :] = (rhat * s.gain2[...]).astype(BF16)
        got_h2.append(exchange(h2.at[0, rows], h2.at[1, rows], 7 + index))
    emit("rhat")
    turn_mix(1)
    for copy in got_ct:
        copy.wait()
    emit("ct1")
    hidden_grad(1)
    feed(0, part_own[...])
    o.h2t0[...] = turned_low(h2[0])
    emit("h2t0")
    for copy in got_h2:
        copy.wait()
    feed(1, None)
    o.h2t1[...] = turned_low(h2[1])
    emit("h2t1")
    for store in stores:
        store.wait()


def front_call(length, smalls, raw, bigs, width):
    seq_len, model = bigs["tok"].shape
    att_pad, ssm_pad, ff_width = bigs["wq"].shape[1], bigs["wz"].shape[1], bigs["wg"].shape[1]
    outs = dict(xhat=shaped((seq_len, model)), rhat=shaped((seq_len, model)))
    outs.update(dict(dh2=shaped((seq_len, model)), ff=shaped((seq_len, model))))
    outs.update(dict(dh2p=shaped((seq_len, model), BF16), ffp=shaped((seq_len, model), BF16)))
    outs["wkv"] = shaped((model, LANES), BF16)
    tiny = dict(inv1=shaped((seq_len, 1)), inv2=shaped((seq_len, 1)))
    tiny.update(dict(
        wt=shaped((16, model), BF16), cxb=shaped((1, ssm_pad)), cbb=shaped((1, 2 * STATE)),
        gain=shaped((1, ssm_pad)), skip=shaped((1, ssm_pad)), bias=shaped((1, 16)), rate=shaped((1, 16)),
        bias_col=shaped((16, 1)), rate_col=shaped((16, 1)),
    ))
    for k in range(2):
        outs.update({f"{name}{k}": shaped((seq_len, ssm_pad)) for name in ("x", "y", "z")})
        outs.update({
            f"q{k}": shaped((seq_len, att_pad), BF16), f"kd{k}": shaped((seq_len, LANES), BF16),
            f"vd{k}": shaped((seq_len, LANES), BF16), f"bcp{k}": shaped((seq_len, 2 * STATE)),
            f"bc{k}": shaped((seq_len, 2 * STATE), BF16), f"ct{k}": shaped((seq_len, model), BF16),
            f"dg{k}": shaped((seq_len, ff_width), BF16), f"du{k}": shaped((seq_len, ff_width), BF16),
            f"hid{k}": shaped((ff_width, seq_len), BF16), f"h2t{k}": shaped((model, seq_len), BF16),
            f"ht{k}": shaped((model, seq_len), BF16), f"mix{k}": shaped((att_pad + ssm_pad, seq_len), BF16),
        })
        tiny.update({
            f"tp{k}": shaped((seq_len, 16)), f"tpr{k}": shaped((16, seq_len)), f"ss{k}": shaped((16, seq_len)),
            f"len{k}": shaped((8, LANES), jnp.int32),
        })
    anywhere, vmem = pl.BlockSpec(memory_space=pl.ANY), pl.BlockSpec(memory_space=pltpu.VMEM)
    scratch = [pltpu.VMEM(array.shape, array.dtype) for array in list(bigs.values()) + list(outs.values())]
    scratch += [
        pltpu.VMEM((2, seq_len, model), BF16), pltpu.VMEM((2, seq_len, model), BF16),
        pltpu.VMEM((2, seq_len, att_pad), BF16), pltpu.VMEM((2, seq_len, ssm_pad), BF16),
        pltpu.VMEM((seq_len, ff_width), BF16), pltpu.VMEM((2, seq_len, ff_width), BF16),
        pltpu.VMEM((2, 16, seq_len), F32), pltpu.VMEM((2, 16, seq_len), F32),
        pltpu.VMEM((seq_len, model), F32), pltpu.VMEM((seq_len, model), BF16), pltpu.VMEM((seq_len, model), BF16),
        pltpu.SemaphoreType.DMA((len(bigs),)), pltpu.SemaphoreType.DMA((len(outs),)),
        pltpu.SemaphoreType.DMA((10,)), pltpu.SemaphoreType.DMA((10,)),
    ]
    results = pl.pallas_call(
        functools.partial(
            front_kernel, small_names=tuple(smalls), raw_names=tuple(raw), big_names=tuple(bigs), out_names=tuple(outs),
            tiny_names=tuple(tiny), width=width,
        ),
        out_shape=list(outs.values()) + list(tiny.values()),
        in_specs=[pl.BlockSpec(memory_space=pltpu.SMEM)] + [vmem] * (len(smalls) + len(raw)) + [anywhere] * len(bigs),
        out_specs=[anywhere] * len(outs) + [vmem] * len(tiny),
        scratch_shapes=scratch,
        compiler_params=pltpu.CompilerParams(
            collective_id=1, has_side_effects=True, vmem_limit_bytes=REDUCE_LIMIT
        ),
        name="front",
    )(length, *smalls.values(), *raw.values(), *bigs.values())
    return Names(zip(list(outs) + list(tiny), results))


def finish_kernel(own_ref, peer_ref, own_misc_ref, peer_misc_ref, *refs, split):
    step = pl.program_id(0)
    sums, refs = refs[:7], refs[7:]
    out_ref = sums[6]
    for source, target in zip(sums[:6], refs[:6]):
        target[...] = source[...].astype(F32)
    (att_ref, ssm_ref, key_ref, value_ref, b_ref, c_ref, stp_ref, cxw_ref, cxb_ref, cbw_ref, cbb_ref, bias_ref,
     decay_ref, skip_ref, sgain_ref, norm_ref, ffn_ref) = refs[6:]

    @pl.when(step < split)
    def _():
        att_ref[...] = out_ref[...].astype(F32)

    @pl.when(step >= split)
    def _():
        ssm_ref[...] = out_ref[...].astype(F32)

    even = lax.axis_index("tensor") == 0
    kv, kv_peer = own_ref[:, :LANES].astype(F32), peer_ref[:, :LANES].astype(F32)
    low, high = jnp.where(even, kv, kv_peer), jnp.where(even, kv_peer, kv)
    first = lane_ids(kv.shape) < HEAD_DIM
    key_ref[...] = jnp.where(first, low, pltpu.roll(high, HEAD_DIM, 1))
    value_ref[...] = jnp.where(first, pltpu.roll(low, HEAD_DIM, 1), high)
    for ref, column in ((b_ref, B_AT), (c_ref, C_AT)):
        lanes = slice(column, column + LANES)
        ref[...] = own_ref[:, lanes].astype(F32) + peer_ref[:, lanes].astype(F32)
    @pl.when(step == 0)
    def _():
        wide_blocks, model_blocks = cxw_ref.shape[1] // LANES, norm_ref.shape[0] // LANES
        mine = own_misc_ref[...].astype(F32)
        both = mine + peer_misc_ref[...].astype(F32)

        def rows(values, block, row, length=1):
            return values[8 * block + row : 8 * block + row + length]

        def flat(values, first, blocks, row):
            parts = [rows(values, first + block, row) for block in range(blocks)]
            return jnp.concatenate(parts, axis=1).reshape(blocks * LANES)

        for block in range(wide_blocks):
            cxw_ref[:, block * LANES : (block + 1) * LANES] = rows(mine, block, 0, 4)
        for block in range(2):
            cbw_ref[:, block * LANES : (block + 1) * LANES] = rows(both, wide_blocks + block, 0, 4)
        cxb_ref[...] = flat(mine, 0, wide_blocks, 4)
        sgain_ref[...] = flat(mine, 0, wide_blocks, 6)
        cbb_ref[...] = flat(both, wide_blocks, 2, 4)
        norm_ref[...] = flat(both, wide_blocks + 3, model_blocks, 0)
        ffn_ref[...] = flat(both, wide_blocks + 3, model_blocks, 1)
        heads = bias_ref.shape[0]
        for row, ref in enumerate((bias_ref, decay_ref, skip_ref)):
            ref[...] = rows(mine, wide_blocks + 2, row)[:, :heads].reshape(heads)
        place = mine.shape[0] - 16 * model_blocks
        for block in range(model_blocks):
            values = mine[place + 16 * block : place + 16 * block + 16]
            stp_ref[:, block * LANES : (block + 1) * LANES] = values[: stp_ref.shape[0]]


def finish_call(results, peer, att_width, heads):
    model, block = results[OUT].shape[0], 256
    ssm_pad = results[ZED].shape[1]
    shared = results[SHARED]
    misc_rows = 8 * (ssm_pad // LANES + 3 + model // LANES)
    misc_rows += -misc_rows % 16 + 16 * (model // LANES)
    sums = [results[part] for part in (GATE, UP, DOWN, QUERY, ZED, EX, OUT)]
    split = att_width // block

    def by_rows(width):
        return pl.BlockSpec((block, width), lambda i: (i, 0))

    def fixed(*shape):
        return pl.BlockSpec(shape, lambda i: (0,) * len(shape))

    misc = pl.BlockSpec((misc_rows, LANES), lambda i: (0, MISC_AT // LANES))
    shapes = [(model, part.shape[1]) for part in sums[:6]]
    specs = [by_rows(part.shape[1]) for part in sums[:6]]
    shapes += [(att_width, model), (model - att_width, model)]
    specs += [
        pl.BlockSpec((block, model), lambda i: (jnp.minimum(i, split - 1), 0)),
        pl.BlockSpec((block, model), lambda i: (jnp.maximum(i - split, 0), 0)),
    ]
    shapes += [(model, LANES)] * 4
    specs += [by_rows(LANES)] * 4
    tiny = [
        (heads, model), (4, ssm_pad), (ssm_pad,), (4, 2 * STATE), (2 * STATE,), (heads,), (heads,), (heads,), (ssm_pad,),
        (model,), (model,),
    ]
    shapes += tiny
    specs += [fixed(*shape) for shape in tiny]
    return pl.pallas_call(
        functools.partial(finish_kernel, split=split),
        grid=(model // block,),
        out_shape=[shaped(shape) for shape in shapes],
        in_specs=[by_rows(SHARED_WIDTH)] * 2 + [misc] * 2 + [by_rows(part.shape[1]) for part in sums],
        out_specs=specs,
        compiler_params=pltpu.CompilerParams(vmem_limit_bytes=VMEM_LIMIT),
        name="finish",
    )(shared, peer, shared, peer, *sums)


def shaped(shape, dtype=F32):
    return jax.ShapeDtypeStruct(shape, dtype)


def whole_call(kernel, outs, scalars, args, flops, name):
    specs = [pl.BlockSpec(memory_space=pltpu.SMEM)] * scalars
    specs += [pl.BlockSpec(memory_space=pltpu.VMEM)] * (len(args) - scalars)
    moved = sum(arg.size * arg.dtype.itemsize for arg in args)
    return pl.pallas_call(
        kernel,
        out_shape=outs,
        in_specs=specs,
        out_specs=[pl.BlockSpec(memory_space=pltpu.VMEM)] * len(outs),
        compiler_params=pltpu.CompilerParams(vmem_limit_bytes=VMEM_LIMIT),
        cost_estimate=pl.CostEstimate(flops=flops, bytes_accessed=moved, transcendentals=0),
        name=name,
    )(*args)


def pad_columns(values, width):
    return jnp.pad(values, ((0, 0), (0, width - values.shape[1]))) if width != values.shape[1] else values


def pad_rows(values, height):
    return jnp.pad(values, ((0, height - values.shape[0]), (0, 0))) if height != values.shape[0] else values


def contract_rows(left, right):
    return mm_tn(jnp.concatenate(left, axis=0), jnp.concatenate(right, axis=0))


def on_device(
    tokens, lengths, cotangent, norm_gain, w_query, w_key, w_value, w_gate_z, w_ssm_x, w_ssm_b, w_ssm_c,
    w_step, conv_x_weight, conv_x_bias, conv_bc_weight, conv_bc_bias, step_bias, decay_log, skip_gain,
    ssm_norm_gain, w_out_att, w_out_ssm, ffn_norm_gain, w_gate, w_up, w_down,
):
    seq_len, model = tokens.shape
    groups = lax.axis_size("tensor")
    position = lax.axis_index("tensor")
    att_width, ssm_width = w_query.shape[1], w_gate_z.shape[1]
    att_pad = -(-att_width // LANES) * LANES
    ssm_pad = -(-ssm_width // LANES) * LANES
    ssm_heads = ssm_width // SSM_DIM
    ssm_width_all = SSM_HEADS * SSM_DIM
    ff_width = w_gate.shape[1]

    def fetch(values, shift):
        return lax.ppermute(values, "tensor", [((i + shift) % groups, i) for i in range(groups)])

    def deliver(values, shift):
        return lax.ppermute(values, "tensor", [(i, (i + shift) % groups) for i in range(groups)])

    def gather(values):
        return [values] + [fetch(values, k) for k in range(1, groups)]

    def scatter_sum(own, others):
        total = own
        for k in range(1, groups):
            total = total + deliver(others[k - 1], k).astype(F32)
        return total

    kv_head = position * (att_width // HEAD_DIM) // (HEADS // KV_HEADS)
    w_kv = jnp.concatenate(
        [lax.dynamic_slice_in_dim(w, kv_head * HEAD_DIM, HEAD_DIM, 1) for w in (w_key, w_value)], axis=1
    )
    wq = pad_columns(w_query, att_pad)
    wz, wx = pad_columns(w_gate_z, ssm_pad), pad_columns(w_ssm_x, ssm_pad)
    wt = pad_rows(w_step.T, 16)
    wa, ws = pad_rows(w_out_att, att_pad), pad_rows(w_out_ssm, ssm_pad)
    cxw, cxb = pad_columns(conv_x_weight, ssm_pad), pad_columns(conv_x_bias[None], ssm_pad)
    cbb = conv_bc_bias[None]
    gain = pad_columns(ssm_norm_gain[None], ssm_pad)
    skip = pad_columns(jnp.repeat(skip_gain, SSM_DIM)[None], ssm_pad)
    bias = pad_columns(step_bias[None], 16)
    rate = pad_columns(jnp.exp(decay_log)[None], 16)
    bias_col, rate_col = bias.T, rate.T
    half = HEAD_DIM // 2
    freqs = np.float64(ROPE_BASE) ** (-np.arange(half) * 2.0 / HEAD_DIM)
    angles = np.arange(seq_len, dtype=np.float32)[:, None] * freqs.astype(np.float32)[None, :]
    cosine, sine = np.cos(angles.astype(np.float64)), np.sin(angles.astype(np.float64))
    cos_table = jnp.asarray(np.concatenate([cosine] * 4, axis=1), F32)
    sine_first = jnp.asarray(np.concatenate([-sine, 0.0 * sine] * 2, axis=1), F32)
    sine_second = jnp.asarray(np.concatenate([0.0 * sine, sine] * 2, axis=1), F32)

    if lax.axis_size("dp") == 16 and groups == 2:
        smalls = dict(
            cxw=conv_x_weight, cbw=conv_bc_weight, cos=cos_table, sa=sine_first, sb=sine_second,
            gain1=norm_gain[None], gain2=ffn_norm_gain[None],
        )
        raw = dict(
            cxb=conv_x_bias, cbb=conv_bc_bias, gain=ssm_norm_gain, skip=skip_gain,
            bias=step_bias, decay=decay_log, step=w_step.T,
        )
        bigs = dict(
            tok=tokens, cot=cotangent, w_key=w_key, w_value=w_value, wz=w_gate_z, wx=w_ssm_x,
            wb=w_ssm_b, wc=w_ssm_c, wq=w_query, wa=w_out_att, ws=w_out_ssm, wg=w_gate, wu=w_up,
            wd=w_down,
        )
        kept = front_call(lengths, smalls, raw, bigs, ssm_width_all)
        wq, wz, wx, wa, ws = w_query, w_gate_z, w_ssm_x, w_out_att, w_out_ssm
        for name in FORMS:
            smalls[name] = kept[name]

        def both(*names):
            return {f"{name}{k}": kept[f"{name}{k}"] for k in range(2) for name in names}

        smalls.update(both("tp", "tpr", "ss", "len"))
        smalls.update(dict(inv1=kept.inv1, inv2=kept.inv2))
        order = both("h2t", "dg")
        order.update(dict(dh2=kept.dh2, rhat=kept.rhat))
        order.update(both("du", "hid", "ct"))
        order.update(dict(wa=wa, ws=ws))
        order.update(both("y", "x", "z", "q", "kd", "vd"))
        order.update(dict(wq=wq, wkv=kept.wkv, wz=wz, wx=wx, wb=w_ssm_b, wc=w_ssm_c))
        order.update(both("bcp", "bc", "mix", "ht"))
        order.update(dict(xhat=kept.xhat, ff=kept.ff))
        widths = (ff_width, ff_width, model, SHARED_WIDTH, att_pad, ssm_pad, ssm_pad, model)
        results = back_call(smalls, order, kept.dh2p, kept.ffp, widths, ssm_width_all)
        peer, grad_input, layer_output = results[PARTS:]
        (grad_gate, grad_up, grad_down, grad_q, grad_z, grad_x, grad_att, grad_ssm, grad_key, grad_value, grad_b,
         grad_c, grad_step, grad_cxw, grad_cxb, grad_cbw, grad_cbb, grad_bias, grad_decay, grad_skip, grad_sgain,
         grad_norm_gain, grad_ffn_gain) = finish_call(results, peer, att_pad, ssm_heads)
        return (
            layer_output, grad_input, grad_norm_gain, grad_q, grad_key, grad_value, grad_z, grad_x, grad_b, grad_c,
            grad_step.T, grad_cxw, grad_cxb, grad_cbw, grad_cbb, grad_bias, grad_decay, grad_skip, grad_sgain, grad_att,
            grad_ssm, grad_ffn_gain, grad_gate, grad_up, grad_down,
        )

    inputs = tokens.astype(F32)
    inv1 = lax.rsqrt(jnp.mean(inputs * inputs, axis=1, keepdims=True) + EPSILON)
    h_own = (inputs * inv1 * norm_gain).astype(BF16)
    own_mask = jnp.arange(seq_len) < lengths[0]
    ct_own = jnp.where(own_mask[:, None], cotangent, jnp.zeros_like(cotangent))
    h_all = gather(h_own)
    len_all = gather(lax.optimization_barrier((lengths, h_own))[0])
    ct_all = gather(lax.optimization_barrier((ct_own, h_all[1]))[0] if groups > 1 else ct_own)

    def forward(k):
        outs = [
            shaped((seq_len, att_pad), BF16), shaped((seq_len, LANES), BF16), shaped((seq_len, LANES), BF16),
            shaped((seq_len, ssm_pad)), shaped((seq_len, ssm_pad)), shaped((seq_len, 2 * STATE)),
            shaped((seq_len, 2 * STATE), BF16), shaped((seq_len, 16)), shaped((16, seq_len)),
            shaped((seq_len, ssm_pad)), shaped((16, seq_len)),
        ]
        args = [
            len_all[k], h_all[k], wq, w_kv, wz, wx, w_ssm_b, w_ssm_c, wt, cxw, cxb, conv_bc_weight, cbb,
            bias, rate, bias_col, rate_col, skip, cos_table, sine_first, sine_second,
        ]
        return whole_call(mixer_forward_kernel, outs, 1, args, 8 * 10**9, "mixer_forward")

    def attend(k):
        q, kd, vd = kept[k][:3]
        return whole_call(
            attend_kernel, [shaped((seq_len, att_pad), BF16)], 1, [len_all[k], q, kd, vd], 2 * 10**9, "attend"
        )[0]

    kept = [forward(k) for k in range(groups)]
    squares_part = [one[10] for one in kept]
    squares = [squares_part[k] for k in range(groups)]
    for shift in range(1, groups):
        for k in range(groups):
            squares[k] = squares[k] + fetch(squares_part[(k - shift) % groups], shift)
    mix_att = [attend(k) for k in range(groups)]

    def project(k, dtype):
        q, kd, vd, z, x, bcp, bc, tp, tpr, y, _ = kept[k]
        return whole_call(
            functools.partial(out_kernel, width=ssm_width_all),
            [shaped((seq_len, model), dtype), shaped((seq_len, ssm_pad), BF16)],
            0,
            [mix_att[k], y, x, z, squares[k], cxw, cxb, skip, gain, wa, ws],
            4 * 10**9,
            "out_project",
        )

    projected = [project(k, F32 if k == 0 else BF16) for k in range(groups)]
    mix_ssm = [one[1] for one in projected]
    branch = scatter_sum(projected[0][0], [one[0] for one in projected[1:]])
    resid = inputs + branch
    inv2 = lax.rsqrt(jnp.mean(resid * resid, axis=1, keepdims=True) + EPSILON)
    h2_own = (resid * inv2 * ffn_norm_gain).astype(BF16)
    h2_all = gather(h2_own)

    def feed(k, rows2):
        dtype = F32 if k == 0 else BF16
        block = min(256, ff_width)
        full = pl.BlockSpec((seq_len, model), lambda i: (0, 0))
        columns = pl.BlockSpec((model, block), lambda i: (0, i))
        rows = pl.BlockSpec((block, model), lambda i: (i, 0))
        tall = pl.BlockSpec((seq_len, block), lambda i: (0, i))
        return pl.pallas_call(
            ffn_kernel,
            grid=(ff_width // block,),
            out_shape=[shaped((ff_width, seq_len), BF16)] + [shaped((seq_len, ff_width), BF16)] * 2
            + [shaped((seq_len, model), dtype)] * 2 + [shaped((model, seq_len), BF16)],
            in_specs=[full, full, columns, columns, rows] + ([full] if k == 0 else []),
            out_specs=[pl.BlockSpec((block, seq_len), lambda i: (i, 0))] + [tall] * 2 + [full] * 2
            + [pl.BlockSpec((model, seq_len), lambda i: (0, 0))],
            scratch_shapes=[pltpu.VMEM((seq_len, model), F32)] * 2,
            compiler_params=pltpu.CompilerParams(vmem_limit_bytes=VMEM_LIMIT),
            cost_estimate=pl.CostEstimate(flops=8 * 10**9, bytes_accessed=10**7, transcendentals=0),
            name="feed_forward",
        )(rows2, ct_all[k], w_gate, w_up, w_down, *([resid] if k == 0 else []))

    fed = [feed(0, h2_own)]
    for k in range(1, groups):
        fed.append(feed(k, lax.optimization_barrier((h2_all[k], fed[0][0]))[0]))
    d_second = scatter_sum(fed[0][4], [one[4] for one in fed[1:]])
    layer_output = scatter_sum(fed[0][3], [one[3] for one in fed[1:]]).astype(BF16)
    h2_turned = jnp.concatenate([one[5] for one in fed], axis=1)
    grad_gate = mm(h2_turned, jnp.concatenate([one[1] for one in fed], axis=0))
    grad_up = mm(h2_turned, jnp.concatenate([one[2] for one in fed], axis=0))
    grad_down = mm(jnp.concatenate([one[0] for one in fed], axis=1), jnp.concatenate(ct_all, axis=0))
    scaled = d_second * ffn_norm_gain
    d_resid = (
        ct_own.astype(F32)
        + inv2 * scaled
        - resid * (inv2**3) * jnp.mean(scaled * resid, axis=1, keepdims=True)
    )
    grad_ffn_gain = jnp.sum(d_second * resid * inv2, axis=0)
    db_all = gather(d_resid.astype(BF16))

    def mix_grad(k):
        q, kd, vd, z, x, bcp, bc, tp, tpr, y, _ = kept[k]
        return whole_call(
            mix_grad_kernel,
            [shaped((seq_len, att_pad), BF16), shaped((seq_len, ssm_pad), BF16), shaped((16, seq_len))],
            0,
            [db_all[k], y, x, z, cxw, cxb, skip, gain, wa, ws],
            4 * 10**9,
            "mix_grad",
        )

    mixed = [mix_grad(k) for k in range(groups)]
    backs_part = [one[2] for one in mixed]
    backs = [backs_part[k] for k in range(groups)]
    for shift in range(1, groups):
        for k in range(groups):
            backs[k] = backs[k] + fetch(backs_part[(k - shift) % groups], shift)

    def attend_back(k):
        q, kd, vd = kept[k][:3]
        return whole_call(
            attend_back_kernel,
            [shaped((seq_len, att_pad), BF16), shaped((seq_len, LANES), BF16)],
            1,
            [len_all[k], q, kd, vd, mixed[k][0], cos_table, sine_first, sine_second],
            4 * 10**9,
            "attend_back",
        )

    turned = [attend_back(k) for k in range(groups)]

    def backward(k):
        q, kd, vd, z, x, bcp, bc, tp, tpr, y, _ = kept[k]
        outs = [
            shaped((seq_len, model), F32 if k == 0 else BF16), shaped((seq_len, ssm_pad), BF16),
            shaped((seq_len, ssm_pad), BF16), shaped((seq_len, 2 * STATE), BF16), shaped((seq_len, 16), BF16),
            shaped((8, ssm_pad)), shaped((8, 2 * STATE)), shaped((8, 16)),
        ]
        args = [
            len_all[k], mixed[k][1], y, x, z, bcp, bc, tp, tpr, squares[k], backs[k], turned[k][0], turned[k][1],
            wq, w_kv, wz, wx, w_ssm_b, w_ssm_c, wt, cxw, cxb, conv_bc_weight, cbb, bias, rate, bias_col, rate_col,
            skip, gain,
        ]
        return whole_call(
            functools.partial(mixer_back_kernel, width=ssm_width_all), outs, 1, args, 16 * 10**9, "mixer_back"
        )

    gone = [None] * groups
    for k in list(range(1, groups)) + [0]:
        gone[k] = backward(k)
    d_first = scatter_sum(gone[0][0], [one[0] for one in gone[1:]])
    grad_norm_gain = jnp.sum(d_first * inputs * inv1, axis=0)

    wide, bcg, small = (sum(one[i] for one in gone) for i in (5, 6, 7))
    grad_q = contract_rows(h_all, [one[0] for one in turned])
    grad_kv = contract_rows(h_all, [one[1] for one in turned])
    grad_bc = contract_rows(h_all, [one[3] for one in gone])
    grad_x = contract_rows(h_all, [one[1] for one in gone])
    grad_z = contract_rows(h_all, [one[2] for one in gone])
    grad_step = contract_rows(h_all, [one[4] for one in gone])
    grad_att = contract_rows(mix_att, db_all)
    grad_ssm = contract_rows(mix_ssm, db_all)
    norms = jnp.concatenate([bcg[:5].reshape(-1), grad_norm_gain, grad_ffn_gain])
    zeros = jnp.zeros((model, KV_HEADS * HEAD_DIM), F32)
    grad_key = lax.dynamic_update_slice(zeros, grad_kv[:, :HEAD_DIM], (0, kv_head * HEAD_DIM))
    grad_value = lax.dynamic_update_slice(zeros, grad_kv[:, HEAD_DIM:], (0, kv_head * HEAD_DIM))
    grad_key, grad_value, grad_bc, norms = lax.psum((grad_key, grad_value, grad_bc, norms), ("dp", "tensor"))
    grad_b, grad_c = grad_bc[:, :STATE], grad_bc[:, STATE:]
    grad_q, grad_z, grad_x, grad_step, grad_att, grad_ssm, wide, small = (
        lax.psum(part.astype(BF16), "dp").astype(F32)
        for part in (grad_q, grad_z, grad_x, grad_step, grad_att, grad_ssm, wide, small)
    )
    grad_gate, grad_up, grad_down = (
        lax.psum(part.astype(BF16), "dp").astype(F32) for part in (grad_gate, grad_up, grad_down)
    )
    grad_step = grad_step[:, :ssm_heads]
    grad_cxw, grad_cxb, grad_sgain = wide[:4], wide[4:5], wide[6:7]
    bcg = norms[: 10 * STATE].reshape(5, 2 * STATE)
    grad_cbw, grad_cbb = bcg[:4], bcg[4:]
    grad_bias, grad_decay, grad_skip = small[0:1, :ssm_heads], small[1:2, :ssm_heads], small[2:3, :ssm_heads]
    grad_norm_gain = norms[10 * STATE : 10 * STATE + model]
    grad_ffn_gain = norms[10 * STATE + model :]

    scaled = d_first * norm_gain
    grad_input = d_resid + inv1 * scaled - inputs * (inv1**3) * jnp.mean(scaled * inputs, axis=1, keepdims=True)

    return (
        layer_output,
        grad_input,
        grad_norm_gain.reshape(-1),
        grad_q[:, :att_width],
        grad_key,
        grad_value,
        grad_z[:, :ssm_width],
        grad_x[:, :ssm_width],
        grad_b,
        grad_c,
        grad_step,
        grad_cxw[:, :ssm_width],
        grad_cxb.reshape(-1)[:ssm_width],
        grad_cbw,
        grad_cbb.reshape(-1),
        grad_bias.reshape(-1),
        grad_decay.reshape(-1),
        grad_skip.reshape(-1),
        grad_sgain.reshape(-1)[:ssm_width],
        grad_att[:att_width],
        grad_ssm[:ssm_width],
        grad_ffn_gain.reshape(-1),
        grad_gate,
        grad_up,
        grad_down,
    )


def solution(mesh):
    rows, split, tall = P(("dp", "tensor"), None), P(None, "tensor"), P("tensor", None)
    vector, copied = P("tensor"), P()
    return jax.shard_map(
        on_device,
        mesh=mesh,
        in_specs=(
            rows, P(("dp", "tensor")), rows, copied, split, copied, copied, split, split, copied, copied, split,
            split, vector, copied, copied, vector, vector, vector, vector, tall, tall, copied, split, split, tall,
        ),
        out_specs=(
            rows, rows, copied, split, copied, copied, split, split, copied, copied, split, split, vector, copied,
            copied, vector, vector, vector, vector, tall, tall, copied, split, split, tall,
        ),
        check_vma=False,
    )
```
